32 devices in a mesh: dp: 16 (over z, y, core), chan: 2 (over x).
Axes of the slice: x: 2, y: 2, z: 4, core: 2. Of those that a mesh axis runs over, the one named last changes fastest.
Arguments:
- patches: bfloat16 [16, 1600, 192], P('dp'), may hold values from -6 to 6
- labels: int32 [16, 1600], P('dp'), may hold values from 0 to 18
- offset_target: float32 [16, 2, 1600], P('dp'), may hold values from -8 to 8
- offset_valid: int32 [16, 1600], P('dp'), may hold values 0 or 1
- depth_target: float32 [16, 1600], P('dp'), may hold values from 0.2 to 2
- lidar_valid: int32 [16, 1600], P('dp'), may hold values from 0 to 1
- crop_mask: int32 [16, 1600], P('dp'), may hold values from 0 to 1, as said below
- stem_weight: float32 [192, 2, 1024], P(None, 'chan', 'dp'), may hold values from -0.4375 to 0.4375
- stem_first: float32 [192, 2, 1024], P(None, 'chan', 'dp'), may hold values from -2.3841858e-06 to 2.3841858e-06
- stem_second: float32 [192, 2, 1024], P(None, 'chan', 'dp'), may hold values from 2.4518851e-14 to 9.8075404e-14
- bottle_weight: float32 [2, 2048, 512], P(None, 'dp', 'chan'), may hold values from -0.125 to 0.125
- bottle_first: float32 [2, 2048, 512], P(None, 'dp', 'chan'), may hold values from -6.67572e-06 to 6.67572e-06
- bottle_second: float32 [2, 2048, 512], P(None, 'dp', 'chan'), may hold values from 1.9155352e-13 to 7.662141e-13
- middle_weight: float32 [9, 512, 512], P(None, 'dp', 'chan'), may hold values from -0.09375 to 0.09375
- middle_first: float32 [9, 512, 512], P(None, 'dp', 'chan'), may hold values from -5.722046e-06 to 5.722046e-06
- middle_second: float32 [9, 512, 512], P(None, 'dp', 'chan'), may hold values from 1.5324282e-13 to 6.1297126e-13
- pyramid_weight: float32 [29, 2048, 256], P(None, 'dp', 'chan'), may hold values from -0.078125 to 0.078125
- pyramid_first: float32 [29, 2048, 256], P(None, 'dp', 'chan'), may hold values from -3.0517578e-05 to 3.0517578e-05
- pyramid_second: float32 [29, 2048, 256], P(None, 'dp', 'chan'), may hold values from 2.451885e-12 to 3.923016e-11
- project_weight: float32 [5, 256, 256], P(None, 'chan', 'dp'), may hold values from -0.15625 to 0.15625
- project_first: float32 [5, 256, 256], P(None, 'chan', 'dp'), may hold values from -3.0517578e-05 to 3.0517578e-05
- project_second: float32 [5, 256, 256], P(None, 'chan', 'dp'), may hold values from 2.451885e-12 to 3.923016e-11
- head_weight: float32 [256, 22], P('dp'), may hold values from -0.375 to 0.375
- head_first: float32 [256, 22], P('dp'), may hold values from -3.0517578e-05 to 3.0517578e-05
- head_second: float32 [256, 22], P('dp'), may hold values from 2.451885e-12 to 3.923016e-11
- norm_gains: float32 [2, 2, 1280], P(None, 'chan'), may hold values from 0.5 to 1.5
- norm_first: float32 [2, 2, 1280], P(None, 'chan'), may hold values from -3.0517578e-05 to 3.0517578e-05
- norm_second: float32 [2, 2, 1280], P(None, 'chan'), may hold values from 2.451885e-12 to 3.923016e-11
- task_params: float32 [25], replicated, may hold values from -1 to 1
- task_first: float32 [25], replicated, may hold values from -3.0517578e-05 to 3.0517578e-05
- task_second: float32 [25], replicated, may hold values from 2.451885e-12 to 3.923016e-11
Outputs:
- total_loss: float32 [], replicated
- grad_norm: float32 [], replicated
- new_stem: float32 [192, 2, 1024], P(None, 'chan', 'dp')
- new_stem_first: float32 [192, 2, 1024], P(None, 'chan', 'dp')
- new_stem_second: float32 [192, 2, 1024], P(None, 'chan', 'dp')
- new_bottle: float32 [2, 2048, 512], P(None, 'dp', 'chan')
- new_bottle_first: float32 [2, 2048, 512], P(None, 'dp', 'chan')
- new_bottle_second: float32 [2, 2048, 512], P(None, 'dp', 'chan')
- new_middle: float32 [9, 512, 512], P(None, 'dp', 'chan')
- new_middle_first: float32 [9, 512, 512], P(None, 'dp', 'chan')
- new_middle_second: float32 [9, 512, 512], P(None, 'dp', 'chan')
- new_pyramid: float32 [29, 2048, 256], P(None, 'dp', 'chan')
- new_pyramid_first: float32 [29, 2048, 256], P(None, 'dp', 'chan')
- new_pyramid_second: float32 [29, 2048, 256], P(None, 'dp', 'chan')
- new_project: float32 [5, 256, 256], P(None, 'chan', 'dp')
- new_project_first: float32 [5, 256, 256], P(None, 'chan', 'dp')
- new_project_second: float32 [5, 256, 256], P(None, 'chan', 'dp')
- new_head: float32 [256, 22], P('dp')
- new_head_first: float32 [256, 22], P('dp')
- new_head_second: float32 [256, 22], P('dp')
- new_norm: float32 [2, 2, 1280], P(None, 'chan')
- new_norm_first: float32 [2, 2, 1280], P(None, 'chan')
- new_norm_second: float32 [2, 2, 1280], P(None, 'chan')
- new_task: float32 [25], replicated
- new_task_first: float32 [25], replicated
- new_task_second: float32 [25], replicated
The draws below stay inside these ranges and needn't reach their ends.
Inputs may be any that keep to these rules, and one draw needn't show every extreme that they name: `crop_mask`: each image's mask is 1 on all positions or on exactly the positions of the first half of its 40 canvas rows.
All inputs are finite; a program needn't handle non-finite values. No bound on the sum of `offset_valid` on one device may be relied on, other than what follows from the above.
Results may differ from the reference program's by a relative error of at most 0.017.
Values may be sent and summed in bfloat16 or wider, within the bound.
A program may use at most 256 MiB of HBM per device.

```python
import math
import jax
import jax.numpy as jnp
from jax import lax

D = 2048
MID = 512
BRANCH = 256
CLASSES = 19
PATCH = 192
NOUT = 22
FH = 40
FW = 40
STEP = 10
IMAGES = 16
POSITIONS = 1600
MID_SHARD = 256
D_SHARD = 1024
NPARAMS = 20392473
N_CHAN = 2


def draw_crop_mask(key, part):
    index_list = jnp.arange(IMAGES)
    level = 30 + 40 * index_list // max(IMAGES - 1, 1)
    whole = jax.random.randint(key, (IMAGES,), 0, 100) < level
    canvas_row = jnp.arange(FH * FW) // FW
    upper = (canvas_row < FH // 2).astype(jnp.int32)
    return jnp.where(whole[:, None], jnp.ones((IMAGES, FH * FW), jnp.int32), upper[None, :]).astype(jnp.int32)


def draw_lidar_valid(key, part):
    index_list = jnp.arange(IMAGES)
    level = 200 + 600 * index_list // max(IMAGES - 1, 1)
    draws = jax.random.randint(jax.random.fold_in(key, 7), (IMAGES, FH * FW), 0, 1000)
    return (draws < level[:, None]).astype(jnp.int32)


def with_ends(entries, rng, low, top_value):
    place = [jax.random.randint(jax.random.fold_in(rng, axis), (), 0, length) for axis, length in enumerate(entries.shape)]
    widest = entries.shape.index(max(entries.shape))
    next_to = place[:widest] + [(place[widest] + 1) % entries.shape[widest]] + place[widest + 1:]
    return entries.at[tuple(place)].set(low).at[tuple(next_to)].set(top_value)


def block_levels(own_key, shape, split, least, top_value):
    level, own = 1.0, jax.random.fold_in(own_key, 6)
    for position, blocks in split:
        steps = jnp.exp(jax.random.uniform(jax.random.fold_in(own, position), (blocks,), jnp.float32, least / len(split), top_value / len(split)))
        level = level * jnp.repeat(steps, shape[position] // blocks).reshape([-1 if axis == position else 1 for axis in range(len(shape))])
    return level


def gaussian(rng, shape, scale, most, shards=(), dtype=jnp.bfloat16):
    loudness = block_levels(rng, shape, shards, -0.22, 0.18) if shards else 1.0
    result = jax.random.normal(rng, shape, jnp.float32) * scale * loudness
    return jnp.minimum(jnp.maximum(result, -most), most).astype(dtype)


def setup_inputs(seed: int = 0) -> dict:
    streams_of = jax.random.split(jax.random.key(seed), 32)
    patches = gaussian(streams_of[0], (IMAGES, POSITIONS, PATCH), 1.0, 6.0, ((0, 16),))
    labels = with_ends(jax.random.randint(streams_of[1], (IMAGES, POSITIONS), 0, CLASSES), jax.random.fold_in(streams_of[1], 1), 0, CLASSES - 1).astype(jnp.int32)
    offset_target = gaussian(streams_of[2], (IMAGES, 2, POSITIONS), 1.5, 8.0, ((0, 16),), jnp.float32)
    offset_valid = with_ends((jax.random.randint(streams_of[3], (IMAGES, POSITIONS), 0, 3) < 2).astype(jnp.int32), jax.random.fold_in(streams_of[3], 1), 0, 1)
    depth_target = jnp.clip(0.2 + 1.8 * jax.random.uniform(streams_of[4], (IMAGES, POSITIONS), jnp.float32) ** block_levels(streams_of[4], (IMAGES, POSITIONS), ((0, 16),), -0.2, 0.2), 0.2, 2.0)
    lidar_valid = draw_lidar_valid(jax.random.fold_in(streams_of[31], 71), 0)
    crop_mask = draw_crop_mask(jax.random.fold_in(streams_of[31], 71), 0)
    stem_weight = gaussian(streams_of[7], (PATCH, N_CHAN, D_SHARD), PATCH ** -0.5, 0.4375, ((1, 2), (2, 16)), jnp.float32)
    stem_first = gaussian(streams_of[8], (PATCH, N_CHAN, D_SHARD), ((0.0128 * NPARAMS ** -1 * (IMAGES * POSITIONS) ** -1) ** 0.5), 2.384185791015625e-06, ((1, 2), (2, 16)), jnp.float32)
    stem_second = jnp.clip(jnp.exp(math.log(9.807540386373367e-14) - 1.3862944 * jax.random.uniform(streams_of[9], (PATCH, N_CHAN, D_SHARD), jnp.float32) ** block_levels(streams_of[9], (PATCH, N_CHAN, D_SHARD), ((1, 2), (2, 16)), -0.2, 0.2)), 2.4518850965933418e-14, 9.807540386373367e-14)
    bottle_weight = gaussian(streams_of[10], (2, D, MID), D ** -0.5, 0.125, ((1, 16), (2, 2)), jnp.float32)
    bottle_first = gaussian(streams_of[11], (2, D, MID), ((0.1 * NPARAMS ** -1 * (IMAGES * POSITIONS) ** -1) ** 0.5), 6.67572021484375e-06, ((1, 16), (2, 2)), jnp.float32)
    bottle_second = jnp.clip(jnp.exp(math.log(7.662140778623427e-13) - 1.3862944 * jax.random.uniform(streams_of[12], (2, D, MID), jnp.float32) ** block_levels(streams_of[12], (2, D, MID), ((1, 16), (2, 2)), -0.2, 0.2)), 1.9155351946558569e-13, 7.662140778623427e-13)
    middle_weight = gaussian(streams_of[13], (9, MID, MID), (9 * MID) ** -0.5, 0.09375, ((1, 16), (2, 2)), jnp.float32)
    middle_first = gaussian(streams_of[14], (9, MID, MID), ((0.08 * NPARAMS ** -1 * (IMAGES * POSITIONS) ** -1) ** 0.5), 5.7220458984375e-06, ((1, 16), (2, 2)), jnp.float32)
    middle_second = jnp.clip(jnp.exp(math.log(6.129712622898742e-13) - 1.3862944 * jax.random.uniform(streams_of[15], (9, MID, MID), jnp.float32) ** block_levels(streams_of[15], (9, MID, MID), ((1, 16), (2, 2)), -0.2, 0.2)), 1.5324281557246855e-13, 6.129712622898742e-13)
    pyramid_weight = gaussian(streams_of[16], (29, D, BRANCH), (3 * D) ** -0.5, 0.078125, ((1, 16), (2, 2)), jnp.float32)
    pyramid_first = gaussian(streams_of[17], (29, D, BRANCH), (0.01 * NPARAMS ** -0.5), 3.0517578125e-05, ((1, 16), (2, 2)), jnp.float32)
    pyramid_second = jnp.clip(jnp.exp(math.log(3.923016078655195e-11) - 2.7725887 * jax.random.uniform(streams_of[18], (29, D, BRANCH), jnp.float32) ** block_levels(streams_of[18], (29, D, BRANCH), ((1, 16), (2, 2)), -0.2, 0.2)), 2.4518850491594968e-12, 3.923016078655195e-11)
    project_weight = gaussian(streams_of[19], (5, BRANCH, BRANCH), (5 * BRANCH) ** -0.5, 0.15625, ((1, 2), (2, 16)), jnp.float32)
    project_first = gaussian(streams_of[20], (5, BRANCH, BRANCH), (0.01 * NPARAMS ** -0.5), 3.0517578125e-05, ((1, 2), (2, 16)), jnp.float32)
    project_second = jnp.clip(jnp.exp(math.log(3.923016078655195e-11) - 2.7725887 * jax.random.uniform(streams_of[21], (5, BRANCH, BRANCH), jnp.float32) ** block_levels(streams_of[21], (5, BRANCH, BRANCH), ((1, 2), (2, 16)), -0.2, 0.2)), 2.4518850491594968e-12, 3.923016078655195e-11)
    head_weight = gaussian(streams_of[22], (BRANCH, NOUT), BRANCH ** -0.5, 0.375, ((0, 16),), jnp.float32)
    head_first = gaussian(streams_of[23], (BRANCH, NOUT), (0.01 * NPARAMS ** -0.5), 3.0517578125e-05, ((0, 16),), jnp.float32)
    head_second = jnp.clip(jnp.exp(math.log(3.923016078655195e-11) - 2.7725887 * jax.random.uniform(streams_of[24], (BRANCH, NOUT), jnp.float32) ** block_levels(streams_of[24], (BRANCH, NOUT), ((0, 16),), -0.2, 0.2)), 2.4518850491594968e-12, 3.923016078655195e-11)
    norm_gains = jnp.clip(1.0 + 0.1 * jax.random.normal(streams_of[25], (2, N_CHAN, MID_SHARD + D_SHARD), jnp.float32), 0.5, 1.5)
    norm_first = gaussian(streams_of[26], (2, N_CHAN, MID_SHARD + D_SHARD), (0.01 * NPARAMS ** -0.5), 3.0517578125e-05, ((1, 2),), jnp.float32)
    norm_second = jnp.clip(jnp.exp(math.log(3.923016078655195e-11) - 2.7725887 * jax.random.uniform(streams_of[27], (2, N_CHAN, MID_SHARD + D_SHARD), jnp.float32) ** block_levels(streams_of[27], (2, N_CHAN, MID_SHARD + D_SHARD), ((1, 2),), -0.2, 0.2)), 2.4518850491594968e-12, 3.923016078655195e-11)
    task_params = jnp.clip(jax.random.uniform(streams_of[28], (NOUT + 3,), jnp.float32, -1.0, 1.0), -1.0, 1.0)
    task_first = gaussian(streams_of[29], (NOUT + 3,), (0.01 * NPARAMS ** -0.5), 3.0517578125e-05, (), jnp.float32)
    task_second = jnp.clip(jnp.exp(jax.random.uniform(streams_of[30], (NOUT + 3,), jnp.float32, math.log(2.4518850491594968e-12), math.log(3.923016078655195e-11))), 2.4518850491594968e-12, 3.923016078655195e-11)
    return dict(patches=patches, labels=labels, offset_target=offset_target, offset_valid=offset_valid, depth_target=depth_target, lidar_valid=lidar_valid, crop_mask=crop_mask, stem_weight=stem_weight, stem_first=stem_first, stem_second=stem_second, bottle_weight=bottle_weight, bottle_first=bottle_first, bottle_second=bottle_second, middle_weight=middle_weight, middle_first=middle_first, middle_second=middle_second, pyramid_weight=pyramid_weight, pyramid_first=pyramid_first, pyramid_second=pyramid_second, project_weight=project_weight, project_first=project_first, project_second=project_second, head_weight=head_weight, head_first=head_first, head_second=head_second, norm_gains=norm_gains, norm_first=norm_first, norm_second=norm_second, task_params=task_params, task_first=task_first, task_second=task_second)


@jax.custom_vjp
def low(v):
    return lax.optimization_barrier(v.astype(jnp.bfloat16)).astype(jnp.float32)

@jax.custom_vjp
def low_back(v):
    return v

def low_keep(v):
    return (low(v), None)

def low_pass(kept, grad):
    return (grad,)

def back_keep(v):
    return (v, None)

def back_low(kept, grad):
    return (low(grad),)
low.defvjp(low_keep, low_pass)
low_back.defvjp(back_keep, back_low)
highest = lax.Precision.HIGHEST
pyramid_rates = (12, 24, 36)
norm_eps = 1e-05
clip_level = 0.01
adam_eps = 1e-08
decay_rate = 0.01

def shift_map(field, row_step, col_step):
    canvas_rows, canvas_cols = (field.shape[1], field.shape[2])
    if abs(row_step) >= canvas_rows or abs(col_step) >= canvas_cols:
        return jnp.zeros_like(field)
    padded = jnp.pad(field, ((0, 0), (max(-row_step, 0), max(row_step, 0)), (max(-col_step, 0), max(col_step, 0)), (0, 0)))
    row_start = max(row_step, 0)
    col_start = max(col_step, 0)
    return padded[:, row_start:row_start + canvas_rows, col_start:col_start + canvas_cols, :]

def dilated(canvas, weight, dilation):
    total = jnp.zeros(canvas.shape[:3] + (weight.shape[2],), jnp.float32)
    for tap_index in range(9):
        row_step = (tap_index // 3 - 1) * dilation
        col_step = (tap_index % 3 - 1) * dilation
        if abs(row_step) < canvas.shape[1] and abs(col_step) < canvas.shape[2]:
            tap_part = jnp.einsum('bhwc,cd->bhwd', canvas, weight[tap_index], precision=highest)
            total = total + shift_map(tap_part, row_step, col_step)
    return total

def batch_norm(values, crop_field, crop_total, gain, shift):
    mean = lax.optimization_barrier(jnp.sum(values * crop_field, axis=(0, 1))) / crop_total
    spread = lax.optimization_barrier(jnp.sum(values * values * crop_field, axis=(0, 1))) / crop_total - mean * mean
    return gain * ((values - mean) * lax.rsqrt(spread + norm_eps)) + shift

def image_terms(stream, crop_image, label, offset_goal, offset_field, depth_goal, lidar_field, pyramid_low, project_low, head_low, head_bias):
    stream_low = low(stream)
    pooled = lax.optimization_barrier(jnp.sum(stream_low * crop_image[:, None], axis=0)) / jnp.sum(crop_image)
    canvas = stream_low.reshape(1, FH, FW, D)
    branch_acts = [jax.nn.gelu(low_back(jnp.dot(stream_low, pyramid_low[0], precision=highest)))]
    for order, dilation in enumerate(pyramid_rates):
        taps = pyramid_low[1 + 9 * order:10 + 9 * order]
        branch_pre = low_back(dilated(canvas, taps, dilation).reshape(POSITIONS, BRANCH))
        branch_acts.append(jax.nn.gelu(branch_pre))
    pool_pre = low_back(jnp.dot(low(pooled)[None, :], pyramid_low[28], precision=highest))
    branch_acts.append(jnp.broadcast_to(jax.nn.gelu(pool_pre), (POSITIONS, BRANCH)))
    concat = low(jnp.stack(branch_acts, 0))
    project_pre = low_back(jnp.einsum('kpc,kcd->pd', concat, project_low, precision=highest))
    feature = low(jax.nn.gelu(project_pre))
    logits = low_back(jnp.dot(feature, head_low, precision=highest) + head_bias)
    class_logits = logits[:, :CLASSES]
    class_top = lax.optimization_barrier(jnp.max(class_logits, axis=1, keepdims=True))
    log_total = class_top[:, 0] + jnp.log(lax.optimization_barrier(jnp.sum(jnp.exp(class_logits - class_top), axis=1)))
    onehot = (label[:, None] == jnp.arange(CLASSES)[None, :]).astype(jnp.float32)
    seg_sum = jnp.sum(crop_image * (log_total - lax.optimization_barrier(jnp.sum(class_logits * onehot, axis=1))))
    offset_err = logits[:, CLASSES:CLASSES + 2] - offset_goal.T
    offset_sum = jnp.sum(offset_field * lax.optimization_barrier(jnp.sum(jnp.sqrt(offset_err * offset_err + 1.0) - 1.0, axis=1)))
    depth_err = jax.nn.softplus(logits[:, CLASSES + 2]) - depth_goal
    depth_sum = jnp.sum(lidar_field * (jnp.sqrt(depth_err * depth_err + 1.0) - 1.0))
    return jnp.stack([seg_sum, offset_sum, depth_sum])

def adam_step(weight, first, second, gradient, factor, rate, decay):
    gradient = gradient * factor
    first_new = 0.5 * first + 0.5 * gradient
    second_new = 0.5 * second + 0.5 * gradient * gradient
    direction = first_new / (1.0 - 0.5 ** STEP) / (jnp.sqrt(second_new / (1.0 - 0.5 ** STEP)) + adam_eps)
    return (weight - rate * (direction + decay * weight), first_new, second_new)

def reference(patches, labels, offset_target, offset_valid, depth_target, lidar_valid, crop_mask, stem_weight, stem_first, stem_second, bottle_weight, bottle_first, bottle_second, middle_weight, middle_first, middle_second, pyramid_weight, pyramid_first, pyramid_second, project_weight, project_first, project_second, head_weight, head_first, head_second, norm_gains, norm_first, norm_second, task_params, task_first, task_second):
    crop_field = crop_mask.astype(jnp.float32)
    offset_field = crop_field * offset_valid.astype(jnp.float32)
    lidar_field = crop_field * lidar_valid.astype(jnp.float32)
    counts = jnp.stack([jnp.sum(crop_field), jnp.sum(offset_field), jnp.sum(lidar_field)])
    inputs = patches.astype(jnp.float32)
    crop_cube = crop_field[:, :, None]
    images = patches.shape[0]

    def forward(stem, bottle, middle, pyramid, project, head, gains, task):
        stem_full = low(stem).reshape(PATCH, D)
        start = low_back(crop_cube * jnp.einsum('bpi,id->bpd', inputs, stem_full, precision=highest))
        first_pre = low_back(jnp.einsum('bpd,dc->bpc', low(start), low(bottle[0]), precision=highest))
        gain_one = gains[0, :, :MID_SHARD].reshape(MID)
        shift_one = gains[1, :, :MID_SHARD].reshape(MID)
        gain_two = gains[0, :, MID_SHARD:].reshape(D)
        shift_two = gains[1, :, MID_SHARD:].reshape(D)
        hidden = crop_cube * jax.nn.gelu(batch_norm(first_pre, crop_cube, counts[0], gain_one, shift_one))
        canvas = low(hidden).reshape(images, FH, FW, MID)
        second_pre = low_back(dilated(canvas, low(middle), 4).reshape(images, POSITIONS, MID))
        expand = low_back(jnp.einsum('bpc,dc->bpd', low(second_pre), low(bottle[1]), precision=highest))
        stream = start + crop_cube * batch_norm(expand, crop_cube, counts[0], gain_two, shift_two)
        pyramid_low = low(pyramid)
        project_low = low(project)
        head_low = low(head)
        head_bias = task[3:]

        def one_image(item):
            return image_terms(item[0], item[1], item[2], item[3], item[4], item[5], item[6], pyramid_low, project_low, head_low, head_bias)
        sums = lax.optimization_barrier(jnp.sum(lax.map(jax.checkpoint(one_image), (stream, crop_field, labels, offset_target, offset_field, depth_target, lidar_field)), axis=0))
        scale = task[:3]
        return jnp.sum(jnp.exp(-scale) * (sums / counts) + scale)
    total_loss, pull = jax.vjp(forward, stem_weight, bottle_weight, middle_weight, pyramid_weight, project_weight, head_weight, norm_gains, task_params)
    grads = pull(jnp.ones_like(total_loss))
    grad_norm = jnp.sqrt(sum((jnp.sum(gradient * gradient) for gradient in grads)))
    factor = clip_level / jnp.maximum(grad_norm, clip_level)
    new_stem = adam_step(stem_weight, stem_first, stem_second, grads[0], factor, PATCH ** (-0.5), decay_rate)
    new_bottle = adam_step(bottle_weight, bottle_first, bottle_second, grads[1], factor, D ** (-0.5), decay_rate)
    new_middle = adam_step(middle_weight, middle_first, middle_second, grads[2], factor, (9 * MID) ** (-0.5), decay_rate)
    new_pyramid = adam_step(pyramid_weight, pyramid_first, pyramid_second, grads[3], factor, (3 * D) ** (-0.5), decay_rate)
    new_project = adam_step(project_weight, project_first, project_second, grads[4], factor, (5 * BRANCH) ** (-0.5), decay_rate)
    new_head = adam_step(head_weight, head_first, head_second, grads[5], factor, BRANCH ** (-0.5), decay_rate)
    new_norm = adam_step(norm_gains, norm_first, norm_second, grads[6], factor, 0.3, 0.0)
    new_task = adam_step(task_params, task_first, task_second, grads[7], factor, 0.3, 0.0)
    return (total_loss, grad_norm, new_stem[0], new_stem[1], new_stem[2], new_bottle[0], new_bottle[1], new_bottle[2], new_middle[0], new_middle[1], new_middle[2], new_pyramid[0], new_pyramid[1], new_pyramid[2], new_project[0], new_project[1], new_project[2], new_head[0], new_head[1], new_head[2], new_norm[0], new_norm[1], new_norm[2], new_task[0], new_task[1], new_task[2])
```

```python
import functools

import jax
import jax.numpy as jnp
from jax import lax
from jax.experimental import pallas as pl
from jax.experimental.pallas import tpu as pltpu
from jax.sharding import PartitionSpec as P

D = 2048
MID = 512
BRANCH = 256
CLASSES = 19
PATCH = 192
FH = 40
FW = 40
STEP = 10
POSITIONS = 1600


pyramid_rates = (0, 12, 24, 36)
norm_eps = 1e-05
clip_level = 0.01
adam_eps = 1e-08
decay_rate = 0.01


MESH_ID = pl.DeviceIdType.MESH


def group_place(sizes, axes):
    place = jnp.int32(0)
    for axis in axes:
        place = place * sizes[axis] + lax.axis_index(axis)
    return place


def group_device(sizes, axes, index):
    coords = {}
    for axis in reversed(axes):
        coords[axis] = lax.rem(index, sizes[axis])
        index = lax.div(index, sizes[axis])
    return tuple(coords.get(axis, lax.axis_index(axis)) for axis in ("dp", "chan"))


def sum_kernel(sizes, axes, count, x_ref, o_ref, slots, send_sem, recv_sem):
    me = group_place(sizes, axes)
    barrier = pltpu.get_barrier_semaphore()

    def greet(step, carry):
        other = lax.rem(me + step, count)
        pl.semaphore_signal(
            barrier, inc=1, device_id=group_device(sizes, axes, other), device_id_type=MESH_ID
        )
        return carry

    lax.fori_loop(1, count, greet, 0)
    pl.semaphore_wait(barrier, count - 1)

    def copy_to(step):
        other = lax.rem(me + step, count)
        return pltpu.make_async_remote_copy(
            src_ref=x_ref,
            dst_ref=slots.at[me],
            send_sem=send_sem.at[step],
            recv_sem=recv_sem.at[me],
            device_id=group_device(sizes, axes, other),
            device_id_type=MESH_ID,
        )

    def copy_from(step):
        other = lax.rem(me + step, count)
        return pltpu.make_async_remote_copy(
            src_ref=x_ref,
            dst_ref=slots.at[other],
            send_sem=send_sem.at[step],
            recv_sem=recv_sem.at[other],
            device_id=group_device(sizes, axes, other),
            device_id_type=MESH_ID,
        )

    def start(step, carry):
        copy_to(step).start()
        return carry

    lax.fori_loop(1, count, start, 0)
    slots[me] = x_ref[...]

    def arrive(step, carry):
        copy_from(step).wait_recv()
        return carry

    lax.fori_loop(1, count, arrive, 0)
    o_ref[...] = lax.fori_loop(
        1, count, lambda index, total: total + slots[index], slots[0]
    )

    def leave(step, carry):
        copy_to(step).wait_send()
        return carry

    lax.fori_loop(1, count, leave, 0)


def small_sum(sizes, parts, axes, collective):
    flat = jnp.concatenate([part.reshape(-1) for part in parts])
    rows = -(-flat.shape[0] // 1024) * 8
    packed = jnp.pad(flat, (0, rows * 128 - flat.shape[0])).reshape(rows, 128)
    count = 1
    for axis in axes:
        count *= sizes[axis]
    summed = pl.pallas_call(
        functools.partial(sum_kernel, sizes, axes, count),
        out_shape=jax.ShapeDtypeStruct((rows, 128), jnp.float32),
        in_specs=[pl.BlockSpec(memory_space=pltpu.VMEM)],
        out_specs=pl.BlockSpec(memory_space=pltpu.VMEM),
        scratch_shapes=[
            pltpu.VMEM((count, rows, 128), jnp.float32),
            pltpu.SemaphoreType.DMA((count,)),
            pltpu.SemaphoreType.DMA((count,)),
        ],
        compiler_params=pltpu.CompilerParams(collective_id=collective, has_side_effects=True),
        name="small_sum",
    )(packed).reshape(-1)
    result = []
    start = 0
    for part in parts:
        size = part.size
        result.append(summed[start : start + size].reshape(part.shape))
        start += size
    return result


def swap_chan(values):
    return lax.ppermute(values, "chan", [(0, 1), (1, 0)])


def valid(step, length):
    return max(0, step), length + min(0, step)


def taps_of(rate):
    return [((tap // 3 - 1) * rate, (tap % 3 - 1) * rate) for tap in range(9)]


def shift_field(field, row_step, col_step):
    rows, cols = field.shape[:2]
    r0, r1 = valid(row_step, rows)
    c0, c1 = valid(col_step, cols)
    return jnp.pad(
        field[r0:r1, c0:c1],
        (
            (r0 - row_step, rows - (r1 - row_step)),
            (c0 - col_step, cols - (c1 - col_step)),
            (0, 0),
        ),
    )


def gelu_grad(values, upstream):
    return jax.vjp(jax.nn.gelu, values)[1](upstream)[0]


def dot(left, right, contract=(1, 0)):
    return lax.dot_general(
        left,
        right,
        (((contract[0],), (contract[1],)), ((), ())),
        preferred_element_type=jnp.float32,
    )


def adam_step(weight, first, second, gradient, factor, rate, decay):
    gradient = gradient * factor
    first_new = 0.5 * first + 0.5 * gradient
    second_new = 0.5 * second + 0.5 * gradient * gradient
    direction = (
        first_new / (1.0 - 0.5**STEP) / (jnp.sqrt(second_new / (1.0 - 0.5**STEP)) + adam_eps)
    )
    return (weight - rate * (direction + decay * weight), first_new, second_new)


def on_device(
    sizes,
    patches,
    labels,
    offset_target,
    offset_valid,
    depth_target,
    lidar_valid,
    crop_mask,
    stem_weight,
    stem_first,
    stem_second,
    bottle_weight,
    bottle_first,
    bottle_second,
    middle_weight,
    middle_first,
    middle_second,
    pyramid_weight,
    pyramid_first,
    pyramid_second,
    project_weight,
    project_first,
    project_second,
    head_weight,
    head_first,
    head_second,
    norm_gains,
    norm_first,
    norm_second,
    task_params,
    task_first,
    task_second,
):
    chan_place = lax.axis_index("chan")
    dp_size = sizes["dp"]
    low = jnp.bfloat16
    crop_field = crop_mask.astype(jnp.float32).reshape(POSITIONS, 1)
    offset_field = crop_field[:, 0] * offset_valid.astype(jnp.float32).reshape(POSITIONS)
    lidar_field = crop_field[:, 0] * lidar_valid.astype(jnp.float32).reshape(POSITIONS)
    local_counts = jnp.stack([jnp.sum(crop_field), jnp.sum(offset_field), jnp.sum(lidar_field)])
    half = D // 2
    mid_half = MID // 2

    row_share = bottle_weight.shape[1]
    mid_share = middle_weight.shape[1]
    stem_share = stem_weight.shape[2]
    project_share = project_weight.shape[2]
    head_share = head_weight.shape[0]
    small_parts = [stem_weight, project_weight, head_weight]
    small_flat = jnp.concatenate([part.astype(low).reshape(-1) for part in small_parts])
    small_rows = -(-small_flat.shape[0] // (16 * 256)) * 16
    small_flat = jnp.pad(small_flat, (0, small_rows * 256 - small_flat.shape[0]))
    packed = jnp.concatenate(
        [
            bottle_weight.astype(low).reshape(2 * row_share, 256),
            middle_weight.astype(low).reshape(9 * mid_share, 256),
            small_flat.reshape(small_rows, 256),
        ]
    )
    trunk = lax.all_gather(packed, ("dp", "chan")).reshape(dp_size, 2, packed.shape[0], 256)
    pyramid_low = lax.all_gather(pyramid_weight.astype(low), "dp", axis=1, tiled=True)
    reduce_low = trunk[:, :, :row_share].transpose(0, 2, 1, 3).reshape(D, MID)
    expand_low = trunk[:, :, row_share : 2 * row_share].transpose(0, 2, 1, 3).reshape(D, MID)
    start = 2 * row_share
    middle_low = (
        trunk[:, :, start : start + 9 * mid_share]
        .reshape(dp_size, 2, 9, mid_share, 256)
        .transpose(2, 0, 3, 1, 4)
        .reshape(9 * MID, MID)
    )
    small = trunk[:, :, start + 9 * mid_share :].reshape(dp_size, 2, small_rows * 256)
    size = PATCH * stem_share
    stem_low = (
        small[:, :, :size]
        .reshape(dp_size, 2, PATCH, stem_share)
        .transpose(2, 1, 0, 3)
        .reshape(PATCH, D)
    )
    own_small = lax.dynamic_index_in_dim(small, chan_place, 1, keepdims=False)
    project_low = (
        own_small[:, size : size + 5 * 128 * project_share]
        .reshape(dp_size, 5, 128, project_share)
        .transpose(1, 2, 0, 3)
        .reshape(5 * 128, BRANCH)
    )
    size += 5 * 128 * project_share
    head_low = own_small[:, size : size + head_share * 22].reshape(BRANCH, 22)

    gains_other = swap_chan(norm_gains)
    gains_all = jnp.where(
        chan_place == 0,
        jnp.concatenate([norm_gains, gains_other], 1),
        jnp.concatenate([gains_other, norm_gains], 1),
    )
    gain_one = gains_all[0, :, :mid_half].reshape(MID)
    shift_one = gains_all[1, :, :mid_half].reshape(MID)
    gain_two = gains_all[0, :, mid_half:].reshape(D)
    shift_two = gains_all[1, :, mid_half:].reshape(D)

    def own_half(values, axis):
        width = values.shape[axis] // 2
        return lax.dynamic_slice_in_dim(values, chan_place * width, width, axis)

    def other_half(values, axis):
        width = values.shape[axis] // 2
        return lax.dynamic_slice_in_dim(values, (1 - chan_place) * width, width, axis)

    patch_rows = patches.reshape(POSITIONS, PATCH)
    stream = crop_field * dot(patch_rows, stem_low)
    stream_low = stream.astype(low)
    first_pre = dot(stream_low, reduce_low)
    sum_one, square_one, counts = small_sum(
        sizes,
        [
            jnp.sum(crop_field * first_pre, 0),
            jnp.sum(crop_field * first_pre * first_pre, 0),
            local_counts,
        ],
        ("dp",),
        0,
    )
    crop_total = counts[0]
    mean_one = sum_one / crop_total
    scale_one = lax.rsqrt(square_one / crop_total - mean_one * mean_one + norm_eps)
    normed_one = (first_pre - mean_one) * scale_one
    act_input = gain_one * normed_one + shift_one
    hidden_low = (crop_field * jax.nn.gelu(act_input)).astype(low)
    hidden_canvas = hidden_low.reshape(FH, FW, MID)
    middle_taps = taps_of(4)
    hidden_stack = jnp.concatenate(
        [shift_field(hidden_canvas, step[0], step[1]) for step in middle_taps], 2
    ).reshape(POSITIONS, 9 * MID)
    second_low = dot(hidden_stack, middle_low).astype(low)
    expand_pre = dot(second_low, expand_low, (1, 1))
    sum_two, square_two = small_sum(
        sizes,
        [jnp.sum(crop_field * expand_pre, 0), jnp.sum(crop_field * expand_pre * expand_pre, 0)],
        ("dp",),
        1,
    )
    mean_two = sum_two / crop_total
    scale_two = lax.rsqrt(square_two / crop_total - mean_two * mean_two + norm_eps)
    stream_out = stream + crop_field * (gain_two * ((expand_pre - mean_two) * scale_two) + shift_two)
    output_low = stream_out.astype(low)
    canvas_two = output_low.reshape(FH, FW, D)
    image_count = jnp.sum(crop_field)
    pooled = jnp.sum(crop_field * output_low.astype(jnp.float32), 0, keepdims=True) / image_count
    pooled_low = pooled.astype(low)

    width = BRANCH // 2
    pyramid_taps = [(0, 0)] + taps_of(12) + taps_of(24) + taps_of(36)
    branch_of = [0] + [1] * 9 + [2] * 9 + [3] * 9
    branch_pre = [jnp.zeros((FH, FW, width), jnp.float32) for branch in range(4)]
    for tap, step in enumerate(pyramid_taps):
        r0, r1 = valid(step[0], FH)
        c0, c1 = valid(step[1], FW)
        part = dot(canvas_two[r0:r1].reshape(-1, D), pyramid_low[tap]).reshape(r1 - r0, FW, width)
        branch_pre[branch_of[tap]] = branch_pre[branch_of[tap]] + jnp.pad(
            part[:, c0:c1],
            (
                (r0 - step[0], FH - (r1 - step[0])),
                (c0 - step[1], FW - (c1 - step[1])),
                (0, 0),
            ),
        )
    branch_pre = [values.reshape(POSITIONS, width) for values in branch_pre]
    pool_pre = dot(pooled_low, pyramid_low[28])
    branch_acts = [jax.nn.gelu(values) for values in branch_pre]
    branch_acts.append(jnp.broadcast_to(jax.nn.gelu(pool_pre), (POSITIONS, width)))
    concat_low = jnp.concatenate(branch_acts, 1).astype(low)
    project_part = dot(concat_low, project_low).astype(low)
    project_pre = project_part.astype(jnp.float32) + swap_chan(project_part).astype(jnp.float32)
    feature_low = jax.nn.gelu(project_pre).astype(low)
    task_scale = task_params[:3]
    logits = dot(feature_low, head_low) + task_params[3:]
    class_logits = logits[:, :CLASSES]
    class_top = jnp.max(class_logits, 1, keepdims=True)
    class_exp = jnp.exp(class_logits - class_top)
    class_total = jnp.sum(class_exp, 1, keepdims=True)
    onehot = (
        labels.reshape(POSITIONS, 1) == lax.broadcasted_iota(jnp.int32, (1, CLASSES), 1)
    ).astype(jnp.float32)
    seg_terms = crop_field[:, 0] * (
        class_top[:, 0] + jnp.log(class_total[:, 0]) - jnp.sum(class_logits * onehot, 1)
    )
    offset_err = logits[:, CLASSES : CLASSES + 2] - jnp.swapaxes(offset_target, 1, 2).reshape(
        POSITIONS, 2
    )
    offset_root = jnp.sqrt(offset_err * offset_err + 1.0)
    depth_pre = logits[:, CLASSES + 2]
    depth_err = jax.nn.softplus(depth_pre) - depth_target.reshape(POSITIONS)
    depth_root = jnp.sqrt(depth_err * depth_err + 1.0)
    local_sums = jnp.stack(
        [
            jnp.sum(seg_terms),
            jnp.sum(offset_field * jnp.sum(offset_root - 1.0, 1)),
            jnp.sum(lidar_field * (depth_root - 1.0)),
        ]
    )
    task_weights = jnp.exp(-task_scale) / counts
    logit_grad = jnp.concatenate(
        [
            task_weights[0] * crop_field * (class_exp / class_total - onehot),
            task_weights[1] * offset_field[:, None] * offset_err / offset_root,
            (task_weights[2] * lidar_field * depth_err / depth_root * jax.nn.sigmoid(depth_pre))[
                :, None
            ],
        ],
        axis=1,
    )
    logit_low = logit_grad.astype(low)
    local_bias = jnp.sum(logit_low.astype(jnp.float32), 0)
    head_grad = dot(feature_low, logit_low, (0, 0))
    feature_grad = dot(logit_low, head_low, (1, 1))
    project_grad_low = gelu_grad(project_pre, feature_grad).astype(low)
    project_grad = dot(concat_low, project_grad_low, (0, 0))
    concat_grad = dot(project_grad_low, project_low, (1, 1))
    branch_grads = [
        gelu_grad(branch_pre[order], concat_grad[:, order * width : (order + 1) * width])
        .astype(low)
        .reshape(FH, FW, width)
        for order in range(4)
    ]
    pool_grad_low = gelu_grad(
        pool_pre, jnp.sum(concat_grad[:, 4 * width :], 0, keepdims=True)
    ).astype(low)
    grad_stack = jnp.concatenate(
        [
            shift_field(branch_grads[branch_of[tap]], -step[0], -step[1])
            for tap, step in enumerate(pyramid_taps)
        ],
        2,
    ).reshape(POSITIONS, 28 * width)

    pooled_grad = dot(pool_grad_low, pyramid_low[28], (1, 1)) / image_count
    weight_rows = pyramid_low[:28].transpose(1, 0, 2).reshape(D, 28 * width)
    other_part = dot(
        grad_stack, other_half(weight_rows, 0), (1, 1)
    ) + crop_field * other_half(pooled_grad, 1)
    other_sent = swap_chan(other_part.astype(low))
    taps_grad = dot(grad_stack, output_low, (0, 0)).astype(low)
    pool_weight_grad = dot(pool_grad_low, pooled_low, (0, 0)).astype(low)
    pyramid_grad = jnp.concatenate([taps_grad, pool_weight_grad], axis=0).reshape(29, width, D)
    pyramid_red = lax.psum_scatter(pyramid_grad, "dp", scatter_dimension=2, tiled=True)
    own_part = dot(grad_stack, own_half(weight_rows, 0), (1, 1)) + crop_field * own_half(
        pooled_grad, 1
    )
    stream_grad = own_part.astype(low).astype(jnp.float32) + other_sent.astype(jnp.float32)

    own_gain_two = own_half(gain_two, 0)
    own_scale_two = own_half(scale_two, 0)
    normed_two = (own_half(expand_pre, 1) - own_half(mean_two, 0)) * own_scale_two
    upstream_two = crop_field * stream_grad
    gain_two_grad, shift_two_grad, loss_sums, bias_grad = small_sum(
        sizes,
        [jnp.sum(upstream_two * normed_two, 0), jnp.sum(upstream_two, 0), local_sums, local_bias],
        ("dp",),
        2,
    )
    task_means = loss_sums / counts
    total_loss = jnp.sum(jnp.exp(-task_scale) * task_means + task_scale)
    scale_grad = 1.0 - jnp.exp(-task_scale) * task_means
    expand_grad_low = (
        crop_field
        * own_gain_two
        * own_scale_two
        * (upstream_two - (shift_two_grad + normed_two * gain_two_grad) / crop_total)
    ).astype(low)
    second_part = dot(expand_grad_low, own_half(expand_low, 0)).astype(low)
    second_other = swap_chan(second_part)
    expand_rows = dot(expand_grad_low, second_low, (0, 0)).astype(low)
    expand_sent = swap_chan(other_half(expand_rows, 1))
    second_grad_low = (
        second_part.astype(jnp.float32) + second_other.astype(jnp.float32)
    ).astype(low)
    second_canvas = second_grad_low.reshape(FH, FW, MID)
    second_stack = jnp.concatenate(
        [shift_field(second_canvas, -step[0], -step[1]) for step in middle_taps], 2
    ).reshape(POSITIONS, 9 * MID)
    middle_back = middle_low.reshape(9, MID, MID).transpose(0, 2, 1).reshape(9 * MID, MID)
    hidden_grad = dot(second_stack, middle_back)
    upstream_one = gelu_grad(act_input, crop_field * hidden_grad)
    gain_one_all, shift_one_all = small_sum(
        sizes,
        [jnp.sum(upstream_one * normed_one, 0), jnp.sum(upstream_one, 0)],
        ("dp",),
        3,
    )
    gain_one_grad = own_half(gain_one_all, 0)
    shift_one_grad = own_half(shift_one_all, 0)
    first_grad_low = (
        crop_field
        * gain_one
        * scale_one
        * (upstream_one - (shift_one_all + normed_one * gain_one_all) / crop_total)
    ).astype(low)
    middle_grad = dot(hidden_stack, own_half(second_grad_low, 1), (0, 0)).astype(low)
    reduce_grad = dot(stream_low, own_half(first_grad_low, 1), (0, 0)).astype(low)
    start_grad = dot(first_grad_low, own_half(reduce_low, 0), (1, 1)) + stream_grad
    start_grad_low = (crop_field * start_grad).astype(low)
    stem_grad = dot(patch_rows, start_grad_low, (0, 0)).astype(low)
    expand_own = own_half(expand_rows, 1)
    expand_grad = jnp.where(
        chan_place == 0,
        jnp.concatenate([expand_own, expand_sent], 0),
        jnp.concatenate([expand_sent, expand_own], 0),
    )

    small_grads = jnp.concatenate(
        [
            stem_grad.reshape(PATCH, dp_size, stem_share)
            .transpose(1, 0, 2)
            .reshape(dp_size, PATCH * stem_share),
            project_grad.astype(low)
            .reshape(5 * 128, dp_size, project_share)
            .transpose(1, 0, 2)
            .reshape(dp_size, 5 * 128 * project_share),
            head_grad.astype(low).reshape(dp_size, head_share * 22),
        ],
        1,
    )
    small_grads = jnp.pad(small_grads, ((0, 0), (0, small_rows * 256 - small_grads.shape[1])))
    packed_grads = jnp.concatenate(
        [
            reduce_grad.reshape(dp_size, row_share, 256),
            expand_grad.reshape(dp_size, row_share, 256),
            middle_grad.reshape(9, dp_size, mid_share, 256)
            .transpose(1, 0, 2, 3)
            .reshape(dp_size, 9 * mid_share, 256),
            small_grads.reshape(dp_size, small_rows, 256),
        ],
        1,
    )
    trunk_red = (
        lax.psum_scatter(packed_grads, "dp", scatter_dimension=0, tiled=True)
        .reshape(packed.shape)
        .astype(jnp.float32)
    )
    bottle_red = trunk_red[: 2 * row_share].reshape(bottle_weight.shape)
    middle_red = trunk_red[start : start + 9 * mid_share].reshape(middle_weight.shape)
    small_red = trunk_red[start + 9 * mid_share :].reshape(-1)
    stem_red = small_red[: stem_weight.size].reshape(stem_weight.shape)
    project_red = small_red[stem_weight.size : stem_weight.size + project_weight.size].reshape(
        project_weight.shape
    )
    size = stem_weight.size + project_weight.size
    head_red = small_red[size : size + head_weight.size].reshape(head_weight.shape)
    pyramid_red = pyramid_red.astype(jnp.float32).transpose(0, 2, 1)
    norm_grad = jnp.stack(
        [
            jnp.concatenate([gain_one_grad, gain_two_grad]),
            jnp.concatenate([shift_one_grad, shift_two_grad]),
        ]
    )[:, None, :]
    task_grad = jnp.concatenate([scale_grad, bias_grad])
    dp_first = (lax.axis_index("dp") == 0).astype(jnp.float32)
    chan_first = (chan_place == 0).astype(jnp.float32)
    own_squares = (
        jnp.sum(stem_red * stem_red)
        + jnp.sum(bottle_red * bottle_red)
        + jnp.sum(middle_red * middle_red)
        + jnp.sum(pyramid_red * pyramid_red)
        + jnp.sum(project_red * project_red)
        + chan_first * jnp.sum(head_red * head_red)
        + dp_first * jnp.sum(norm_grad * norm_grad)
        + dp_first * chan_first * jnp.sum(task_grad * task_grad)
    )
    grad_norm = jnp.sqrt(small_sum(sizes, [own_squares], ("dp", "chan"), 4)[0])
    factor = clip_level / jnp.maximum(grad_norm, clip_level)
    new_stem = adam_step(
        stem_weight, stem_first, stem_second, stem_red, factor, PATCH ** (-0.5), decay_rate
    )
    new_bottle = adam_step(
        bottle_weight, bottle_first, bottle_second, bottle_red, factor, D ** (-0.5), decay_rate
    )
    new_middle = adam_step(
        middle_weight,
        middle_first,
        middle_second,
        middle_red,
        factor,
        (9 * MID) ** (-0.5),
        decay_rate,
    )
    new_pyramid = adam_step(
        pyramid_weight,
        pyramid_first,
        pyramid_second,
        pyramid_red,
        factor,
        (3 * D) ** (-0.5),
        decay_rate,
    )
    new_project = adam_step(
        project_weight,
        project_first,
        project_second,
        project_red,
        factor,
        (5 * BRANCH) ** (-0.5),
        decay_rate,
    )
    new_head = adam_step(
        head_weight, head_first, head_second, head_red, factor, BRANCH ** (-0.5), decay_rate
    )
    new_norm = adam_step(norm_gains, norm_first, norm_second, norm_grad, factor, 0.3, 0.0)
    new_task = adam_step(task_params, task_first, task_second, task_grad, factor, 0.3, 0.0)
    return (
        total_loss,
        grad_norm,
        new_stem[0],
        new_stem[1],
        new_stem[2],
        new_bottle[0],
        new_bottle[1],
        new_bottle[2],
        new_middle[0],
        new_middle[1],
        new_middle[2],
        new_pyramid[0],
        new_pyramid[1],
        new_pyramid[2],
        new_project[0],
        new_project[1],
        new_project[2],
        new_head[0],
        new_head[1],
        new_head[2],
        new_norm[0],
        new_norm[1],
        new_norm[2],
        new_task[0],
        new_task[1],
        new_task[2],
    )


def solution(mesh):
    return jax.shard_map(
        functools.partial(on_device, dict(mesh.shape)),
        mesh=mesh,
        in_specs=(
            P("dp", None, None),
            P("dp", None),
            P("dp", None, None),
            P("dp", None),
            P("dp", None),
            P("dp", None),
            P("dp", None),
            P(None, "chan", "dp"),
            P(None, "chan", "dp"),
            P(None, "chan", "dp"),
            P(None, "dp", "chan"),
            P(None, "dp", "chan"),
            P(None, "dp", "chan"),
            P(None, "dp", "chan"),
            P(None, "dp", "chan"),
            P(None, "dp", "chan"),
            P(None, "dp", "chan"),
            P(None, "dp", "chan"),
            P(None, "dp", "chan"),
            P(None, "chan", "dp"),
            P(None, "chan", "dp"),
            P(None, "chan", "dp"),
            P("dp", None),
            P("dp", None),
            P("dp", None),
            P(None, "chan", None),
            P(None, "chan", None),
            P(None, "chan", None),
            P(),
            P(),
            P(),
        ),
        out_specs=(
            P(),
            P(),
            P(None, "chan", "dp"),
            P(None, "chan", "dp"),
            P(None, "chan", "dp"),
            P(None, "dp", "chan"),
            P(None, "dp", "chan"),
            P(None, "dp", "chan"),
            P(None, "dp", "chan"),
            P(None, "dp", "chan"),
            P(None, "dp", "chan"),
            P(None, "dp", "chan"),
            P(None, "dp", "chan"),
            P(None, "dp", "chan"),
            P(None, "chan", "dp"),
            P(None, "chan", "dp"),
            P(None, "chan", "dp"),
            P("dp", None),
            P("dp", None),
            P("dp", None),
            P(None, "chan", None),
            P(None, "chan", None),
            P(None, "chan", None),
            P(),
            P(),
            P(),
        ),
        check_vma=False,
    )
```

```python
import functools

import jax
import jax.numpy as jnp
from jax import lax
from jax.experimental import pallas as pl
from jax.experimental.pallas import tpu as pltpu
from jax.sharding import PartitionSpec as P

D = 2048
MID = 512
BRANCH = 256
CLASSES = 19
PATCH = 192
FH = 40
FW = 40
STEP = 10
POSITIONS = 1600


pyramid_rates = (0, 12, 24, 36)
norm_eps = 1e-05
clip_level = 0.01
adam_eps = 1e-08
decay_rate = 0.01


MESH_ID = pl.DeviceIdType.MESH


def group_place(sizes, axes):
    place = jnp.int32(0)
    for axis in axes:
        place = place * sizes[axis] + lax.axis_index(axis)
    return place


def group_device(sizes, axes, index):
    coords = {}
    for axis in reversed(axes):
        coords[axis] = lax.rem(index, sizes[axis])
        index = lax.div(index, sizes[axis])
    return tuple(coords.get(axis, lax.axis_index(axis)) for axis in ("dp", "chan"))


def sum_kernel(sizes, axes, count, x_ref, o_ref, slots, send_sem, recv_sem):
    me = group_place(sizes, axes)
    barrier = pltpu.get_barrier_semaphore()

    def greet(step, carry):
        other = lax.rem(me + step, count)
        pl.semaphore_signal(
            barrier, inc=1, device_id=group_device(sizes, axes, other), device_id_type=MESH_ID
        )
        return carry

    lax.fori_loop(1, count, greet, 0)
    pl.semaphore_wait(barrier, count - 1)

    def copy_to(step):
        other = lax.rem(me + step, count)
        return pltpu.make_async_remote_copy(
            src_ref=x_ref,
            dst_ref=slots.at[me],
            send_sem=send_sem.at[step],
            recv_sem=recv_sem.at[me],
            device_id=group_device(sizes, axes, other),
            device_id_type=MESH_ID,
        )

    def copy_from(step):
        other = lax.rem(me + step, count)
        return pltpu.make_async_remote_copy(
            src_ref=x_ref,
            dst_ref=slots.at[other],
            send_sem=send_sem.at[step],
            recv_sem=recv_sem.at[other],
            device_id=group_device(sizes, axes, other),
            device_id_type=MESH_ID,
        )

    def start(step, carry):
        copy_to(step).start()
        return carry

    lax.fori_loop(1, count, start, 0)
    slots[me] = x_ref[...]

    def arrive(step, carry):
        copy_from(step).wait_recv()
        return carry

    lax.fori_loop(1, count, arrive, 0)
    o_ref[...] = lax.fori_loop(
        1, count, lambda index, total: total + slots[index], slots[0]
    )

    def leave(step, carry):
        copy_to(step).wait_send()
        return carry

    lax.fori_loop(1, count, leave, 0)


def small_sum(sizes, parts, axes, collective):
    flat = jnp.concatenate([part.reshape(-1) for part in parts])
    rows = -(-flat.shape[0] // 1024) * 8
    packed = jnp.pad(flat, (0, rows * 128 - flat.shape[0])).reshape(rows, 128)
    count = 1
    for axis in axes:
        count *= sizes[axis]
    summed = pl.pallas_call(
        functools.partial(sum_kernel, sizes, axes, count),
        out_shape=jax.ShapeDtypeStruct((rows, 128), jnp.float32),
        in_specs=[pl.BlockSpec(memory_space=pltpu.VMEM)],
        out_specs=pl.BlockSpec(memory_space=pltpu.VMEM),
        scratch_shapes=[
            pltpu.VMEM((count, rows, 128), jnp.float32),
            pltpu.SemaphoreType.DMA((count,)),
            pltpu.SemaphoreType.DMA((count,)),
        ],
        compiler_params=pltpu.CompilerParams(collective_id=collective, has_side_effects=True),
        name="small_sum",
    )(packed).reshape(-1)
    result = []
    start = 0
    for part in parts:
        size = part.size
        result.append(summed[start : start + size].reshape(part.shape))
        start += size
    return result


def swap_chan(values):
    return lax.ppermute(values, "chan", [(0, 1), (1, 0)])


def valid(step, length):
    return max(0, step), length + min(0, step)


def taps_of(rate):
    return [((tap // 3 - 1) * rate, (tap % 3 - 1) * rate) for tap in range(9)]


def shift_field(field, row_step, col_step):
    rows, cols = field.shape[:2]
    r0, r1 = valid(row_step, rows)
    c0, c1 = valid(col_step, cols)
    return jnp.pad(
        field[r0:r1, c0:c1],
        (
            (r0 - row_step, rows - (r1 - row_step)),
            (c0 - col_step, cols - (c1 - col_step)),
            (0, 0),
        ),
    )


def gelu_grad(values, upstream):
    return jax.vjp(jax.nn.gelu, values)[1](upstream)[0]


def dot(left, right, contract=(1, 0)):
    return lax.dot_general(
        left,
        right,
        (((contract[0],), (contract[1],)), ((), ())),
        preferred_element_type=jnp.float32,
    )


PAD = 128
PYRAMID_ROWS = (-36, -24, -12, 0, 12, 24, 36)


def taps_by_row():
    fields = [(0, 0)] + [(rate, col * rate) for rate in (12, 24, 36) for col in (-1, 0, 1)]
    groups = []
    for row_step in PYRAMID_ROWS:
        group = []
        for place, (rate, col_step) in enumerate(fields):
            if rate == 0:
                if row_step == 0:
                    group.append((0, place))
            elif row_step == 0 or abs(row_step) == rate:
                turn = (1 if row_step > 0 else -1 if row_step < 0 else 0) + 1
                tap = 1 + 9 * (rate // 12 - 1) + 3 * turn + (col_step // rate + 1)
                group.append((tap, place))
        groups.append(group)
    return fields, groups


FIELDS, ROW_GROUPS = taps_by_row()
TAP_ORDER = [tap for group in ROW_GROUPS for tap, place in group]
PLACE_ORDER = [place for group in ROW_GROUPS for tap, place in group]


def roll_cols(values, columns, step):
    if step == 0:
        return values
    moved = pltpu.roll(values, (-step) % values.shape[0], 0)
    target = columns[:, :1] + float(step)
    return jnp.where((target >= 0.0) & (target < float(FW)), moved, 0.0)


def vmem(count):
    return [pl.BlockSpec(memory_space=pltpu.VMEM)] * count


def middle_kernel(back, x_ref, w_ref, col_ref, o_ref, canvas):
    edge = 4 * FW
    mid = x_ref.shape[1]
    values = x_ref[...].astype(jnp.float32)
    sign = -1 if back else 1
    for turn in range(3):
        canvas[turn, :edge] = jnp.zeros((edge, mid), canvas.dtype)
        canvas[turn, POSITIONS + edge :] = jnp.zeros((edge, mid), canvas.dtype)
        canvas[turn, edge : POSITIONS + edge] = roll_cols(
            values, col_ref, sign * 4 * (turn - 1)
        ).astype(canvas.dtype)
    block = 400

    def step(index, carry):
        total = None
        for row in range(3):
            first = pl.multiple_of(index * block + edge * (1 + sign * (row - 1)), 16)
            for turn in range(3):
                part = dot(
                    canvas[turn, pl.ds(first, block)],
                    w_ref[3 * row + turn],
                    (1, 1) if back else (1, 0),
                )
                total = part if total is None else total + part
        o_ref[pl.ds(pl.multiple_of(index * block, 16), block)] = total.astype(o_ref.dtype)
        return carry

    lax.fori_loop(0, POSITIONS // block, step, 0)


def middle_conv(field, weights, columns, back, dtype):
    return pl.pallas_call(
        functools.partial(middle_kernel, back),
        out_shape=jax.ShapeDtypeStruct((POSITIONS, MID), dtype),
        in_specs=vmem(3),
        out_specs=vmem(1)[0],
        scratch_shapes=[pltpu.VMEM((3, POSITIONS + 8 * FW, MID), jnp.bfloat16)],
        compiler_params=pltpu.CompilerParams(vmem_limit_bytes=40 << 20),
        cost_estimate=pl.CostEstimate(
            flops=2 * POSITIONS * 9 * MID * MID, bytes_accessed=16 << 20, transcendentals=0
        ),
        name="middle_back" if back else "middle_fwd",
    )(field, weights, columns)


def middle_weight_kernel(xt_ref, g_ref, col_ref, o_ref, fields):
    width = g_ref.shape[1]
    values = g_ref[...].astype(jnp.float32)
    for turn in range(3):
        fields[turn, :PAD] = jnp.zeros((PAD, width), fields.dtype)
        fields[turn, PAD + POSITIONS :] = jnp.zeros((PAD, width), fields.dtype)
        fields[turn, PAD : PAD + POSITIONS] = roll_cols(values, col_ref, -4 * (turn - 1)).astype(
            fields.dtype
        )
    for row in range(3):
        row_step = 4 * (row - 1)
        r0, r1 = valid(row_step, FH)
        first = r0 * FW // 128 * 128
        last = min(POSITIONS, -(-r1 * FW // 128) * 128)
        base = PAD + first - row_step * FW
        for turn in range(3):
            o_ref[3 * row + turn] = dot(
                xt_ref[:, first:last], fields[turn, base : base + last - first]
            ).astype(o_ref.dtype)


def middle_weights(field_t, grads, columns):
    depth, width = field_t.shape[0], grads.shape[1]
    return pl.pallas_call(
        middle_weight_kernel,
        out_shape=jax.ShapeDtypeStruct((9, depth, width), jnp.bfloat16),
        in_specs=vmem(3),
        out_specs=vmem(1)[0],
        scratch_shapes=[pltpu.VMEM((3, POSITIONS + 2 * PAD, width), jnp.bfloat16)],
        compiler_params=pltpu.CompilerParams(vmem_limit_bytes=40 << 20),
        cost_estimate=pl.CostEstimate(
            flops=2 * POSITIONS * 9 * depth * width, bytes_accessed=6 << 20, transcendentals=0
        ),
        name="middle_weights",
    )(field_t, grads, columns)


def pyramid_kernel(x_ref, w_hbm, col_ref, o_ref, weights, fields, sems):
    width = o_ref.shape[2]
    copies = []
    order = [3, 2, 4, 1, 5, 0, 6]
    starts = []
    place = 0
    for group in ROW_GROUPS:
        starts.append(place)
        place += len(group)
    for turn in order:
        group_copies = []
        for offset, (tap, _) in enumerate(ROW_GROUPS[turn]):
            slot = starts[turn] + offset
            copy = pltpu.make_async_copy(
                w_hbm.at[tap], weights.at[:, pl.ds(slot * width, width)], sems.at[slot]
            )
            copy.start()
            group_copies.append(copy)
        copies.append(group_copies)
    for turn, group_copies in zip(order, copies):
        for copy in group_copies:
            copy.wait()
        row_step = PYRAMID_ROWS[turn]
        group = ROW_GROUPS[turn]
        r0, r1 = valid(row_step, FH)
        count = (r1 - r0) * FW
        block = {1600: 800, 1120: 560, 640: 640, 160: 160}[count]
        cols = pl.ds(starts[turn] * width, len(group) * width)

        def step(index, carry):
            source = pl.multiple_of(index * block + r0 * FW, 16)
            target = pl.multiple_of(index * block + (r0 - row_step) * FW, 16)
            part = dot(x_ref[pl.ds(source, block)], weights[:, cols])
            for offset, (tap, field) in enumerate(group):
                piece = part[:, offset * width : (offset + 1) * width]
                rows = pl.ds(target, block)
                if row_step == 0:
                    fields[field, rows] = piece
                else:
                    fields[field, rows] += piece
            return carry

        lax.fori_loop(0, count // block, step, 0)
    o_ref[0] = fields[0]
    for branch in range(3):
        total = fields[2 + 3 * branch]
        for turn in (0, 2):
            place = 1 + 3 * branch + turn
            total = total + roll_cols(fields[place], col_ref, FIELDS[place][1])
        o_ref[1 + branch] = total


def pyramid_forward(field, weights, columns):
    depth, width = weights.shape[1:]
    return pl.pallas_call(
        pyramid_kernel,
        out_shape=jax.ShapeDtypeStruct((4, POSITIONS, width), jnp.float32),
        in_specs=[
            pl.BlockSpec(memory_space=pltpu.VMEM),
            pl.BlockSpec(memory_space=pl.ANY),
            pl.BlockSpec(memory_space=pltpu.VMEM),
        ],
        out_specs=vmem(1)[0],
        scratch_shapes=[
            pltpu.VMEM((depth, 28 * width), jnp.bfloat16),
            pltpu.VMEM((10, POSITIONS, width), jnp.float32),
            pltpu.SemaphoreType.DMA((28,)),
        ],
        compiler_params=pltpu.CompilerParams(vmem_limit_bytes=56 << 20),
        cost_estimate=pl.CostEstimate(
            flops=2 * POSITIONS * 17 * depth * width, bytes_accessed=25 << 20, transcendentals=0
        ),
        name="pyramid_fwd",
    )(field, weights, columns)


def fill_fields(g_ref, col_ref, fields):
    width = g_ref.shape[2]
    for place, (rate, col_step) in enumerate(FIELDS):
        fields[place, :PAD] = jnp.zeros((PAD, width), fields.dtype)
        fields[place, PAD + POSITIONS :] = jnp.zeros((PAD, width), fields.dtype)
        values = g_ref[rate // 12]
        fields[place, PAD : PAD + POSITIONS] = roll_cols(
            values.astype(jnp.float32), col_ref, -col_step
        ).astype(fields.dtype)


def weight_kernel(xt_ref, g_ref, col_ref, pool_ref, pool_grad_ref, o_ref, fields):
    width = g_ref.shape[2]
    depth = xt_ref.shape[0]
    fill_fields(g_ref, col_ref, fields)
    block = 512
    for row_step, group in zip(PYRAMID_ROWS, ROW_GROUPS):
        r0, r1 = valid(row_step, FH)
        first = r0 * FW // 128 * 128
        last = min(POSITIONS, -(-r1 * FW // 128) * 128)
        base = PAD + first - row_step * FW
        sets = [group[at : at + 2] for at in range(0, 10, 2)] if row_step == 0 else [group]
        for chosen in sets:
            right = jnp.concatenate(
                [fields[place, base : base + last - first] for tap, place in chosen], 1
            )

            def step(index, carry):
                rows = pl.ds(pl.multiple_of(index * block, 16), block)
                part = dot(xt_ref[rows, first:last], right)
                for offset, (tap, place) in enumerate(chosen):
                    o_ref[tap, rows] = part[:, offset * width : (offset + 1) * width].astype(
                        o_ref.dtype
                    )
                return carry

            lax.fori_loop(0, depth // block, step, 0)
    o_ref[28] = (pool_ref[...] * pool_grad_ref[...]).astype(o_ref.dtype)


def pyramid_weights(field_t, grads, columns, pooled, pool_grad):
    depth = field_t.shape[0]
    width = grads.shape[2]
    return pl.pallas_call(
        weight_kernel,
        out_shape=jax.ShapeDtypeStruct((29, depth, width), jnp.bfloat16),
        in_specs=vmem(5),
        out_specs=vmem(1)[0],
        scratch_shapes=[pltpu.VMEM((10, POSITIONS + 2 * PAD, width), jnp.bfloat16)],
        compiler_params=pltpu.CompilerParams(vmem_limit_bytes=56 << 20),
        cost_estimate=pl.CostEstimate(
            flops=2 * POSITIONS * 18 * depth * width, bytes_accessed=25 << 20, transcendentals=0
        ),
        name="pyramid_weights",
    )(field_t, grads, columns, pooled, pool_grad)


def field_kernel(half_ref, w_hbm, g_ref, col_ref, o_ref, weights, fields, stack, sems):
    width = g_ref.shape[2]
    depth = o_ref.shape[1]
    half = pl.ds(pl.multiple_of(half_ref[0] * depth, 16), depth)
    copies = []
    for slot, tap in enumerate(TAP_ORDER):
        copy = pltpu.make_async_copy(
            w_hbm.at[tap, half], weights.at[:, pl.ds(slot * width, width)], sems.at[slot]
        )
        copy.start()
        copies.append(copy)
    fill_fields(g_ref, col_ref, fields)
    for copy in copies:
        copy.wait()
    step_of = [step for step, group in zip(PYRAMID_ROWS, ROW_GROUPS) for entry in group]
    for r0, r1 in ((0, 4), (4, 12), (12, 16), (16, 24), (24, 28), (28, 36), (36, 40)):
        slots = [
            slot for slot, step in enumerate(step_of) if r0 - step >= 0 and r1 - step <= FH
        ]
        count = (r1 - r0) * FW
        for at, slot in enumerate(slots):
            base = PAD + (r0 - step_of[slot]) * FW
            stack[:count, at * width : (at + 1) * width] = fields[
                PLACE_ORDER[slot], base : base + count
            ]
        o_ref[r0 * FW : r1 * FW] = dot(
            stack[:count, : len(slots) * width],
            weights[:, slots[0] * width : (slots[-1] + 1) * width],
            (1, 1),
        ).astype(o_ref.dtype)


def pyramid_field(half, weights, grads, columns):
    depth, width = weights.shape[1] // 2, weights.shape[2]
    return pl.pallas_call(
        field_kernel,
        out_shape=jax.ShapeDtypeStruct((POSITIONS, depth), jnp.bfloat16),
        in_specs=[
            pl.BlockSpec(memory_space=pltpu.SMEM),
            pl.BlockSpec(memory_space=pl.ANY),
            pl.BlockSpec(memory_space=pltpu.VMEM),
            pl.BlockSpec(memory_space=pltpu.VMEM),
        ],
        out_specs=vmem(1)[0],
        scratch_shapes=[
            pltpu.VMEM((depth, 28 * width), jnp.bfloat16),
            pltpu.VMEM((10, POSITIONS + 2 * PAD, width), jnp.bfloat16),
            pltpu.VMEM((8 * FW, 19 * width), jnp.bfloat16),
            pltpu.SemaphoreType.DMA((28,)),
        ],
        compiler_params=pltpu.CompilerParams(vmem_limit_bytes=56 << 20),
        cost_estimate=pl.CostEstimate(
            flops=2 * POSITIONS * 17 * depth * width, bytes_accessed=15 << 20, transcendentals=0
        ),
        name="pyramid_field",
    )(half, weights, grads, columns)


def adam_step(weight, first, second, gradient, factor, rate, decay):
    gradient = gradient * factor
    first_new = 0.5 * first + 0.5 * gradient
    second_new = 0.5 * second + 0.5 * gradient * gradient
    direction = (
        first_new / (1.0 - 0.5**STEP) / (jnp.sqrt(second_new / (1.0 - 0.5**STEP)) + adam_eps)
    )
    return (weight - rate * (direction + decay * weight), first_new, second_new)


def on_device(
    sizes,
    patches,
    labels,
    offset_target,
    offset_valid,
    depth_target,
    lidar_valid,
    crop_mask,
    stem_weight,
    stem_first,
    stem_second,
    bottle_weight,
    bottle_first,
    bottle_second,
    middle_weight,
    middle_first,
    middle_second,
    pyramid_weight,
    pyramid_first,
    pyramid_second,
    project_weight,
    project_first,
    project_second,
    head_weight,
    head_first,
    head_second,
    norm_gains,
    norm_first,
    norm_second,
    task_params,
    task_first,
    task_second,
):
    chan_place = lax.axis_index("chan")
    dp_size = sizes["dp"]
    low = jnp.bfloat16
    crop_field = crop_mask.astype(jnp.float32).reshape(POSITIONS, 1)
    offset_field = crop_field[:, 0] * offset_valid.astype(jnp.float32).reshape(POSITIONS)
    lidar_field = crop_field[:, 0] * lidar_valid.astype(jnp.float32).reshape(POSITIONS)
    local_counts = jnp.stack([jnp.sum(crop_field), jnp.sum(offset_field), jnp.sum(lidar_field)])
    half = D // 2
    mid_half = MID // 2

    row_share = bottle_weight.shape[1]
    mid_share = middle_weight.shape[1]
    stem_share = stem_weight.shape[2]
    project_share = project_weight.shape[2]
    head_share = head_weight.shape[0]
    small_parts = [stem_weight, project_weight, head_weight]
    small_flat = jnp.concatenate([part.astype(low).reshape(-1) for part in small_parts])
    small_rows = -(-small_flat.shape[0] // (16 * 256)) * 16
    small_flat = jnp.pad(small_flat, (0, small_rows * 256 - small_flat.shape[0]))
    packed = jnp.concatenate(
        [
            bottle_weight.astype(low).reshape(2 * row_share, 256),
            middle_weight.astype(low).reshape(9 * mid_share, 256),
            small_flat.reshape(small_rows, 256),
        ]
    )
    trunk = lax.all_gather(packed, ("dp", "chan")).reshape(dp_size, 2, packed.shape[0], 256)
    pyramid_low = lax.all_gather(pyramid_weight.astype(low), "dp", axis=1, tiled=True)
    reduce_low = trunk[:, :, :row_share].transpose(0, 2, 1, 3).reshape(D, MID)
    expand_low = trunk[:, :, row_share : 2 * row_share].transpose(0, 2, 1, 3).reshape(D, MID)
    start = 2 * row_share
    middle_low = (
        trunk[:, :, start : start + 9 * mid_share]
        .reshape(dp_size, 2, 9, mid_share, 256)
        .transpose(2, 0, 3, 1, 4)
        .reshape(9, MID, MID)
    )
    small = trunk[:, :, start + 9 * mid_share :].reshape(dp_size, 2, small_rows * 256)
    size = PATCH * stem_share
    stem_low = (
        small[:, :, :size]
        .reshape(dp_size, 2, PATCH, stem_share)
        .transpose(2, 1, 0, 3)
        .reshape(PATCH, D)
    )
    own_small = lax.dynamic_index_in_dim(small, chan_place, 1, keepdims=False)
    project_low = (
        own_small[:, size : size + 5 * 128 * project_share]
        .reshape(dp_size, 5, 128, project_share)
        .transpose(1, 2, 0, 3)
        .reshape(5 * 128, BRANCH)
    )
    size += 5 * 128 * project_share
    head_low = own_small[:, size : size + head_share * 22].reshape(BRANCH, 22)

    gains_other = swap_chan(norm_gains)
    gains_all = jnp.where(
        chan_place == 0,
        jnp.concatenate([norm_gains, gains_other], 1),
        jnp.concatenate([gains_other, norm_gains], 1),
    )
    gain_one = gains_all[0, :, :mid_half].reshape(MID)
    shift_one = gains_all[1, :, :mid_half].reshape(MID)
    gain_two = gains_all[0, :, mid_half:].reshape(D)
    shift_two = gains_all[1, :, mid_half:].reshape(D)

    def own_half(values, axis):
        width = values.shape[axis] // 2
        return lax.dynamic_slice_in_dim(values, chan_place * width, width, axis)

    def other_half(values, axis):
        width = values.shape[axis] // 2
        return lax.dynamic_slice_in_dim(values, (1 - chan_place) * width, width, axis)

    patch_rows = patches.reshape(POSITIONS, PATCH)
    stream = crop_field * dot(patch_rows, stem_low)
    stream_low = stream.astype(low)
    first_pre = dot(stream_low, reduce_low)
    sum_one, square_one, counts = small_sum(
        sizes,
        [
            jnp.sum(crop_field * first_pre, 0),
            jnp.sum(crop_field * first_pre * first_pre, 0),
            local_counts,
        ],
        ("dp",),
        0,
    )
    crop_total = counts[0]
    mean_one = sum_one / crop_total
    scale_one = lax.rsqrt(square_one / crop_total - mean_one * mean_one + norm_eps)
    normed_one = (first_pre - mean_one) * scale_one
    act_input = gain_one * normed_one + shift_one
    hidden_low = (crop_field * jax.nn.gelu(act_input)).astype(low)
    columns = jnp.broadcast_to(
        lax.rem(lax.broadcasted_iota(jnp.int32, (POSITIONS, 1), 0), FW).astype(jnp.float32),
        (POSITIONS, 128),
    )
    second_low = middle_conv(hidden_low, middle_low, columns, False, low)
    expand_pre = dot(second_low, expand_low, (1, 1))
    sum_two, square_two = small_sum(
        sizes,
        [jnp.sum(crop_field * expand_pre, 0), jnp.sum(crop_field * expand_pre * expand_pre, 0)],
        ("dp",),
        1,
    )
    mean_two = sum_two / crop_total
    scale_two = lax.rsqrt(square_two / crop_total - mean_two * mean_two + norm_eps)
    stream_out = stream + crop_field * (gain_two * ((expand_pre - mean_two) * scale_two) + shift_two)
    output_low = stream_out.astype(low)
    image_count = jnp.sum(crop_field)
    pooled = jnp.sum(crop_field * output_low.astype(jnp.float32), 0, keepdims=True) / image_count
    pooled_low = pooled.astype(low)

    width = BRANCH // 2
    branch_pre = pyramid_forward(output_low, pyramid_low, columns)
    pool_pre = dot(pooled_low, pyramid_low[28])
    branch_acts = [jax.nn.gelu(branch_pre[order]) for order in range(4)]
    branch_acts.append(jnp.broadcast_to(jax.nn.gelu(pool_pre), (POSITIONS, width)))
    concat_low = jnp.concatenate(branch_acts, 1).astype(low)
    project_part = dot(concat_low, project_low).astype(low)
    project_pre = project_part.astype(jnp.float32) + swap_chan(project_part).astype(jnp.float32)
    feature_low = jax.nn.gelu(project_pre).astype(low)
    task_scale = task_params[:3]
    logits = dot(feature_low, head_low) + task_params[3:]
    class_logits = logits[:, :CLASSES]
    class_top = jnp.max(class_logits, 1, keepdims=True)
    class_exp = jnp.exp(class_logits - class_top)
    class_total = jnp.sum(class_exp, 1, keepdims=True)
    onehot = (
        labels.reshape(POSITIONS, 1) == lax.broadcasted_iota(jnp.int32, (1, CLASSES), 1)
    ).astype(jnp.float32)
    seg_terms = crop_field[:, 0] * (
        class_top[:, 0] + jnp.log(class_total[:, 0]) - jnp.sum(class_logits * onehot, 1)
    )
    offset_err = logits[:, CLASSES : CLASSES + 2] - jnp.swapaxes(offset_target, 1, 2).reshape(
        POSITIONS, 2
    )
    offset_root = jnp.sqrt(offset_err * offset_err + 1.0)
    depth_pre = logits[:, CLASSES + 2]
    depth_err = jax.nn.softplus(depth_pre) - depth_target.reshape(POSITIONS)
    depth_root = jnp.sqrt(depth_err * depth_err + 1.0)
    local_sums = jnp.stack(
        [
            jnp.sum(seg_terms),
            jnp.sum(offset_field * jnp.sum(offset_root - 1.0, 1)),
            jnp.sum(lidar_field * (depth_root - 1.0)),
        ]
    )
    task_weights = jnp.exp(-task_scale) / counts
    logit_grad = jnp.concatenate(
        [
            task_weights[0] * crop_field * (class_exp / class_total - onehot),
            task_weights[1] * offset_field[:, None] * offset_err / offset_root,
            (task_weights[2] * lidar_field * depth_err / depth_root * jax.nn.sigmoid(depth_pre))[
                :, None
            ],
        ],
        axis=1,
    )
    logit_low = logit_grad.astype(low)
    local_bias = jnp.sum(logit_low.astype(jnp.float32), 0)
    head_grad = dot(feature_low, logit_low, (0, 0))
    feature_grad = dot(logit_low, head_low, (1, 1))
    project_grad_low = gelu_grad(project_pre, feature_grad).astype(low)
    project_grad = dot(concat_low, project_grad_low, (0, 0))
    concat_grad = dot(project_grad_low, project_low, (1, 1))
    branch_grads = jnp.stack(
        [
            gelu_grad(branch_pre[order], concat_grad[:, order * width : (order + 1) * width])
            for order in range(4)
        ]
    ).astype(low)
    pool_grad_low = gelu_grad(
        pool_pre, jnp.sum(concat_grad[:, 4 * width :], 0, keepdims=True)
    ).astype(low)
    own_place = chan_place.reshape(1)
    other_part = pyramid_field(1 - own_place, pyramid_low, branch_grads, columns)
    other_sent = swap_chan(other_part)
    later_grads, other_part = lax.optimization_barrier((branch_grads, other_part))
    pyramid_grad = pyramid_weights(
        output_low.T,
        later_grads,
        columns,
        pooled_low.astype(jnp.float32).reshape(D, 1),
        pool_grad_low.astype(jnp.float32),
    )
    pyramid_red = lax.psum_scatter(pyramid_grad, "dp", scatter_dimension=1, tiled=True)
    later_grads, pyramid_grad = lax.optimization_barrier((later_grads, pyramid_grad))
    own_part = pyramid_field(own_place, pyramid_low, later_grads, columns)
    pool_part = dot(pool_grad_low, pyramid_low[28], (1, 1)) / image_count
    pool_sum = own_half(pool_part, 1) + swap_chan(other_half(pool_part, 1))
    stream_grad = (
        own_part.astype(jnp.float32) + other_sent.astype(jnp.float32) + crop_field * pool_sum
    )

    own_gain_two = own_half(gain_two, 0)
    own_scale_two = own_half(scale_two, 0)
    normed_two = (own_half(expand_pre, 1) - own_half(mean_two, 0)) * own_scale_two
    upstream_two = crop_field * stream_grad
    gain_two_grad, shift_two_grad, loss_sums, bias_grad = small_sum(
        sizes,
        [jnp.sum(upstream_two * normed_two, 0), jnp.sum(upstream_two, 0), local_sums, local_bias],
        ("dp",),
        2,
    )
    task_means = loss_sums / counts
    total_loss = jnp.sum(jnp.exp(-task_scale) * task_means + task_scale)
    scale_grad = 1.0 - jnp.exp(-task_scale) * task_means
    expand_grad_low = (
        crop_field
        * own_gain_two
        * own_scale_two
        * (upstream_two - (shift_two_grad + normed_two * gain_two_grad) / crop_total)
    ).astype(low)
    second_part = dot(expand_grad_low, own_half(expand_low, 0)).astype(low)
    second_other = swap_chan(second_part)
    expand_rows = dot(expand_grad_low, second_low, (0, 0)).astype(low)
    expand_sent = swap_chan(other_half(expand_rows, 1))
    second_grad_low = (
        second_part.astype(jnp.float32) + second_other.astype(jnp.float32)
    ).astype(low)
    hidden_grad = middle_conv(second_grad_low, middle_low, columns, True, jnp.float32)
    upstream_one = gelu_grad(act_input, crop_field * hidden_grad)
    gain_one_all, shift_one_all = small_sum(
        sizes,
        [jnp.sum(upstream_one * normed_one, 0), jnp.sum(upstream_one, 0)],
        ("dp",),
        3,
    )
    gain_one_grad = own_half(gain_one_all, 0)
    shift_one_grad = own_half(shift_one_all, 0)
    first_grad_low = (
        crop_field
        * gain_one
        * scale_one
        * (upstream_one - (shift_one_all + normed_one * gain_one_all) / crop_total)
    ).astype(low)
    middle_grad = middle_weights(hidden_low.T, own_half(second_grad_low, 1), columns)
    reduce_grad = dot(stream_low, own_half(first_grad_low, 1), (0, 0)).astype(low)
    start_grad = dot(first_grad_low, own_half(reduce_low, 0), (1, 1)) + stream_grad
    start_grad_low = (crop_field * start_grad).astype(low)
    stem_grad = dot(patch_rows, start_grad_low, (0, 0)).astype(low)
    expand_own = own_half(expand_rows, 1)
    expand_grad = jnp.where(
        chan_place == 0,
        jnp.concatenate([expand_own, expand_sent], 0),
        jnp.concatenate([expand_sent, expand_own], 0),
    )

    small_grads = jnp.concatenate(
        [
            stem_grad.reshape(PATCH, dp_size, stem_share)
            .transpose(1, 0, 2)
            .reshape(dp_size, PATCH * stem_share),
            project_grad.astype(low)
            .reshape(5 * 128, dp_size, project_share)
            .transpose(1, 0, 2)
            .reshape(dp_size, 5 * 128 * project_share),
            head_grad.astype(low).reshape(dp_size, head_share * 22),
        ],
        1,
    )
    small_grads = jnp.pad(small_grads, ((0, 0), (0, small_rows * 256 - small_grads.shape[1])))
    packed_grads = jnp.concatenate(
        [
            reduce_grad.reshape(dp_size, row_share, 256),
            expand_grad.reshape(dp_size, row_share, 256),
            middle_grad.reshape(9, dp_size, mid_share, 256)
            .transpose(1, 0, 2, 3)
            .reshape(dp_size, 9 * mid_share, 256),
            small_grads.reshape(dp_size, small_rows, 256),
        ],
        1,
    )
    trunk_red = (
        lax.psum_scatter(packed_grads, "dp", scatter_dimension=0, tiled=True)
        .reshape(packed.shape)
        .astype(jnp.float32)
    )
    bottle_red = trunk_red[: 2 * row_share].reshape(bottle_weight.shape)
    middle_red = trunk_red[start : start + 9 * mid_share].reshape(middle_weight.shape)
    small_red = trunk_red[start + 9 * mid_share :].reshape(-1)
    stem_red = small_red[: stem_weight.size].reshape(stem_weight.shape)
    project_red = small_red[stem_weight.size : stem_weight.size + project_weight.size].reshape(
        project_weight.shape
    )
    size = stem_weight.size + project_weight.size
    head_red = small_red[size : size + head_weight.size].reshape(head_weight.shape)
    pyramid_red = pyramid_red.astype(jnp.float32)
    norm_grad = jnp.stack(
        [
            jnp.concatenate([gain_one_grad, gain_two_grad]),
            jnp.concatenate([shift_one_grad, shift_two_grad]),
        ]
    )[:, None, :]
    task_grad = jnp.concatenate([scale_grad, bias_grad])
    dp_first = (lax.axis_index("dp") == 0).astype(jnp.float32)
    chan_first = (chan_place == 0).astype(jnp.float32)
    own_squares = (
        jnp.sum(stem_red * stem_red)
        + jnp.sum(bottle_red * bottle_red)
        + jnp.sum(middle_red * middle_red)
        + jnp.sum(pyramid_red * pyramid_red)
        + jnp.sum(project_red * project_red)
        + chan_first * jnp.sum(head_red * head_red)
        + dp_first * jnp.sum(norm_grad * norm_grad)
        + dp_first * chan_first * jnp.sum(task_grad * task_grad)
    )
    grad_norm = jnp.sqrt(small_sum(sizes, [own_squares], ("dp", "chan"), 4)[0])
    factor = clip_level / jnp.maximum(grad_norm, clip_level)
    new_stem = adam_step(
        stem_weight, stem_first, stem_second, stem_red, factor, PATCH ** (-0.5), decay_rate
    )
    new_bottle = adam_step(
        bottle_weight, bottle_first, bottle_second, bottle_red, factor, D ** (-0.5), decay_rate
    )
    new_middle = adam_step(
        middle_weight,
        middle_first,
        middle_second,
        middle_red,
        factor,
        (9 * MID) ** (-0.5),
        decay_rate,
    )
    new_pyramid = adam_step(
        pyramid_weight,
        pyramid_first,
        pyramid_second,
        pyramid_red,
        factor,
        (3 * D) ** (-0.5),
        decay_rate,
    )
    new_project = adam_step(
        project_weight,
        project_first,
        project_second,
        project_red,
        factor,
        (5 * BRANCH) ** (-0.5),
        decay_rate,
    )
    new_head = adam_step(
        head_weight, head_first, head_second, head_red, factor, BRANCH ** (-0.5), decay_rate
    )
    new_norm = adam_step(norm_gains, norm_first, norm_second, norm_grad, factor, 0.3, 0.0)
    new_task = adam_step(task_params, task_first, task_second, task_grad, factor, 0.3, 0.0)
    return (
        total_loss,
        grad_norm,
        new_stem[0],
        new_stem[1],
        new_stem[2],
        new_bottle[0],
        new_bottle[1],
        new_bottle[2],
        new_middle[0],
        new_middle[1],
        new_middle[2],
        new_pyramid[0],
        new_pyramid[1],
        new_pyramid[2],
        new_project[0],
        new_project[1],
        new_project[2],
        new_head[0],
        new_head[1],
        new_head[2],
        new_norm[0],
        new_norm[1],
        new_norm[2],
        new_task[0],
        new_task[1],
        new_task[2],
    )


def solution(mesh):
    return jax.shard_map(
        functools.partial(on_device, dict(mesh.shape)),
        mesh=mesh,
        in_specs=(
            P("dp", None, None),
            P("dp", None),
            P("dp", None, None),
            P("dp", None),
            P("dp", None),
            P("dp", None),
            P("dp", None),
            P(None, "chan", "dp"),
            P(None, "chan", "dp"),
            P(None, "chan", "dp"),
            P(None, "dp", "chan"),
            P(None, "dp", "chan"),
            P(None, "dp", "chan"),
            P(None, "dp", "chan"),
            P(None, "dp", "chan"),
            P(None, "dp", "chan"),
            P(None, "dp", "chan"),
            P(None, "dp", "chan"),
            P(None, "dp", "chan"),
            P(None, "chan", "dp"),
            P(None, "chan", "dp"),
            P(None, "chan", "dp"),
            P("dp", None),
            P("dp", None),
            P("dp", None),
            P(None, "chan", None),
            P(None, "chan", None),
            P(None, "chan", None),
            P(),
            P(),
            P(),
        ),
        out_specs=(
            P(),
            P(),
            P(None, "chan", "dp"),
            P(None, "chan", "dp"),
            P(None, "chan", "dp"),
            P(None, "dp", "chan"),
            P(None, "dp", "chan"),
            P(None, "dp", "chan"),
            P(None, "dp", "chan"),
            P(None, "dp", "chan"),
            P(None, "dp", "chan"),
            P(None, "dp", "chan"),
            P(None, "dp", "chan"),
            P(None, "dp", "chan"),
            P(None, "chan", "dp"),
            P(None, "chan", "dp"),
            P(None, "chan", "dp"),
            P("dp", None),
            P("dp", None),
            P("dp", None),
            P(None, "chan", None),
            P(None, "chan", None),
            P(None, "chan", None),
            P(),
            P(),
            P(),
        ),
        check_vma=False,
    )
```

```python
import functools

import jax
import jax.numpy as jnp
from jax import lax
from jax.experimental import pallas as pl
from jax.experimental.pallas import tpu as pltpu
from jax.sharding import PartitionSpec as P

D = 2048
MID = 512
BRANCH = 256
CLASSES = 19
PATCH = 192
FH = 40
FW = 40
STEP = 10
POSITIONS = 1600


pyramid_rates = (0, 12, 24, 36)
norm_eps = 1e-05
clip_level = 0.01
adam_eps = 1e-08
decay_rate = 0.01


MESH_ID = pl.DeviceIdType.MESH


def group_place(sizes, axes):
    place = jnp.int32(0)
    for axis in axes:
        place = place * sizes[axis] + lax.axis_index(axis)
    return place


def group_device(sizes, axes, index):
    coords = {}
    for axis in reversed(axes):
        coords[axis] = lax.rem(index, sizes[axis])
        index = lax.div(index, sizes[axis])
    return tuple(coords.get(axis, lax.axis_index(axis)) for axis in ("dp", "chan"))


def sum_kernel(sizes, axes, count, x_ref, o_ref, slots, send_sem, recv_sem):
    me = group_place(sizes, axes)
    barrier = pltpu.get_barrier_semaphore()

    def greet(step, carry):
        other = lax.rem(me + step, count)
        pl.semaphore_signal(
            barrier, inc=1, device_id=group_device(sizes, axes, other), device_id_type=MESH_ID
        )
        return carry

    lax.fori_loop(1, count, greet, 0)
    pl.semaphore_wait(barrier, count - 1)

    def copy_to(step):
        other = lax.rem(me + step, count)
        return pltpu.make_async_remote_copy(
            src_ref=x_ref,
            dst_ref=slots.at[me],
            send_sem=send_sem.at[step],
            recv_sem=recv_sem.at[me],
            device_id=group_device(sizes, axes, other),
            device_id_type=MESH_ID,
        )

    def copy_from(step):
        other = lax.rem(me + step, count)
        return pltpu.make_async_remote_copy(
            src_ref=x_ref,
            dst_ref=slots.at[other],
            send_sem=send_sem.at[step],
            recv_sem=recv_sem.at[other],
            device_id=group_device(sizes, axes, other),
            device_id_type=MESH_ID,
        )

    def start(step, carry):
        copy_to(step).start()
        return carry

    lax.fori_loop(1, count, start, 0)
    slots[me] = x_ref[...]

    def arrive(step, carry):
        copy_from(step).wait_recv()
        return carry

    lax.fori_loop(1, count, arrive, 0)
    o_ref[...] = lax.fori_loop(
        1, count, lambda index, total: total + slots[index], slots[0]
    )

    def leave(step, carry):
        copy_to(step).wait_send()
        return carry

    lax.fori_loop(1, count, leave, 0)


def all_sum(sizes, values, axes, collective):
    count = 1
    for axis in axes:
        count *= sizes[axis]
    return pl.pallas_call(
        functools.partial(sum_kernel, sizes, axes, count),
        out_shape=jax.ShapeDtypeStruct(values.shape, jnp.float32),
        in_specs=[pl.BlockSpec(memory_space=pltpu.VMEM)],
        out_specs=pl.BlockSpec(memory_space=pltpu.VMEM),
        scratch_shapes=[
            pltpu.VMEM((count,) + values.shape, jnp.float32),
            pltpu.SemaphoreType.DMA((count,)),
            pltpu.SemaphoreType.DMA((count,)),
        ],
        compiler_params=pltpu.CompilerParams(
            collective_id=collective, has_side_effects=True, vmem_limit_bytes=32 << 20
        ),
        name="small_sum",
    )(values)


def small_sum(sizes, parts, axes, collective):
    flat = jnp.concatenate([part.reshape(-1) for part in parts])
    rows = -(-flat.shape[0] // 1024) * 8
    packed = jnp.pad(flat, (0, rows * 128 - flat.shape[0])).reshape(rows, 128)
    summed = all_sum(sizes, packed, axes, collective).reshape(-1)
    result = []
    start = 0
    for part in parts:
        size = part.size
        result.append(summed[start : start + size].reshape(part.shape))
        start += size
    return result


def swap_chan(values):
    return lax.ppermute(values, "chan", [(0, 1), (1, 0)])


def valid(step, length):
    return max(0, step), length + min(0, step)


def taps_of(rate):
    return [((tap // 3 - 1) * rate, (tap % 3 - 1) * rate) for tap in range(9)]


def shift_field(field, row_step, col_step):
    rows, cols = field.shape[:2]
    r0, r1 = valid(row_step, rows)
    c0, c1 = valid(col_step, cols)
    return jnp.pad(
        field[r0:r1, c0:c1],
        (
            (r0 - row_step, rows - (r1 - row_step)),
            (c0 - col_step, cols - (c1 - col_step)),
            (0, 0),
        ),
    )


def gelu_grad(values, upstream):
    return jax.vjp(jax.nn.gelu, values)[1](upstream)[0]


def dot(left, right, contract=(1, 0)):
    return lax.dot_general(
        left,
        right,
        (((contract[0],), (contract[1],)), ((), ())),
        preferred_element_type=jnp.float32,
    )


def place_of():
    dp = lax.axis_index("dp")
    return lax.div(dp, 4), lax.rem(lax.div(dp, 2), 2), lax.rem(dp, 2), lax.axis_index("chan")


def device_at(z, y, core, x):
    return ((z * 2 + y) * 2 + core, x)


def flip(value, turn):
    return lax.rem(value + turn, 2)


def z_flip(z, turn):
    return flip(lax.div(z, 2), turn // 2) * 2 + flip(lax.rem(z, 2), turn % 2)


def greet_neighbours(layers):
    z, y, core, x = place_of()
    barrier = pltpu.get_barrier_semaphore()
    for target in (
        device_at(z, y, 1 - core, x),
        device_at(z, 1 - y, core, x),
        device_at(z, y, core, 1 - x),
    ):
        pl.semaphore_signal(barrier, inc=1, device_id=target, device_id_type=MESH_ID)

    @pl.when(z > 0)
    def _():
        pl.semaphore_signal(
            barrier, inc=1, device_id=device_at(z - 1, y, core, x), device_id_type=MESH_ID
        )

    @pl.when(z < layers - 1)
    def _():
        pl.semaphore_signal(
            barrier, inc=1, device_id=device_at(z + 1, y, core, x), device_id_type=MESH_ID
        )

    peers = 3 + jnp.where(z > 0, 1, 0) + jnp.where(z < layers - 1, 1, 0)
    pl.semaphore_wait(barrier, peers)


def gather_kernel(
    layers,
    bottle,
    middle,
    small,
    bottle_all,
    middle_all,
    small_all,
    send_sems,
    recv_sems,
    local_sems,
):
    z, y, core, x = place_of()
    rows = bottle.shape[1]
    mid_rows = middle.shape[1]
    own_refs = (bottle, middle, small)

    def region(kind, block):
        zz, yy, kk, xx = block
        index = (zz * 2 + yy) * 2 + kk
        cols = pl.ds(pl.multiple_of(xx * 256, 256), 256)
        if kind == 0:
            return bottle_all.at[:, pl.ds(pl.multiple_of(index * rows, 16), rows), cols]
        if kind == 1:
            return middle_all.at[:, pl.ds(pl.multiple_of(index * mid_rows, 16), mid_rows), cols]
        return small_all.at[index, xx]

    def semaphore(kind, block):
        zz, yy, kk, xx = block
        return recv_sems.at[kind, ((zz * 2 + yy) * 2 + kk) * 2 + xx]

    own = (z, y, core, x)
    pending = []

    def send(kind, block, target, when=None):
        copy = pltpu.make_async_remote_copy(
            src_ref=own_refs[kind] if block is own else region(kind, block),
            dst_ref=region(kind, block),
            send_sem=send_sems.at[len(pending)],
            recv_sem=semaphore(kind, block),
            device_id=target,
            device_id_type=MESH_ID,
        )
        if when is None:
            copy.start()
        else:
            pl.when(when)(copy.start)
        pending.append((when, copy))

    def arrive(kind, block):
        pltpu.make_async_remote_copy(
            src_ref=region(kind, block),
            dst_ref=region(kind, block),
            send_sem=send_sems.at[0],
            recv_sem=semaphore(kind, block),
            device_id=device_at(z, y, 1 - core, x),
            device_id_type=MESH_ID,
        ).wait_recv()

    locals_ = [
        pltpu.make_async_copy(own_refs[kind], region(kind, own), local_sems.at[kind])
        for kind in range(3)
    ]
    for copy in locals_:
        copy.start()
    greet_neighbours(layers)
    sibling = device_at(z, y, 1 - core, x)
    other_x = device_at(z, y, core, 1 - x)
    other_y = device_at(z, 1 - y, core, x)

    def along_z(kind, block):
        if block[0] is z:
            send(kind, block, device_at(z + 1, y, core, x), z < layers - 1)
            send(kind, block, device_at(z - 1, y, core, x), z > 0)
        else:
            below = block[0] < z
            ahead = z + jnp.where(below, 1, -1)
            send(
                kind,
                block,
                device_at(ahead, y, core, x),
                jnp.logical_and(ahead >= 0, ahead < layers),
            )

    for kind in (0, 1):
        along_z(kind, own)
    send(2, own, other_x)
    send(2, own, other_y)
    send(1, own, other_x)
    send(0, own, other_y)
    along_z(2, own)
    send(0, own, other_x)
    send(1, own, other_y)
    for kind in range(3):
        send(kind, own, sibling)

    block = (z, y, core, 1 - x)
    arrive(2, block)
    send(2, block, other_y)
    along_z(2, block)
    send(2, block, sibling)
    for xx in (x, 1 - x):
        block = (z, 1 - y, core, xx)
        arrive(2, block)
        along_z(2, block)
        send(2, block, sibling)

    for turn in range(layers):
        zz = z if turn == 0 else z_flip(z, turn)
        if turn:
            for kind, near, far in ((0, other_y, other_x), (1, other_x, other_y)):
                block = (zz, y, core, x)
                arrive(kind, block)
                along_z(kind, block)
                send(kind, block, near)
                send(kind, block, far)
                send(kind, block, sibling)
        block = (zz, 1 - y, core, x)
        arrive(0, block)
        send(0, block, other_x)
        send(0, block, sibling)
        block = (zz, y, core, 1 - x)
        arrive(1, block)
        send(1, block, other_y)
        send(1, block, sibling)
        if turn:
            for yy, xx in ((y, x), (y, 1 - x), (1 - y, x), (1 - y, 1 - x)):
                block = (zz, yy, core, xx)
                arrive(2, block)
                along_z(2, block)
                send(2, block, sibling)
    for turn in range(layers):
        zz = z if turn == 0 else z_flip(z, turn)
        for yy in (y, 1 - y):
            block = (zz, yy, core, 1 - x)
            arrive(0, block)
            send(0, block, sibling)
        for xx in (x, 1 - x):
            block = (zz, 1 - y, core, xx)
            arrive(1, block)
            send(1, block, sibling)
    for kind in range(3):
        for turn in range(layers):
            zz = z if turn == 0 else z_flip(z, turn)
            for yy in (y, 1 - y):
                for xx in (x, 1 - x):
                    arrive(kind, (zz, yy, 1 - core, xx))
    for copy in locals_:
        copy.wait()
    for when, copy in pending:
        if when is None:
            copy.wait_send()
        else:
            pl.when(when)(copy.wait_send)


def gather_trunk(sizes, bottle, middle, small):
    count = sizes["dp"]
    if count != 16 or middle.shape[1] % 16:
        packed = [
            lax.all_gather(
                lax.all_gather(part, "dp", axis=1, tiled=True), "chan", axis=2, tiled=True
            )
            for part in (bottle, middle)
        ]
        return packed + [lax.all_gather(small, ("dp", "chan")).reshape((count, 2) + small.shape)]
    return pl.pallas_call(
        functools.partial(gather_kernel, count // 4),
        out_shape=[
            jax.ShapeDtypeStruct((2, D, MID), jnp.bfloat16),
            jax.ShapeDtypeStruct((9, MID, MID), jnp.bfloat16),
            jax.ShapeDtypeStruct((count, 2) + small.shape, jnp.bfloat16),
        ],
        in_specs=[pl.BlockSpec(memory_space=pl.ANY)] * 3,
        out_specs=[pl.BlockSpec(memory_space=pl.ANY)] * 3,
        scratch_shapes=[
            pltpu.SemaphoreType.DMA((160,)),
            pltpu.SemaphoreType.DMA((3, 2 * count)),
            pltpu.SemaphoreType.DMA((3,)),
        ],
        compiler_params=pltpu.CompilerParams(collective_id=5, has_side_effects=True),
        name="gather_trunk",
    )(bottle, middle, small)


PAD = 128
PYRAMID_ROWS = (-36, -24, -12, 0, 12, 24, 36)


def taps_by_row():
    fields = [(0, 0)] + [(rate, col * rate) for rate in (12, 24, 36) for col in (-1, 0, 1)]
    groups = []
    for row_step in PYRAMID_ROWS:
        group = []
        for place, (rate, col_step) in enumerate(fields):
            if rate == 0:
                if row_step == 0:
                    group.append((0, place))
            elif row_step == 0 or abs(row_step) == rate:
                turn = (1 if row_step > 0 else -1 if row_step < 0 else 0) + 1
                tap = 1 + 9 * (rate // 12 - 1) + 3 * turn + (col_step // rate + 1)
                group.append((tap, place))
        groups.append(group)
    return fields, groups


FIELDS, ROW_GROUPS = taps_by_row()
TAP_ORDER = [tap for group in ROW_GROUPS for tap, place in group]
PLACE_ORDER = [place for group in ROW_GROUPS for tap, place in group]


def roll_cols(values, columns, step):
    if step == 0:
        return values
    moved = pltpu.roll(values, (-step) % values.shape[0], 0)
    target = columns[:, :1] + float(step)
    return jnp.where((target >= 0.0) & (target < float(FW)), moved, 0.0)


def vmem(count):
    return [pl.BlockSpec(memory_space=pltpu.VMEM)] * count


def middle_kernel(back, x_ref, w_ref, col_ref, o_ref, canvas):
    edge = 4 * FW
    mid = x_ref.shape[1]
    values = x_ref[...].astype(jnp.float32)
    sign = -1 if back else 1
    for turn in range(3):
        canvas[turn, :edge] = jnp.zeros((edge, mid), canvas.dtype)
        canvas[turn, POSITIONS + edge :] = jnp.zeros((edge, mid), canvas.dtype)
        canvas[turn, edge : POSITIONS + edge] = roll_cols(
            values, col_ref, sign * 4 * (turn - 1)
        ).astype(canvas.dtype)
    block = 400

    def step(index, carry):
        total = None
        for row in range(3):
            first = pl.multiple_of(index * block + edge * (1 + sign * (row - 1)), 16)
            for turn in range(3):
                part = dot(
                    canvas[turn, pl.ds(first, block)],
                    w_ref[3 * row + turn],
                    (1, 1) if back else (1, 0),
                )
                total = part if total is None else total + part
        o_ref[pl.ds(pl.multiple_of(index * block, 16), block)] = total.astype(o_ref.dtype)
        return carry

    lax.fori_loop(0, POSITIONS // block, step, 0)


def middle_conv(field, weights, columns, back, dtype):
    return pl.pallas_call(
        functools.partial(middle_kernel, back),
        out_shape=jax.ShapeDtypeStruct((POSITIONS, MID), dtype),
        in_specs=vmem(3),
        out_specs=vmem(1)[0],
        scratch_shapes=[pltpu.VMEM((3, POSITIONS + 8 * FW, MID), jnp.bfloat16)],
        compiler_params=pltpu.CompilerParams(vmem_limit_bytes=40 << 20),
        cost_estimate=pl.CostEstimate(
            flops=2 * POSITIONS * 9 * MID * MID, bytes_accessed=16 << 20, transcendentals=0
        ),
        name="middle_back" if back else "middle_fwd",
    )(field, weights, columns)


def middle_weight_kernel(xt_ref, g_ref, col_ref, o_ref, fields):
    width = g_ref.shape[1]
    values = g_ref[...].astype(jnp.float32)
    for turn in range(3):
        fields[turn, :PAD] = jnp.zeros((PAD, width), fields.dtype)
        fields[turn, PAD + POSITIONS :] = jnp.zeros((PAD, width), fields.dtype)
        fields[turn, PAD : PAD + POSITIONS] = roll_cols(values, col_ref, -4 * (turn - 1)).astype(
            fields.dtype
        )
    for row in range(3):
        row_step = 4 * (row - 1)
        r0, r1 = valid(row_step, FH)
        first = r0 * FW // 128 * 128
        last = min(POSITIONS, -(-r1 * FW // 128) * 128)
        base = PAD + first - row_step * FW
        for turn in range(3):
            o_ref[3 * row + turn] = dot(
                xt_ref[:, first:last], fields[turn, base : base + last - first]
            ).astype(o_ref.dtype)


def middle_weights(field_t, grads, columns):
    depth, width = field_t.shape[0], grads.shape[1]
    return pl.pallas_call(
        middle_weight_kernel,
        out_shape=jax.ShapeDtypeStruct((9, depth, width), jnp.bfloat16),
        in_specs=vmem(3),
        out_specs=vmem(1)[0],
        scratch_shapes=[pltpu.VMEM((3, POSITIONS + 2 * PAD, width), jnp.bfloat16)],
        compiler_params=pltpu.CompilerParams(vmem_limit_bytes=40 << 20),
        cost_estimate=pl.CostEstimate(
            flops=2 * POSITIONS * 9 * depth * width, bytes_accessed=6 << 20, transcendentals=0
        ),
        name="middle_weights",
    )(field_t, grads, columns)


def fill_fields(g_ref, col_ref, fields):
    width = g_ref.shape[2]
    for place, (rate, col_step) in enumerate(FIELDS):
        fields[place, :PAD] = jnp.zeros((PAD, width), fields.dtype)
        fields[place, PAD + POSITIONS :] = jnp.zeros((PAD, width), fields.dtype)
        values = g_ref[rate // 12]
        fields[place, PAD : PAD + POSITIONS] = roll_cols(
            values.astype(jnp.float32), col_ref, -col_step
        ).astype(fields.dtype)


def weight_kernel(xt_ref, g_ref, col_ref, pool_ref, pool_grad_ref, o_ref, fields):
    width = g_ref.shape[2]
    depth = xt_ref.shape[0]
    fill_fields(g_ref, col_ref, fields)
    block = 512
    for row_step, group in zip(PYRAMID_ROWS, ROW_GROUPS):
        r0, r1 = valid(row_step, FH)
        first = r0 * FW // 128 * 128
        last = min(POSITIONS, -(-r1 * FW // 128) * 128)
        base = PAD + first - row_step * FW
        sets = [group[at : at + 2] for at in range(0, 10, 2)] if row_step == 0 else [group]
        for chosen in sets:
            right = jnp.concatenate(
                [fields[place, base : base + last - first] for tap, place in chosen], 1
            )

            def step(index, carry):
                rows = pl.ds(pl.multiple_of(index * block, 16), block)
                part = dot(xt_ref[rows, first:last], right)
                for offset, (tap, place) in enumerate(chosen):
                    o_ref[tap, rows] = part[:, offset * width : (offset + 1) * width].astype(
                        o_ref.dtype
                    )
                return carry

            lax.fori_loop(0, depth // block, step, 0)
    o_ref[28] = (pool_ref[...] * pool_grad_ref[...]).astype(o_ref.dtype)


def pyramid_weights(field_t, grads, columns, pooled, pool_grad):
    depth = field_t.shape[0]
    width = grads.shape[2]
    return pl.pallas_call(
        weight_kernel,
        out_shape=jax.ShapeDtypeStruct((29, depth, width), jnp.bfloat16),
        in_specs=vmem(5),
        out_specs=vmem(1)[0],
        scratch_shapes=[pltpu.VMEM((10, POSITIONS + 2 * PAD, width), jnp.bfloat16)],
        compiler_params=pltpu.CompilerParams(vmem_limit_bytes=56 << 20),
        cost_estimate=pl.CostEstimate(
            flops=2 * POSITIONS * 18 * depth * width, bytes_accessed=25 << 20, transcendentals=0
        ),
        name="pyramid_weights",
    )(field_t, grads, columns, pooled, pool_grad)


def field_kernel(half_ref, w_hbm, g_ref, col_ref, o_ref, weights, fields, stack, sems):
    width = g_ref.shape[2]
    depth = o_ref.shape[1]
    half = pl.ds(pl.multiple_of(half_ref[0] * depth, 16), depth)
    copies = []
    for slot, tap in enumerate(TAP_ORDER):
        copy = pltpu.make_async_copy(
            w_hbm.at[tap, half], weights.at[:, pl.ds(slot * width, width)], sems.at[slot]
        )
        copy.start()
        copies.append(copy)
    fill_fields(g_ref, col_ref, fields)
    for copy in copies:
        copy.wait()
    step_of = [step for step, group in zip(PYRAMID_ROWS, ROW_GROUPS) for entry in group]
    for r0, r1 in ((0, 4), (4, 12), (12, 16), (16, 24), (24, 28), (28, 36), (36, 40)):
        slots = [
            slot for slot, step in enumerate(step_of) if r0 - step >= 0 and r1 - step <= FH
        ]
        count = (r1 - r0) * FW
        for at, slot in enumerate(slots):
            base = PAD + (r0 - step_of[slot]) * FW
            stack[:count, at * width : (at + 1) * width] = fields[
                PLACE_ORDER[slot], base : base + count
            ]
        o_ref[r0 * FW : r1 * FW] = dot(
            stack[:count, : len(slots) * width],
            weights[:, slots[0] * width : (slots[-1] + 1) * width],
            (1, 1),
        ).astype(o_ref.dtype)


def pyramid_field(half, weights, grads, columns):
    depth, width = weights.shape[1] // 2, weights.shape[2]
    return pl.pallas_call(
        field_kernel,
        out_shape=jax.ShapeDtypeStruct((POSITIONS, depth), jnp.bfloat16),
        in_specs=[
            pl.BlockSpec(memory_space=pltpu.SMEM),
            pl.BlockSpec(memory_space=pl.ANY),
            pl.BlockSpec(memory_space=pltpu.VMEM),
            pl.BlockSpec(memory_space=pltpu.VMEM),
        ],
        out_specs=vmem(1)[0],
        scratch_shapes=[
            pltpu.VMEM((depth, 28 * width), jnp.bfloat16),
            pltpu.VMEM((10, POSITIONS + 2 * PAD, width), jnp.bfloat16),
            pltpu.VMEM((8 * FW, 19 * width), jnp.bfloat16),
            pltpu.SemaphoreType.DMA((28,)),
        ],
        compiler_params=pltpu.CompilerParams(vmem_limit_bytes=56 << 20),
        cost_estimate=pl.CostEstimate(
            flops=2 * POSITIONS * 17 * depth * width, bytes_accessed=15 << 20, transcendentals=0
        ),
        name="pyramid_field",
    )(half, weights, grads, columns)


BLOCK = 320


def block_rows(index):
    return pl.ds(pl.multiple_of(index * BLOCK, 16), BLOCK)


def gelu_slope(values, upstream):
    return jax.vjp(jax.nn.gelu, values)[1](upstream)[0]


def stem_kernel(p_ref, stem_ref, reduce_ref, crop_ref, count_ref, x_ref, a_ref, stat_ref):
    def step(index, carry):
        rows = block_rows(index)
        low = (crop_ref[rows] * dot(p_ref[rows], stem_ref[...])).astype(x_ref.dtype)
        x_ref[rows] = low
        value = dot(low, reduce_ref[0])
        a_ref[rows] = value
        return (
            carry[0] + jnp.sum(value, 0, keepdims=True),
            carry[1] + jnp.sum(value * value, 0, keepdims=True),
        )

    zero = jnp.zeros((1, MID), jnp.float32)
    total, square = lax.fori_loop(0, POSITIONS // BLOCK, step, (zero, zero))
    stat_ref[...] = jnp.concatenate(
        [total, square, count_ref[...], jnp.zeros((5, MID), jnp.float32)], 0
    )


def stem_reduce(patches, stem, bottle, crop, counts):
    return pl.pallas_call(
        stem_kernel,
        grid=(1,),
        out_shape=[
            jax.ShapeDtypeStruct((POSITIONS, D), jnp.bfloat16),
            jax.ShapeDtypeStruct((POSITIONS, MID), jnp.float32),
            jax.ShapeDtypeStruct((8, MID), jnp.float32),
        ],
        in_specs=[
            pl.BlockSpec((POSITIONS, PATCH), lambda i: (0, 0)),
            pl.BlockSpec((PATCH, D), lambda i: (0, 0)),
            pl.BlockSpec((1, D, MID), lambda i: (0, 0, 0)),
            pl.BlockSpec((POSITIONS, 1), lambda i: (0, 0)),
            pl.BlockSpec((1, MID), lambda i: (0, 0)),
        ],
        out_specs=[
            pl.BlockSpec((POSITIONS, D), lambda i: (0, 0)),
            pl.BlockSpec((POSITIONS, MID), lambda i: (0, 0)),
            pl.BlockSpec((8, MID), lambda i: (0, 0)),
        ],
        compiler_params=pltpu.CompilerParams(vmem_limit_bytes=50 << 20),
        cost_estimate=pl.CostEstimate(flops=5 * 10**9, bytes_accessed=14 << 20, transcendentals=0),
        name="stem_reduce",
    )(patches, stem, bottle, crop, counts)


def norm_rows(stat, count):
    mean = stat[0:1] / count
    return mean, lax.rsqrt(stat[1:2] / count - mean * mean + norm_eps)


def norm_middle_kernel(
    a_ref, stat_ref, gain_ref, crop_ref, w_ref, col_ref, h_ref, ht_ref, o_ref, canvas
):
    edge = 4 * FW
    mean, scale = norm_rows(stat_ref[...], stat_ref[2:3, 0:1])
    gain = gain_ref[0:1] * scale
    shift = gain_ref[1:2] - mean * gain
    low = (crop_ref[...] * jax.nn.gelu(a_ref[...] * gain + shift)).astype(h_ref.dtype)
    h_ref[...] = low
    ht_ref[...] = low.T
    values = low.astype(jnp.float32)
    for turn in range(3):
        canvas[turn, :edge] = jnp.zeros((edge, MID), canvas.dtype)
        canvas[turn, POSITIONS + edge :] = jnp.zeros((edge, MID), canvas.dtype)
        canvas[turn, edge : POSITIONS + edge] = roll_cols(values, col_ref, 4 * (turn - 1)).astype(
            canvas.dtype
        )
    block = 400

    def step(index, carry):
        total = None
        for row in range(3):
            first = pl.multiple_of(index * block + edge * row, 16)
            for turn in range(3):
                part = dot(canvas[turn, pl.ds(first, block)], w_ref[3 * row + turn])
                total = part if total is None else total + part
        o_ref[pl.ds(pl.multiple_of(index * block, 16), block)] = total.astype(o_ref.dtype)
        return carry

    lax.fori_loop(0, POSITIONS // block, step, 0)


def norm_middle(first_pre, stat, gains, crop, weights, columns):
    return pl.pallas_call(
        norm_middle_kernel,
        out_shape=[
            jax.ShapeDtypeStruct((POSITIONS, MID), jnp.bfloat16),
            jax.ShapeDtypeStruct((MID, POSITIONS), jnp.bfloat16),
            jax.ShapeDtypeStruct((POSITIONS, MID), jnp.bfloat16),
        ],
        in_specs=vmem(6),
        out_specs=vmem(3),
        scratch_shapes=[pltpu.VMEM((3, POSITIONS + 8 * FW, MID), jnp.bfloat16)],
        compiler_params=pltpu.CompilerParams(vmem_limit_bytes=50 << 20),
        cost_estimate=pl.CostEstimate(flops=8 * 10**9, bytes_accessed=14 << 20, transcendentals=0),
        name="norm_middle",
    )(first_pre, stat, gains, crop, weights, columns)


def expand_kernel(a_ref, w_ref, crop_ref, y_ref, stat_ref):
    def step(index, carry):
        rows = block_rows(index)
        value = dot(a_ref[rows], w_ref[0], (1, 1))
        y_ref[rows] = value.astype(y_ref.dtype)
        kept = crop_ref[rows] * value
        return (
            carry[0] + jnp.sum(kept, 0, keepdims=True),
            carry[1] + jnp.sum(kept * value, 0, keepdims=True),
        )

    zero = jnp.zeros((1, D), jnp.float32)
    sums = lax.fori_loop(0, POSITIONS // BLOCK, step, (zero, zero))
    for turn, values in enumerate(sums):
        for part in range(4):
            stat_ref[4 * turn + part : 4 * turn + part + 1] = values[
                :, part * MID : (part + 1) * MID
            ]


def expand_forward(second, bottle, crop):
    return pl.pallas_call(
        expand_kernel,
        grid=(1,),
        out_shape=[
            jax.ShapeDtypeStruct((POSITIONS, D), jnp.bfloat16),
            jax.ShapeDtypeStruct((8, MID), jnp.float32),
        ],
        in_specs=[
            pl.BlockSpec((POSITIONS, MID), lambda i: (0, 0)),
            pl.BlockSpec((1, D, MID), lambda i: (1, 0, 0)),
            pl.BlockSpec((POSITIONS, 1), lambda i: (0, 0)),
        ],
        out_specs=[
            pl.BlockSpec((POSITIONS, D), lambda i: (0, 0)),
            pl.BlockSpec((8, MID), lambda i: (0, 0)),
        ],
        compiler_params=pltpu.CompilerParams(vmem_limit_bytes=50 << 20),
        cost_estimate=pl.CostEstimate(flops=4 * 10**9, bytes_accessed=12 << 20, transcendentals=0),
        name="expand_forward",
    )(second, bottle, crop)


def pyramid_kernel(
    p_ref,
    stem_ref,
    y_ref,
    stat_ref,
    count_ref,
    gain_ref,
    crop_ref,
    w_hbm,
    project_ref,
    col_ref,
    x_ref,
    xt_ref,
    pool_ref,
    o_ref,
    pool_pre_ref,
    cat_ref,
    part_ref,
    weights,
    pool_weights,
    fields,
    sems,
):
    width = o_ref.shape[2]
    copies = []
    order = [3, 2, 4, 1, 5, 0, 6]
    starts = []
    place = 0
    for group in ROW_GROUPS:
        starts.append(place)
        place += len(group)
    for turn in order:
        group_copies = []
        for offset, (tap, _) in enumerate(ROW_GROUPS[turn]):
            slot = starts[turn] + offset
            copy = pltpu.make_async_copy(
                w_hbm.at[tap], weights.at[:, pl.ds(slot * width, width)], sems.at[slot]
            )
            copy.start()
            group_copies.append(copy)
        copies.append(group_copies)
    pool_copy = pltpu.make_async_copy(w_hbm.at[28], pool_weights, sems.at[28])
    pool_copy.start()

    count = count_ref[2:3, 0:1]
    stat = stat_ref[...]
    total = jnp.concatenate([stat[part : part + 1] for part in range(4)], 1)
    square = jnp.concatenate([stat[part : part + 1] for part in range(4, 8)], 1)
    mean = total / count
    gain = gain_ref[0:1] * lax.rsqrt(square / count - mean * mean + norm_eps)
    shift = gain_ref[1:2] - mean * gain

    def residual(index, carry):
        rows = block_rows(index)
        value = dot(p_ref[rows], stem_ref[...]) + (y_ref[rows].astype(jnp.float32) * gain + shift)
        low = (crop_ref[rows] * value).astype(x_ref.dtype)
        x_ref[rows] = low
        return carry + jnp.sum(low.astype(jnp.float32), 0, keepdims=True)

    pooled = lax.fori_loop(0, POSITIONS // BLOCK, residual, jnp.zeros((1, D), jnp.float32))
    pooled = (pooled / jnp.sum(crop_ref[...], keepdims=True)).astype(jnp.bfloat16)
    pool_ref[...] = pooled.astype(jnp.float32)
    for at in range(0, D, 256):
        xt_ref[at : at + 256] = x_ref[:, at : at + 256].T

    for turn, group_copies in zip(order, copies):
        for copy in group_copies:
            copy.wait()
        row_step = PYRAMID_ROWS[turn]
        group = ROW_GROUPS[turn]
        r0, r1 = valid(row_step, FH)
        length = (r1 - r0) * FW
        block = {1600: 800, 1120: 560, 640: 640, 160: 160}[length]
        cols = pl.ds(starts[turn] * width, len(group) * width)

        def step(index, carry):
            source = pl.multiple_of(index * block + r0 * FW, 16)
            target = pl.multiple_of(index * block + (r0 - row_step) * FW, 16)
            part = dot(x_ref[pl.ds(source, block)], weights[:, cols])
            for offset, (tap, field) in enumerate(group):
                piece = part[:, offset * width : (offset + 1) * width]
                rows = pl.ds(target, block)
                if row_step == 0:
                    fields[field, rows] = piece
                else:
                    fields[field, rows] += piece
            return carry

        lax.fori_loop(0, length // block, step, 0)
    pool_copy.wait()
    pool_pre = dot(jnp.broadcast_to(pooled, (16, D)), pool_weights[...])[0:1]
    pool_pre_ref[...] = pool_pre
    for branch in range(4):
        values = fields[0] if branch == 0 else fields[3 * branch - 1]
        if branch:
            for turn in (0, 2):
                place = 3 * branch - 2 + turn
                values = values + roll_cols(fields[place], col_ref, FIELDS[place][1])
        o_ref[branch] = values
        cat_ref[:, branch * width : (branch + 1) * width] = jax.nn.gelu(values).astype(
            cat_ref.dtype
        )
    cat_ref[:, 4 * width :] = jnp.broadcast_to(
        jax.nn.gelu(pool_pre).astype(cat_ref.dtype), (POSITIONS, width)
    )

    def project(index, carry):
        rows = block_rows(index)
        part_ref[rows] = dot(cat_ref[rows], project_ref[...]).astype(part_ref.dtype)
        return carry

    lax.fori_loop(0, POSITIONS // BLOCK, project, 0)


def pyramid_forward(patches, stem, expanded, stat, counts, gains, crop, weights, project, columns):
    depth, width = weights.shape[1:]
    low = jnp.bfloat16
    return pl.pallas_call(
        pyramid_kernel,
        out_shape=[
            jax.ShapeDtypeStruct((POSITIONS, depth), low),
            jax.ShapeDtypeStruct((depth, POSITIONS), low),
            jax.ShapeDtypeStruct((1, depth), jnp.float32),
            jax.ShapeDtypeStruct((4, POSITIONS, width), jnp.float32),
            jax.ShapeDtypeStruct((1, width), jnp.float32),
            jax.ShapeDtypeStruct((POSITIONS, 5 * width), low),
            jax.ShapeDtypeStruct((POSITIONS, BRANCH), low),
        ],
        in_specs=vmem(7) + [pl.BlockSpec(memory_space=pl.ANY)] + vmem(2),
        out_specs=vmem(7),
        scratch_shapes=[
            pltpu.VMEM((depth, 28 * width), low),
            pltpu.VMEM((depth, width), low),
            pltpu.VMEM((10, POSITIONS, width), jnp.float32),
            pltpu.SemaphoreType.DMA((29,)),
        ],
        compiler_params=pltpu.CompilerParams(vmem_limit_bytes=60 << 20),
        cost_estimate=pl.CostEstimate(
            flops=2 * POSITIONS * 19 * depth * width, bytes_accessed=40 << 20, transcendentals=0
        ),
        name="pyramid_fwd",
    )(patches, stem, expanded, stat, counts, gains, crop, weights, project, columns)


def head_kernel(
    own_ref,
    other_ref,
    head_ref,
    row_ref,
    label_ref,
    target_ref,
    mask_ref,
    project_ref,
    z_ref,
    pool_pre_ref,
    feature_ref,
    logit_ref,
    mixed_ref,
    grad_ref,
    pool_ref,
    stat_ref,
):
    width = grad_ref.shape[2]
    bias, scale = row_ref[0:1], row_ref[1:2]
    class_lane, depth_lane = row_ref[2:3], row_ref[4:5]

    def step(index, carry):
        rows = block_rows(index)
        mixed = own_ref[rows].astype(jnp.float32) + other_ref[rows].astype(jnp.float32)
        feature = jax.nn.gelu(mixed).astype(feature_ref.dtype)
        feature_ref[rows] = feature
        logits = dot(feature, head_ref[...]) + bias
        is_class = class_lane > 0.0
        top = jnp.max(jnp.where(is_class, logits, -jnp.inf), 1, keepdims=True)
        powers = jnp.where(is_class, jnp.exp(jnp.where(is_class, logits - top, 0.0)), 0.0)
        total = jnp.sum(powers, 1, keepdims=True)
        onehot = label_ref[rows]
        mask = mask_ref[rows]
        seg = mask[:, 0:1] * (
            top + jnp.log(total) - jnp.sum(logits * onehot, 1, keepdims=True)
        )
        is_depth = depth_lane > 0.0
        inverse = jnp.exp(-jnp.abs(logits))
        soft = jnp.maximum(logits, 0.0) + jnp.log(1.0 + inverse)
        slope = jnp.where(logits >= 0.0, 1.0, inverse) / (1.0 + inverse)
        error = jnp.where(is_depth, soft, logits) - target_ref[rows]
        root = jnp.sqrt(error * error + 1.0)
        other = error / root * jnp.where(is_depth, slope, 1.0)
        grad = scale * mask * jnp.where(is_class, powers / total - onehot, other)
        low = grad.astype(logit_ref.dtype)
        logit_ref[rows] = low
        up = gelu_slope(mixed, dot(low, head_ref[...], (1, 1))).astype(mixed_ref.dtype)
        mixed_ref[rows] = up
        cat = dot(up, project_ref[...], (1, 1))
        for branch in range(4):
            grad_ref[branch, rows] = gelu_slope(
                z_ref[branch, rows], cat[:, branch * width : (branch + 1) * width]
            ).astype(grad_ref.dtype)
        return (
            carry[0] + jnp.sum(low.astype(jnp.float32), 0, keepdims=True),
            carry[1] + jnp.sum(mask * (root - 1.0), 0, keepdims=True),
            carry[2] + jnp.sum(seg, 0, keepdims=True),
            carry[3] + jnp.sum(cat[:, 4 * width :], 0, keepdims=True),
        )

    zero = jnp.zeros((1, 128), jnp.float32)
    bias_sum, error_sum, seg_sum, pool_sum = lax.fori_loop(
        0,
        POSITIONS // BLOCK,
        step,
        (zero, zero, jnp.zeros((1, 1), jnp.float32), jnp.zeros((1, width), jnp.float32)),
    )
    pool_ref[...] = gelu_slope(pool_pre_ref[...], pool_sum).astype(jnp.bfloat16).astype(jnp.float32)
    stat_ref[...] = jnp.concatenate(
        [bias_sum, error_sum, jnp.broadcast_to(seg_sum, (1, 128)), jnp.zeros((5, 128))], 0
    )


def head_step(own, other, head, rows, label, target, mask, project, branches, pool_pre):
    width = branches.shape[2]
    low = jnp.bfloat16
    return pl.pallas_call(
        head_kernel,
        out_shape=[
            jax.ShapeDtypeStruct((POSITIONS, BRANCH), low),
            jax.ShapeDtypeStruct((POSITIONS, 128), low),
            jax.ShapeDtypeStruct((POSITIONS, BRANCH), low),
            jax.ShapeDtypeStruct((4, POSITIONS, width), low),
            jax.ShapeDtypeStruct((1, width), jnp.float32),
            jax.ShapeDtypeStruct((8, 128), jnp.float32),
        ],
        in_specs=vmem(10),
        out_specs=vmem(6),
        compiler_params=pltpu.CompilerParams(vmem_limit_bytes=50 << 20),
        cost_estimate=pl.CostEstimate(flops=2 * 10**9, bytes_accessed=16 << 20, transcendentals=0),
        name="head_step",
    )(own, other, head, rows, label, target, mask, project, branches, pool_pre)


def adam_step(weight, first, second, gradient, factor, rate, decay):
    gradient = gradient * factor
    first_new = 0.5 * first + 0.5 * gradient
    second_new = 0.5 * second + 0.5 * gradient * gradient
    direction = (
        first_new / (1.0 - 0.5**STEP) / (jnp.sqrt(second_new / (1.0 - 0.5**STEP)) + adam_eps)
    )
    return (weight - rate * (direction + decay * weight), first_new, second_new)


def on_device(
    sizes,
    patches,
    labels,
    offset_target,
    offset_valid,
    depth_target,
    lidar_valid,
    crop_mask,
    stem_weight,
    stem_first,
    stem_second,
    bottle_weight,
    bottle_first,
    bottle_second,
    middle_weight,
    middle_first,
    middle_second,
    pyramid_weight,
    pyramid_first,
    pyramid_second,
    project_weight,
    project_first,
    project_second,
    head_weight,
    head_first,
    head_second,
    norm_gains,
    norm_first,
    norm_second,
    task_params,
    task_first,
    task_second,
):
    chan_place = lax.axis_index("chan")
    dp_size = sizes["dp"]
    low = jnp.bfloat16
    crop_field = crop_mask.astype(jnp.float32).reshape(POSITIONS, 1)
    offset_field = crop_field[:, 0] * offset_valid.astype(jnp.float32).reshape(POSITIONS)
    lidar_field = crop_field[:, 0] * lidar_valid.astype(jnp.float32).reshape(POSITIONS)
    local_counts = jnp.stack([jnp.sum(crop_field), jnp.sum(offset_field), jnp.sum(lidar_field)])
    half = D // 2
    mid_half = MID // 2

    row_share = bottle_weight.shape[1]
    mid_share = middle_weight.shape[1]
    stem_share = stem_weight.shape[2]
    project_share = project_weight.shape[2]
    head_share = head_weight.shape[0]
    small_parts = [stem_weight, project_weight, head_weight]
    small_flat = jnp.concatenate([part.astype(low).reshape(-1) for part in small_parts])
    small_rows = -(-small_flat.shape[0] // (16 * 256)) * 16
    small_flat = jnp.pad(small_flat, (0, small_rows * 256 - small_flat.shape[0]))
    small_flat = small_flat.reshape(small_rows, 256)
    pyramid_low = lax.all_gather(pyramid_weight.astype(low), "dp", axis=1, tiled=True)
    bottle_low, middle_low, small = gather_trunk(
        sizes, bottle_weight.astype(low), middle_weight.astype(low), small_flat
    )
    small = small.reshape(dp_size, 2, small_rows * 256)
    size = PATCH * stem_share
    stem_low = (
        small[:, :, :size]
        .reshape(dp_size, 2, PATCH, stem_share)
        .transpose(2, 1, 0, 3)
        .reshape(PATCH, D)
    )
    own_small = lax.dynamic_index_in_dim(small, chan_place, 1, keepdims=False)
    project_low = (
        own_small[:, size : size + 5 * 128 * project_share]
        .reshape(dp_size, 5, 128, project_share)
        .transpose(1, 2, 0, 3)
        .reshape(5 * 128, BRANCH)
    )
    size += 5 * 128 * project_share
    head_low = own_small[:, size : size + head_share * 22].reshape(BRANCH, 22)

    gains_other = swap_chan(norm_gains)
    gains_all = jnp.where(
        chan_place == 0,
        jnp.concatenate([norm_gains, gains_other], 1),
        jnp.concatenate([gains_other, norm_gains], 1),
    )
    gain_one = gains_all[0, :, :mid_half].reshape(MID)
    shift_one = gains_all[1, :, :mid_half].reshape(MID)
    gain_two = gains_all[0, :, mid_half:].reshape(D)
    shift_two = gains_all[1, :, mid_half:].reshape(D)

    def own_half(values, axis):
        width = values.shape[axis] // 2
        return lax.dynamic_slice_in_dim(values, chan_place * width, width, axis)

    def other_half(values, axis):
        width = values.shape[axis] // 2
        return lax.dynamic_slice_in_dim(values, (1 - chan_place) * width, width, axis)

    columns = jnp.broadcast_to(
        lax.rem(lax.broadcasted_iota(jnp.int32, (POSITIONS, 1), 0), FW).astype(jnp.float32),
        (POSITIONS, 128),
    )
    lane = lax.broadcasted_iota(jnp.int32, (1, 128), 1)
    class_lane = (lane < CLASSES).astype(jnp.float32)
    offset_lane = ((lane >= CLASSES) & (lane < CLASSES + 2)).astype(jnp.float32)
    depth_lane = (lane == CLASSES + 2).astype(jnp.float32)
    onehot = (labels.reshape(POSITIONS, 1) == lane).astype(jnp.float32)
    mask = (
        class_lane * crop_field
        + offset_lane * offset_field[:, None]
        + depth_lane * lidar_field[:, None]
    )
    target = jnp.pad(
        jnp.concatenate([offset_target[0], depth_target], 0).T,
        ((0, 0), (CLASSES, 128 - CLASSES - 3)),
    )
    head_wide = jnp.pad(head_low, ((0, 0), (0, 128 - 22)))
    task_scale = task_params[:3]

    patch_rows = patches.reshape(POSITIONS, PATCH)
    stream_low, first_pre, stat_one = stem_reduce(
        patch_rows,
        stem_low,
        bottle_low,
        crop_field,
        jnp.pad(local_counts, (0, MID - 3)).reshape(1, MID),
    )
    stat_one = all_sum(sizes, stat_one, ("dp",), 0)
    hidden_low, hidden_t, second_low = norm_middle(
        first_pre, stat_one, jnp.stack([gain_one, shift_one]), crop_field, middle_low, columns
    )
    expand_pre, stat_two = expand_forward(second_low, bottle_low, crop_field)
    stat_two = all_sum(sizes, stat_two, ("dp",), 1)
    output_low, output_t, pooled, branch_pre, pool_pre, concat_low, project_part = pyramid_forward(
        patch_rows,
        stem_low,
        expand_pre,
        stat_two,
        stat_one,
        jnp.stack([gain_two, shift_two]),
        crop_field,
        pyramid_low,
        project_low,
        columns,
    )
    counts = stat_one[2, :3]
    crop_total = counts[0]
    mean_one = stat_one[0] / crop_total
    scale_one = lax.rsqrt(stat_one[1] / crop_total - mean_one * mean_one + norm_eps)
    mean_two = stat_two[:4].reshape(D) / crop_total
    scale_two = lax.rsqrt(stat_two[4:].reshape(D) / crop_total - mean_two * mean_two + norm_eps)
    image_count = jnp.sum(crop_field)
    task_weights = jnp.exp(-task_scale) / counts
    lane_rows = jnp.concatenate(
        [
            jnp.pad(task_params[3:], (0, 128 - 22)).reshape(1, 128),
            task_weights[0] * class_lane
            + task_weights[1] * offset_lane
            + task_weights[2] * depth_lane,
            class_lane,
            offset_lane,
            depth_lane,
            jnp.zeros((3, 128), jnp.float32),
        ],
        0,
    )
    feature_low, logit_low, project_grad_low, branch_grads, pool_grad, head_stat = head_step(
        project_part,
        swap_chan(project_part),
        head_wide,
        lane_rows,
        onehot,
        target,
        mask,
        project_low,
        branch_pre,
        pool_pre,
    )
    local_bias = head_stat[0, :22]
    local_sums = jnp.stack(
        [
            head_stat[2, 0],
            head_stat[1, CLASSES] + head_stat[1, CLASSES + 1],
            head_stat[1, CLASSES + 2],
        ]
    )
    head_grad = dot(feature_low, logit_low, (0, 0))[:, :22]
    project_grad = dot(concat_low, project_grad_low, (0, 0))
    pool_grad_low = pool_grad.astype(low)

    own_place = chan_place.reshape(1)
    other_part = pyramid_field(1 - own_place, pyramid_low, branch_grads, columns)
    other_sent = swap_chan(other_part)
    later_grads, other_part = lax.optimization_barrier((branch_grads, other_part))
    pyramid_grad = pyramid_weights(
        output_t,
        later_grads,
        columns,
        pooled.reshape(D, 1),
        pool_grad,
    )
    pyramid_red = lax.psum_scatter(pyramid_grad, "dp", scatter_dimension=1, tiled=True)
    later_grads, pyramid_grad = lax.optimization_barrier((later_grads, pyramid_grad))
    own_part = pyramid_field(own_place, pyramid_low, later_grads, columns)
    pool_part = dot(pool_grad_low, pyramid_low[28], (1, 1)) / image_count
    pool_sum = own_half(pool_part, 1) + swap_chan(other_half(pool_part, 1))
    stream_grad = (
        own_part.astype(jnp.float32) + other_sent.astype(jnp.float32) + crop_field * pool_sum
    )

    own_gain_two = own_half(gain_two, 0)
    own_scale_two = own_half(scale_two, 0)
    normed_two = (own_half(expand_pre, 1).astype(jnp.float32) - own_half(mean_two, 0)) * own_scale_two
    upstream_two = crop_field * stream_grad
    gain_two_grad, shift_two_grad, loss_sums, bias_grad = small_sum(
        sizes,
        [jnp.sum(upstream_two * normed_two, 0), jnp.sum(upstream_two, 0), local_sums, local_bias],
        ("dp",),
        2,
    )
    task_means = loss_sums / counts
    total_loss = jnp.sum(jnp.exp(-task_scale) * task_means + task_scale)
    scale_grad = 1.0 - jnp.exp(-task_scale) * task_means
    expand_grad_low = (
        crop_field
        * own_gain_two
        * own_scale_two
        * (upstream_two - (shift_two_grad + normed_two * gain_two_grad) / crop_total)
    ).astype(low)
    second_part = dot(expand_grad_low, own_half(bottle_low[1], 0)).astype(low)
    second_other = swap_chan(second_part)
    expand_rows = dot(expand_grad_low, second_low, (0, 0)).astype(low)
    expand_sent = swap_chan(other_half(expand_rows, 1))
    second_grad_low = (
        second_part.astype(jnp.float32) + second_other.astype(jnp.float32)
    ).astype(low)
    hidden_grad = middle_conv(second_grad_low, middle_low, columns, True, jnp.float32)
    normed_one = (first_pre - mean_one) * scale_one
    act_input = gain_one * normed_one + shift_one
    upstream_one = gelu_grad(act_input, crop_field * hidden_grad)
    gain_one_all, shift_one_all = small_sum(
        sizes,
        [jnp.sum(upstream_one * normed_one, 0), jnp.sum(upstream_one, 0)],
        ("dp",),
        3,
    )
    gain_one_grad = own_half(gain_one_all, 0)
    shift_one_grad = own_half(shift_one_all, 0)
    first_grad_low = (
        crop_field
        * gain_one
        * scale_one
        * (upstream_one - (shift_one_all + normed_one * gain_one_all) / crop_total)
    ).astype(low)
    middle_grad = middle_weights(hidden_t, own_half(second_grad_low, 1), columns)
    reduce_grad = dot(stream_low, own_half(first_grad_low, 1), (0, 0)).astype(low)
    start_grad = dot(first_grad_low, own_half(bottle_low[0], 0), (1, 1)) + stream_grad
    start_grad_low = (crop_field * start_grad).astype(low)
    stem_grad = dot(patch_rows, start_grad_low, (0, 0)).astype(low)
    expand_own = own_half(expand_rows, 1)
    expand_grad = jnp.where(
        chan_place == 0,
        jnp.concatenate([expand_own, expand_sent], 0),
        jnp.concatenate([expand_sent, expand_own], 0),
    )

    small_grads = jnp.concatenate(
        [
            stem_grad.reshape(PATCH, dp_size, stem_share)
            .transpose(1, 0, 2)
            .reshape(dp_size, PATCH * stem_share),
            project_grad.astype(low)
            .reshape(5 * 128, dp_size, project_share)
            .transpose(1, 0, 2)
            .reshape(dp_size, 5 * 128 * project_share),
            head_grad.astype(low).reshape(dp_size, head_share * 22),
        ],
        1,
    )
    small_grads = jnp.pad(small_grads, ((0, 0), (0, small_rows * 256 - small_grads.shape[1])))
    packed_grads = jnp.concatenate(
        [
            reduce_grad.reshape(dp_size, row_share, 256),
            expand_grad.reshape(dp_size, row_share, 256),
            middle_grad.reshape(9, dp_size, mid_share, 256)
            .transpose(1, 0, 2, 3)
            .reshape(dp_size, 9 * mid_share, 256),
            small_grads.reshape(dp_size, small_rows, 256),
        ],
        1,
    )
    packed_grads, pyramid_red = lax.optimization_barrier((packed_grads, pyramid_red))
    trunk_red = (
        lax.psum_scatter(packed_grads, "dp", scatter_dimension=0, tiled=True)
        .reshape(packed_grads.shape[1:])
        .astype(jnp.float32)
    )
    start = 2 * row_share
    bottle_red = trunk_red[: 2 * row_share].reshape(bottle_weight.shape)
    middle_red = trunk_red[start : start + 9 * mid_share].reshape(middle_weight.shape)
    small_red = trunk_red[start + 9 * mid_share :].reshape(-1)
    stem_red = small_red[: stem_weight.size].reshape(stem_weight.shape)
    project_red = small_red[stem_weight.size : stem_weight.size + project_weight.size].reshape(
        project_weight.shape
    )
    size = stem_weight.size + project_weight.size
    head_red = small_red[size : size + head_weight.size].reshape(head_weight.shape)
    pyramid_red = pyramid_red.astype(jnp.float32)
    norm_grad = jnp.stack(
        [
            jnp.concatenate([gain_one_grad, gain_two_grad]),
            jnp.concatenate([shift_one_grad, shift_two_grad]),
        ]
    )[:, None, :]
    task_grad = jnp.concatenate([scale_grad, bias_grad])
    dp_first = (lax.axis_index("dp") == 0).astype(jnp.float32)
    chan_first = (chan_place == 0).astype(jnp.float32)
    own_squares = (
        jnp.sum(stem_red * stem_red)
        + jnp.sum(bottle_red * bottle_red)
        + jnp.sum(middle_red * middle_red)
        + jnp.sum(pyramid_red * pyramid_red)
        + jnp.sum(project_red * project_red)
        + chan_first * jnp.sum(head_red * head_red)
        + dp_first * jnp.sum(norm_grad * norm_grad)
        + dp_first * chan_first * jnp.sum(task_grad * task_grad)
    )
    grad_norm = jnp.sqrt(small_sum(sizes, [own_squares], ("dp", "chan"), 4)[0])
    factor = clip_level / jnp.maximum(grad_norm, clip_level)
    new_stem = adam_step(
        stem_weight, stem_first, stem_second, stem_red, factor, PATCH ** (-0.5), decay_rate
    )
    new_bottle = adam_step(
        bottle_weight, bottle_first, bottle_second, bottle_red, factor, D ** (-0.5), decay_rate
    )
    new_middle = adam_step(
        middle_weight,
        middle_first,
        middle_second,
        middle_red,
        factor,
        (9 * MID) ** (-0.5),
        decay_rate,
    )
    new_pyramid = adam_step(
        pyramid_weight,
        pyramid_first,
        pyramid_second,
        pyramid_red,
        factor,
        (3 * D) ** (-0.5),
        decay_rate,
    )
    new_project = adam_step(
        project_weight,
        project_first,
        project_second,
        project_red,
        factor,
        (5 * BRANCH) ** (-0.5),
        decay_rate,
    )
    new_head = adam_step(
        head_weight, head_first, head_second, head_red, factor, BRANCH ** (-0.5), decay_rate
    )
    new_norm = adam_step(norm_gains, norm_first, norm_second, norm_grad, factor, 0.3, 0.0)
    new_task = adam_step(task_params, task_first, task_second, task_grad, factor, 0.3, 0.0)
    return (
        total_loss,
        grad_norm,
        new_stem[0],
        new_stem[1],
        new_stem[2],
        new_bottle[0],
        new_bottle[1],
        new_bottle[2],
        new_middle[0],
        new_middle[1],
        new_middle[2],
        new_pyramid[0],
        new_pyramid[1],
        new_pyramid[2],
        new_project[0],
        new_project[1],
        new_project[2],
        new_head[0],
        new_head[1],
        new_head[2],
        new_norm[0],
        new_norm[1],
        new_norm[2],
        new_task[0],
        new_task[1],
        new_task[2],
    )


def solution(mesh):
    return jax.shard_map(
        functools.partial(on_device, dict(mesh.shape)),
        mesh=mesh,
        in_specs=(
            P("dp", None, None),
            P("dp", None),
            P("dp", None, None),
            P("dp", None),
            P("dp", None),
            P("dp", None),
            P("dp", None),
            P(None, "chan", "dp"),
            P(None, "chan", "dp"),
            P(None, "chan", "dp"),
            P(None, "dp", "chan"),
            P(None, "dp", "chan"),
            P(None, "dp", "chan"),
            P(None, "dp", "chan"),
            P(None, "dp", "chan"),
            P(None, "dp", "chan"),
            P(None, "dp", "chan"),
            P(None, "dp", "chan"),
            P(None, "dp", "chan"),
            P(None, "chan", "dp"),
            P(None, "chan", "dp"),
            P(None, "chan", "dp"),
            P("dp", None),
            P("dp", None),
            P("dp", None),
            P(None, "chan", None),
            P(None, "chan", None),
            P(None, "chan", None),
            P(),
            P(),
            P(),
        ),
        out_specs=(
            P(),
            P(),
            P(None, "chan", "dp"),
            P(None, "chan", "dp"),
            P(None, "chan", "dp"),
            P(None, "dp", "chan"),
            P(None, "dp", "chan"),
            P(None, "dp", "chan"),
            P(None, "dp", "chan"),
            P(None, "dp", "chan"),
            P(None, "dp", "chan"),
            P(None, "dp", "chan"),
            P(None, "dp", "chan"),
            P(None, "dp", "chan"),
            P(None, "chan", "dp"),
            P(None, "chan", "dp"),
            P(None, "chan", "dp"),
            P("dp", None),
            P("dp", None),
            P("dp", None),
            P(None, "chan", None),
            P(None, "chan", None),
            P(None, "chan", None),
            P(),
            P(),
            P(),
        ),
        check_vma=False,
    )
```

```python
import functools

import jax
import jax.numpy as jnp
from jax import lax
from jax.experimental import pallas as pl
from jax.experimental.pallas import tpu as pltpu
from jax.sharding import PartitionSpec as P

D = 2048
MID = 512
BRANCH = 256
CLASSES = 19
PATCH = 192
FH = 40
FW = 40
STEP = 10
POSITIONS = 1600


pyramid_rates = (0, 12, 24, 36)
norm_eps = 1e-05
clip_level = 0.01
adam_eps = 1e-08
decay_rate = 0.01


MESH_ID = pl.DeviceIdType.MESH


def group_place(sizes, axes):
    place = jnp.int32(0)
    for axis in axes:
        place = place * sizes[axis] + lax.axis_index(axis)
    return place


def group_device(sizes, axes, index):
    coords = {}
    for axis in reversed(axes):
        coords[axis] = lax.rem(index, sizes[axis])
        index = lax.div(index, sizes[axis])
    return tuple(coords.get(axis, lax.axis_index(axis)) for axis in ("dp", "chan"))


def sum_kernel(sizes, axes, count, x_ref, o_ref, slots, send_sem, recv_sem):
    me = group_place(sizes, axes)
    barrier = pltpu.get_barrier_semaphore()

    def greet(step, carry):
        other = lax.rem(me + step, count)
        pl.semaphore_signal(
            barrier, inc=1, device_id=group_device(sizes, axes, other), device_id_type=MESH_ID
        )
        return carry

    lax.fori_loop(1, count, greet, 0)
    pl.semaphore_wait(barrier, count - 1)

    def copy_to(step):
        other = lax.rem(me + step, count)
        return pltpu.make_async_remote_copy(
            src_ref=x_ref,
            dst_ref=slots.at[me],
            send_sem=send_sem.at[step],
            recv_sem=recv_sem.at[me],
            device_id=group_device(sizes, axes, other),
            device_id_type=MESH_ID,
        )

    def copy_from(step):
        other = lax.rem(me + step, count)
        return pltpu.make_async_remote_copy(
            src_ref=x_ref,
            dst_ref=slots.at[other],
            send_sem=send_sem.at[step],
            recv_sem=recv_sem.at[other],
            device_id=group_device(sizes, axes, other),
            device_id_type=MESH_ID,
        )

    def start(step, carry):
        copy_to(step).start()
        return carry

    lax.fori_loop(1, count, start, 0)
    slots[me] = x_ref[...]

    def arrive(step, carry):
        copy_from(step).wait_recv()
        return carry

    lax.fori_loop(1, count, arrive, 0)
    o_ref[...] = lax.fori_loop(
        1, count, lambda index, total: total + slots[index], slots[0]
    )

    def leave(step, carry):
        copy_to(step).wait_send()
        return carry

    lax.fori_loop(1, count, leave, 0)


def all_sum(sizes, values, axes, collective):
    count = 1
    for axis in axes:
        count *= sizes[axis]
    return pl.pallas_call(
        functools.partial(sum_kernel, sizes, axes, count),
        out_shape=jax.ShapeDtypeStruct(values.shape, jnp.float32),
        in_specs=[pl.BlockSpec(memory_space=pltpu.VMEM)],
        out_specs=pl.BlockSpec(memory_space=pltpu.VMEM),
        scratch_shapes=[
            pltpu.VMEM((count,) + values.shape, jnp.float32),
            pltpu.SemaphoreType.DMA((count,)),
            pltpu.SemaphoreType.DMA((count,)),
        ],
        compiler_params=pltpu.CompilerParams(
            collective_id=collective, has_side_effects=True, vmem_limit_bytes=32 << 20
        ),
        name="small_sum",
    )(values)


def small_sum(sizes, parts, axes, collective):
    flat = jnp.concatenate([part.reshape(-1) for part in parts])
    rows = -(-flat.shape[0] // 1024) * 8
    packed = jnp.pad(flat, (0, rows * 128 - flat.shape[0])).reshape(rows, 128)
    summed = all_sum(sizes, packed, axes, collective).reshape(-1)
    result = []
    start = 0
    for part in parts:
        size = part.size
        result.append(summed[start : start + size].reshape(part.shape))
        start += size
    return result


def swap_chan(values):
    return lax.ppermute(values, "chan", [(0, 1), (1, 0)])


def valid(step, length):
    return max(0, step), length + min(0, step)


def taps_of(rate):
    return [((tap // 3 - 1) * rate, (tap % 3 - 1) * rate) for tap in range(9)]


def shift_field(field, row_step, col_step):
    rows, cols = field.shape[:2]
    r0, r1 = valid(row_step, rows)
    c0, c1 = valid(col_step, cols)
    return jnp.pad(
        field[r0:r1, c0:c1],
        (
            (r0 - row_step, rows - (r1 - row_step)),
            (c0 - col_step, cols - (c1 - col_step)),
            (0, 0),
        ),
    )


def gelu_grad(values, upstream):
    return jax.vjp(jax.nn.gelu, values)[1](upstream)[0]


def dot(left, right, contract=(1, 0)):
    return lax.dot_general(
        left,
        right,
        (((contract[0],), (contract[1],)), ((), ())),
        preferred_element_type=jnp.float32,
    )


def place_of():
    dp = lax.axis_index("dp")
    return lax.div(dp, 4), lax.rem(lax.div(dp, 2), 2), lax.rem(dp, 2), lax.axis_index("chan")


def device_at(z, y, core, x):
    return ((z * 2 + y) * 2 + core, x)


def flip(value, turn):
    return lax.rem(value + turn, 2)


def z_flip(z, turn):
    return flip(lax.div(z, 2), turn // 2) * 2 + flip(lax.rem(z, 2), turn % 2)


def greet_neighbours(layers):
    z, y, core, x = place_of()
    barrier = pltpu.get_barrier_semaphore()
    for target in (
        device_at(z, y, 1 - core, x),
        device_at(z, 1 - y, core, x),
        device_at(z, y, core, 1 - x),
    ):
        pl.semaphore_signal(barrier, inc=1, device_id=target, device_id_type=MESH_ID)

    @pl.when(z > 0)
    def _():
        pl.semaphore_signal(
            barrier, inc=1, device_id=device_at(z - 1, y, core, x), device_id_type=MESH_ID
        )

    @pl.when(z < layers - 1)
    def _():
        pl.semaphore_signal(
            barrier, inc=1, device_id=device_at(z + 1, y, core, x), device_id_type=MESH_ID
        )

    peers = 3 + jnp.where(z > 0, 1, 0) + jnp.where(z < layers - 1, 1, 0)
    pl.semaphore_wait(barrier, peers)


def gather_kernel(
    layers,
    bottle,
    middle,
    small,
    bottle_all,
    middle_all,
    small_all,
    send_sems,
    recv_sems,
    local_sems,
):
    z, y, core, x = place_of()
    rows = bottle.shape[1]
    mid_rows = middle.shape[1]
    small_rows = small.shape[0]
    own_refs = (bottle, middle, small)

    def region(kind, block):
        zz, yy, kk, xx = block
        index = (zz * 2 + yy) * 2 + kk
        cols = pl.ds(pl.multiple_of(xx * 256, 256), 256)
        if kind == 0:
            return bottle_all.at[:, pl.ds(pl.multiple_of(index * rows, 16), rows), cols]
        if kind == 1:
            return middle_all.at[:, pl.ds(pl.multiple_of(index * mid_rows, 16), mid_rows), cols]
        first = xx * (small_all.shape[0] // 2) + index * small_rows
        return small_all.at[pl.ds(pl.multiple_of(first, 16), small_rows)]

    def semaphore(kind, block):
        zz, yy, kk, xx = block
        return recv_sems.at[kind, ((zz * 2 + yy) * 2 + kk) * 2 + xx]

    own = (z, y, core, x)
    pending = []

    def send(kind, block, target, when=None):
        copy = pltpu.make_async_remote_copy(
            src_ref=own_refs[kind] if block is own else region(kind, block),
            dst_ref=region(kind, block),
            send_sem=send_sems.at[len(pending)],
            recv_sem=semaphore(kind, block),
            device_id=target,
            device_id_type=MESH_ID,
        )
        if when is None:
            copy.start()
        else:
            pl.when(when)(copy.start)
        pending.append((when, copy))

    def arrive(kind, block):
        pltpu.make_async_remote_copy(
            src_ref=region(kind, block),
            dst_ref=region(kind, block),
            send_sem=send_sems.at[0],
            recv_sem=semaphore(kind, block),
            device_id=device_at(z, y, 1 - core, x),
            device_id_type=MESH_ID,
        ).wait_recv()

    locals_ = [
        pltpu.make_async_copy(own_refs[kind], region(kind, own), local_sems.at[kind])
        for kind in range(3)
    ]
    for copy in locals_:
        copy.start()
    greet_neighbours(layers)
    sibling = device_at(z, y, 1 - core, x)
    other_x = device_at(z, y, core, 1 - x)
    other_y = device_at(z, 1 - y, core, x)

    def along_z(kind, block):
        if block[0] is z:
            send(kind, block, device_at(z + 1, y, core, x), z < layers - 1)
            send(kind, block, device_at(z - 1, y, core, x), z > 0)
        else:
            below = block[0] < z
            ahead = z + jnp.where(below, 1, -1)
            send(
                kind,
                block,
                device_at(ahead, y, core, x),
                jnp.logical_and(ahead >= 0, ahead < layers),
            )

    for kind in (0, 1):
        along_z(kind, own)
    send(2, own, other_x)
    send(2, own, other_y)
    send(1, own, other_x)
    send(0, own, other_y)
    along_z(2, own)
    send(0, own, other_x)
    send(1, own, other_y)
    for kind in range(3):
        send(kind, own, sibling)

    block = (z, y, core, 1 - x)
    arrive(2, block)
    send(2, block, other_y)
    along_z(2, block)
    send(2, block, sibling)
    for xx in (x, 1 - x):
        block = (z, 1 - y, core, xx)
        arrive(2, block)
        along_z(2, block)
        send(2, block, sibling)

    for turn in range(layers):
        zz = z if turn == 0 else z_flip(z, turn)
        if turn:
            for kind, near, far in ((0, other_y, other_x), (1, other_x, other_y)):
                block = (zz, y, core, x)
                arrive(kind, block)
                along_z(kind, block)
                send(kind, block, near)
                send(kind, block, far)
                send(kind, block, sibling)
        block = (zz, 1 - y, core, x)
        arrive(0, block)
        send(0, block, other_x)
        send(0, block, sibling)
        block = (zz, y, core, 1 - x)
        arrive(1, block)
        send(1, block, other_y)
        send(1, block, sibling)
        if turn:
            for yy, xx in ((y, x), (y, 1 - x), (1 - y, x), (1 - y, 1 - x)):
                block = (zz, yy, core, xx)
                arrive(2, block)
                along_z(2, block)
                send(2, block, sibling)
    for turn in range(layers):
        zz = z if turn == 0 else z_flip(z, turn)
        for yy in (y, 1 - y):
            block = (zz, yy, core, 1 - x)
            arrive(0, block)
            send(0, block, sibling)
        for xx in (x, 1 - x):
            block = (zz, 1 - y, core, xx)
            arrive(1, block)
            send(1, block, sibling)
    for kind in range(3):
        for turn in range(layers):
            zz = z if turn == 0 else z_flip(z, turn)
            for yy in (y, 1 - y):
                for xx in (x, 1 - x):
                    arrive(kind, (zz, yy, 1 - core, xx))
    for copy in locals_:
        copy.wait()
    for when, copy in pending:
        if when is None:
            copy.wait_send()
        else:
            pl.when(when)(copy.wait_send)


def gather_trunk(sizes, bottle, middle, small):
    count = sizes["dp"]
    if count != 16 or middle.shape[1] % 16:
        packed = [
            lax.all_gather(
                lax.all_gather(part, "dp", axis=1, tiled=True), "chan", axis=2, tiled=True
            )
            for part in (bottle, middle)
        ]
        return packed + [lax.all_gather(small, ("chan", "dp")).reshape(D, small.shape[1])]
    return pl.pallas_call(
        functools.partial(gather_kernel, count // 4),
        out_shape=[
            jax.ShapeDtypeStruct((2, D, MID), jnp.bfloat16),
            jax.ShapeDtypeStruct((9, MID, MID), jnp.bfloat16),
            jax.ShapeDtypeStruct((D, small.shape[1]), jnp.bfloat16),
        ],
        in_specs=[pl.BlockSpec(memory_space=pl.ANY)] * 3,
        out_specs=[pl.BlockSpec(memory_space=pl.ANY)] * 3,
        scratch_shapes=[
            pltpu.SemaphoreType.DMA((160,)),
            pltpu.SemaphoreType.DMA((3, 2 * count)),
            pltpu.SemaphoreType.DMA((3,)),
        ],
        compiler_params=pltpu.CompilerParams(collective_id=5, has_side_effects=True),
        name="gather_trunk",
    )(bottle, middle, small)


PAD = 128
PYRAMID_ROWS = (-36, -24, -12, 0, 12, 24, 36)


def taps_by_row():
    fields = [(0, 0)] + [(rate, col * rate) for rate in (12, 24, 36) for col in (-1, 0, 1)]
    groups = []
    for row_step in PYRAMID_ROWS:
        group = []
        for place, (rate, col_step) in enumerate(fields):
            if rate == 0:
                if row_step == 0:
                    group.append((0, place))
            elif row_step == 0 or abs(row_step) == rate:
                turn = (1 if row_step > 0 else -1 if row_step < 0 else 0) + 1
                tap = 1 + 9 * (rate // 12 - 1) + 3 * turn + (col_step // rate + 1)
                group.append((tap, place))
        groups.append(group)
    return fields, groups


FIELDS, ROW_GROUPS = taps_by_row()
TAP_ORDER = [tap for group in ROW_GROUPS for tap, place in group]
PLACE_ORDER = [place for group in ROW_GROUPS for tap, place in group]


def roll_cols(values, columns, step):
    if step == 0:
        return values
    moved = pltpu.roll(values, (-step) % values.shape[0], 0)
    target = columns[:, :1] + float(step)
    return jnp.where((target >= 0.0) & (target < float(FW)), moved, 0.0)


def vmem(count):
    return [pl.BlockSpec(memory_space=pltpu.VMEM)] * count


def middle_kernel(back, x_ref, w_ref, col_ref, o_ref, canvas):
    edge = 4 * FW
    mid = x_ref.shape[1]
    values = x_ref[...].astype(jnp.float32)
    sign = -1 if back else 1
    for turn in range(3):
        canvas[turn, :edge] = jnp.zeros((edge, mid), canvas.dtype)
        canvas[turn, POSITIONS + edge :] = jnp.zeros((edge, mid), canvas.dtype)
        canvas[turn, edge : POSITIONS + edge] = roll_cols(
            values, col_ref, sign * 4 * (turn - 1)
        ).astype(canvas.dtype)
    block = 400

    def step(index, carry):
        total = None
        for row in range(3):
            first = pl.multiple_of(index * block + edge * (1 + sign * (row - 1)), 16)
            for turn in range(3):
                part = dot(
                    canvas[turn, pl.ds(first, block)],
                    w_ref[3 * row + turn],
                    (1, 1) if back else (1, 0),
                )
                total = part if total is None else total + part
        o_ref[pl.ds(pl.multiple_of(index * block, 16), block)] = total.astype(o_ref.dtype)
        return carry

    lax.fori_loop(0, POSITIONS // block, step, 0)


def middle_conv(field, weights, columns, back, dtype):
    return pl.pallas_call(
        functools.partial(middle_kernel, back),
        out_shape=jax.ShapeDtypeStruct((POSITIONS, MID), dtype),
        in_specs=vmem(3),
        out_specs=vmem(1)[0],
        scratch_shapes=[pltpu.VMEM((3, POSITIONS + 8 * FW, MID), jnp.bfloat16)],
        compiler_params=pltpu.CompilerParams(vmem_limit_bytes=40 << 20),
        cost_estimate=pl.CostEstimate(
            flops=2 * POSITIONS * 9 * MID * MID, bytes_accessed=16 << 20, transcendentals=0
        ),
        name="middle_back" if back else "middle_fwd",
    )(field, weights, columns)


def middle_weight_kernel(xt_ref, g_ref, col_ref, o_ref, fields):
    width = g_ref.shape[1]
    values = g_ref[...].astype(jnp.float32)
    for turn in range(3):
        fields[turn, :PAD] = jnp.zeros((PAD, width), fields.dtype)
        fields[turn, PAD + POSITIONS :] = jnp.zeros((PAD, width), fields.dtype)
        fields[turn, PAD : PAD + POSITIONS] = roll_cols(values, col_ref, -4 * (turn - 1)).astype(
            fields.dtype
        )
    for row in range(3):
        row_step = 4 * (row - 1)
        r0, r1 = valid(row_step, FH)
        first = r0 * FW // 128 * 128
        last = min(POSITIONS, -(-r1 * FW // 128) * 128)
        base = PAD + first - row_step * FW
        for turn in range(3):
            o_ref[3 * row + turn] = dot(
                xt_ref[:, first:last], fields[turn, base : base + last - first]
            ).astype(o_ref.dtype)


def middle_weights(field_t, grads, columns):
    depth, width = field_t.shape[0], grads.shape[1]
    return pl.pallas_call(
        middle_weight_kernel,
        out_shape=jax.ShapeDtypeStruct((9, depth, width), jnp.bfloat16),
        in_specs=vmem(3),
        out_specs=vmem(1)[0],
        scratch_shapes=[pltpu.VMEM((3, POSITIONS + 2 * PAD, width), jnp.bfloat16)],
        compiler_params=pltpu.CompilerParams(vmem_limit_bytes=40 << 20),
        cost_estimate=pl.CostEstimate(
            flops=2 * POSITIONS * 9 * depth * width, bytes_accessed=6 << 20, transcendentals=0
        ),
        name="middle_weights",
    )(field_t, grads, columns)


def fill_fields(g_ref, col_ref, fields):
    width = g_ref.shape[2]
    for place, (rate, col_step) in enumerate(FIELDS):
        fields[place, :PAD] = jnp.zeros((PAD, width), fields.dtype)
        fields[place, PAD + POSITIONS :] = jnp.zeros((PAD, width), fields.dtype)
        values = g_ref[rate // 12]
        fields[place, PAD : PAD + POSITIONS] = roll_cols(
            values.astype(jnp.float32), col_ref, -col_step
        ).astype(fields.dtype)


def weight_kernel(xt_ref, g_ref, col_ref, pool_ref, pool_grad_ref, o_ref, fields):
    width = g_ref.shape[2]
    depth = xt_ref.shape[0]
    fill_fields(g_ref, col_ref, fields)
    block = 512
    for row_step, group in zip(PYRAMID_ROWS, ROW_GROUPS):
        r0, r1 = valid(row_step, FH)
        first = r0 * FW // 128 * 128
        last = min(POSITIONS, -(-r1 * FW // 128) * 128)
        base = PAD + first - row_step * FW
        sets = [group[at : at + 2] for at in range(0, 10, 2)] if row_step == 0 else [group]
        for chosen in sets:
            right = jnp.concatenate(
                [fields[place, base : base + last - first] for tap, place in chosen], 1
            )

            def step(index, carry):
                rows = pl.ds(pl.multiple_of(index * block, 16), block)
                part = dot(xt_ref[rows, first:last], right)
                for offset, (tap, place) in enumerate(chosen):
                    o_ref[tap, rows] = part[:, offset * width : (offset + 1) * width].astype(
                        o_ref.dtype
                    )
                return carry

            lax.fori_loop(0, depth // block, step, 0)
    o_ref[28] = (pool_ref[...] * pool_grad_ref[...]).astype(o_ref.dtype)


def pyramid_weights(field_t, grads, columns, pooled, pool_grad):
    depth = field_t.shape[0]
    width = grads.shape[2]
    return pl.pallas_call(
        weight_kernel,
        out_shape=jax.ShapeDtypeStruct((29, depth, width), jnp.bfloat16),
        in_specs=vmem(5),
        out_specs=vmem(1)[0],
        scratch_shapes=[pltpu.VMEM((10, POSITIONS + 2 * PAD, width), jnp.bfloat16)],
        compiler_params=pltpu.CompilerParams(vmem_limit_bytes=56 << 20),
        cost_estimate=pl.CostEstimate(
            flops=2 * POSITIONS * 18 * depth * width, bytes_accessed=25 << 20, transcendentals=0
        ),
        name="pyramid_weights",
    )(field_t, grads, columns, pooled, pool_grad)


def field_kernel(
    place_ref, w_hbm, near_hbm, far_hbm, g_ref, other_ref, col_ref, o_ref, weights, fields, stack, sems
):
    width = g_ref.shape[2]
    both = 2 * width
    depth = o_ref.shape[1]
    half = pl.ds(pl.multiple_of(place_ref[0] * depth, 16), depth)
    core = place_ref[1]
    part = near_hbm.shape[0]
    own = []
    other = []
    for slot, tap in enumerate(TAP_ORDER):
        copy = pltpu.make_async_copy(
            w_hbm.at[tap, half], weights.at[:, pl.ds(slot * both, width)], sems.at[0, slot]
        )
        copy.start()
        own.append(copy)
        target = weights.at[:, pl.ds(slot * both + width, width)]
        near = pltpu.make_async_copy(near_hbm.at[tap % part], target, sems.at[1, slot])
        far = pltpu.make_async_copy(far_hbm.at[tap % part], target, sems.at[1, slot])
        is_near = core == tap // part
        pl.when(is_near)(near.start)
        pl.when(jnp.logical_not(is_near))(far.start)
        other.append(near)
    for place, (rate, col_step) in enumerate(FIELDS):
        fields[place, :PAD] = jnp.zeros((PAD, both), fields.dtype)
        fields[place, PAD + POSITIONS :] = jnp.zeros((PAD, both), fields.dtype)
        for side, ref in enumerate((g_ref, other_ref)):
            fields[place, PAD : PAD + POSITIONS, side * width : (side + 1) * width] = roll_cols(
                ref[rate // 12].astype(jnp.float32), col_ref, -col_step
            ).astype(fields.dtype)
    step_of = [step for step, group in zip(PYRAMID_ROWS, ROW_GROUPS) for entry in group]
    waited = set()
    for r0, r1 in ((16, 24), (12, 16), (24, 28), (4, 12), (28, 36), (0, 4), (36, 40)):
        slots = [
            slot for slot, step in enumerate(step_of) if r0 - step >= 0 and r1 - step <= FH
        ]
        count = (r1 - r0) * FW
        for at, slot in enumerate(slots):
            if slot not in waited:
                waited.add(slot)
                own[slot].wait()
                other[slot].wait()
            base = PAD + (r0 - step_of[slot]) * FW
            stack[:count, at * both : (at + 1) * both] = fields[
                PLACE_ORDER[slot], base : base + count
            ]
        o_ref[r0 * FW : r1 * FW] = dot(
            stack[:count, : len(slots) * both],
            weights[:, slots[0] * both : (slots[-1] + 1) * both],
            (1, 1),
        ).astype(o_ref.dtype)


def pyramid_field(place, weights, near, far, grads, other, columns):
    depth, width = weights.shape[1] // 2, weights.shape[2]
    hbm = pl.BlockSpec(memory_space=pl.ANY)
    return pl.pallas_call(
        field_kernel,
        out_shape=jax.ShapeDtypeStruct((POSITIONS, depth), jnp.float32),
        in_specs=[pl.BlockSpec(memory_space=pltpu.SMEM), hbm, hbm, hbm] + vmem(3),
        out_specs=vmem(1)[0],
        scratch_shapes=[
            pltpu.VMEM((depth, 28 * 2 * width), jnp.bfloat16),
            pltpu.VMEM((10, POSITIONS + 2 * PAD, 2 * width), jnp.bfloat16),
            pltpu.VMEM((8 * FW, 19 * 2 * width), jnp.bfloat16),
            pltpu.SemaphoreType.DMA((2, 28)),
        ],
        compiler_params=pltpu.CompilerParams(vmem_limit_bytes=56 << 20),
        cost_estimate=pl.CostEstimate(
            flops=2 * POSITIONS * 34 * depth * width, bytes_accessed=25 << 20, transcendentals=0
        ),
        name="pyramid_field",
    )(place, weights, near, far, grads, other, columns)


BLOCK = 320


def block_rows(index):
    return pl.ds(pl.multiple_of(index * BLOCK, 16), BLOCK)


def gelu_slope(values, upstream):
    return jax.vjp(jax.nn.gelu, values)[1](upstream)[0]


def stem_kernel(p_ref, stem_ref, reduce_ref, crop_ref, count_ref, x_ref, a_ref, stat_ref):
    def step(index, carry):
        rows = block_rows(index)
        low = (crop_ref[rows] * dot(p_ref[rows], stem_ref[:, :PATCH], (1, 1))).astype(x_ref.dtype)
        x_ref[rows] = low
        value = dot(low, reduce_ref[0])
        a_ref[rows] = value
        return (
            carry[0] + jnp.sum(value, 0, keepdims=True),
            carry[1] + jnp.sum(value * value, 0, keepdims=True),
        )

    zero = jnp.zeros((1, MID), jnp.float32)
    total, square = lax.fori_loop(0, POSITIONS // BLOCK, step, (zero, zero))
    stat_ref[...] = jnp.concatenate(
        [total, square, count_ref[...], jnp.zeros((5, MID), jnp.float32)], 0
    )


def stem_reduce(patches, stem, bottle, crop, counts):
    return pl.pallas_call(
        stem_kernel,
        grid=(1,),
        out_shape=[
            jax.ShapeDtypeStruct((POSITIONS, D), jnp.bfloat16),
            jax.ShapeDtypeStruct((POSITIONS, MID), jnp.float32),
            jax.ShapeDtypeStruct((8, MID), jnp.float32),
        ],
        in_specs=[
            pl.BlockSpec((POSITIONS, PATCH), lambda i: (0, 0)),
            pl.BlockSpec(stem.shape, lambda i: (0, 0)),
            pl.BlockSpec((1, D, MID), lambda i: (0, 0, 0)),
            pl.BlockSpec((POSITIONS, 1), lambda i: (0, 0)),
            pl.BlockSpec((1, MID), lambda i: (0, 0)),
        ],
        out_specs=[
            pl.BlockSpec((POSITIONS, D), lambda i: (0, 0)),
            pl.BlockSpec((POSITIONS, MID), lambda i: (0, 0)),
            pl.BlockSpec((8, MID), lambda i: (0, 0)),
        ],
        compiler_params=pltpu.CompilerParams(vmem_limit_bytes=50 << 20),
        cost_estimate=pl.CostEstimate(flops=5 * 10**9, bytes_accessed=14 << 20, transcendentals=0),
        name="stem_reduce",
    )(patches, stem, bottle, crop, counts)


def norm_rows(stat, count):
    mean = stat[0:1] / count
    return mean, lax.rsqrt(stat[1:2] / count - mean * mean + norm_eps)


def norm_middle_kernel(
    a_ref, stat_ref, gain_ref, crop_ref, w_ref, col_ref, h_ref, ht_ref, o_ref, canvas
):
    edge = 4 * FW
    mean, scale = norm_rows(stat_ref[...], stat_ref[2:3, 0:1])
    gain = gain_ref[0:1] * scale
    shift = gain_ref[1:2] - mean * gain
    low = (crop_ref[...] * jax.nn.gelu(a_ref[...] * gain + shift)).astype(h_ref.dtype)
    h_ref[...] = low
    ht_ref[...] = low.T
    values = low.astype(jnp.float32)
    for turn in range(3):
        canvas[turn, :edge] = jnp.zeros((edge, MID), canvas.dtype)
        canvas[turn, POSITIONS + edge :] = jnp.zeros((edge, MID), canvas.dtype)
        canvas[turn, edge : POSITIONS + edge] = roll_cols(values, col_ref, 4 * (turn - 1)).astype(
            canvas.dtype
        )
    block = 400

    def step(index, carry):
        total = None
        for row in range(3):
            first = pl.multiple_of(index * block + edge * row, 16)
            for turn in range(3):
                part = dot(canvas[turn, pl.ds(first, block)], w_ref[3 * row + turn])
                total = part if total is None else total + part
        o_ref[pl.ds(pl.multiple_of(index * block, 16), block)] = total.astype(o_ref.dtype)
        return carry

    lax.fori_loop(0, POSITIONS // block, step, 0)


def norm_middle(first_pre, stat, gains, crop, weights, columns):
    return pl.pallas_call(
        norm_middle_kernel,
        out_shape=[
            jax.ShapeDtypeStruct((POSITIONS, MID), jnp.bfloat16),
            jax.ShapeDtypeStruct((MID, POSITIONS), jnp.bfloat16),
            jax.ShapeDtypeStruct((POSITIONS, MID), jnp.bfloat16),
        ],
        in_specs=vmem(6),
        out_specs=vmem(3),
        scratch_shapes=[pltpu.VMEM((3, POSITIONS + 8 * FW, MID), jnp.bfloat16)],
        compiler_params=pltpu.CompilerParams(vmem_limit_bytes=50 << 20),
        cost_estimate=pl.CostEstimate(flops=8 * 10**9, bytes_accessed=14 << 20, transcendentals=0),
        name="norm_middle",
    )(first_pre, stat, gains, crop, weights, columns)


def expand_kernel(a_ref, w_ref, crop_ref, y_ref, stat_ref):
    def step(index, carry):
        rows = block_rows(index)
        value = dot(a_ref[rows], w_ref[0], (1, 1))
        y_ref[rows] = value.astype(y_ref.dtype)
        kept = crop_ref[rows] * value
        return (
            carry[0] + jnp.sum(kept, 0, keepdims=True),
            carry[1] + jnp.sum(kept * value, 0, keepdims=True),
        )

    zero = jnp.zeros((1, D), jnp.float32)
    sums = lax.fori_loop(0, POSITIONS // BLOCK, step, (zero, zero))
    for turn, values in enumerate(sums):
        for part in range(4):
            stat_ref[4 * turn + part : 4 * turn + part + 1] = values[
                :, part * MID : (part + 1) * MID
            ]


def expand_forward(second, bottle, crop):
    return pl.pallas_call(
        expand_kernel,
        grid=(1,),
        out_shape=[
            jax.ShapeDtypeStruct((POSITIONS, D), jnp.bfloat16),
            jax.ShapeDtypeStruct((8, MID), jnp.float32),
        ],
        in_specs=[
            pl.BlockSpec((POSITIONS, MID), lambda i: (0, 0)),
            pl.BlockSpec((1, D, MID), lambda i: (1, 0, 0)),
            pl.BlockSpec((POSITIONS, 1), lambda i: (0, 0)),
        ],
        out_specs=[
            pl.BlockSpec((POSITIONS, D), lambda i: (0, 0)),
            pl.BlockSpec((8, MID), lambda i: (0, 0)),
        ],
        compiler_params=pltpu.CompilerParams(vmem_limit_bytes=50 << 20),
        cost_estimate=pl.CostEstimate(flops=4 * 10**9, bytes_accessed=12 << 20, transcendentals=0),
        name="expand_forward",
    )(second, bottle, crop)


def pyramid_kernel(
    p_ref,
    stem_ref,
    y_ref,
    stat_ref,
    count_ref,
    gain_ref,
    crop_ref,
    w_hbm,
    project_ref,
    col_ref,
    x_ref,
    xt_ref,
    pool_ref,
    o_ref,
    pool_pre_ref,
    cat_ref,
    part_ref,
    weights,
    pool_weights,
    fields,
    sems,
):
    width = o_ref.shape[2]
    copies = []
    order = [3, 2, 4, 1, 5, 0, 6]
    starts = []
    place = 0
    for group in ROW_GROUPS:
        starts.append(place)
        place += len(group)
    for turn in order:
        group_copies = []
        for offset, (tap, _) in enumerate(ROW_GROUPS[turn]):
            slot = starts[turn] + offset
            copy = pltpu.make_async_copy(
                w_hbm.at[tap], weights.at[:, pl.ds(slot * width, width)], sems.at[slot]
            )
            copy.start()
            group_copies.append(copy)
        copies.append(group_copies)
    pool_copy = pltpu.make_async_copy(w_hbm.at[28], pool_weights, sems.at[28])
    pool_copy.start()

    count = count_ref[2:3, 0:1]
    stat = stat_ref[...]
    total = jnp.concatenate([stat[part : part + 1] for part in range(4)], 1)
    square = jnp.concatenate([stat[part : part + 1] for part in range(4, 8)], 1)
    mean = total / count
    gain = gain_ref[0:1] * lax.rsqrt(square / count - mean * mean + norm_eps)
    shift = gain_ref[1:2] - mean * gain

    def residual(index, carry):
        rows = block_rows(index)
        value = dot(p_ref[rows], stem_ref[:, :PATCH], (1, 1)) + (y_ref[rows].astype(jnp.float32) * gain + shift)
        low = (crop_ref[rows] * value).astype(x_ref.dtype)
        x_ref[rows] = low
        return carry + jnp.sum(low.astype(jnp.float32), 0, keepdims=True)

    pooled = lax.fori_loop(0, POSITIONS // BLOCK, residual, jnp.zeros((1, D), jnp.float32))
    pooled = (pooled / jnp.sum(crop_ref[...], keepdims=True)).astype(jnp.bfloat16)
    pool_ref[...] = pooled.astype(jnp.float32)
    for at in range(0, D, 256):
        xt_ref[at : at + 256] = x_ref[:, at : at + 256].T

    for turn, group_copies in zip(order, copies):
        for copy in group_copies:
            copy.wait()
        row_step = PYRAMID_ROWS[turn]
        group = ROW_GROUPS[turn]
        r0, r1 = valid(row_step, FH)
        length = (r1 - r0) * FW
        block = {1600: 800, 1120: 560, 640: 640, 160: 160}[length]
        cols = pl.ds(starts[turn] * width, len(group) * width)

        def step(index, carry):
            source = pl.multiple_of(index * block + r0 * FW, 16)
            target = pl.multiple_of(index * block + (r0 - row_step) * FW, 16)
            part = dot(x_ref[pl.ds(source, block)], weights[:, cols])
            for offset, (tap, field) in enumerate(group):
                piece = part[:, offset * width : (offset + 1) * width]
                rows = pl.ds(target, block)
                if row_step == 0:
                    fields[field, rows] = piece
                else:
                    fields[field, rows] += piece
            return carry

        lax.fori_loop(0, length // block, step, 0)
    pool_copy.wait()
    pool_pre = dot(jnp.broadcast_to(pooled, (16, D)), pool_weights[...])[0:1]
    pool_pre_ref[...] = pool_pre
    for branch in range(4):
        values = fields[0] if branch == 0 else fields[3 * branch - 1]
        if branch:
            for turn in (0, 2):
                place = 3 * branch - 2 + turn
                values = values + roll_cols(fields[place], col_ref, FIELDS[place][1])
        o_ref[branch] = values
        cat_ref[:, branch * width : (branch + 1) * width] = jax.nn.gelu(values).astype(
            cat_ref.dtype
        )
    cat_ref[:, 4 * width :] = jnp.broadcast_to(
        jax.nn.gelu(pool_pre).astype(cat_ref.dtype), (POSITIONS, width)
    )

    def project(index, carry):
        rows = block_rows(index)
        part_ref[rows] = dot(cat_ref[rows], project_ref[...]).astype(part_ref.dtype)
        return carry

    lax.fori_loop(0, POSITIONS // BLOCK, project, 0)


def pyramid_forward(patches, stem, expanded, stat, counts, gains, crop, weights, project, columns):
    depth, width = weights.shape[1:]
    low = jnp.bfloat16
    return pl.pallas_call(
        pyramid_kernel,
        out_shape=[
            jax.ShapeDtypeStruct((POSITIONS, depth), low),
            jax.ShapeDtypeStruct((depth, POSITIONS), low),
            jax.ShapeDtypeStruct((1, depth), jnp.float32),
            jax.ShapeDtypeStruct((4, POSITIONS, width), jnp.float32),
            jax.ShapeDtypeStruct((1, width), jnp.float32),
            jax.ShapeDtypeStruct((POSITIONS, 5 * width), low),
            jax.ShapeDtypeStruct((POSITIONS, BRANCH), low),
        ],
        in_specs=vmem(7) + [pl.BlockSpec(memory_space=pl.ANY)] + vmem(2),
        out_specs=vmem(7),
        scratch_shapes=[
            pltpu.VMEM((depth, 28 * width), low),
            pltpu.VMEM((depth, width), low),
            pltpu.VMEM((10, POSITIONS, width), jnp.float32),
            pltpu.SemaphoreType.DMA((29,)),
        ],
        compiler_params=pltpu.CompilerParams(vmem_limit_bytes=60 << 20),
        cost_estimate=pl.CostEstimate(
            flops=2 * POSITIONS * 19 * depth * width, bytes_accessed=40 << 20, transcendentals=0
        ),
        name="pyramid_fwd",
    )(patches, stem, expanded, stat, counts, gains, crop, weights, project, columns)


def head_kernel(
    own_ref,
    other_ref,
    head_ref,
    row_ref,
    label_ref,
    target_ref,
    mask_ref,
    project_ref,
    z_ref,
    pool_pre_ref,
    feature_ref,
    logit_ref,
    mixed_ref,
    grad_ref,
    pool_ref,
    stat_ref,
):
    width = grad_ref.shape[2]
    bias, scale = row_ref[0:1], row_ref[1:2]
    class_lane, depth_lane = row_ref[2:3], row_ref[4:5]

    def step(index, carry):
        rows = block_rows(index)
        mixed = own_ref[rows].astype(jnp.float32) + other_ref[rows].astype(jnp.float32)
        feature = jax.nn.gelu(mixed).astype(feature_ref.dtype)
        feature_ref[rows] = feature
        logits = dot(feature, head_ref[...]) + bias
        is_class = class_lane > 0.0
        top = jnp.max(jnp.where(is_class, logits, -jnp.inf), 1, keepdims=True)
        powers = jnp.where(is_class, jnp.exp(jnp.where(is_class, logits - top, 0.0)), 0.0)
        total = jnp.sum(powers, 1, keepdims=True)
        onehot = label_ref[rows]
        mask = mask_ref[rows]
        seg = mask[:, 0:1] * (
            top + jnp.log(total) - jnp.sum(logits * onehot, 1, keepdims=True)
        )
        is_depth = depth_lane > 0.0
        inverse = jnp.exp(-jnp.abs(logits))
        soft = jnp.maximum(logits, 0.0) + jnp.log(1.0 + inverse)
        slope = jnp.where(logits >= 0.0, 1.0, inverse) / (1.0 + inverse)
        error = jnp.where(is_depth, soft, logits) - target_ref[rows]
        root = jnp.sqrt(error * error + 1.0)
        other = error / root * jnp.where(is_depth, slope, 1.0)
        grad = scale * mask * jnp.where(is_class, powers / total - onehot, other)
        low = grad.astype(logit_ref.dtype)
        logit_ref[rows] = low
        up = gelu_slope(mixed, dot(low, head_ref[...], (1, 1))).astype(mixed_ref.dtype)
        mixed_ref[rows] = up
        cat = dot(up, project_ref[...], (1, 1))
        for branch in range(4):
            grad_ref[branch, rows] = gelu_slope(
                z_ref[branch, rows], cat[:, branch * width : (branch + 1) * width]
            ).astype(grad_ref.dtype)
        return (
            carry[0] + jnp.sum(low.astype(jnp.float32), 0, keepdims=True),
            carry[1] + jnp.sum(mask * (root - 1.0), 0, keepdims=True),
            carry[2] + jnp.sum(seg, 0, keepdims=True),
            carry[3] + jnp.sum(cat[:, 4 * width :], 0, keepdims=True),
        )

    zero = jnp.zeros((1, 128), jnp.float32)
    bias_sum, error_sum, seg_sum, pool_sum = lax.fori_loop(
        0,
        POSITIONS // BLOCK,
        step,
        (zero, zero, jnp.zeros((1, 1), jnp.float32), jnp.zeros((1, width), jnp.float32)),
    )
    pool_ref[...] = gelu_slope(pool_pre_ref[...], pool_sum).astype(jnp.bfloat16).astype(jnp.float32)
    stat_ref[...] = jnp.concatenate(
        [bias_sum, error_sum, jnp.broadcast_to(seg_sum, (1, 128)), jnp.zeros((5, 128))], 0
    )


def head_step(own, other, head, rows, label, target, mask, project, branches, pool_pre):
    width = branches.shape[2]
    low = jnp.bfloat16
    return pl.pallas_call(
        head_kernel,
        out_shape=[
            jax.ShapeDtypeStruct((POSITIONS, BRANCH), low),
            jax.ShapeDtypeStruct((POSITIONS, 128), low),
            jax.ShapeDtypeStruct((POSITIONS, BRANCH), low),
            jax.ShapeDtypeStruct((4, POSITIONS, width), low),
            jax.ShapeDtypeStruct((1, width), jnp.float32),
            jax.ShapeDtypeStruct((8, 128), jnp.float32),
        ],
        in_specs=vmem(10),
        out_specs=vmem(6),
        compiler_params=pltpu.CompilerParams(vmem_limit_bytes=50 << 20),
        cost_estimate=pl.CostEstimate(flops=2 * 10**9, bytes_accessed=16 << 20, transcendentals=0),
        name="head_step",
    )(own, other, head, rows, label, target, mask, project, branches, pool_pre)


def adam_step(weight, first, second, gradient, factor, rate, decay):
    gradient = gradient * factor
    first_new = 0.5 * first + 0.5 * gradient
    second_new = 0.5 * second + 0.5 * gradient * gradient
    direction = (
        first_new / (1.0 - 0.5**STEP) / (jnp.sqrt(second_new / (1.0 - 0.5**STEP)) + adam_eps)
    )
    return (weight - rate * (direction + decay * weight), first_new, second_new)


def on_device(
    sizes,
    patches,
    labels,
    offset_target,
    offset_valid,
    depth_target,
    lidar_valid,
    crop_mask,
    stem_weight,
    stem_first,
    stem_second,
    bottle_weight,
    bottle_first,
    bottle_second,
    middle_weight,
    middle_first,
    middle_second,
    pyramid_weight,
    pyramid_first,
    pyramid_second,
    project_weight,
    project_first,
    project_second,
    head_weight,
    head_first,
    head_second,
    norm_gains,
    norm_first,
    norm_second,
    task_params,
    task_first,
    task_second,
):
    chan_place = lax.axis_index("chan")
    dp_size = sizes["dp"]
    low = jnp.bfloat16
    crop_field = crop_mask.astype(jnp.float32).reshape(POSITIONS, 1)
    offset_field = crop_field[:, 0] * offset_valid.astype(jnp.float32).reshape(POSITIONS)
    lidar_field = crop_field[:, 0] * lidar_valid.astype(jnp.float32).reshape(POSITIONS)
    local_counts = jnp.stack([jnp.sum(crop_field), jnp.sum(offset_field), jnp.sum(lidar_field)])
    half = D // 2
    mid_half = MID // 2

    row_share = bottle_weight.shape[1]
    mid_share = middle_weight.shape[1]
    stem_share = stem_weight.shape[2]
    project_share = project_weight.shape[2]
    head_share = head_weight.shape[0]
    small_flat = jnp.concatenate(
        [project_weight.astype(low).reshape(-1), head_weight.astype(low).reshape(-1)]
    )
    small_room = stem_share * PATCH
    small_flat = jnp.pad(small_flat, (0, small_room - small_flat.shape[0]))
    stem_shard = jnp.concatenate(
        [stem_weight.astype(low).reshape(PATCH, stem_share).T, small_flat.reshape(stem_share, PATCH)],
        1,
    )
    bottle_low, middle_low, stem_low = gather_trunk(
        sizes, bottle_weight.astype(low), middle_weight.astype(low), stem_shard
    )
    pyramid_shard, bottle_low = lax.optimization_barrier((pyramid_weight.astype(low), bottle_low))
    pyramid_low = lax.all_gather(pyramid_shard, "dp", axis=1, tiled=True)
    own_small = lax.dynamic_slice_in_dim(stem_low, chan_place * half, half, 0)[:, PATCH:].reshape(
        dp_size, small_room
    )
    size = 5 * 128 * project_share
    project_low = (
        own_small[:, :size]
        .reshape(dp_size, 5, 128, project_share)
        .transpose(1, 2, 0, 3)
        .reshape(5 * 128, BRANCH)
    )
    head_low = own_small[:, size : size + head_share * 22].reshape(BRANCH, 22)

    core = lax.rem(lax.axis_index("dp"), 2)
    near_rows = swap_chan(
        lax.dynamic_slice(
            pyramid_low, (14 * core, (1 - chan_place) * half, 0), (14, half, BRANCH // 2)
        )
    )
    far_rows = lax.ppermute(
        near_rows, "dp", [(place, place + 1 - 2 * (place % 2)) for place in range(dp_size)]
    )

    gains_other = swap_chan(norm_gains)
    gains_all = jnp.where(
        chan_place == 0,
        jnp.concatenate([norm_gains, gains_other], 1),
        jnp.concatenate([gains_other, norm_gains], 1),
    )
    gain_one = gains_all[0, :, :mid_half].reshape(MID)
    shift_one = gains_all[1, :, :mid_half].reshape(MID)
    gain_two = gains_all[0, :, mid_half:].reshape(D)
    shift_two = gains_all[1, :, mid_half:].reshape(D)

    def own_half(values, axis):
        width = values.shape[axis] // 2
        return lax.dynamic_slice_in_dim(values, chan_place * width, width, axis)

    def other_half(values, axis):
        width = values.shape[axis] // 2
        return lax.dynamic_slice_in_dim(values, (1 - chan_place) * width, width, axis)

    columns = jnp.broadcast_to(
        lax.rem(lax.broadcasted_iota(jnp.int32, (POSITIONS, 1), 0), FW).astype(jnp.float32),
        (POSITIONS, 128),
    )
    lane = lax.broadcasted_iota(jnp.int32, (1, 128), 1)
    class_lane = (lane < CLASSES).astype(jnp.float32)
    offset_lane = ((lane >= CLASSES) & (lane < CLASSES + 2)).astype(jnp.float32)
    depth_lane = (lane == CLASSES + 2).astype(jnp.float32)
    onehot = (labels.reshape(POSITIONS, 1) == lane).astype(jnp.float32)
    mask = (
        class_lane * crop_field
        + offset_lane * offset_field[:, None]
        + depth_lane * lidar_field[:, None]
    )
    target = jnp.pad(
        jnp.concatenate([offset_target[0], depth_target], 0).T,
        ((0, 0), (CLASSES, 128 - CLASSES - 3)),
    )
    head_wide = jnp.pad(head_low, ((0, 0), (0, 128 - 22)))
    task_scale = task_params[:3]

    patch_rows = patches.reshape(POSITIONS, PATCH)
    stream_low, first_pre, stat_one = stem_reduce(
        patch_rows,
        stem_low,
        bottle_low,
        crop_field,
        jnp.pad(local_counts, (0, MID - 3)).reshape(1, MID),
    )
    stat_one = all_sum(sizes, stat_one, ("dp",), 0)
    hidden_low, hidden_t, second_low = norm_middle(
        first_pre, stat_one, jnp.stack([gain_one, shift_one]), crop_field, middle_low, columns
    )
    expand_pre, stat_two = expand_forward(second_low, bottle_low, crop_field)
    stat_two = all_sum(sizes, stat_two, ("dp",), 1)
    output_low, output_t, pooled, branch_pre, pool_pre, concat_low, project_part = pyramid_forward(
        patch_rows,
        stem_low,
        expand_pre,
        stat_two,
        stat_one,
        jnp.stack([gain_two, shift_two]),
        crop_field,
        pyramid_low,
        project_low,
        columns,
    )
    counts = stat_one[2, :3]
    crop_total = counts[0]
    mean_one = stat_one[0] / crop_total
    scale_one = lax.rsqrt(stat_one[1] / crop_total - mean_one * mean_one + norm_eps)
    mean_two = stat_two[:4].reshape(D) / crop_total
    scale_two = lax.rsqrt(stat_two[4:].reshape(D) / crop_total - mean_two * mean_two + norm_eps)
    image_count = jnp.sum(crop_field)
    task_weights = jnp.exp(-task_scale) / counts
    lane_rows = jnp.concatenate(
        [
            jnp.pad(task_params[3:], (0, 128 - 22)).reshape(1, 128),
            task_weights[0] * class_lane
            + task_weights[1] * offset_lane
            + task_weights[2] * depth_lane,
            class_lane,
            offset_lane,
            depth_lane,
            jnp.zeros((3, 128), jnp.float32),
        ],
        0,
    )
    feature_low, logit_low, project_grad_low, branch_grads, pool_grad, head_stat = head_step(
        project_part,
        swap_chan(project_part),
        head_wide,
        lane_rows,
        onehot,
        target,
        mask,
        project_low,
        branch_pre,
        pool_pre,
    )
    local_bias = head_stat[0, :22]
    local_sums = jnp.stack(
        [
            head_stat[2, 0],
            head_stat[1, CLASSES] + head_stat[1, CLASSES + 1],
            head_stat[1, CLASSES + 2],
        ]
    )
    head_grad = dot(feature_low, logit_low, (0, 0))[:, :22]
    project_grad = dot(concat_low, project_grad_low, (0, 0))
    pool_grad_low = pool_grad.astype(low)

    other_grads = swap_chan(branch_grads)
    pyramid_grad = pyramid_weights(
        output_t, branch_grads, columns, pooled.reshape(D, 1), pool_grad
    )
    pyramid_red = lax.psum_scatter(pyramid_grad, "dp", scatter_dimension=1, tiled=True)
    later_grads, pyramid_grad = lax.optimization_barrier((branch_grads, pyramid_grad))
    field_grad = pyramid_field(
        jnp.stack([chan_place, core]),
        pyramid_low,
        near_rows,
        far_rows,
        later_grads,
        other_grads,
        columns,
    )
    pool_part = dot(pool_grad_low, pyramid_low[28], (1, 1)) / image_count
    pool_sum = own_half(pool_part, 1) + swap_chan(other_half(pool_part, 1))
    stream_grad = field_grad + crop_field * pool_sum

    own_gain_two = own_half(gain_two, 0)
    own_scale_two = own_half(scale_two, 0)
    normed_two = (own_half(expand_pre, 1).astype(jnp.float32) - own_half(mean_two, 0)) * own_scale_two
    upstream_two = crop_field * stream_grad
    gain_two_grad, shift_two_grad, loss_sums, bias_grad = small_sum(
        sizes,
        [jnp.sum(upstream_two * normed_two, 0), jnp.sum(upstream_two, 0), local_sums, local_bias],
        ("dp",),
        2,
    )
    task_means = loss_sums / counts
    total_loss = jnp.sum(jnp.exp(-task_scale) * task_means + task_scale)
    scale_grad = 1.0 - jnp.exp(-task_scale) * task_means
    expand_grad_low = (
        crop_field
        * own_gain_two
        * own_scale_two
        * (upstream_two - (shift_two_grad + normed_two * gain_two_grad) / crop_total)
    ).astype(low)
    second_part = dot(expand_grad_low, own_half(bottle_low[1], 0)).astype(low)
    second_other = swap_chan(second_part)
    expand_rows = dot(expand_grad_low, second_low, (0, 0)).astype(low)
    expand_sent = swap_chan(other_half(expand_rows, 1))
    second_grad_low = (
        second_part.astype(jnp.float32) + second_other.astype(jnp.float32)
    ).astype(low)
    hidden_grad = middle_conv(second_grad_low, middle_low, columns, True, jnp.float32)
    normed_one = (first_pre - mean_one) * scale_one
    act_input = gain_one * normed_one + shift_one
    upstream_one = gelu_grad(act_input, crop_field * hidden_grad)
    gain_one_all, shift_one_all = small_sum(
        sizes,
        [jnp.sum(upstream_one * normed_one, 0), jnp.sum(upstream_one, 0)],
        ("dp",),
        3,
    )
    gain_one_grad = own_half(gain_one_all, 0)
    shift_one_grad = own_half(shift_one_all, 0)
    first_grad_low = (
        crop_field
        * gain_one
        * scale_one
        * (upstream_one - (shift_one_all + normed_one * gain_one_all) / crop_total)
    ).astype(low)
    middle_grad = middle_weights(hidden_t, own_half(second_grad_low, 1), columns)
    reduce_grad = dot(stream_low, own_half(first_grad_low, 1), (0, 0)).astype(low)
    start_grad = dot(first_grad_low, own_half(bottle_low[0], 0), (1, 1)) + stream_grad
    start_grad_low = (crop_field * start_grad).astype(low)
    stem_grad = dot(start_grad_low, patch_rows, (0, 0)).astype(low)
    expand_own = own_half(expand_rows, 1)
    expand_grad = jnp.where(
        chan_place == 0,
        jnp.concatenate([expand_own, expand_sent], 0),
        jnp.concatenate([expand_sent, expand_own], 0),
    )

    small_grads = jnp.concatenate(
        [
            project_grad.astype(low)
            .reshape(5 * 128, dp_size, project_share)
            .transpose(1, 0, 2)
            .reshape(dp_size, size),
            head_grad.astype(low).reshape(dp_size, head_share * 22),
        ],
        1,
    )
    small_rows = -(-small_grads.shape[1] // 4096) * 16
    small_grads = jnp.pad(small_grads, ((0, 0), (0, small_rows * 256 - small_grads.shape[1])))
    early_grads = jnp.concatenate(
        [
            expand_grad.reshape(dp_size, row_share, 256),
            middle_grad.reshape(9, dp_size, mid_share, 256)
            .transpose(1, 0, 2, 3)
            .reshape(dp_size, 9 * mid_share, 256),
            small_grads.reshape(dp_size, small_rows, 256),
        ],
        1,
    )
    early_grads, pyramid_red = lax.optimization_barrier((early_grads, pyramid_red))
    early_red = lax.psum_scatter(early_grads, "dp", scatter_dimension=0, tiled=True)
    late_grads = jnp.concatenate(
        [
            reduce_grad.reshape(dp_size, row_share * 256),
            stem_grad.reshape(dp_size, stem_share * PATCH),
        ],
        1,
    ).reshape(dp_size, -1, 256)
    late_grads, early_red = lax.optimization_barrier((late_grads, early_red))
    late_red = lax.psum_scatter(late_grads, "dp", scatter_dimension=0, tiled=True)
    early_red = early_red[0].astype(jnp.float32)
    late_red = late_red[0].astype(jnp.float32)
    bottle_red = jnp.stack([late_red[:row_share], early_red[:row_share]])
    middle_red = early_red[row_share : row_share + 9 * mid_share].reshape(middle_weight.shape)
    small_red = early_red[row_share + 9 * mid_share :].reshape(-1)
    project_red = small_red[:size].reshape(project_weight.shape)
    head_red = small_red[size : size + head_weight.size].reshape(head_weight.shape)
    stem_red = late_red[row_share:].reshape(stem_share, PATCH).T.reshape(stem_weight.shape)
    pyramid_red = pyramid_red.astype(jnp.float32)
    norm_grad = jnp.stack(
        [
            jnp.concatenate([gain_one_grad, gain_two_grad]),
            jnp.concatenate([shift_one_grad, shift_two_grad]),
        ]
    )[:, None, :]
    task_grad = jnp.concatenate([scale_grad, bias_grad])
    dp_first = (lax.axis_index("dp") == 0).astype(jnp.float32)
    chan_first = (chan_place == 0).astype(jnp.float32)
    own_squares = (
        jnp.sum(stem_red * stem_red)
        + jnp.sum(bottle_red * bottle_red)
        + jnp.sum(middle_red * middle_red)
        + jnp.sum(pyramid_red * pyramid_red)
        + jnp.sum(project_red * project_red)
        + chan_first * jnp.sum(head_red * head_red)
        + dp_first * jnp.sum(norm_grad * norm_grad)
        + dp_first * chan_first * jnp.sum(task_grad * task_grad)
    )
    grad_norm = jnp.sqrt(small_sum(sizes, [own_squares], ("dp", "chan"), 4)[0])
    factor = clip_level / jnp.maximum(grad_norm, clip_level)
    new_stem = adam_step(
        stem_weight, stem_first, stem_second, stem_red, factor, PATCH ** (-0.5), decay_rate
    )
    new_bottle = adam_step(
        bottle_weight, bottle_first, bottle_second, bottle_red, factor, D ** (-0.5), decay_rate
    )
    new_middle = adam_step(
        middle_weight,
        middle_first,
        middle_second,
        middle_red,
        factor,
        (9 * MID) ** (-0.5),
        decay_rate,
    )
    new_pyramid = adam_step(
        pyramid_weight,
        pyramid_first,
        pyramid_second,
        pyramid_red,
        factor,
        (3 * D) ** (-0.5),
        decay_rate,
    )
    new_project = adam_step(
        project_weight,
        project_first,
        project_second,
        project_red,
        factor,
        (5 * BRANCH) ** (-0.5),
        decay_rate,
    )
    new_head = adam_step(
        head_weight, head_first, head_second, head_red, factor, BRANCH ** (-0.5), decay_rate
    )
    new_norm = adam_step(norm_gains, norm_first, norm_second, norm_grad, factor, 0.3, 0.0)
    new_task = adam_step(task_params, task_first, task_second, task_grad, factor, 0.3, 0.0)
    return (
        total_loss,
        grad_norm,
        new_stem[0],
        new_stem[1],
        new_stem[2],
        new_bottle[0],
        new_bottle[1],
        new_bottle[2],
        new_middle[0],
        new_middle[1],
        new_middle[2],
        new_pyramid[0],
        new_pyramid[1],
        new_pyramid[2],
        new_project[0],
        new_project[1],
        new_project[2],
        new_head[0],
        new_head[1],
        new_head[2],
        new_norm[0],
        new_norm[1],
        new_norm[2],
        new_task[0],
        new_task[1],
        new_task[2],
    )


def solution(mesh):
    return jax.shard_map(
        functools.partial(on_device, dict(mesh.shape)),
        mesh=mesh,
        in_specs=(
            P("dp", None, None),
            P("dp", None),
            P("dp", None, None),
            P("dp", None),
            P("dp", None),
            P("dp", None),
            P("dp", None),
            P(None, "chan", "dp"),
            P(None, "chan", "dp"),
            P(None, "chan", "dp"),
            P(None, "dp", "chan"),
            P(None, "dp", "chan"),
            P(None, "dp", "chan"),
            P(None, "dp", "chan"),
            P(None, "dp", "chan"),
            P(None, "dp", "chan"),
            P(None, "dp", "chan"),
            P(None, "dp", "chan"),
            P(None, "dp", "chan"),
            P(None, "chan", "dp"),
            P(None, "chan", "dp"),
            P(None, "chan", "dp"),
            P("dp", None),
            P("dp", None),
            P("dp", None),
            P(None, "chan", None),
            P(None, "chan", None),
            P(None, "chan", None),
            P(),
            P(),
            P(),
        ),
        out_specs=(
            P(),
            P(),
            P(None, "chan", "dp"),
            P(None, "chan", "dp"),
            P(None, "chan", "dp"),
            P(None, "dp", "chan"),
            P(None, "dp", "chan"),
            P(None, "dp", "chan"),
            P(None, "dp", "chan"),
            P(None, "dp", "chan"),
            P(None, "dp", "chan"),
            P(None, "dp", "chan"),
            P(None, "dp", "chan"),
            P(None, "dp", "chan"),
            P(None, "chan", "dp"),
            P(None, "chan", "dp"),
            P(None, "chan", "dp"),
            P("dp", None),
            P("dp", None),
            P("dp", None),
            P(None, "chan", None),
            P(None, "chan", None),
            P(None, "chan", None),
            P(),
            P(),
            P(),
        ),
        check_vma=False,
    )
```

```python
import functools

import jax
import jax.numpy as jnp
from jax import lax
from jax.experimental import pallas as pl
from jax.experimental.pallas import tpu as pltpu
from jax.sharding import PartitionSpec as P

D = 2048
MID = 512
BRANCH = 256
CLASSES = 19
PATCH = 192
FH = 40
FW = 40
STEP = 10
POSITIONS = 1600


pyramid_rates = (0, 12, 24, 36)
norm_eps = 1e-05
clip_level = 0.01
adam_eps = 1e-08
decay_rate = 0.01


MESH_ID = pl.DeviceIdType.MESH


def group_place(sizes, axes):
    place = jnp.int32(0)
    for axis in axes:
        place = place * sizes[axis] + lax.axis_index(axis)
    return place


def group_device(sizes, axes, index):
    coords = {}
    for axis in reversed(axes):
        coords[axis] = lax.rem(index, sizes[axis])
        index = lax.div(index, sizes[axis])
    return tuple(coords.get(axis, lax.axis_index(axis)) for axis in ("dp", "chan"))


def sum_kernel(sizes, axes, count, x_ref, o_ref, slots, send_sem, recv_sem):
    me = group_place(sizes, axes)
    barrier = pltpu.get_barrier_semaphore()

    def greet(step, carry):
        other = lax.rem(me + step, count)
        pl.semaphore_signal(
            barrier, inc=1, device_id=group_device(sizes, axes, other), device_id_type=MESH_ID
        )
        return carry

    lax.fori_loop(1, count, greet, 0)
    pl.semaphore_wait(barrier, count - 1)

    def copy_to(step):
        other = lax.rem(me + step, count)
        return pltpu.make_async_remote_copy(
            src_ref=x_ref,
            dst_ref=slots.at[me],
            send_sem=send_sem.at[step],
            recv_sem=recv_sem.at[me],
            device_id=group_device(sizes, axes, other),
            device_id_type=MESH_ID,
        )

    def copy_from(step):
        other = lax.rem(me + step, count)
        return pltpu.make_async_remote_copy(
            src_ref=x_ref,
            dst_ref=slots.at[other],
            send_sem=send_sem.at[step],
            recv_sem=recv_sem.at[other],
            device_id=group_device(sizes, axes, other),
            device_id_type=MESH_ID,
        )

    def start(step, carry):
        copy_to(step).start()
        return carry

    lax.fori_loop(1, count, start, 0)
    slots[me] = x_ref[...]

    def arrive(step, carry):
        copy_from(step).wait_recv()
        return carry

    lax.fori_loop(1, count, arrive, 0)
    o_ref[...] = lax.fori_loop(
        1, count, lambda index, total: total + slots[index], slots[0]
    )

    def leave(step, carry):
        copy_to(step).wait_send()
        return carry

    lax.fori_loop(1, count, leave, 0)


def all_sum(sizes, values, axes, collective):
    count = 1
    for axis in axes:
        count *= sizes[axis]
    return pl.pallas_call(
        functools.partial(sum_kernel, sizes, axes, count),
        out_shape=jax.ShapeDtypeStruct(values.shape, jnp.float32),
        in_specs=[pl.BlockSpec(memory_space=pltpu.VMEM)],
        out_specs=pl.BlockSpec(memory_space=pltpu.VMEM),
        scratch_shapes=[
            pltpu.VMEM((count,) + values.shape, jnp.float32),
            pltpu.SemaphoreType.DMA((count,)),
            pltpu.SemaphoreType.DMA((count,)),
        ],
        compiler_params=pltpu.CompilerParams(
            collective_id=collective, has_side_effects=True, vmem_limit_bytes=32 << 20
        ),
        name="small_sum",
    )(values)


def small_sum(sizes, parts, axes, collective):
    flat = jnp.concatenate([part.reshape(-1) for part in parts])
    rows = -(-flat.shape[0] // 1024) * 8
    packed = jnp.pad(flat, (0, rows * 128 - flat.shape[0])).reshape(rows, 128)
    summed = all_sum(sizes, packed, axes, collective).reshape(-1)
    result = []
    start = 0
    for part in parts:
        size = part.size
        result.append(summed[start : start + size].reshape(part.shape))
        start += size
    return result


def swap_chan(values):
    return lax.ppermute(values, "chan", [(0, 1), (1, 0)])


def valid(step, length):
    return max(0, step), length + min(0, step)


def taps_of(rate):
    return [((tap // 3 - 1) * rate, (tap % 3 - 1) * rate) for tap in range(9)]


def shift_field(field, row_step, col_step):
    rows, cols = field.shape[:2]
    r0, r1 = valid(row_step, rows)
    c0, c1 = valid(col_step, cols)
    return jnp.pad(
        field[r0:r1, c0:c1],
        (
            (r0 - row_step, rows - (r1 - row_step)),
            (c0 - col_step, cols - (c1 - col_step)),
            (0, 0),
        ),
    )


def gelu_grad(values, upstream):
    return jax.vjp(jax.nn.gelu, values)[1](upstream)[0]


def dot(left, right, contract=(1, 0)):
    return lax.dot_general(
        left,
        right,
        (((contract[0],), (contract[1],)), ((), ())),
        preferred_element_type=jnp.float32,
    )


def place_of():
    dp = lax.axis_index("dp")
    return lax.div(dp, 4), lax.rem(lax.div(dp, 2), 2), lax.rem(dp, 2), lax.axis_index("chan")


def device_at(z, y, core, x):
    return ((z * 2 + y) * 2 + core, x)


def flip(value, turn):
    return lax.rem(value + turn, 2)


def z_flip(z, turn):
    return flip(lax.div(z, 2), turn // 2) * 2 + flip(lax.rem(z, 2), turn % 2)


def greet_neighbours(layers):
    z, y, core, x = place_of()
    barrier = pltpu.get_barrier_semaphore()
    for target in (
        device_at(z, y, 1 - core, x),
        device_at(z, 1 - y, core, x),
        device_at(z, y, core, 1 - x),
    ):
        pl.semaphore_signal(barrier, inc=1, device_id=target, device_id_type=MESH_ID)

    @pl.when(z > 0)
    def _():
        pl.semaphore_signal(
            barrier, inc=1, device_id=device_at(z - 1, y, core, x), device_id_type=MESH_ID
        )

    @pl.when(z < layers - 1)
    def _():
        pl.semaphore_signal(
            barrier, inc=1, device_id=device_at(z + 1, y, core, x), device_id_type=MESH_ID
        )

    peers = 3 + jnp.where(z > 0, 1, 0) + jnp.where(z < layers - 1, 1, 0)
    pl.semaphore_wait(barrier, peers)


def gather_kernel(
    layers,
    bottle,
    middle,
    small,
    head,
    bottle_all,
    middle_all,
    small_all,
    head_all,
    send_sems,
    recv_sems,
    local_sems,
):
    z, y, core, x = place_of()
    rows = bottle.shape[1]
    mid_rows = middle.shape[1]
    small_rows = small.shape[0]
    head_rows = head.shape[0]
    own_refs = (bottle, middle, small, head)

    def region(kind, block):
        zz, yy, kk, xx = block
        index = (zz * 2 + yy) * 2 + kk
        cols = pl.ds(pl.multiple_of(xx * 256, 256), 256)
        if kind == 0:
            return bottle_all.at[:, pl.ds(pl.multiple_of(index * rows, 16), rows), cols]
        if kind == 1:
            return middle_all.at[:, pl.ds(pl.multiple_of(index * mid_rows, 16), mid_rows), cols]
        if kind == 3:
            return head_all.at[pl.ds(pl.multiple_of(index * head_rows, 16), head_rows)]
        first = xx * (small_all.shape[0] // 2) + index * small_rows
        return small_all.at[pl.ds(pl.multiple_of(first, 16), small_rows)]

    def semaphore(kind, block):
        zz, yy, kk, xx = block
        return recv_sems.at[kind, ((zz * 2 + yy) * 2 + kk) * 2 + xx]

    own = (z, y, core, x)
    pending = []

    def send(kind, block, target, when=None):
        copy = pltpu.make_async_remote_copy(
            src_ref=own_refs[kind] if block is own else region(kind, block),
            dst_ref=region(kind, block),
            send_sem=send_sems.at[len(pending)],
            recv_sem=semaphore(kind, block),
            device_id=target,
            device_id_type=MESH_ID,
        )
        if when is None:
            copy.start()
        else:
            pl.when(when)(copy.start)
        pending.append((when, copy))

    def arrive(kind, block):
        pltpu.make_async_remote_copy(
            src_ref=region(kind, block),
            dst_ref=region(kind, block),
            send_sem=send_sems.at[0],
            recv_sem=semaphore(kind, block),
            device_id=device_at(z, y, 1 - core, x),
            device_id_type=MESH_ID,
        ).wait_recv()

    locals_ = [
        pltpu.make_async_copy(own_refs[kind], region(kind, own), local_sems.at[kind])
        for kind in range(4)
    ]
    for copy in locals_:
        copy.start()
    greet_neighbours(layers)
    sibling = device_at(z, y, 1 - core, x)
    other_x = device_at(z, y, core, 1 - x)
    other_y = device_at(z, 1 - y, core, x)

    def along_z(kind, block):
        if block[0] is z:
            send(kind, block, device_at(z + 1, y, core, x), z < layers - 1)
            send(kind, block, device_at(z - 1, y, core, x), z > 0)
        else:
            below = block[0] < z
            ahead = z + jnp.where(below, 1, -1)
            send(
                kind,
                block,
                device_at(ahead, y, core, x),
                jnp.logical_and(ahead >= 0, ahead < layers),
            )

    for kind in (0, 1):
        along_z(kind, own)
    send(2, own, other_x)
    send(2, own, other_y)
    send(1, own, other_x)
    send(0, own, other_y)
    along_z(2, own)
    along_z(3, own)
    send(3, own, other_y)
    send(0, own, other_x)
    send(1, own, other_y)
    for kind in range(4):
        send(kind, own, sibling)

    block = (z, y, core, 1 - x)
    arrive(2, block)
    send(2, block, other_y)
    along_z(2, block)
    send(2, block, sibling)
    for xx in (x, 1 - x):
        block = (z, 1 - y, core, xx)
        arrive(2, block)
        along_z(2, block)
        send(2, block, sibling)

    for turn in range(layers):
        zz = z if turn == 0 else z_flip(z, turn)
        if turn:
            for kind, near, far in ((0, other_y, other_x), (1, other_x, other_y)):
                block = (zz, y, core, x)
                arrive(kind, block)
                along_z(kind, block)
                send(kind, block, near)
                send(kind, block, far)
                send(kind, block, sibling)
            block = (zz, y, core, x)
            arrive(3, block)
            along_z(3, block)
            send(3, block, other_y)
            send(3, block, sibling)
        block = (zz, 1 - y, core, x)
        arrive(0, block)
        send(0, block, other_x)
        send(0, block, sibling)
        block = (zz, y, core, 1 - x)
        arrive(1, block)
        send(1, block, other_y)
        send(1, block, sibling)
        if turn:
            for yy, xx in ((y, x), (y, 1 - x), (1 - y, x), (1 - y, 1 - x)):
                block = (zz, yy, core, xx)
                arrive(2, block)
                along_z(2, block)
                send(2, block, sibling)
    for turn in range(layers):
        zz = z if turn == 0 else z_flip(z, turn)
        for yy in (y, 1 - y):
            block = (zz, yy, core, 1 - x)
            arrive(0, block)
            send(0, block, sibling)
        for xx in (x, 1 - x):
            block = (zz, 1 - y, core, xx)
            arrive(1, block)
            send(1, block, sibling)
        block = (zz, 1 - y, core, x)
        arrive(3, block)
        send(3, block, sibling)
    for kind in range(4):
        for turn in range(layers):
            zz = z if turn == 0 else z_flip(z, turn)
            for yy in (y, 1 - y):
                for xx in (x, 1 - x) if kind < 3 else (x,):
                    arrive(kind, (zz, yy, 1 - core, xx))
    for copy in locals_:
        copy.wait()
    for when, copy in pending:
        if when is None:
            copy.wait_send()
        else:
            pl.when(when)(copy.wait_send)


def gather_trunk(sizes, bottle, middle, small, head):
    count = sizes["dp"]
    if count != 16 or middle.shape[1] % 16:
        packed = [
            lax.all_gather(
                lax.all_gather(part, "dp", axis=1, tiled=True), "chan", axis=2, tiled=True
            )
            for part in (bottle, middle)
        ]
        return packed + [
            lax.all_gather(small, ("chan", "dp")).reshape(D, small.shape[1]),
            lax.all_gather(head, "dp", axis=0, tiled=True),
        ]
    return pl.pallas_call(
        functools.partial(gather_kernel, count // 4),
        out_shape=[
            jax.ShapeDtypeStruct((2, D, MID), jnp.bfloat16),
            jax.ShapeDtypeStruct((9, MID, MID), jnp.bfloat16),
            jax.ShapeDtypeStruct((D, small.shape[1]), jnp.bfloat16),
            jax.ShapeDtypeStruct((BRANCH, head.shape[1]), jnp.bfloat16),
        ],
        in_specs=[pl.BlockSpec(memory_space=pl.ANY)] * 4,
        out_specs=[pl.BlockSpec(memory_space=pl.ANY)] * 4,
        scratch_shapes=[
            pltpu.SemaphoreType.DMA((176,)),
            pltpu.SemaphoreType.DMA((4, 2 * count)),
            pltpu.SemaphoreType.DMA((4,)),
        ],
        compiler_params=pltpu.CompilerParams(collective_id=5, has_side_effects=True),
        name="gather_trunk",
    )(bottle, middle, small, head)


PAD = 128
PYRAMID_ROWS = (-36, -24, -12, 0, 12, 24, 36)


def taps_by_row():
    fields = [(0, 0)] + [(rate, col * rate) for rate in (12, 24, 36) for col in (-1, 0, 1)]
    groups = []
    for row_step in PYRAMID_ROWS:
        group = []
        for place, (rate, col_step) in enumerate(fields):
            if rate == 0:
                if row_step == 0:
                    group.append((0, place))
            elif row_step == 0 or abs(row_step) == rate:
                turn = (1 if row_step > 0 else -1 if row_step < 0 else 0) + 1
                tap = 1 + 9 * (rate // 12 - 1) + 3 * turn + (col_step // rate + 1)
                group.append((tap, place))
        groups.append(group)
    return fields, groups


FIELDS, ROW_GROUPS = taps_by_row()
TAP_ORDER = [tap for group in ROW_GROUPS for tap, place in group]
PLACE_ORDER = [place for group in ROW_GROUPS for tap, place in group]


EARLY_TAPS = 10


def tap_of(early, late, tap):
    return early.at[tap] if tap < EARLY_TAPS else late.at[tap - EARLY_TAPS]


def roll_cols(values, columns, step):
    if step == 0:
        return values
    moved = pltpu.roll(values, (-step) % values.shape[0], 0)
    target = columns[:, :1] + float(step)
    return jnp.where((target >= 0.0) & (target < float(FW)), moved, 0.0)


def vmem(count):
    return [pl.BlockSpec(memory_space=pltpu.VMEM)] * count


def middle_kernel(back, x_ref, w_ref, col_ref, o_ref, canvas):
    edge = 4 * FW
    mid = x_ref.shape[1]
    values = x_ref[...].astype(jnp.float32)
    sign = -1 if back else 1
    for turn in range(3):
        canvas[turn, :edge] = jnp.zeros((edge, mid), canvas.dtype)
        canvas[turn, POSITIONS + edge :] = jnp.zeros((edge, mid), canvas.dtype)
        canvas[turn, edge : POSITIONS + edge] = roll_cols(
            values, col_ref, sign * 4 * (turn - 1)
        ).astype(canvas.dtype)
    block = 400

    def step(index, carry):
        total = None
        for row in range(3):
            first = pl.multiple_of(index * block + edge * (1 + sign * (row - 1)), 16)
            for turn in range(3):
                part = dot(
                    canvas[turn, pl.ds(first, block)],
                    w_ref[3 * row + turn],
                    (1, 1) if back else (1, 0),
                )
                total = part if total is None else total + part
        o_ref[pl.ds(pl.multiple_of(index * block, 16), block)] = total.astype(o_ref.dtype)
        return carry

    lax.fori_loop(0, POSITIONS // block, step, 0)


def middle_conv(field, weights, columns, back, dtype):
    return pl.pallas_call(
        functools.partial(middle_kernel, back),
        out_shape=jax.ShapeDtypeStruct((POSITIONS, MID), dtype),
        in_specs=vmem(3),
        out_specs=vmem(1)[0],
        scratch_shapes=[pltpu.VMEM((3, POSITIONS + 8 * FW, MID), jnp.bfloat16)],
        compiler_params=pltpu.CompilerParams(vmem_limit_bytes=40 << 20),
        cost_estimate=pl.CostEstimate(
            flops=2 * POSITIONS * 9 * MID * MID, bytes_accessed=16 << 20, transcendentals=0
        ),
        name="middle_back" if back else "middle_fwd",
    )(field, weights, columns)


def middle_weight_kernel(xt_ref, g_ref, col_ref, o_ref, fields):
    width = g_ref.shape[1]
    values = g_ref[...].astype(jnp.float32)
    for turn in range(3):
        fields[turn, :PAD] = jnp.zeros((PAD, width), fields.dtype)
        fields[turn, PAD + POSITIONS :] = jnp.zeros((PAD, width), fields.dtype)
        fields[turn, PAD : PAD + POSITIONS] = roll_cols(values, col_ref, -4 * (turn - 1)).astype(
            fields.dtype
        )
    for row in range(3):
        row_step = 4 * (row - 1)
        r0, r1 = valid(row_step, FH)
        first = r0 * FW // 128 * 128
        last = min(POSITIONS, -(-r1 * FW // 128) * 128)
        base = PAD + first - row_step * FW
        for turn in range(3):
            o_ref[3 * row + turn] = dot(
                xt_ref[:, first:last], fields[turn, base : base + last - first]
            ).astype(o_ref.dtype)


def middle_weights(field_t, grads, columns):
    depth, width = field_t.shape[0], grads.shape[1]
    return pl.pallas_call(
        middle_weight_kernel,
        out_shape=jax.ShapeDtypeStruct((9, depth, width), jnp.bfloat16),
        in_specs=vmem(3),
        out_specs=vmem(1)[0],
        scratch_shapes=[pltpu.VMEM((3, POSITIONS + 2 * PAD, width), jnp.bfloat16)],
        compiler_params=pltpu.CompilerParams(vmem_limit_bytes=40 << 20),
        cost_estimate=pl.CostEstimate(
            flops=2 * POSITIONS * 9 * depth * width, bytes_accessed=6 << 20, transcendentals=0
        ),
        name="middle_weights",
    )(field_t, grads, columns)


def fill_fields(g_ref, col_ref, fields):
    width = g_ref.shape[2]
    for place, (rate, col_step) in enumerate(FIELDS):
        fields[place, :PAD] = jnp.zeros((PAD, width), fields.dtype)
        fields[place, PAD + POSITIONS :] = jnp.zeros((PAD, width), fields.dtype)
        values = g_ref[rate // 12]
        fields[place, PAD : PAD + POSITIONS] = roll_cols(
            values.astype(jnp.float32), col_ref, -col_step
        ).astype(fields.dtype)


def weight_kernel(xt_ref, g_ref, col_ref, pool_ref, pool_grad_ref, o_ref, fields):
    width = g_ref.shape[2]
    depth = xt_ref.shape[0]
    fill_fields(g_ref, col_ref, fields)
    block = 512
    for row_step, group in zip(PYRAMID_ROWS, ROW_GROUPS):
        r0, r1 = valid(row_step, FH)
        first = r0 * FW // 128 * 128
        last = min(POSITIONS, -(-r1 * FW // 128) * 128)
        base = PAD + first - row_step * FW
        sets = [group[at : at + 2] for at in range(0, 10, 2)] if row_step == 0 else [group]
        for chosen in sets:
            right = jnp.concatenate(
                [fields[place, base : base + last - first] for tap, place in chosen], 1
            )

            def step(index, carry):
                rows = pl.ds(pl.multiple_of(index * block, 16), block)
                part = dot(xt_ref[rows, first:last], right)
                for offset, (tap, place) in enumerate(chosen):
                    o_ref[tap, rows] = part[:, offset * width : (offset + 1) * width].astype(
                        o_ref.dtype
                    )
                return carry

            lax.fori_loop(0, depth // block, step, 0)
    o_ref[28] = (pool_ref[...] * pool_grad_ref[...]).astype(o_ref.dtype)


def pyramid_weights(field_t, grads, columns, pooled, pool_grad):
    depth = field_t.shape[0]
    width = grads.shape[2]
    return pl.pallas_call(
        weight_kernel,
        out_shape=jax.ShapeDtypeStruct((29, depth, width), jnp.bfloat16),
        in_specs=vmem(5),
        out_specs=vmem(1)[0],
        scratch_shapes=[pltpu.VMEM((10, POSITIONS + 2 * PAD, width), jnp.bfloat16)],
        compiler_params=pltpu.CompilerParams(vmem_limit_bytes=56 << 20),
        cost_estimate=pl.CostEstimate(
            flops=3 * 10**10, bytes_accessed=20 << 20, transcendentals=0
        ),
        name="pyramid_weights",
    )(field_t, grads, columns, pooled, pool_grad)


def field_kernel(
    half_ref, a_hbm, b_hbm, g_ref, pool_ref, crop_ref, col_ref, o_ref, weights, pool_weights, fields, stack, sems
):
    width = g_ref.shape[2]
    depth = o_ref.shape[1]
    half = pl.ds(pl.multiple_of(half_ref[0] * depth, 16), depth)
    copies = []
    for slot, tap in enumerate(TAP_ORDER):
        copy = pltpu.make_async_copy(
            tap_of(a_hbm, b_hbm, tap).at[half], weights.at[:, pl.ds(slot * width, width)], sems.at[slot]
        )
        copy.start()
        copies.append(copy)
    copies.append(
        pltpu.make_async_copy(tap_of(a_hbm, b_hbm, 28).at[half], pool_weights, sems.at[28])
    )
    copies[-1].start()
    fill_fields(g_ref, col_ref, fields)
    for copy in copies:
        copy.wait()
    pooled = dot(
        jnp.broadcast_to(pool_ref[...], (16, width)).astype(jnp.bfloat16), pool_weights[...], (1, 1)
    )[0:1] / jnp.sum(crop_ref[...], keepdims=True)
    step_of = [step for step, group in zip(PYRAMID_ROWS, ROW_GROUPS) for entry in group]
    for r0, r1 in ((0, 4), (4, 12), (12, 16), (16, 24), (24, 28), (28, 36), (36, 40)):
        slots = [
            slot for slot, step in enumerate(step_of) if r0 - step >= 0 and r1 - step <= FH
        ]
        count = (r1 - r0) * FW
        for at, slot in enumerate(slots):
            base = PAD + (r0 - step_of[slot]) * FW
            stack[:count, at * width : (at + 1) * width] = fields[
                PLACE_ORDER[slot], base : base + count
            ]
        part = dot(
            stack[:count, : len(slots) * width],
            weights[:, slots[0] * width : (slots[-1] + 1) * width],
            (1, 1),
        )
        o_ref[r0 * FW : r1 * FW] = (part + crop_ref[r0 * FW : r1 * FW] * pooled).astype(
            o_ref.dtype
        )


def pyramid_field(half, weights, grads, pool_grad, crop, columns):
    depth, width = weights[0].shape[1] // 2, weights[0].shape[2]
    return pl.pallas_call(
        field_kernel,
        out_shape=jax.ShapeDtypeStruct((POSITIONS, depth), jnp.bfloat16),
        in_specs=[
            pl.BlockSpec(memory_space=pltpu.SMEM),
            pl.BlockSpec(memory_space=pl.ANY),
            pl.BlockSpec(memory_space=pl.ANY),
            pl.BlockSpec(memory_space=pltpu.VMEM),
            pl.BlockSpec(memory_space=pltpu.VMEM),
            pl.BlockSpec(memory_space=pltpu.VMEM),
            pl.BlockSpec(memory_space=pltpu.VMEM),
        ],
        out_specs=vmem(1)[0],
        scratch_shapes=[
            pltpu.VMEM((depth, 28 * width), jnp.bfloat16),
            pltpu.VMEM((depth, width), jnp.bfloat16),
            pltpu.VMEM((10, POSITIONS + 2 * PAD, width), jnp.bfloat16),
            pltpu.VMEM((8 * FW, 19 * width), jnp.bfloat16),
            pltpu.SemaphoreType.DMA((29,)),
        ],
        compiler_params=pltpu.CompilerParams(vmem_limit_bytes=56 << 20),
        cost_estimate=pl.CostEstimate(
            flops=3 * 10**10, bytes_accessed=20 << 20, transcendentals=0
        ),
        name="pyramid_field",
    )(half, weights[0], weights[1], grads, pool_grad, crop, columns)


BLOCK = 320


def block_rows(index):
    return pl.ds(pl.multiple_of(index * BLOCK, 16), BLOCK)


def gelu_slope(values, upstream):
    return jax.vjp(jax.nn.gelu, values)[1](upstream)[0]


def stem_kernel(p_ref, stem_ref, reduce_ref, crop_ref, count_ref, x_ref, a_ref, stat_ref):
    def step(index, carry):
        rows = block_rows(index)
        low = (crop_ref[rows] * dot(p_ref[rows], stem_ref[...], (1, 1))).astype(x_ref.dtype)
        x_ref[rows] = low
        value = dot(low, reduce_ref[0])
        a_ref[rows] = value
        return (
            carry[0] + jnp.sum(value, 0, keepdims=True),
            carry[1] + jnp.sum(value * value, 0, keepdims=True),
        )

    zero = jnp.zeros((1, MID), jnp.float32)
    total, square = lax.fori_loop(0, POSITIONS // BLOCK, step, (zero, zero))
    stat_ref[...] = jnp.concatenate(
        [total, square, count_ref[...], jnp.zeros((5, MID), jnp.float32)], 0
    )


def stem_reduce(patches, stem, bottle, crop, counts):
    return pl.pallas_call(
        stem_kernel,
        grid=(1,),
        out_shape=[
            jax.ShapeDtypeStruct((POSITIONS, D), jnp.bfloat16),
            jax.ShapeDtypeStruct((POSITIONS, MID), jnp.float32),
            jax.ShapeDtypeStruct((8, MID), jnp.float32),
        ],
        in_specs=[
            pl.BlockSpec((POSITIONS, PATCH), lambda i: (0, 0)),
            pl.BlockSpec(stem.shape, lambda i: (0, 0)),
            pl.BlockSpec((1, D, MID), lambda i: (0, 0, 0)),
            pl.BlockSpec((POSITIONS, 1), lambda i: (0, 0)),
            pl.BlockSpec((1, MID), lambda i: (0, 0)),
        ],
        out_specs=[
            pl.BlockSpec((POSITIONS, D), lambda i: (0, 0)),
            pl.BlockSpec((POSITIONS, MID), lambda i: (0, 0)),
            pl.BlockSpec((8, MID), lambda i: (0, 0)),
        ],
        compiler_params=pltpu.CompilerParams(vmem_limit_bytes=50 << 20),
        cost_estimate=pl.CostEstimate(flops=5 * 10**9, bytes_accessed=14 << 20, transcendentals=0),
        name="stem_reduce",
    )(patches, stem, bottle, crop, counts)


def both_halves(gain_refs, first, last):
    place_ref, own_ref, other_ref = gain_refs
    own, other = own_ref[:, first:last], other_ref[:, first:last]
    lower = place_ref[0] == 0
    return jnp.concatenate([jnp.where(lower, own, other), jnp.where(lower, other, own)], 1)


def norm_rows(stat, count):
    mean = stat[0:1] / count
    return mean, lax.rsqrt(stat[1:2] / count - mean * mean + norm_eps)


def norm_middle_kernel(
    a_ref, stat_ref, place_ref, own_ref, other_ref, crop_ref, w_ref, col_ref, h_ref, ht_ref, o_ref, canvas
):
    edge = 4 * FW
    mean, scale = norm_rows(stat_ref[...], stat_ref[2:3, 0:1])
    pair = both_halves((place_ref, own_ref, other_ref), 0, MID // 2)
    gain = pair[0:1] * scale
    shift = pair[1:2] - mean * gain
    low = (crop_ref[...] * jax.nn.gelu(a_ref[...] * gain + shift)).astype(h_ref.dtype)
    h_ref[...] = low
    ht_ref[...] = low.T
    values = low.astype(jnp.float32)
    for turn in range(3):
        canvas[turn, :edge] = jnp.zeros((edge, MID), canvas.dtype)
        canvas[turn, POSITIONS + edge :] = jnp.zeros((edge, MID), canvas.dtype)
        canvas[turn, edge : POSITIONS + edge] = roll_cols(values, col_ref, 4 * (turn - 1)).astype(
            canvas.dtype
        )
    block = 400

    def step(index, carry):
        total = None
        for row in range(3):
            first = pl.multiple_of(index * block + edge * row, 16)
            for turn in range(3):
                part = dot(canvas[turn, pl.ds(first, block)], w_ref[3 * row + turn])
                total = part if total is None else total + part
        o_ref[pl.ds(pl.multiple_of(index * block, 16), block)] = total.astype(o_ref.dtype)
        return carry

    lax.fori_loop(0, POSITIONS // block, step, 0)


def norm_middle(first_pre, stat, gains, crop, weights, columns):
    return pl.pallas_call(
        norm_middle_kernel,
        out_shape=[
            jax.ShapeDtypeStruct((POSITIONS, MID), jnp.bfloat16),
            jax.ShapeDtypeStruct((MID, POSITIONS), jnp.bfloat16),
            jax.ShapeDtypeStruct((POSITIONS, MID), jnp.bfloat16),
        ],
        in_specs=vmem(2) + [pl.BlockSpec(memory_space=pltpu.SMEM)] + vmem(5),
        out_specs=vmem(3),
        scratch_shapes=[pltpu.VMEM((3, POSITIONS + 8 * FW, MID), jnp.bfloat16)],
        compiler_params=pltpu.CompilerParams(vmem_limit_bytes=50 << 20),
        cost_estimate=pl.CostEstimate(flops=8 * 10**9, bytes_accessed=14 << 20, transcendentals=0),
        name="norm_middle",
    )(first_pre, stat, *gains, crop, weights, columns)


def expand_kernel(a_ref, w_ref, crop_ref, y_ref, stat_ref):
    def step(index, carry):
        rows = block_rows(index)
        value = dot(a_ref[rows], w_ref[0], (1, 1))
        y_ref[rows] = value.astype(y_ref.dtype)
        kept = crop_ref[rows] * value
        return (
            carry[0] + jnp.sum(kept, 0, keepdims=True),
            carry[1] + jnp.sum(kept * value, 0, keepdims=True),
        )

    zero = jnp.zeros((1, D), jnp.float32)
    sums = lax.fori_loop(0, POSITIONS // BLOCK, step, (zero, zero))
    for turn, values in enumerate(sums):
        for part in range(4):
            stat_ref[4 * turn + part : 4 * turn + part + 1] = values[
                :, part * MID : (part + 1) * MID
            ]


def expand_forward(second, bottle, crop):
    return pl.pallas_call(
        expand_kernel,
        grid=(1,),
        out_shape=[
            jax.ShapeDtypeStruct((POSITIONS, D), jnp.bfloat16),
            jax.ShapeDtypeStruct((8, MID), jnp.float32),
        ],
        in_specs=[
            pl.BlockSpec((POSITIONS, MID), lambda i: (0, 0)),
            pl.BlockSpec((1, D, MID), lambda i: (1, 0, 0)),
            pl.BlockSpec((POSITIONS, 1), lambda i: (0, 0)),
        ],
        out_specs=[
            pl.BlockSpec((POSITIONS, D), lambda i: (0, 0)),
            pl.BlockSpec((8, MID), lambda i: (0, 0)),
        ],
        compiler_params=pltpu.CompilerParams(vmem_limit_bytes=50 << 20),
        cost_estimate=pl.CostEstimate(flops=4 * 10**9, bytes_accessed=12 << 20, transcendentals=0),
        name="expand_forward",
    )(second, bottle, crop)


def residual_kernel(
    p_ref, stem_ref, y_ref, stat_ref, count_ref, place_ref, own_ref, other_ref, crop_ref, x_ref, xt_ref, pool_ref
):
    count = count_ref[2:3, 0:1]
    stat = stat_ref[...]
    total = jnp.concatenate([stat[part : part + 1] for part in range(4)], 1)
    square = jnp.concatenate([stat[part : part + 1] for part in range(4, 8)], 1)
    mean = total / count
    pair = both_halves((place_ref, own_ref, other_ref), MID // 2, MID // 2 + D // 2)
    gain = pair[0:1] * lax.rsqrt(square / count - mean * mean + norm_eps)
    shift = pair[1:2] - mean * gain

    def residual(index, carry):
        rows = block_rows(index)
        value = dot(p_ref[rows], stem_ref[...], (1, 1)) + (
            y_ref[rows].astype(jnp.float32) * gain + shift
        )
        low = (crop_ref[rows] * value).astype(x_ref.dtype)
        x_ref[rows] = low
        return carry + jnp.sum(low.astype(jnp.float32), 0, keepdims=True)

    pooled = lax.fori_loop(0, POSITIONS // BLOCK, residual, jnp.zeros((1, D), jnp.float32))
    pooled = (pooled / jnp.sum(crop_ref[...], keepdims=True)).astype(jnp.bfloat16)
    pool_ref[...] = pooled.astype(jnp.float32)
    for at in range(0, D, 256):
        xt_ref[at : at + 256] = x_ref[:, at : at + 256].T


def residual_stream(patches, stem, expanded, stat, counts, gains, crop):
    low = jnp.bfloat16
    return pl.pallas_call(
        residual_kernel,
        out_shape=[
            jax.ShapeDtypeStruct((POSITIONS, D), low),
            jax.ShapeDtypeStruct((D, POSITIONS), low),
            jax.ShapeDtypeStruct((1, D), jnp.float32),
        ],
        in_specs=vmem(5) + [pl.BlockSpec(memory_space=pltpu.SMEM)] + vmem(3),
        out_specs=vmem(3),
        compiler_params=pltpu.CompilerParams(vmem_limit_bytes=50 << 20),
        cost_estimate=pl.CostEstimate(flops=2 * 10**9, bytes_accessed=22 << 20, transcendentals=0),
        name="residual_stream",
    )(patches, stem, expanded, stat, counts, *gains, crop)


def pyramid_kernel(
    x_ref,
    pool_ref,
    a_hbm,
    b_hbm,
    project_ref,
    col_ref,
    o_ref,
    pool_pre_ref,
    cat_ref,
    part_ref,
    weights,
    pool_weights,
    fields,
    sems,
):
    width = o_ref.shape[2]
    copies = []
    order = [3, 2, 4, 1, 5, 0, 6]
    starts = []
    place = 0
    for group in ROW_GROUPS:
        starts.append(place)
        place += len(group)
    for turn in order:
        group_copies = []
        for offset, (tap, _) in enumerate(ROW_GROUPS[turn]):
            slot = starts[turn] + offset
            copy = pltpu.make_async_copy(
                tap_of(a_hbm, b_hbm, tap), weights.at[:, pl.ds(slot * width, width)], sems.at[slot]
            )
            copy.start()
            group_copies.append(copy)
        copies.append(group_copies)
    pool_copy = pltpu.make_async_copy(tap_of(a_hbm, b_hbm, 28), pool_weights, sems.at[28])
    pool_copy.start()

    for turn, group_copies in zip(order, copies):
        for copy in group_copies:
            copy.wait()
        row_step = PYRAMID_ROWS[turn]
        group = ROW_GROUPS[turn]
        r0, r1 = valid(row_step, FH)
        length = (r1 - r0) * FW
        block = {1600: 800, 1120: 560, 640: 640, 160: 160}[length]
        cols = pl.ds(starts[turn] * width, len(group) * width)

        def step(index, carry):
            source = pl.multiple_of(index * block + r0 * FW, 16)
            target = pl.multiple_of(index * block + (r0 - row_step) * FW, 16)
            part = dot(x_ref[pl.ds(source, block)], weights[:, cols])
            for offset, (tap, field) in enumerate(group):
                piece = part[:, offset * width : (offset + 1) * width]
                rows = pl.ds(target, block)
                if row_step == 0:
                    fields[field, rows] = piece
                else:
                    fields[field, rows] += piece
            return carry

        lax.fori_loop(0, length // block, step, 0)
    pool_copy.wait()
    pool_pre = dot(jnp.broadcast_to(pool_ref[...], (16, D)).astype(jnp.bfloat16), pool_weights[...])[0:1]
    pool_pre_ref[...] = pool_pre
    for branch in range(4):
        values = fields[0] if branch == 0 else fields[3 * branch - 1]
        if branch:
            for turn in (0, 2):
                place = 3 * branch - 2 + turn
                values = values + roll_cols(fields[place], col_ref, FIELDS[place][1])
        o_ref[branch] = values
        cat_ref[:, branch * width : (branch + 1) * width] = jax.nn.gelu(values).astype(
            cat_ref.dtype
        )
    cat_ref[:, 4 * width :] = jnp.broadcast_to(
        jax.nn.gelu(pool_pre).astype(cat_ref.dtype), (POSITIONS, width)
    )

    def project(index, carry):
        rows = block_rows(index)
        part_ref[rows] = dot(cat_ref[rows], project_ref[:, : 5 * width], (1, 1)).astype(part_ref.dtype)
        return carry

    lax.fori_loop(0, POSITIONS // BLOCK, project, 0)


def pyramid_forward(field, pooled, weights, project, columns):
    depth, width = weights[0].shape[1:]
    low = jnp.bfloat16
    return pl.pallas_call(
        pyramid_kernel,
        out_shape=[
            jax.ShapeDtypeStruct((4, POSITIONS, width), jnp.float32),
            jax.ShapeDtypeStruct((1, width), jnp.float32),
            jax.ShapeDtypeStruct((POSITIONS, 5 * width), low),
            jax.ShapeDtypeStruct((POSITIONS, BRANCH), low),
        ],
        in_specs=vmem(2) + [pl.BlockSpec(memory_space=pl.ANY)] * 2 + vmem(2),
        out_specs=vmem(4),
        scratch_shapes=[
            pltpu.VMEM((depth, 28 * width), low),
            pltpu.VMEM((depth, width), low),
            pltpu.VMEM((10, POSITIONS, width), jnp.float32),
            pltpu.SemaphoreType.DMA((29,)),
        ],
        compiler_params=pltpu.CompilerParams(vmem_limit_bytes=60 << 20),
        cost_estimate=pl.CostEstimate(
            flops=2 * POSITIONS * 19 * depth * width, bytes_accessed=40 << 20, transcendentals=0
        ),
        name="pyramid_fwd",
    )(field, pooled, weights[0], weights[1], project, columns)


def head_kernel(
    own_ref,
    other_ref,
    row_ref,
    label_ref,
    target_ref,
    mask_ref,
    project_ref,
    z_ref,
    pool_pre_ref,
    feature_ref,
    logit_ref,
    mixed_ref,
    grad_ref,
    pool_ref,
    stat_ref,
):
    width = grad_ref.shape[2]
    bias, scale = row_ref[0:1], row_ref[1:2]
    class_lane, depth_lane = row_ref[2:3], row_ref[4:5]

    def step(index, carry):
        rows = block_rows(index)
        mixed = own_ref[rows].astype(jnp.float32) + other_ref[rows].astype(jnp.float32)
        feature = jax.nn.gelu(mixed).astype(feature_ref.dtype)
        feature_ref[rows] = feature
        logits = dot(feature, project_ref[:, 5 * width :]) + bias
        is_class = class_lane > 0.0
        top = jnp.max(jnp.where(is_class, logits, -jnp.inf), 1, keepdims=True)
        powers = jnp.where(is_class, jnp.exp(jnp.where(is_class, logits - top, 0.0)), 0.0)
        total = jnp.sum(powers, 1, keepdims=True)
        onehot = label_ref[rows]
        mask = mask_ref[rows]
        seg = mask[:, 0:1] * (
            top + jnp.log(total) - jnp.sum(logits * onehot, 1, keepdims=True)
        )
        is_depth = depth_lane > 0.0
        inverse = jnp.exp(-jnp.abs(logits))
        soft = jnp.maximum(logits, 0.0) + jnp.log(1.0 + inverse)
        slope = jnp.where(logits >= 0.0, 1.0, inverse) / (1.0 + inverse)
        error = jnp.where(is_depth, soft, logits) - target_ref[rows]
        root = jnp.sqrt(error * error + 1.0)
        other = error / root * jnp.where(is_depth, slope, 1.0)
        grad = scale * mask * jnp.where(is_class, powers / total - onehot, other)
        low = grad.astype(logit_ref.dtype)
        logit_ref[rows] = low
        up = gelu_slope(mixed, dot(low, project_ref[:, 5 * width :], (1, 1))).astype(mixed_ref.dtype)
        mixed_ref[rows] = up
        cat = dot(up, project_ref[:, : 5 * width])
        for branch in range(4):
            grad_ref[branch, rows] = gelu_slope(
                z_ref[branch, rows], cat[:, branch * width : (branch + 1) * width]
            ).astype(grad_ref.dtype)
        return (
            carry[0] + jnp.sum(low.astype(jnp.float32), 0, keepdims=True),
            carry[1] + jnp.sum(mask * (root - 1.0), 0, keepdims=True),
            carry[2] + jnp.sum(seg, 0, keepdims=True),
            carry[3] + jnp.sum(cat[:, 4 * width :], 0, keepdims=True),
        )

    zero = jnp.zeros((1, 128), jnp.float32)
    bias_sum, error_sum, seg_sum, pool_sum = lax.fori_loop(
        0,
        POSITIONS // BLOCK,
        step,
        (zero, zero, jnp.zeros((1, 1), jnp.float32), jnp.zeros((1, width), jnp.float32)),
    )
    pool_ref[...] = gelu_slope(pool_pre_ref[...], pool_sum).astype(jnp.bfloat16).astype(jnp.float32)
    stat_ref[...] = jnp.concatenate(
        [bias_sum, error_sum, jnp.broadcast_to(seg_sum, (1, 128)), jnp.zeros((5, 128))], 0
    )


def head_step(own, other, rows, label, target, mask, project, branches, pool_pre):
    width = branches.shape[2]
    low = jnp.bfloat16
    return pl.pallas_call(
        head_kernel,
        out_shape=[
            jax.ShapeDtypeStruct((POSITIONS, BRANCH), low),
            jax.ShapeDtypeStruct((POSITIONS, 128), low),
            jax.ShapeDtypeStruct((POSITIONS, BRANCH), low),
            jax.ShapeDtypeStruct((4, POSITIONS, width), low),
            jax.ShapeDtypeStruct((1, width), jnp.float32),
            jax.ShapeDtypeStruct((8, 128), jnp.float32),
        ],
        in_specs=vmem(9),
        out_specs=vmem(6),
        compiler_params=pltpu.CompilerParams(vmem_limit_bytes=50 << 20),
        cost_estimate=pl.CostEstimate(flops=2 * 10**9, bytes_accessed=16 << 20, transcendentals=0),
        name="head_step",
    )(own, other, rows, label, target, mask, project, branches, pool_pre)


def own_rows(stat, place_ref, first):
    lower = place_ref[0] == 0
    return jnp.concatenate(
        [
            jnp.where(lower, stat[first + part : first + part + 1], stat[first + 2 + part : first + 3 + part])
            for part in range(2)
        ],
        1,
    )


def own_norm(place_ref, stat_ref, count_ref):
    stat = stat_ref[...]
    count = count_ref[2:3, 0:1]
    mean = own_rows(stat, place_ref, 0) / count
    return mean, lax.rsqrt(own_rows(stat, place_ref, 4) / count - mean * mean + norm_eps), count


def residual_sums_kernel(
    place_ref,
    own_ref,
    other_hbm,
    y_hbm,
    stat_ref,
    count_ref,
    crop_ref,
    head_ref,
    o_ref,
    y_ref,
    other_ref,
    sems,
):
    depth = own_ref.shape[1]
    half = pl.ds(pl.multiple_of(place_ref[0] * depth, 128), depth)
    copy = pltpu.make_async_copy(y_hbm.at[:, half], y_ref, sems.at[0])
    copy.start()
    other_copy = pltpu.make_async_copy(other_hbm.at[1 - place_ref[0]], other_ref, sems.at[1])
    other_copy.start()
    mean, scale, count = own_norm(place_ref, stat_ref, count_ref)
    copy.wait()
    other_copy.wait()

    def step(index, carry):
        rows = block_rows(index)
        up = crop_ref[rows] * (
            own_ref[rows].astype(jnp.float32) + other_ref[rows].astype(jnp.float32)
        )
        normed = (y_ref[rows].astype(jnp.float32) - mean) * scale
        return (
            carry[0] + jnp.sum(up * normed, 0, keepdims=True),
            carry[1] + jnp.sum(up, 0, keepdims=True),
        )

    zero = jnp.zeros((1, depth), jnp.float32)
    sums = lax.fori_loop(0, POSITIONS // BLOCK, step, (zero, zero))
    for turn, values in enumerate(sums):
        for part in range(2):
            row = 2 * turn + part
            o_ref[row : row + 1] = values[:, part * MID : (part + 1) * MID]
    o_ref[4:5] = jnp.concatenate(
        [head_ref[0:1], head_ref[1:2], head_ref[2:3], jnp.zeros((1, 128), jnp.float32)], 1
    )
    o_ref[5:8] = jnp.zeros((3, MID), jnp.float32)


def residual_sums(place, own, other, expanded, stat, counts, crop, head_stat):
    return pl.pallas_call(
        residual_sums_kernel,
        out_shape=jax.ShapeDtypeStruct((8, MID), jnp.float32),
        in_specs=[pl.BlockSpec(memory_space=pltpu.SMEM)]
        + vmem(1)
        + [pl.BlockSpec(memory_space=pl.ANY)] * 2
        + vmem(4),
        out_specs=vmem(1)[0],
        scratch_shapes=[
            pltpu.VMEM(own.shape, jnp.bfloat16),
            pltpu.VMEM(own.shape, jnp.bfloat16),
            pltpu.SemaphoreType.DMA((2,)),
        ],
        compiler_params=pltpu.CompilerParams(vmem_limit_bytes=40 << 20),
        cost_estimate=pl.CostEstimate(flops=10**8, bytes_accessed=12 << 20, transcendentals=0),
        name="residual_sums",
    )(place, own, other, expanded, stat, counts, crop, head_stat)


def residual_back_kernel(
    place_ref,
    own_ref,
    other_hbm,
    y_hbm,
    stat_ref,
    count_ref,
    sum_ref,
    gain_ref,
    crop_ref,
    bottle_hbm,
    o_ref,
    part_ref,
    y_ref,
    other_ref,
    weights,
    sems,
):
    depth = own_ref.shape[1]
    half = pl.ds(pl.multiple_of(place_ref[0] * depth, 128), depth)
    copy = pltpu.make_async_copy(y_hbm.at[:, half], y_ref, sems.at[0])
    copy.start()
    weight_copy = pltpu.make_async_copy(bottle_hbm.at[1, half], weights, sems.at[1])
    weight_copy.start()
    other_copy = pltpu.make_async_copy(other_hbm.at[1 - place_ref[0]], other_ref, sems.at[2])
    other_copy.start()
    mean, scale, count = own_norm(place_ref, stat_ref, count_ref)
    sums = sum_ref[...]
    gain_grad = jnp.concatenate([sums[0:1], sums[1:2]], 1) / count
    shift_grad = jnp.concatenate([sums[2:3], sums[3:4]], 1) / count
    factor = gain_ref[0:1, MID // 2 :] * scale
    copy.wait()
    weight_copy.wait()
    other_copy.wait()

    def step(index, carry):
        rows = block_rows(index)
        crop = crop_ref[rows]
        up = crop * (own_ref[rows].astype(jnp.float32) + other_ref[rows].astype(jnp.float32))
        normed = (y_ref[rows].astype(jnp.float32) - mean) * scale
        low = (crop * factor * (up - (shift_grad + normed * gain_grad))).astype(o_ref.dtype)
        o_ref[rows] = low
        part_ref[rows] = dot(low, weights[...]).astype(part_ref.dtype)
        return carry

    lax.fori_loop(0, POSITIONS // BLOCK, step, 0)


def residual_back(place, own, other, expanded, stat, counts, sums, gains, crop, bottle):
    hbm = pl.BlockSpec(memory_space=pl.ANY)
    depth = own.shape[1]
    return pl.pallas_call(
        residual_back_kernel,
        out_shape=[
            jax.ShapeDtypeStruct((POSITIONS, depth), jnp.bfloat16),
            jax.ShapeDtypeStruct((POSITIONS, MID), jnp.bfloat16),
        ],
        in_specs=[pl.BlockSpec(memory_space=pltpu.SMEM)] + vmem(1) + [hbm] * 2 + vmem(5) + [hbm],
        out_specs=vmem(2),
        scratch_shapes=[
            pltpu.VMEM(own.shape, jnp.bfloat16),
            pltpu.VMEM(own.shape, jnp.bfloat16),
            pltpu.VMEM((depth, MID), jnp.bfloat16),
            pltpu.SemaphoreType.DMA((3,)),
        ],
        compiler_params=pltpu.CompilerParams(vmem_limit_bytes=40 << 20),
        cost_estimate=pl.CostEstimate(flops=2 * 10**9, bytes_accessed=16 << 20, transcendentals=0),
        name="residual_back",
    )(place, own, other, expanded, stat, counts, sums, gains, crop, bottle)


def adam_step(weight, first, second, gradient, factor, rate, decay):
    gradient = gradient * factor
    first_new = 0.5 * first + 0.5 * gradient
    second_new = 0.5 * second + 0.5 * gradient * gradient
    direction = (
        first_new / (1.0 - 0.5**STEP) / (jnp.sqrt(second_new / (1.0 - 0.5**STEP)) + adam_eps)
    )
    return (weight - rate * (direction + decay * weight), first_new, second_new)


def on_device(
    sizes,
    patches,
    labels,
    offset_target,
    offset_valid,
    depth_target,
    lidar_valid,
    crop_mask,
    stem_weight,
    stem_first,
    stem_second,
    bottle_weight,
    bottle_first,
    bottle_second,
    middle_weight,
    middle_first,
    middle_second,
    pyramid_weight,
    pyramid_first,
    pyramid_second,
    project_weight,
    project_first,
    project_second,
    head_weight,
    head_first,
    head_second,
    norm_gains,
    norm_first,
    norm_second,
    task_params,
    task_first,
    task_second,
):
    chan_place = lax.axis_index("chan")
    dp_size = sizes["dp"]
    low = jnp.bfloat16
    crop_field = crop_mask.astype(jnp.float32).reshape(POSITIONS, 1)
    offset_field = crop_field[:, 0] * offset_valid.astype(jnp.float32).reshape(POSITIONS)
    lidar_field = crop_field[:, 0] * lidar_valid.astype(jnp.float32).reshape(POSITIONS)
    local_counts = jnp.stack([jnp.sum(crop_field), jnp.sum(offset_field), jnp.sum(lidar_field)])
    half = D // 2
    mid_half = MID // 2

    row_share = bottle_weight.shape[1]
    mid_share = middle_weight.shape[1]
    stem_share = stem_weight.shape[2]
    project_share = project_weight.shape[2]
    head_share = head_weight.shape[0]
    stem_shard = stem_weight.astype(low).reshape(PATCH, stem_share).T
    head_shard = jnp.concatenate(
        [
            project_weight.astype(low).transpose(2, 0, 1).reshape(project_share, 5 * 128),
            jnp.pad(head_weight.astype(low), ((0, 0), (0, 128 - 22))),
        ],
        1,
    )
    bottle_low, middle_low, stem_low, head_low = gather_trunk(
        sizes, bottle_weight.astype(low), middle_weight.astype(low), stem_shard, head_shard
    )
    pyramid_shard = pyramid_weight.astype(low)
    late_shard, bottle_low = lax.optimization_barrier((pyramid_shard[EARLY_TAPS:], bottle_low))
    pyramid_low = (
        lax.all_gather(pyramid_shard[:EARLY_TAPS], "dp", axis=1, tiled=True),
        lax.all_gather(late_shard, "dp", axis=1, tiled=True),
    )
    own_place = chan_place.reshape(1)
    own_gains = norm_gains.reshape(2, mid_half + half)
    gains = (own_place, own_gains, swap_chan(own_gains))
    gain_low = jnp.where(chan_place == 0, own_gains[:, :mid_half], gains[2][:, :mid_half])
    gain_high = jnp.where(chan_place == 0, gains[2][:, :mid_half], own_gains[:, :mid_half])
    gain_one, shift_one = jnp.concatenate([gain_low, gain_high], 1)

    def own_bottle(which):
        return lax.dynamic_slice(bottle_low, (which, chan_place * half, 0), (1, half, MID))[0]

    def own_half(values, axis):
        width = values.shape[axis] // 2
        return lax.dynamic_slice_in_dim(values, chan_place * width, width, axis)

    def other_half(values, axis):
        width = values.shape[axis] // 2
        return lax.dynamic_slice_in_dim(values, (1 - chan_place) * width, width, axis)

    columns = jnp.broadcast_to(
        lax.rem(lax.broadcasted_iota(jnp.int32, (POSITIONS, 1), 0), FW).astype(jnp.float32),
        (POSITIONS, 128),
    )
    patch_rows = patches.reshape(POSITIONS, PATCH)
    stream_low, first_pre, stat_one = stem_reduce(
        patch_rows,
        stem_low,
        bottle_low,
        crop_field,
        jnp.pad(local_counts, (0, MID - 3)).reshape(1, MID),
    )
    stat_one = all_sum(sizes, stat_one, ("dp",), 0)
    hidden_low, hidden_t, second_low = norm_middle(
        first_pre, stat_one, gains, crop_field, middle_low, columns
    )
    expand_pre, stat_two = expand_forward(second_low, bottle_low, crop_field)
    stat_two = all_sum(sizes, stat_two, ("dp",), 1)
    output_low, output_t, pooled = residual_stream(
        patch_rows,
        stem_low,
        expand_pre,
        stat_two,
        stat_one,
        gains,
        crop_field,
    )
    branch_pre, pool_pre, concat_low, project_part = pyramid_forward(
        output_low, pooled, pyramid_low, head_low, columns
    )
    labels, offset_valid, lidar_valid, offset_target, depth_target, project_part = (
        lax.optimization_barrier(
            (labels, offset_valid, lidar_valid, offset_target, depth_target, project_part)
        )
    )
    offset_field = crop_field[:, 0] * offset_valid.astype(jnp.float32).reshape(POSITIONS)
    lidar_field = crop_field[:, 0] * lidar_valid.astype(jnp.float32).reshape(POSITIONS)
    lane = lax.broadcasted_iota(jnp.int32, (1, 128), 1)
    class_lane = (lane < CLASSES).astype(jnp.float32)
    offset_lane = ((lane >= CLASSES) & (lane < CLASSES + 2)).astype(jnp.float32)
    depth_lane = (lane == CLASSES + 2).astype(jnp.float32)
    onehot = (labels.reshape(POSITIONS, 1) == lane).astype(jnp.float32)
    mask = (
        class_lane * crop_field
        + offset_lane * offset_field[:, None]
        + depth_lane * lidar_field[:, None]
    )
    target = jnp.pad(
        jnp.concatenate([offset_target[0], depth_target], 0).T,
        ((0, 0), (CLASSES, 128 - CLASSES - 3)),
    )
    task_scale = task_params[:3]
    counts = stat_one[2, :3]
    crop_total = counts[0]
    task_weights = jnp.exp(-task_scale) / counts
    lane_rows = jnp.concatenate(
        [
            jnp.pad(task_params[3:], (0, 128 - 22)).reshape(1, 128),
            task_weights[0] * class_lane
            + task_weights[1] * offset_lane
            + task_weights[2] * depth_lane,
            class_lane,
            offset_lane,
            depth_lane,
            jnp.zeros((3, 128), jnp.float32),
        ],
        0,
    )
    feature_low, logit_low, project_grad_low, branch_grads, pool_grad, head_stat = head_step(
        project_part,
        swap_chan(project_part),
        lane_rows,
        onehot,
        target,
        mask,
        head_low,
        branch_pre,
        pool_pre,
    )
    other_part = pyramid_field(
        1 - own_place, pyramid_low, branch_grads, pool_grad, crop_field, columns
    )
    other_sent = lax.all_gather(other_part, "chan")
    later_grads, other_part = lax.optimization_barrier((branch_grads, other_part))
    own_part = pyramid_field(own_place, pyramid_low, later_grads, pool_grad, crop_field, columns)
    later_grads, own_part = lax.optimization_barrier((later_grads, own_part))
    pyramid_grad = pyramid_weights(
        output_t, later_grads, columns, pooled.reshape(D, 1), pool_grad
    )
    pyramid_red = lax.psum_scatter(pyramid_grad, "dp", scatter_dimension=1, tiled=True)

    stat_three = residual_sums(
        own_place, own_part, other_sent, expand_pre, stat_two, stat_one, crop_field, head_stat
    )
    stat_three = all_sum(sizes, stat_three, ("dp",), 2)
    expand_grad_low, second_part = residual_back(
        own_place,
        own_part,
        other_sent,
        expand_pre,
        stat_two,
        stat_one,
        stat_three,
        own_gains,
        crop_field,
        bottle_low,
    )
    stat_one, stat_three, own_part, second_part = lax.optimization_barrier(
        (stat_one, stat_three, own_part, second_part)
    )
    gain_two_grad = stat_three[:2].reshape(half)
    shift_two_grad = stat_three[2:4].reshape(half)
    bias_grad = stat_three[4, :22]
    error_sums = stat_three[4, 128:256]
    loss_sums = jnp.stack(
        [
            stat_three[4, 256],
            error_sums[CLASSES] + error_sums[CLASSES + 1],
            error_sums[CLASSES + 2],
        ]
    )
    mean_one = stat_one[0] / crop_total
    scale_one = lax.rsqrt(stat_one[1] / crop_total - mean_one * mean_one + norm_eps)
    stream_grad = own_part.astype(jnp.float32) + lax.dynamic_index_in_dim(
        other_sent, 1 - chan_place, 0, keepdims=False
    ).astype(jnp.float32)
    task_means = loss_sums / counts
    total_loss = jnp.sum(jnp.exp(-task_scale) * task_means + task_scale)
    scale_grad = 1.0 - jnp.exp(-task_scale) * task_means
    second_part, feature_low, logit_low, concat_low, project_grad_low = lax.optimization_barrier(
        (second_part, feature_low, logit_low, concat_low, project_grad_low)
    )
    second_other = swap_chan(second_part)
    expand_rows = dot(expand_grad_low, second_low, (0, 0)).astype(low)
    expand_sent = swap_chan(other_half(expand_rows, 1))
    second_grad_low = (
        second_part.astype(jnp.float32) + second_other.astype(jnp.float32)
    ).astype(low)
    hidden_grad = middle_conv(second_grad_low, middle_low, columns, True, jnp.float32)
    normed_one = (first_pre - mean_one) * scale_one
    act_input = gain_one * normed_one + shift_one
    upstream_one = gelu_grad(act_input, crop_field * hidden_grad)
    gain_one_all, shift_one_all = small_sum(
        sizes,
        [jnp.sum(upstream_one * normed_one, 0), jnp.sum(upstream_one, 0)],
        ("dp",),
        3,
    )
    gain_one_grad = own_half(gain_one_all, 0)
    shift_one_grad = own_half(shift_one_all, 0)
    first_grad_low = (
        crop_field
        * gain_one
        * scale_one
        * (upstream_one - (shift_one_all + normed_one * gain_one_all) / crop_total)
    ).astype(low)
    middle_grad = middle_weights(hidden_t, own_half(second_grad_low, 1), columns)
    reduce_grad = dot(stream_low, own_half(first_grad_low, 1), (0, 0)).astype(low)
    start_grad = dot(first_grad_low, own_bottle(0), (1, 1)) + stream_grad
    start_grad_low = (crop_field * start_grad).astype(low)
    stem_grad = dot(start_grad_low, patch_rows, (0, 0)).astype(low)
    expand_own = own_half(expand_rows, 1)
    expand_grad = jnp.where(
        chan_place == 0,
        jnp.concatenate([expand_own, expand_sent], 0),
        jnp.concatenate([expand_sent, expand_own], 0),
    )

    small_grads = jnp.concatenate(
        [
            dot(project_grad_low, concat_low, (0, 0)).astype(low),
            dot(feature_low, logit_low, (0, 0)).astype(low),
        ],
        1,
    )
    small_rows = project_share * 3
    trunk_grads = jnp.concatenate(
        [
            reduce_grad.reshape(dp_size, row_share, 256),
            expand_grad.reshape(dp_size, row_share, 256),
            middle_grad.reshape(9, dp_size, mid_share, 256)
            .transpose(1, 0, 2, 3)
            .reshape(dp_size, 9 * mid_share, 256),
            stem_grad.reshape(dp_size, stem_share * PATCH // 256, 256),
            small_grads.reshape(dp_size, small_rows, 256),
        ],
        1,
    )
    trunk_grads, pyramid_red = lax.optimization_barrier((trunk_grads, pyramid_red))
    trunk_red = lax.psum_scatter(trunk_grads, "dp", scatter_dimension=0, tiled=True)[0]
    trunk_red = trunk_red.astype(jnp.float32)
    bottle_red = trunk_red[: 2 * row_share].reshape(bottle_weight.shape)
    start = 2 * row_share
    middle_red = trunk_red[start : start + 9 * mid_share].reshape(middle_weight.shape)
    start += 9 * mid_share
    stem_rows = stem_share * PATCH // 256
    stem_red = trunk_red[start : start + stem_rows]
    stem_red = stem_red.reshape(stem_share, PATCH).T.reshape(stem_weight.shape)
    small_red = trunk_red[start + stem_rows :].reshape(project_share, 768)
    project_red = small_red[:, : 5 * 128].reshape(project_share, 5, 128).transpose(1, 2, 0)
    head_red = small_red[:, 5 * 128 : 5 * 128 + 22]
    pyramid_red = pyramid_red.astype(jnp.float32)
    norm_grad = jnp.stack(
        [
            jnp.concatenate([gain_one_grad, gain_two_grad]),
            jnp.concatenate([shift_one_grad, shift_two_grad]),
        ]
    )[:, None, :]
    task_grad = jnp.concatenate([scale_grad, bias_grad])
    dp_first = (lax.axis_index("dp") == 0).astype(jnp.float32)
    chan_first = (chan_place == 0).astype(jnp.float32)
    own_squares = (
        jnp.sum(stem_red * stem_red)
        + jnp.sum(bottle_red * bottle_red)
        + jnp.sum(middle_red * middle_red)
        + jnp.sum(pyramid_red * pyramid_red)
        + jnp.sum(project_red * project_red)
        + chan_first * jnp.sum(head_red * head_red)
        + dp_first * jnp.sum(norm_grad * norm_grad)
        + dp_first * chan_first * jnp.sum(task_grad * task_grad)
    )
    grad_norm = jnp.sqrt(small_sum(sizes, [own_squares], ("dp", "chan"), 4)[0])
    factor = clip_level / jnp.maximum(grad_norm, clip_level)
    new_stem = adam_step(
        stem_weight, stem_first, stem_second, stem_red, factor, PATCH ** (-0.5), decay_rate
    )
    new_bottle = adam_step(
        bottle_weight, bottle_first, bottle_second, bottle_red, factor, D ** (-0.5), decay_rate
    )
    new_middle = adam_step(
        middle_weight,
        middle_first,
        middle_second,
        middle_red,
        factor,
        (9 * MID) ** (-0.5),
        decay_rate,
    )
    new_pyramid = adam_step(
        pyramid_weight,
        pyramid_first,
        pyramid_second,
        pyramid_red,
        factor,
        (3 * D) ** (-0.5),
        decay_rate,
    )
    new_project = adam_step(
        project_weight,
        project_first,
        project_second,
        project_red,
        factor,
        (5 * BRANCH) ** (-0.5),
        decay_rate,
    )
    new_head = adam_step(
        head_weight, head_first, head_second, head_red, factor, BRANCH ** (-0.5), decay_rate
    )
    new_norm = adam_step(norm_gains, norm_first, norm_second, norm_grad, factor, 0.3, 0.0)
    new_task = adam_step(task_params, task_first, task_second, task_grad, factor, 0.3, 0.0)
    return (
        total_loss,
        grad_norm,
        new_stem[0],
        new_stem[1],
        new_stem[2],
        new_bottle[0],
        new_bottle[1],
        new_bottle[2],
        new_middle[0],
        new_middle[1],
        new_middle[2],
        new_pyramid[0],
        new_pyramid[1],
        new_pyramid[2],
        new_project[0],
        new_project[1],
        new_project[2],
        new_head[0],
        new_head[1],
        new_head[2],
        new_norm[0],
        new_norm[1],
        new_norm[2],
        new_task[0],
        new_task[1],
        new_task[2],
    )


def solution(mesh):
    return jax.shard_map(
        functools.partial(on_device, dict(mesh.shape)),
        mesh=mesh,
        in_specs=(
            P("dp", None, None),
            P("dp", None),
            P("dp", None, None),
            P("dp", None),
            P("dp", None),
            P("dp", None),
            P("dp", None),
            P(None, "chan", "dp"),
            P(None, "chan", "dp"),
            P(None, "chan", "dp"),
            P(None, "dp", "chan"),
            P(None, "dp", "chan"),
            P(None, "dp", "chan"),
            P(None, "dp", "chan"),
            P(None, "dp", "chan"),
            P(None, "dp", "chan"),
            P(None, "dp", "chan"),
            P(None, "dp", "chan"),
            P(None, "dp", "chan"),
            P(None, "chan", "dp"),
            P(None, "chan", "dp"),
            P(None, "chan", "dp"),
            P("dp", None),
            P("dp", None),
            P("dp", None),
            P(None, "chan", None),
            P(None, "chan", None),
            P(None, "chan", None),
            P(),
            P(),
            P(),
        ),
        out_specs=(
            P(),
            P(),
            P(None, "chan", "dp"),
            P(None, "chan", "dp"),
            P(None, "chan", "dp"),
            P(None, "dp", "chan"),
            P(None, "dp", "chan"),
            P(None, "dp", "chan"),
            P(None, "dp", "chan"),
            P(None, "dp", "chan"),
            P(None, "dp", "chan"),
            P(None, "dp", "chan"),
            P(None, "dp", "chan"),
            P(None, "dp", "chan"),
            P(None, "chan", "dp"),
            P(None, "chan", "dp"),
            P(None, "chan", "dp"),
            P("dp", None),
            P("dp", None),
            P("dp", None),
            P(None, "chan", None),
            P(None, "chan", None),
            P(None, "chan", None),
            P(),
            P(),
            P(),
        ),
        check_vma=False,
    )
```

```python
import functools

import jax
import jax.numpy as jnp
from jax import lax
from jax.experimental import pallas as pl
from jax.experimental.pallas import tpu as pltpu
from jax.sharding import PartitionSpec as P

D = 2048
MID = 512
BRANCH = 256
CLASSES = 19
PATCH = 192
FH = 40
FW = 40
STEP = 10
POSITIONS = 1600


pyramid_rates = (0, 12, 24, 36)
norm_eps = 1e-05
clip_level = 0.01
adam_eps = 1e-08
decay_rate = 0.01


MESH_ID = pl.DeviceIdType.MESH


def group_place(sizes, axes):
    place = jnp.int32(0)
    for axis in axes:
        place = place * sizes[axis] + lax.axis_index(axis)
    return place


def group_device(sizes, axes, index):
    coords = {}
    for axis in reversed(axes):
        coords[axis] = lax.rem(index, sizes[axis])
        index = lax.div(index, sizes[axis])
    return tuple(coords.get(axis, lax.axis_index(axis)) for axis in ("dp", "chan"))


def sum_kernel(sizes, axes, count, x_ref, o_ref, slots, send_sem, recv_sem):
    me = group_place(sizes, axes)
    barrier = pltpu.get_barrier_semaphore()

    def greet(step, carry):
        other = lax.rem(me + step, count)
        pl.semaphore_signal(
            barrier, inc=1, device_id=group_device(sizes, axes, other), device_id_type=MESH_ID
        )
        return carry

    lax.fori_loop(1, count, greet, 0)
    pl.semaphore_wait(barrier, count - 1)

    def copy_to(step):
        other = lax.rem(me + step, count)
        return pltpu.make_async_remote_copy(
            src_ref=x_ref,
            dst_ref=slots.at[me],
            send_sem=send_sem.at[step],
            recv_sem=recv_sem.at[me],
            device_id=group_device(sizes, axes, other),
            device_id_type=MESH_ID,
        )

    def copy_from(step):
        other = lax.rem(me + step, count)
        return pltpu.make_async_remote_copy(
            src_ref=x_ref,
            dst_ref=slots.at[other],
            send_sem=send_sem.at[step],
            recv_sem=recv_sem.at[other],
            device_id=group_device(sizes, axes, other),
            device_id_type=MESH_ID,
        )

    def start(step, carry):
        copy_to(step).start()
        return carry

    lax.fori_loop(1, count, start, 0)
    slots[me] = x_ref[...]

    def arrive(step, carry):
        copy_from(step).wait_recv()
        return carry

    lax.fori_loop(1, count, arrive, 0)
    o_ref[...] = lax.fori_loop(
        1, count, lambda index, total: total + slots[index], slots[0]
    )

    def leave(step, carry):
        copy_to(step).wait_send()
        return carry

    lax.fori_loop(1, count, leave, 0)


def all_sum(sizes, values, axes, collective):
    count = 1
    for axis in axes:
        count *= sizes[axis]
    return pl.pallas_call(
        functools.partial(sum_kernel, sizes, axes, count),
        out_shape=jax.ShapeDtypeStruct(values.shape, jnp.float32),
        in_specs=[pl.BlockSpec(memory_space=pltpu.VMEM)],
        out_specs=pl.BlockSpec(memory_space=pltpu.VMEM),
        scratch_shapes=[
            pltpu.VMEM((count,) + values.shape, jnp.float32),
            pltpu.SemaphoreType.DMA((count,)),
            pltpu.SemaphoreType.DMA((count,)),
        ],
        compiler_params=pltpu.CompilerParams(
            collective_id=collective, has_side_effects=True, vmem_limit_bytes=32 << 20
        ),
        name="small_sum",
    )(values)


def small_sum(sizes, parts, axes, collective):
    flat = jnp.concatenate([part.reshape(-1) for part in parts])
    rows = -(-flat.shape[0] // 1024) * 8
    packed = jnp.pad(flat, (0, rows * 128 - flat.shape[0])).reshape(rows, 128)
    summed = all_sum(sizes, packed, axes, collective).reshape(-1)
    result = []
    start = 0
    for part in parts:
        size = part.size
        result.append(summed[start : start + size].reshape(part.shape))
        start += size
    return result


def swap_chan(values):
    return lax.ppermute(values, "chan", [(0, 1), (1, 0)])


def valid(step, length):
    return max(0, step), length + min(0, step)


def taps_of(rate):
    return [((tap // 3 - 1) * rate, (tap % 3 - 1) * rate) for tap in range(9)]


def shift_field(field, row_step, col_step):
    rows, cols = field.shape[:2]
    r0, r1 = valid(row_step, rows)
    c0, c1 = valid(col_step, cols)
    return jnp.pad(
        field[r0:r1, c0:c1],
        (
            (r0 - row_step, rows - (r1 - row_step)),
            (c0 - col_step, cols - (c1 - col_step)),
            (0, 0),
        ),
    )


def gelu_grad(values, upstream):
    return jax.vjp(jax.nn.gelu, values)[1](upstream)[0]


def dot(left, right, contract=(1, 0)):
    return lax.dot_general(
        left,
        right,
        (((contract[0],), (contract[1],)), ((), ())),
        preferred_element_type=jnp.float32,
    )


def place_of():
    dp = lax.axis_index("dp")
    return lax.div(dp, 4), lax.rem(lax.div(dp, 2), 2), lax.rem(dp, 2), lax.axis_index("chan")


def device_at(z, y, core, x):
    return ((z * 2 + y) * 2 + core, x)


def flip(value, turn):
    return lax.rem(value + turn, 2)


def z_flip(z, turn):
    return flip(lax.div(z, 2), turn // 2) * 2 + flip(lax.rem(z, 2), turn % 2)


def greet_neighbours(layers):
    z, y, core, x = place_of()
    barrier = pltpu.get_barrier_semaphore()
    for target in (
        device_at(z, y, 1 - core, x),
        device_at(z, 1 - y, core, x),
        device_at(z, y, core, 1 - x),
    ):
        pl.semaphore_signal(barrier, inc=1, device_id=target, device_id_type=MESH_ID)

    @pl.when(z > 0)
    def _():
        pl.semaphore_signal(
            barrier, inc=1, device_id=device_at(z - 1, y, core, x), device_id_type=MESH_ID
        )

    @pl.when(z < layers - 1)
    def _():
        pl.semaphore_signal(
            barrier, inc=1, device_id=device_at(z + 1, y, core, x), device_id_type=MESH_ID
        )

    peers = 3 + jnp.where(z > 0, 1, 0) + jnp.where(z < layers - 1, 1, 0)
    pl.semaphore_wait(barrier, peers)


def gather_kernel(
    layers,
    bottle,
    middle,
    small,
    head,
    bottle_all,
    middle_all,
    small_all,
    head_all,
    send_sems,
    recv_sems,
    local_sems,
):
    z, y, core, x = place_of()
    rows = bottle.shape[1]
    mid_rows = middle.shape[1]
    small_rows = small.shape[0]
    head_rows = head.shape[0]
    own_refs = (bottle, middle, small, head)

    def region(kind, block):
        zz, yy, kk, xx = block
        index = (zz * 2 + yy) * 2 + kk
        cols = pl.ds(pl.multiple_of(xx * 256, 256), 256)
        if kind == 0:
            return bottle_all.at[:, pl.ds(pl.multiple_of(index * rows, 16), rows), cols]
        if kind == 1:
            return middle_all.at[:, pl.ds(pl.multiple_of(index * mid_rows, 16), mid_rows), cols]
        if kind == 3:
            return head_all.at[pl.ds(pl.multiple_of(index * head_rows, 16), head_rows)]
        first = xx * (small_all.shape[0] // 2) + index * small_rows
        return small_all.at[pl.ds(pl.multiple_of(first, 16), small_rows)]

    def semaphore(kind, block):
        zz, yy, kk, xx = block
        return recv_sems.at[kind, ((zz * 2 + yy) * 2 + kk) * 2 + xx]

    own = (z, y, core, x)
    pending = []

    def send(kind, block, target, when=None):
        copy = pltpu.make_async_remote_copy(
            src_ref=own_refs[kind] if block is own else region(kind, block),
            dst_ref=region(kind, block),
            send_sem=send_sems.at[len(pending)],
            recv_sem=semaphore(kind, block),
            device_id=target,
            device_id_type=MESH_ID,
        )
        if when is None:
            copy.start()
        else:
            pl.when(when)(copy.start)
        pending.append((when, copy))

    def arrive(kind, block):
        pltpu.make_async_remote_copy(
            src_ref=region(kind, block),
            dst_ref=region(kind, block),
            send_sem=send_sems.at[0],
            recv_sem=semaphore(kind, block),
            device_id=device_at(z, y, 1 - core, x),
            device_id_type=MESH_ID,
        ).wait_recv()

    locals_ = [
        pltpu.make_async_copy(own_refs[kind], region(kind, own), local_sems.at[kind])
        for kind in range(4)
    ]
    for copy in locals_:
        copy.start()
    greet_neighbours(layers)
    sibling = device_at(z, y, 1 - core, x)
    other_x = device_at(z, y, core, 1 - x)
    other_y = device_at(z, 1 - y, core, x)

    def along_z(kind, block):
        if block[0] is z:
            send(kind, block, device_at(z + 1, y, core, x), z < layers - 1)
            send(kind, block, device_at(z - 1, y, core, x), z > 0)
        else:
            below = block[0] < z
            ahead = z + jnp.where(below, 1, -1)
            send(
                kind,
                block,
                device_at(ahead, y, core, x),
                jnp.logical_and(ahead >= 0, ahead < layers),
            )

    for kind in (0, 1):
        along_z(kind, own)
    send(2, own, other_x)
    send(2, own, other_y)
    send(1, own, other_x)
    send(0, own, other_y)
    along_z(2, own)
    along_z(3, own)
    send(3, own, other_y)
    send(0, own, other_x)
    send(1, own, other_y)
    for kind in range(4):
        send(kind, own, sibling)

    block = (z, y, core, 1 - x)
    arrive(2, block)
    send(2, block, other_y)
    along_z(2, block)
    send(2, block, sibling)
    for xx in (x, 1 - x):
        block = (z, 1 - y, core, xx)
        arrive(2, block)
        along_z(2, block)
        send(2, block, sibling)

    for turn in range(layers):
        zz = z if turn == 0 else z_flip(z, turn)
        if turn:
            for kind, near, far in ((0, other_y, other_x), (1, other_x, other_y)):
                block = (zz, y, core, x)
                arrive(kind, block)
                along_z(kind, block)
                send(kind, block, near)
                send(kind, block, far)
                send(kind, block, sibling)
            block = (zz, y, core, x)
            arrive(3, block)
            along_z(3, block)
            send(3, block, other_y)
            send(3, block, sibling)
        block = (zz, 1 - y, core, x)
        arrive(0, block)
        send(0, block, other_x)
        send(0, block, sibling)
        block = (zz, y, core, 1 - x)
        arrive(1, block)
        send(1, block, other_y)
        send(1, block, sibling)
        if turn:
            for yy, xx in ((y, x), (y, 1 - x), (1 - y, x), (1 - y, 1 - x)):
                block = (zz, yy, core, xx)
                arrive(2, block)
                along_z(2, block)
                send(2, block, sibling)
    for turn in range(layers):
        zz = z if turn == 0 else z_flip(z, turn)
        for yy in (y, 1 - y):
            block = (zz, yy, core, 1 - x)
            arrive(0, block)
            send(0, block, sibling)
        for xx in (x, 1 - x):
            block = (zz, 1 - y, core, xx)
            arrive(1, block)
            send(1, block, sibling)
        block = (zz, 1 - y, core, x)
        arrive(3, block)
        send(3, block, sibling)
    for kind in range(4):
        for turn in range(layers):
            zz = z if turn == 0 else z_flip(z, turn)
            for yy in (y, 1 - y):
                for xx in (x, 1 - x) if kind < 3 else (x,):
                    arrive(kind, (zz, yy, 1 - core, xx))
    for copy in locals_:
        copy.wait()
    for when, copy in pending:
        if when is None:
            copy.wait_send()
        else:
            pl.when(when)(copy.wait_send)


def gather_trunk(sizes, bottle, middle, small, head):
    count = sizes["dp"]
    if count != 16 or middle.shape[1] % 16:
        packed = [
            lax.all_gather(
                lax.all_gather(part, "dp", axis=1, tiled=True), "chan", axis=2, tiled=True
            )
            for part in (bottle, middle)
        ]
        return packed + [
            lax.all_gather(small, ("chan", "dp")).reshape(D, small.shape[1]),
            lax.all_gather(head, "dp", axis=0, tiled=True),
        ]
    return pl.pallas_call(
        functools.partial(gather_kernel, count // 4),
        out_shape=[
            jax.ShapeDtypeStruct((2, D, MID), jnp.bfloat16),
            jax.ShapeDtypeStruct((9, MID, MID), jnp.bfloat16),
            jax.ShapeDtypeStruct((D, small.shape[1]), jnp.bfloat16),
            jax.ShapeDtypeStruct((BRANCH, head.shape[1]), jnp.bfloat16),
        ],
        in_specs=[pl.BlockSpec(memory_space=pl.ANY)] * 4,
        out_specs=[pl.BlockSpec(memory_space=pl.ANY)] * 4,
        scratch_shapes=[
            pltpu.SemaphoreType.DMA((176,)),
            pltpu.SemaphoreType.DMA((4, 2 * count)),
            pltpu.SemaphoreType.DMA((4,)),
        ],
        compiler_params=pltpu.CompilerParams(collective_id=5, has_side_effects=True),
        name="gather_trunk",
    )(bottle, middle, small, head)


PAD = 128
PYRAMID_ROWS = (-36, -24, -12, 0, 12, 24, 36)


def taps_by_row():
    fields = [(0, 0)] + [(rate, col * rate) for rate in (12, 24, 36) for col in (-1, 0, 1)]
    groups = []
    for row_step in PYRAMID_ROWS:
        group = []
        for place, (rate, col_step) in enumerate(fields):
            if rate == 0:
                if row_step == 0:
                    group.append((0, place))
            elif row_step == 0 or abs(row_step) == rate:
                turn = (1 if row_step > 0 else -1 if row_step < 0 else 0) + 1
                tap = 1 + 9 * (rate // 12 - 1) + 3 * turn + (col_step // rate + 1)
                group.append((tap, place))
        groups.append(group)
    return fields, groups


FIELDS, ROW_GROUPS = taps_by_row()
TAP_ORDER = [tap for group in ROW_GROUPS for tap, place in group]
PLACE_ORDER = [place for group in ROW_GROUPS for tap, place in group]


EARLY_TAPS = 10


def tap_of(early, late, tap):
    return early.at[tap] if tap < EARLY_TAPS else late.at[tap - EARLY_TAPS]


def roll_cols(values, columns, step):
    if step == 0:
        return values
    moved = pltpu.roll(values, (-step) % values.shape[0], 0)
    target = columns[:, :1] + float(step)
    return jnp.where((target >= 0.0) & (target < float(FW)), moved, 0.0)


def vmem(count):
    return [pl.BlockSpec(memory_space=pltpu.VMEM)] * count


def middle_kernel(back, x_ref, w_ref, col_ref, o_ref, canvas):
    edge = 4 * FW
    mid = x_ref.shape[1]
    values = x_ref[...].astype(jnp.float32)
    sign = -1 if back else 1
    for turn in range(3):
        canvas[turn, :edge] = jnp.zeros((edge, mid), canvas.dtype)
        canvas[turn, POSITIONS + edge :] = jnp.zeros((edge, mid), canvas.dtype)
        canvas[turn, edge : POSITIONS + edge] = roll_cols(
            values, col_ref, sign * 4 * (turn - 1)
        ).astype(canvas.dtype)
    block = 400

    def step(index, carry):
        total = None
        for row in range(3):
            first = pl.multiple_of(index * block + edge * (1 + sign * (row - 1)), 16)
            for turn in range(3):
                part = dot(
                    canvas[turn, pl.ds(first, block)],
                    w_ref[3 * row + turn],
                    (1, 1) if back else (1, 0),
                )
                total = part if total is None else total + part
        o_ref[pl.ds(pl.multiple_of(index * block, 16), block)] = total.astype(o_ref.dtype)
        return carry

    lax.fori_loop(0, POSITIONS // block, step, 0)


def middle_conv(field, weights, columns, back, dtype):
    return pl.pallas_call(
        functools.partial(middle_kernel, back),
        out_shape=jax.ShapeDtypeStruct((POSITIONS, MID), dtype),
        in_specs=vmem(3),
        out_specs=vmem(1)[0],
        scratch_shapes=[pltpu.VMEM((3, POSITIONS + 8 * FW, MID), jnp.bfloat16)],
        compiler_params=pltpu.CompilerParams(vmem_limit_bytes=40 << 20),
        cost_estimate=pl.CostEstimate(
            flops=2 * POSITIONS * 9 * MID * MID, bytes_accessed=16 << 20, transcendentals=0
        ),
        name="middle_back" if back else "middle_fwd",
    )(field, weights, columns)


def middle_weight_kernel(xt_ref, g_ref, col_ref, o_ref, fields):
    width = g_ref.shape[1]
    values = g_ref[...].astype(jnp.float32)
    for turn in range(3):
        fields[turn, :PAD] = jnp.zeros((PAD, width), fields.dtype)
        fields[turn, PAD + POSITIONS :] = jnp.zeros((PAD, width), fields.dtype)
        fields[turn, PAD : PAD + POSITIONS] = roll_cols(values, col_ref, -4 * (turn - 1)).astype(
            fields.dtype
        )
    for row in range(3):
        row_step = 4 * (row - 1)
        r0, r1 = valid(row_step, FH)
        first = r0 * FW // 128 * 128
        last = min(POSITIONS, -(-r1 * FW // 128) * 128)
        base = PAD + first - row_step * FW
        for turn in range(3):
            o_ref[3 * row + turn] = dot(
                xt_ref[:, first:last], fields[turn, base : base + last - first]
            ).astype(o_ref.dtype)


def middle_weights(field_t, grads, columns):
    depth, width = field_t.shape[0], grads.shape[1]
    return pl.pallas_call(
        middle_weight_kernel,
        out_shape=jax.ShapeDtypeStruct((9, depth, width), jnp.bfloat16),
        in_specs=vmem(3),
        out_specs=vmem(1)[0],
        scratch_shapes=[pltpu.VMEM((3, POSITIONS + 2 * PAD, width), jnp.bfloat16)],
        compiler_params=pltpu.CompilerParams(vmem_limit_bytes=40 << 20),
        cost_estimate=pl.CostEstimate(
            flops=2 * POSITIONS * 9 * depth * width, bytes_accessed=6 << 20, transcendentals=0
        ),
        name="middle_weights",
    )(field_t, grads, columns)


def fill_fields(g_ref, col_ref, fields):
    width = g_ref.shape[2]
    for place, (rate, col_step) in enumerate(FIELDS):
        fields[place, :PAD] = jnp.zeros((PAD, width), fields.dtype)
        fields[place, PAD + POSITIONS :] = jnp.zeros((PAD, width), fields.dtype)
        values = g_ref[rate // 12]
        fields[place, PAD : PAD + POSITIONS] = roll_cols(
            values.astype(jnp.float32), col_ref, -col_step
        ).astype(fields.dtype)


def start_field_copies(place_ref, a_hbm, b_hbm, depth, weights, pool_weights, sems):
    width = pool_weights.shape[1]
    rows = pl.ds(pl.multiple_of(place_ref[0] * depth, 16), depth)
    copies = [
        pltpu.make_async_copy(
            tap_of(a_hbm, b_hbm, tap).at[rows],
            weights.at[:, pl.ds(slot * width, width)],
            sems.at[slot],
        )
        for slot, tap in enumerate(TAP_ORDER)
    ]
    copies.append(
        pltpu.make_async_copy(tap_of(a_hbm, b_hbm, 28).at[rows], pool_weights, sems.at[28])
    )
    for copy in copies:
        copy.start()
    return copies


def field_products(pool_ref, crop_ref, o_ref, weights, pool_weights, fields, stack):
    width = pool_weights.shape[1]
    pooled = dot(
        jnp.broadcast_to(pool_ref[...], (16, width)).astype(jnp.bfloat16), pool_weights[...], (1, 1)
    )[0:1] / jnp.sum(crop_ref[...], keepdims=True)
    step_of = [step for step, group in zip(PYRAMID_ROWS, ROW_GROUPS) for entry in group]
    for r0, r1 in ((0, 4), (4, 12), (12, 16), (16, 24), (24, 28), (28, 36), (36, 40)):
        slots = [
            slot for slot, step in enumerate(step_of) if r0 - step >= 0 and r1 - step <= FH
        ]
        count = (r1 - r0) * FW
        for at, slot in enumerate(slots):
            base = PAD + (r0 - step_of[slot]) * FW
            stack[:count, at * width : (at + 1) * width] = fields[
                PLACE_ORDER[slot], base : base + count
            ]
        part = dot(
            stack[:count, : len(slots) * width],
            weights[:, slots[0] * width : (slots[-1] + 1) * width],
            (1, 1),
        )
        o_ref[r0 * FW : r1 * FW] = (part + crop_ref[r0 * FW : r1 * FW] * pooled).astype(
            o_ref.dtype
        )


def field_kernel(
    place_ref, a_hbm, b_hbm, g_ref, pool_ref, crop_ref, col_ref, o_ref, weights, pool_weights, fields, stack, sems
):
    copies = start_field_copies(
        place_ref, a_hbm, b_hbm, o_ref.shape[1], weights, pool_weights, sems
    )
    fill_fields(g_ref, col_ref, fields)
    for copy in copies:
        copy.wait()
    field_products(pool_ref, crop_ref, o_ref, weights, pool_weights, fields, stack)


def own_kernel(
    place_ref,
    a_hbm,
    b_hbm,
    xt_hbm,
    g_ref,
    pool_ref,
    crop_ref,
    col_ref,
    pooled_ref,
    o_ref,
    w_out,
    weights,
    pool_weights,
    fields,
    stack,
    xt_ref,
    stage,
    sems,
    xt_sem,
    out_sems,
):
    copies = start_field_copies(
        place_ref, a_hbm, b_hbm, o_ref.shape[1], weights, pool_weights, sems
    )
    xt_copy = pltpu.make_async_copy(xt_hbm, xt_ref, xt_sem)
    xt_copy.start()
    fill_fields(g_ref, col_ref, fields)
    for copy in copies:
        copy.wait()
    field_products(pool_ref, crop_ref, o_ref, weights, pool_weights, fields, stack)
    xt_copy.wait()
    width = g_ref.shape[2]
    depth = xt_ref.shape[0]
    block = 1024
    waiting = [[], []]
    turn = 0
    for row_step, group in zip(PYRAMID_ROWS, ROW_GROUPS):
        r0, r1 = valid(row_step, FH)
        first = r0 * FW // 128 * 128
        last = min(POSITIONS, -(-r1 * FW // 128) * 128)
        base = PAD + first - row_step * FW
        sets = [group[at : at + 2] for at in range(0, 10, 2)] if row_step == 0 else [group]
        for chosen in sets:
            slot = turn % 2
            turn += 1
            for copy in waiting[slot]:
                copy.wait()
            right = jnp.concatenate(
                [fields[place, base : base + last - first] for tap, place in chosen], 1
            )

            def step(index, carry):
                rows = pl.ds(pl.multiple_of(index * block, 16), block)
                part = dot(xt_ref[rows, first:last], right)
                for offset in range(len(chosen)):
                    stage[slot, offset, rows] = part[
                        :, offset * width : (offset + 1) * width
                    ].astype(stage.dtype)
                return carry

            lax.fori_loop(0, depth // block, step, 0)
            waiting[slot] = [
                pltpu.make_async_copy(
                    stage.at[slot, offset], w_out.at[tap], out_sems.at[slot, offset]
                )
                for offset, (tap, place) in enumerate(chosen)
            ]
            for copy in waiting[slot]:
                copy.start()
    slot = turn % 2
    for copy in waiting[slot]:
        copy.wait()
    stage[slot, 0] = (pooled_ref[...] * pool_ref[...]).astype(stage.dtype)
    last_copy = pltpu.make_async_copy(stage.at[slot, 0], w_out.at[28], out_sems.at[slot, 0])
    last_copy.start()
    for copy in waiting[1 - slot]:
        copy.wait()
    last_copy.wait()


def own_gradients(place, weights, field_t, grads, pool_grad, crop, columns, pooled):
    depth, width = weights[0].shape[1:]
    hbm = pl.BlockSpec(memory_space=pltpu.HBM)
    half = depth // 2
    return pl.pallas_call(
        own_kernel,
        out_shape=[
            jax.ShapeDtypeStruct((POSITIONS, half), jnp.bfloat16),
            jax.ShapeDtypeStruct((29, depth, width), jnp.bfloat16),
        ],
        in_specs=[pl.BlockSpec(memory_space=pltpu.SMEM), hbm, hbm, hbm] + vmem(5),
        out_specs=[pl.BlockSpec(memory_space=pltpu.VMEM), hbm],
        scratch_shapes=[
            pltpu.VMEM((half, 28 * width), jnp.bfloat16),
            pltpu.VMEM((half, width), jnp.bfloat16),
            pltpu.VMEM((10, POSITIONS + 2 * PAD, width), jnp.bfloat16),
            pltpu.VMEM((8 * FW, 19 * width), jnp.bfloat16),
            pltpu.VMEM((depth, POSITIONS), jnp.bfloat16),
            pltpu.VMEM((2, 3, depth, width), jnp.bfloat16),
            pltpu.SemaphoreType.DMA((29,)),
            pltpu.SemaphoreType.DMA,
            pltpu.SemaphoreType.DMA((2, 3)),
        ],
        compiler_params=pltpu.CompilerParams(vmem_limit_bytes=60 << 20),
        cost_estimate=pl.CostEstimate(flops=1000, bytes_accessed=1024, transcendentals=0),
        name="own_gradients",
    )(place, weights[0], weights[1], field_t, grads, pool_grad, crop, columns, pooled)


def pyramid_field(place, depth, weights, grads, pool_grad, crop, columns):
    width = weights[0].shape[2]
    return pl.pallas_call(
        field_kernel,
        out_shape=jax.ShapeDtypeStruct((POSITIONS, depth), jnp.bfloat16),
        in_specs=[
            pl.BlockSpec(memory_space=pltpu.SMEM),
            pl.BlockSpec(memory_space=pltpu.HBM),
            pl.BlockSpec(memory_space=pltpu.HBM),
            pl.BlockSpec(memory_space=pltpu.VMEM),
            pl.BlockSpec(memory_space=pltpu.VMEM),
            pl.BlockSpec(memory_space=pltpu.VMEM),
            pl.BlockSpec(memory_space=pltpu.VMEM),
        ],
        out_specs=vmem(1)[0],
        scratch_shapes=[
            pltpu.VMEM((depth, 28 * width), jnp.bfloat16),
            pltpu.VMEM((depth, width), jnp.bfloat16),
            pltpu.VMEM((10, POSITIONS + 2 * PAD, width), jnp.bfloat16),
            pltpu.VMEM((8 * FW, 19 * width), jnp.bfloat16),
            pltpu.SemaphoreType.DMA((29,)),
        ],
        compiler_params=pltpu.CompilerParams(vmem_limit_bytes=60 << 20),
        cost_estimate=pl.CostEstimate(
            flops=1000, bytes_accessed=1024, transcendentals=0
        ),
        name="pyramid_field",
    )(place, weights[0], weights[1], grads, pool_grad, crop, columns)


BLOCK = 320


def block_rows(index):
    return pl.ds(pl.multiple_of(index * BLOCK, 16), BLOCK)


def gelu_slope(values, upstream):
    return jax.vjp(jax.nn.gelu, values)[1](upstream)[0]


def stem_kernel(p_ref, stem_ref, reduce_ref, crop_ref, mask_ref, xt_ref, a_ref, stat_ref, x_ref):
    def step(index, carry):
        rows = block_rows(index)
        low = (crop_ref[rows] * dot(p_ref[rows], stem_ref[...], (1, 1))).astype(x_ref.dtype)
        x_ref[rows] = low
        value = dot(low, reduce_ref[0])
        a_ref[rows] = value
        return (
            carry[0] + jnp.sum(value, 0, keepdims=True),
            carry[1] + jnp.sum(value * value, 0, keepdims=True),
        )

    zero = jnp.zeros((1, MID), jnp.float32)
    total, square = lax.fori_loop(0, POSITIONS // BLOCK, step, (zero, zero))
    for at in range(0, D, 256):
        xt_ref[at : at + 256] = x_ref[:, at : at + 256].T
    masks = mask_ref[...].astype(jnp.float32)
    lane = lax.broadcasted_iota(jnp.int32, (1, MID), 1)
    counts = jnp.zeros((1, MID), jnp.float32)
    for place in range(3):
        kept = masks[0:1] if place == 0 else masks[0:1] * masks[place : place + 1]
        counts = jnp.where(lane == place, jnp.sum(kept, 1, keepdims=True), counts)
    stat_ref[...] = jnp.concatenate([total, square, counts, jnp.zeros((5, MID), jnp.float32)], 0)


def stem_reduce(patches, stem, bottle, crop, masks):
    return pl.pallas_call(
        stem_kernel,
        grid=(1,),
        out_shape=[
            jax.ShapeDtypeStruct((D, POSITIONS), jnp.bfloat16),
            jax.ShapeDtypeStruct((POSITIONS, MID), jnp.float32),
            jax.ShapeDtypeStruct((8, MID), jnp.float32),
        ],
        in_specs=[
            pl.BlockSpec((POSITIONS, PATCH), lambda i: (0, 0)),
            pl.BlockSpec(stem.shape, lambda i: (0, 0)),
            pl.BlockSpec((1, D, MID), lambda i: (0, 0, 0)),
            pl.BlockSpec((POSITIONS, 1), lambda i: (0, 0)),
            pl.BlockSpec((3, POSITIONS), lambda i: (0, 0)),
        ],
        out_specs=[
            pl.BlockSpec((D, POSITIONS), lambda i: (0, 0)),
            pl.BlockSpec((POSITIONS, MID), lambda i: (0, 0)),
            pl.BlockSpec((8, MID), lambda i: (0, 0)),
        ],
        scratch_shapes=[pltpu.VMEM((POSITIONS, D), jnp.bfloat16)],
        compiler_params=pltpu.CompilerParams(vmem_limit_bytes=50 << 20),
        cost_estimate=pl.CostEstimate(flops=5 * 10**9, bytes_accessed=14 << 20, transcendentals=0),
        name="stem_reduce",
    )(patches, stem, bottle, crop, masks)


def both_halves(gain_refs, first, last):
    place_ref, own_ref, other_ref = gain_refs
    own, other = own_ref[:, first:last], other_ref[:, first:last]
    lower = place_ref[0] == 0
    return jnp.concatenate([jnp.where(lower, own, other), jnp.where(lower, other, own)], 1)


def norm_rows(stat, count):
    mean = stat[0:1] / count
    return mean, lax.rsqrt(stat[1:2] / count - mean * mean + norm_eps)


def norm_middle_kernel(
    a_ref, stat_ref, place_ref, own_ref, other_ref, crop_ref, w_ref, col_ref, h_ref, ht_ref, o_ref, canvas
):
    edge = 4 * FW
    mean, scale = norm_rows(stat_ref[...], stat_ref[2:3, 0:1])
    pair = both_halves((place_ref, own_ref, other_ref), 0, MID // 2)
    gain = pair[0:1] * scale
    shift = pair[1:2] - mean * gain
    low = (crop_ref[...] * jax.nn.gelu(a_ref[...] * gain + shift)).astype(h_ref.dtype)
    h_ref[...] = low
    ht_ref[...] = low.T
    values = low.astype(jnp.float32)
    for turn in range(3):
        canvas[turn, :edge] = jnp.zeros((edge, MID), canvas.dtype)
        canvas[turn, POSITIONS + edge :] = jnp.zeros((edge, MID), canvas.dtype)
        canvas[turn, edge : POSITIONS + edge] = roll_cols(values, col_ref, 4 * (turn - 1)).astype(
            canvas.dtype
        )
    block = 400

    def step(index, carry):
        total = None
        for row in range(3):
            first = pl.multiple_of(index * block + edge * row, 16)
            for turn in range(3):
                part = dot(canvas[turn, pl.ds(first, block)], w_ref[3 * row + turn])
                total = part if total is None else total + part
        o_ref[pl.ds(pl.multiple_of(index * block, 16), block)] = total.astype(o_ref.dtype)
        return carry

    lax.fori_loop(0, POSITIONS // block, step, 0)


def norm_middle(first_pre, stat, gains, crop, weights, columns):
    return pl.pallas_call(
        norm_middle_kernel,
        out_shape=[
            jax.ShapeDtypeStruct((POSITIONS, MID), jnp.bfloat16),
            jax.ShapeDtypeStruct((MID, POSITIONS), jnp.bfloat16),
            jax.ShapeDtypeStruct((POSITIONS, MID), jnp.bfloat16),
        ],
        in_specs=vmem(2) + [pl.BlockSpec(memory_space=pltpu.SMEM)] + vmem(5),
        out_specs=vmem(3),
        scratch_shapes=[pltpu.VMEM((3, POSITIONS + 8 * FW, MID), jnp.bfloat16)],
        compiler_params=pltpu.CompilerParams(vmem_limit_bytes=50 << 20),
        cost_estimate=pl.CostEstimate(flops=8 * 10**9, bytes_accessed=14 << 20, transcendentals=0),
        name="norm_middle",
    )(first_pre, stat, *gains, crop, weights, columns)


def expand_kernel(a_ref, w_ref, crop_ref, y_ref, stat_ref):
    def step(index, carry):
        rows = block_rows(index)
        value = dot(a_ref[rows], w_ref[0], (1, 1))
        y_ref[rows] = value.astype(y_ref.dtype)
        kept = crop_ref[rows] * value
        return (
            carry[0] + jnp.sum(kept, 0, keepdims=True),
            carry[1] + jnp.sum(kept * value, 0, keepdims=True),
        )

    zero = jnp.zeros((1, D), jnp.float32)
    sums = lax.fori_loop(0, POSITIONS // BLOCK, step, (zero, zero))
    for turn, values in enumerate(sums):
        for part in range(4):
            stat_ref[4 * turn + part : 4 * turn + part + 1] = values[
                :, part * MID : (part + 1) * MID
            ]


def expand_forward(second, bottle, crop):
    return pl.pallas_call(
        expand_kernel,
        grid=(1,),
        out_shape=[
            jax.ShapeDtypeStruct((POSITIONS, D), jnp.bfloat16),
            jax.ShapeDtypeStruct((8, MID), jnp.float32),
        ],
        in_specs=[
            pl.BlockSpec((POSITIONS, MID), lambda i: (0, 0)),
            pl.BlockSpec((1, D, MID), lambda i: (1, 0, 0)),
            pl.BlockSpec((POSITIONS, 1), lambda i: (0, 0)),
        ],
        out_specs=[
            pl.BlockSpec((POSITIONS, D), lambda i: (0, 0)),
            pl.BlockSpec((8, MID), lambda i: (0, 0)),
        ],
        compiler_params=pltpu.CompilerParams(vmem_limit_bytes=50 << 20),
        cost_estimate=pl.CostEstimate(flops=4 * 10**9, bytes_accessed=12 << 20, transcendentals=0),
        name="expand_forward",
    )(second, bottle, crop)


def residual_kernel(
    p_ref, stem_ref, y_ref, stat_ref, count_ref, place_ref, own_ref, other_ref, crop_ref, x_ref, xt_ref, pool_ref
):
    count = count_ref[2:3, 0:1]
    stat = stat_ref[...]
    total = jnp.concatenate([stat[part : part + 1] for part in range(4)], 1)
    square = jnp.concatenate([stat[part : part + 1] for part in range(4, 8)], 1)
    mean = total / count
    pair = both_halves((place_ref, own_ref, other_ref), MID // 2, MID // 2 + D // 2)
    gain = pair[0:1] * lax.rsqrt(square / count - mean * mean + norm_eps)
    shift = pair[1:2] - mean * gain

    def residual(index, carry):
        rows = block_rows(index)
        value = dot(p_ref[rows], stem_ref[...], (1, 1)) + (
            y_ref[rows].astype(jnp.float32) * gain + shift
        )
        low = (crop_ref[rows] * value).astype(x_ref.dtype)
        x_ref[rows] = low
        return carry + jnp.sum(low.astype(jnp.float32), 0, keepdims=True)

    pooled = lax.fori_loop(0, POSITIONS // BLOCK, residual, jnp.zeros((1, D), jnp.float32))
    pooled = (pooled / jnp.sum(crop_ref[...], keepdims=True)).astype(jnp.bfloat16)
    pool_ref[...] = pooled.astype(jnp.float32)
    for at in range(0, D, 256):
        xt_ref[at : at + 256] = x_ref[:, at : at + 256].T


def residual_stream(patches, stem, expanded, stat, counts, gains, crop):
    low = jnp.bfloat16
    return pl.pallas_call(
        residual_kernel,
        out_shape=[
            jax.ShapeDtypeStruct((POSITIONS, D), low),
            jax.ShapeDtypeStruct((D, POSITIONS), low),
            jax.ShapeDtypeStruct((1, D), jnp.float32),
        ],
        in_specs=vmem(5) + [pl.BlockSpec(memory_space=pltpu.SMEM)] + vmem(3),
        out_specs=vmem(3),
        compiler_params=pltpu.CompilerParams(vmem_limit_bytes=50 << 20),
        cost_estimate=pl.CostEstimate(flops=2 * 10**9, bytes_accessed=22 << 20, transcendentals=0),
        name="residual_stream",
    )(patches, stem, expanded, stat, counts, *gains, crop)


def pyramid_kernel(
    x_ref,
    pool_ref,
    a_hbm,
    b_hbm,
    project_ref,
    col_ref,
    o_ref,
    pool_pre_ref,
    cat_ref,
    part_ref,
    weights,
    pool_weights,
    fields,
    sems,
):
    width = o_ref.shape[2]
    copies = []
    order = [3, 2, 4, 1, 5, 0, 6]
    starts = []
    place = 0
    for group in ROW_GROUPS:
        starts.append(place)
        place += len(group)
    for turn in order:
        group_copies = []
        for offset, (tap, _) in enumerate(ROW_GROUPS[turn]):
            slot = starts[turn] + offset
            copy = pltpu.make_async_copy(
                tap_of(a_hbm, b_hbm, tap), weights.at[:, pl.ds(slot * width, width)], sems.at[slot]
            )
            copy.start()
            group_copies.append(copy)
        copies.append(group_copies)
    pool_copy = pltpu.make_async_copy(tap_of(a_hbm, b_hbm, 28), pool_weights, sems.at[28])
    pool_copy.start()

    for turn, group_copies in zip(order, copies):
        for copy in group_copies:
            copy.wait()
        row_step = PYRAMID_ROWS[turn]
        group = ROW_GROUPS[turn]
        r0, r1 = valid(row_step, FH)
        length = (r1 - r0) * FW
        block = {1600: 800, 1120: 560, 640: 640, 160: 160}[length]
        cols = pl.ds(starts[turn] * width, len(group) * width)

        def step(index, carry):
            source = pl.multiple_of(index * block + r0 * FW, 16)
            target = pl.multiple_of(index * block + (r0 - row_step) * FW, 16)
            part = dot(x_ref[pl.ds(source, block)], weights[:, cols])
            for offset, (tap, field) in enumerate(group):
                piece = part[:, offset * width : (offset + 1) * width]
                rows = pl.ds(target, block)
                if row_step == 0:
                    fields[field, rows] = piece
                else:
                    fields[field, rows] += piece
            return carry

        lax.fori_loop(0, length // block, step, 0)
    pool_copy.wait()
    pool_pre = dot(jnp.broadcast_to(pool_ref[...], (16, D)).astype(jnp.bfloat16), pool_weights[...])[0:1]
    pool_pre_ref[...] = pool_pre
    for branch in range(4):
        values = fields[0] if branch == 0 else fields[3 * branch - 1]
        if branch:
            for turn in (0, 2):
                place = 3 * branch - 2 + turn
                values = values + roll_cols(fields[place], col_ref, FIELDS[place][1])
        o_ref[branch] = values
        cat_ref[:, branch * width : (branch + 1) * width] = jax.nn.gelu(values).astype(
            cat_ref.dtype
        )
    cat_ref[:, 4 * width :] = jnp.broadcast_to(
        jax.nn.gelu(pool_pre).astype(cat_ref.dtype), (POSITIONS, width)
    )

    def project(index, carry):
        rows = block_rows(index)
        part_ref[rows] = dot(cat_ref[rows], project_ref[:, : 5 * width], (1, 1)).astype(part_ref.dtype)
        return carry

    lax.fori_loop(0, POSITIONS // BLOCK, project, 0)


def pyramid_forward(field, pooled, weights, project, columns):
    depth, width = weights[0].shape[1:]
    low = jnp.bfloat16
    return pl.pallas_call(
        pyramid_kernel,
        out_shape=[
            jax.ShapeDtypeStruct((4, POSITIONS, width), jnp.float32),
            jax.ShapeDtypeStruct((1, width), jnp.float32),
            jax.ShapeDtypeStruct((POSITIONS, 5 * width), low),
            jax.ShapeDtypeStruct((POSITIONS, BRANCH), low),
        ],
        in_specs=vmem(2) + [pl.BlockSpec(memory_space=pltpu.HBM)] * 2 + vmem(2),
        out_specs=vmem(4),
        scratch_shapes=[
            pltpu.VMEM((depth, 28 * width), low),
            pltpu.VMEM((depth, width), low),
            pltpu.VMEM((10, POSITIONS, width), jnp.float32),
            pltpu.SemaphoreType.DMA((29,)),
        ],
        compiler_params=pltpu.CompilerParams(vmem_limit_bytes=60 << 20),
        cost_estimate=pl.CostEstimate(
            flops=2 * POSITIONS * 19 * depth * width, bytes_accessed=40 << 20, transcendentals=0
        ),
        name="pyramid_fwd",
    )(field, pooled, weights[0], weights[1], project, columns)


def head_kernel(
    own_ref,
    other_ref,
    row_ref,
    label_ref,
    target_ref,
    mask_ref,
    project_ref,
    z_ref,
    pool_pre_ref,
    feature_ref,
    logit_ref,
    mixed_ref,
    grad_ref,
    pool_ref,
    stat_ref,
):
    width = grad_ref.shape[2]
    bias, scale = row_ref[0:1], row_ref[1:2]
    class_lane, depth_lane = row_ref[2:3], row_ref[4:5]

    def step(index, carry):
        rows = block_rows(index)
        mixed = own_ref[rows].astype(jnp.float32) + other_ref[rows].astype(jnp.float32)
        feature = jax.nn.gelu(mixed).astype(feature_ref.dtype)
        feature_ref[rows] = feature
        logits = dot(feature, project_ref[:, 5 * width :]) + bias
        is_class = class_lane > 0.0
        top = jnp.max(jnp.where(is_class, logits, -jnp.inf), 1, keepdims=True)
        powers = jnp.where(is_class, jnp.exp(jnp.where(is_class, logits - top, 0.0)), 0.0)
        total = jnp.sum(powers, 1, keepdims=True)
        onehot = label_ref[rows]
        mask = mask_ref[rows]
        seg = mask[:, 0:1] * (
            top + jnp.log(total) - jnp.sum(logits * onehot, 1, keepdims=True)
        )
        is_depth = depth_lane > 0.0
        inverse = jnp.exp(-jnp.abs(logits))
        soft = jnp.maximum(logits, 0.0) + jnp.log(1.0 + inverse)
        slope = jnp.where(logits >= 0.0, 1.0, inverse) / (1.0 + inverse)
        error = jnp.where(is_depth, soft, logits) - target_ref[rows]
        root = jnp.sqrt(error * error + 1.0)
        other = error / root * jnp.where(is_depth, slope, 1.0)
        grad = scale * mask * jnp.where(is_class, powers / total - onehot, other)
        low = grad.astype(logit_ref.dtype)
        logit_ref[rows] = low
        up = gelu_slope(mixed, dot(low, project_ref[:, 5 * width :], (1, 1))).astype(mixed_ref.dtype)
        mixed_ref[rows] = up
        cat = dot(up, project_ref[:, : 5 * width])
        for branch in range(4):
            grad_ref[branch, rows] = gelu_slope(
                z_ref[branch, rows], cat[:, branch * width : (branch + 1) * width]
            ).astype(grad_ref.dtype)
        return (
            carry[0] + jnp.sum(low.astype(jnp.float32), 0, keepdims=True),
            carry[1] + jnp.sum(mask * (root - 1.0), 0, keepdims=True),
            carry[2] + jnp.sum(seg, 0, keepdims=True),
            carry[3] + jnp.sum(cat[:, 4 * width :], 0, keepdims=True),
        )

    zero = jnp.zeros((1, 128), jnp.float32)
    bias_sum, error_sum, seg_sum, pool_sum = lax.fori_loop(
        0,
        POSITIONS // BLOCK,
        step,
        (zero, zero, jnp.zeros((1, 1), jnp.float32), jnp.zeros((1, width), jnp.float32)),
    )
    pool_ref[...] = gelu_slope(pool_pre_ref[...], pool_sum).astype(jnp.bfloat16).astype(jnp.float32)
    stat_ref[...] = jnp.concatenate(
        [bias_sum, error_sum, jnp.broadcast_to(seg_sum, (1, 128)), jnp.zeros((5, 128))], 0
    )


def head_step(own, other, rows, label, target, mask, project, branches, pool_pre):
    width = branches.shape[2]
    low = jnp.bfloat16
    return pl.pallas_call(
        head_kernel,
        out_shape=[
            jax.ShapeDtypeStruct((POSITIONS, BRANCH), low),
            jax.ShapeDtypeStruct((POSITIONS, 128), low),
            jax.ShapeDtypeStruct((POSITIONS, BRANCH), low),
            jax.ShapeDtypeStruct((4, POSITIONS, width), low),
            jax.ShapeDtypeStruct((1, width), jnp.float32),
            jax.ShapeDtypeStruct((8, 128), jnp.float32),
        ],
        in_specs=vmem(9),
        out_specs=vmem(6),
        compiler_params=pltpu.CompilerParams(vmem_limit_bytes=50 << 20),
        cost_estimate=pl.CostEstimate(flops=2 * 10**9, bytes_accessed=16 << 20, transcendentals=0),
        name="head_step",
    )(own, other, rows, label, target, mask, project, branches, pool_pre)


def own_rows(stat, place_ref, first):
    lower = place_ref[0] == 0
    return jnp.concatenate(
        [
            jnp.where(lower, stat[first + part : first + part + 1], stat[first + 2 + part : first + 3 + part])
            for part in range(2)
        ],
        1,
    )


def own_norm(place_ref, stat_ref, count_ref):
    stat = stat_ref[...]
    count = count_ref[2:3, 0:1]
    mean = own_rows(stat, place_ref, 0) / count
    return mean, lax.rsqrt(own_rows(stat, place_ref, 4) / count - mean * mean + norm_eps), count


def start_rows(place_ref, sources, targets, sems):
    depth = targets[0].shape[1]
    half = pl.ds(pl.multiple_of(place_ref[0] * depth, 128), depth)
    own_hbm, first_hbm, second_hbm, y_hbm = sources
    own_ref, other_ref, y_ref = targets
    blocks = []
    for index in range(POSITIONS // BLOCK):
        rows = pl.ds(index * BLOCK, BLOCK)
        pairs = (
            (own_hbm.at[rows], own_ref.at[rows]),
            (first_hbm.at[rows], other_ref.at[rows, : depth // 2]),
            (second_hbm.at[rows], other_ref.at[rows, depth // 2 :]),
            (y_hbm.at[rows, half], y_ref.at[rows]),
        )
        copies = [
            pltpu.make_async_copy(source, target, sems.at[index, at])
            for at, (source, target) in enumerate(pairs)
        ]
        for copy in copies:
            copy.start()
        blocks.append(copies)
    return blocks


def residual_sums_kernel(
    place_ref,
    own_hbm,
    first_hbm,
    second_hbm,
    y_hbm,
    stat_ref,
    count_ref,
    crop_ref,
    head_ref,
    o_ref,
    own_ref,
    other_ref,
    y_ref,
    sems,
):
    depth = own_ref.shape[1]
    blocks = start_rows(
        place_ref, (own_hbm, first_hbm, second_hbm, y_hbm), (own_ref, other_ref, y_ref), sems
    )
    mean, scale, count = own_norm(place_ref, stat_ref, count_ref)
    sums = [jnp.zeros((1, depth), jnp.float32)] * 2
    for index, copies in enumerate(blocks):
        for copy in copies:
            copy.wait()
        rows = slice(index * BLOCK, (index + 1) * BLOCK)
        up = crop_ref[rows] * (
            own_ref[rows].astype(jnp.float32) + other_ref[rows].astype(jnp.float32)
        )
        normed = (y_ref[rows].astype(jnp.float32) - mean) * scale
        sums[0] = sums[0] + jnp.sum(up * normed, 0, keepdims=True)
        sums[1] = sums[1] + jnp.sum(up, 0, keepdims=True)
    for turn, values in enumerate(sums):
        for part in range(2):
            row = 2 * turn + part
            o_ref[row : row + 1] = values[:, part * MID : (part + 1) * MID]
    o_ref[4:5] = jnp.concatenate(
        [head_ref[0:1], head_ref[1:2], head_ref[2:3], jnp.zeros((1, 128), jnp.float32)], 1
    )
    o_ref[5:8] = jnp.zeros((3, MID), jnp.float32)


def residual_sums(place, own, other, expanded, stat, counts, crop, head_stat):
    hbm = pl.BlockSpec(memory_space=pltpu.HBM)
    return pl.pallas_call(
        residual_sums_kernel,
        out_shape=jax.ShapeDtypeStruct((8, MID), jnp.float32),
        in_specs=[pl.BlockSpec(memory_space=pltpu.SMEM)] + [hbm] * 4 + vmem(4),
        out_specs=vmem(1)[0],
        scratch_shapes=[pltpu.VMEM(own.shape, jnp.bfloat16)] * 3
        + [pltpu.SemaphoreType.DMA((POSITIONS // BLOCK, 4))],
        compiler_params=pltpu.CompilerParams(vmem_limit_bytes=60 << 20),
        cost_estimate=pl.CostEstimate(flops=10**8, bytes_accessed=12 << 20, transcendentals=0),
        name="residual_sums",
    )(place, own, *other, expanded, stat, counts, crop, head_stat)


def residual_back_kernel(
    place_ref,
    own_hbm,
    first_hbm,
    second_hbm,
    y_hbm,
    stat_ref,
    count_ref,
    sum_ref,
    gain_ref,
    crop_ref,
    bottle_hbm,
    o_ref,
    part_ref,
    own_ref,
    other_ref,
    y_ref,
    weights,
    sems,
    weight_sem,
):
    depth = own_ref.shape[1]
    half = pl.ds(pl.multiple_of(place_ref[0] * depth, 16), depth)
    weight_copy = pltpu.make_async_copy(bottle_hbm.at[1, half], weights, weight_sem)
    weight_copy.start()
    blocks = start_rows(
        place_ref, (own_hbm, first_hbm, second_hbm, y_hbm), (own_ref, other_ref, y_ref), sems
    )
    mean, scale, count = own_norm(place_ref, stat_ref, count_ref)
    sums = sum_ref[...]
    gain_grad = jnp.concatenate([sums[0:1], sums[1:2]], 1) / count
    shift_grad = jnp.concatenate([sums[2:3], sums[3:4]], 1) / count
    factor = gain_ref[0:1, MID // 2 :] * scale
    weight_copy.wait()
    for index, copies in enumerate(blocks):
        for copy in copies:
            copy.wait()
        rows = slice(index * BLOCK, (index + 1) * BLOCK)
        crop = crop_ref[rows]
        up = crop * (own_ref[rows].astype(jnp.float32) + other_ref[rows].astype(jnp.float32))
        normed = (y_ref[rows].astype(jnp.float32) - mean) * scale
        low = (crop * factor * (up - (shift_grad + normed * gain_grad))).astype(o_ref.dtype)
        o_ref[rows] = low
        part_ref[rows] = dot(low, weights[...]).astype(part_ref.dtype)


def residual_back(place, own, other, expanded, stat, counts, sums, gains, crop, bottle):
    hbm = pl.BlockSpec(memory_space=pltpu.HBM)
    depth = own.shape[1]
    return pl.pallas_call(
        residual_back_kernel,
        out_shape=[
            jax.ShapeDtypeStruct((POSITIONS, depth), jnp.bfloat16),
            jax.ShapeDtypeStruct((POSITIONS, MID), jnp.bfloat16),
        ],
        in_specs=[pl.BlockSpec(memory_space=pltpu.SMEM)] + [hbm] * 4 + vmem(5) + [hbm],
        out_specs=vmem(2),
        scratch_shapes=[pltpu.VMEM(own.shape, jnp.bfloat16)] * 3
        + [
            pltpu.VMEM((depth, MID), jnp.bfloat16),
            pltpu.SemaphoreType.DMA((POSITIONS // BLOCK, 4)),
            pltpu.SemaphoreType.DMA,
        ],
        compiler_params=pltpu.CompilerParams(vmem_limit_bytes=60 << 20),
        cost_estimate=pl.CostEstimate(flops=2 * 10**9, bytes_accessed=16 << 20, transcendentals=0),
        name="residual_back",
    )(place, own, *other, expanded, stat, counts, sums, gains, crop, bottle)


def late_kernel(
    place_ref,
    up_ref,
    a_ref,
    stat_ref,
    sum_ref,
    gain_ref,
    other_gain_ref,
    crop_ref,
    patch_ref,
    bottle_hbm,
    own_hbm,
    first_hbm,
    second_hbm,
    xt_hbm,
    reduce_ref,
    stem_ref,
    weights,
    own_ref,
    other_ref,
    xt_ref,
    low_ref,
    start_ref,
    sems,
):
    depth = own_ref.shape[1]
    half = pl.ds(pl.multiple_of(place_ref[0] * depth, 16), depth)
    copies = [
        pltpu.make_async_copy(source, target, sems.at[at])
        for at, (source, target) in enumerate(
            (
                (bottle_hbm.at[0, half], weights),
                (own_hbm, own_ref),
                (first_hbm, other_ref.at[:, : depth // 2]),
                (second_hbm, other_ref.at[:, depth // 2 :]),
                (xt_hbm, xt_ref),
            )
        )
    ]
    for copy in copies:
        copy.start()
    count = stat_ref[2:3, 0:1]
    mean, scale = norm_rows(stat_ref[...], count)
    pair = both_halves((place_ref, gain_ref, other_gain_ref), 0, MID // 2)
    factor = pair[0:1] * scale
    gain_grad = sum_ref[0:1] / count
    shift_grad = sum_ref[1:2] / count

    def step(index, carry):
        rows = block_rows(index)
        normed = (a_ref[rows] - mean) * scale
        low_ref[rows] = (
            crop_ref[rows] * factor * (up_ref[rows] - (shift_grad + normed * gain_grad))
        ).astype(low_ref.dtype)
        return carry

    lax.fori_loop(0, POSITIONS // BLOCK, step, 0)
    for copy in copies[:4]:
        copy.wait()

    def start_step(index, carry):
        rows = block_rows(index)
        total = dot(low_ref[rows], weights[...], (1, 1)) + (
            own_ref[rows].astype(jnp.float32) + other_ref[rows].astype(jnp.float32)
        )
        start_ref[rows] = (crop_ref[rows] * total).astype(start_ref.dtype)
        return carry

    lax.fori_loop(0, POSITIONS // BLOCK, start_step, 0)
    for at in range(0, depth, 256):
        part = dot(patch_ref[...], start_ref[:, at : at + 256]).astype(stem_ref.dtype)
        stem_ref[at : at + 256] = part.T
    copies[4].wait()
    low = low_ref[...]
    own_low = jnp.where(place_ref[0] == 0, low[:, : MID // 2], low[:, MID // 2 :])
    block = 512

    def reduce_step(index, carry):
        rows = pl.ds(pl.multiple_of(index * block, 16), block)
        reduce_ref[rows] = dot(xt_ref[rows], own_low).astype(reduce_ref.dtype)
        return carry

    lax.fori_loop(0, D // block, reduce_step, 0)


def late_gradients(place, up, first_pre, stat, sums, gains, crop, patches_t, bottle, own, other, xt):
    hbm = pl.BlockSpec(memory_space=pltpu.HBM)
    depth = own.shape[1]
    low = jnp.bfloat16
    return pl.pallas_call(
        late_kernel,
        out_shape=[
            jax.ShapeDtypeStruct((D, MID // 2), low),
            jax.ShapeDtypeStruct((depth, PATCH), low),
        ],
        in_specs=[pl.BlockSpec(memory_space=pltpu.SMEM)] + vmem(8) + [hbm] * 5,
        out_specs=vmem(2),
        scratch_shapes=[
            pltpu.VMEM((depth, MID), low),
            pltpu.VMEM(own.shape, low),
            pltpu.VMEM(own.shape, low),
            pltpu.VMEM(xt.shape, low),
            pltpu.VMEM((POSITIONS, MID), low),
            pltpu.VMEM(own.shape, low),
            pltpu.SemaphoreType.DMA((5,)),
        ],
        compiler_params=pltpu.CompilerParams(vmem_limit_bytes=60 << 20),
        cost_estimate=pl.CostEstimate(flops=4 * 10**9, bytes_accessed=24 << 20, transcendentals=0),
        name="late_gradients",
    )(place, up, first_pre, stat, sums, gains[1], gains[2], crop, patches_t, bottle, own, *other, xt)


def scatter_kernel(
    layers,
    p_ref,
    o_ref,
    square_ref,
    core_in,
    y_out,
    kept,
    y_in,
    z_out,
    z_in,
    core_send,
    core_recv,
    y_send,
    y_recv,
    z_send,
    z_recv,
):
    z, y, core, x = place_of()
    barrier = pltpu.get_barrier_semaphore()
    sibling = device_at(z, y, 1 - core, x)
    other_y = device_at(z, 1 - y, core, x)
    layer_order = [z_flip(z, turn) for turn in range(1, layers)]
    for target in [sibling, other_y] + [device_at(zz, y, core, x) for zz in layer_order]:
        pl.semaphore_signal(barrier, inc=1, device_id=target, device_id_type=MESH_ID)
    pl.semaphore_wait(barrier, layers + 1)
    order = layer_order + [z]
    pending = []

    def send(source, target_ref, sems, place, device):
        copy = pltpu.make_async_remote_copy(
            src_ref=source,
            dst_ref=target_ref,
            send_sem=sems[0].at[place],
            recv_sem=sems[1].at[place],
            device_id=device,
            device_id_type=MESH_ID,
        )
        copy.start()
        pending.append(copy)

    def arrive(target_ref, sems, place):
        pltpu.make_async_remote_copy(
            src_ref=target_ref,
            dst_ref=target_ref,
            send_sem=sems[0].at[place],
            recv_sem=sems[1].at[place],
            device_id=sibling,
            device_id_type=MESH_ID,
        ).wait_recv()

    core_sems, y_sems, z_sems = (core_send, core_recv), (y_send, y_recv), (z_send, z_recv)
    for zz in order:
        for yy in (1 - y, y):
            pair = zz * 2 + yy
            send(p_ref.at[pair * 2 + 1 - core], core_in.at[pair], core_sems, pair, sibling)
    for zz in order:
        for yy in (1 - y, y):
            pair = zz * 2 + yy
            arrive(core_in.at[pair], core_sems, pair)
            total = p_ref[pair * 2 + core].astype(jnp.float32) + core_in[pair].astype(jnp.float32)
            if yy is y:
                kept[zz] = total
            else:
                y_out[zz] = total.astype(y_out.dtype)
                send(y_out.at[zz], y_in.at[zz], y_sems, zz, other_y)
    for zz in order:
        arrive(y_in.at[zz], y_sems, zz)
        total = kept[zz] + y_in[zz].astype(jnp.float32)
        if zz is z:
            o_ref[...] = total
        else:
            z_out[zz] = total.astype(z_out.dtype)
            copy = pltpu.make_async_remote_copy(
                src_ref=z_out.at[zz],
                dst_ref=z_in.at[z],
                send_sem=z_send.at[zz],
                recv_sem=z_recv.at[z],
                device_id=device_at(zz, y, core, x),
                device_id_type=MESH_ID,
            )
            copy.start()
            pending.append(copy)
    for zz in layer_order:
        arrive(z_in.at[zz], z_sems, zz)
        o_ref[...] += z_in[zz].astype(jnp.float32)
    rows = o_ref.shape[0] - 48
    values = o_ref[:rows]
    small = o_ref[rows:]
    row = lax.broadcasted_iota(jnp.int32, (48, 256), 0)
    lane = lax.broadcasted_iota(jnp.int32, (48, 256), 1)
    is_head = jnp.logical_and(row % 3 == 2, lane >= 128)
    small = jnp.where(jnp.logical_and(is_head, x != 0), 0.0, small)
    squares = jnp.sum(values * values, 0, keepdims=True) + jnp.sum(small * small, 0, keepdims=True)
    square_ref[...] = jnp.concatenate(
        [squares[:, :128] + squares[:, 128:], jnp.zeros((7, 128), jnp.float32)], 0
    )
    for copy in pending:
        copy.wait_send()


def scatter_trunk(sizes, grads):
    count, rows = grads.shape[:2]
    if count != 16:
        summed = lax.psum_scatter(grads, "dp", scatter_dimension=0, tiled=True)[0]
        summed = summed.astype(jnp.float32)
        flat = jnp.square(summed).reshape(-1)
        small = 3 * 256 * (BRANCH // count)
        place = lax.rem(lax.broadcasted_iota(jnp.int32, (small,), 0), 768)
        keep = jnp.logical_or(place < 640, lax.axis_index("chan") == 0)
        total = jnp.sum(flat[:-small]) + jnp.sum(jnp.where(keep, flat[-small:], 0.0))
        return summed, jnp.pad(total.reshape(1, 1), ((0, 7), (0, 127)))
    layers = count // 4
    low = jnp.bfloat16
    return pl.pallas_call(
        functools.partial(scatter_kernel, layers),
        out_shape=[
            jax.ShapeDtypeStruct((rows, 256), jnp.float32),
            jax.ShapeDtypeStruct((8, 128), jnp.float32),
        ],
        in_specs=vmem(1),
        out_specs=vmem(2),
        scratch_shapes=[
            pltpu.VMEM((count // 2, rows, 256), low),
            pltpu.VMEM((layers, rows, 256), low),
            pltpu.VMEM((layers, rows, 256), jnp.float32),
            pltpu.VMEM((layers, rows, 256), low),
            pltpu.VMEM((layers, rows, 256), low),
            pltpu.VMEM((layers, rows, 256), low),
            pltpu.SemaphoreType.DMA((count // 2,)),
            pltpu.SemaphoreType.DMA((count // 2,)),
            pltpu.SemaphoreType.DMA((layers,)),
            pltpu.SemaphoreType.DMA((layers,)),
            pltpu.SemaphoreType.DMA((layers,)),
            pltpu.SemaphoreType.DMA((layers,)),
        ],
        compiler_params=pltpu.CompilerParams(
            collective_id=6, has_side_effects=True, vmem_limit_bytes=48 << 20
        ),
        name="scatter_trunk",
    )(grads)


def first_back_kernel(
    place_ref,
    part_ref,
    other_ref,
    w_ref,
    col_ref,
    a_ref,
    stat_ref,
    own_ref,
    gain_ref,
    crop_ref,
    up_ref,
    g_ref,
    o_ref,
    canvas,
):
    edge = 4 * FW
    values = part_ref[...].astype(jnp.float32) + other_ref[...].astype(jnp.float32)
    low = values.astype(jnp.bfloat16)
    g_ref[...] = jnp.where(place_ref[0] == 0, low[:, : MID // 2], low[:, MID // 2 :])
    values = low.astype(jnp.float32)
    for turn in range(3):
        canvas[turn, :edge] = jnp.zeros((edge, MID), canvas.dtype)
        canvas[turn, POSITIONS + edge :] = jnp.zeros((edge, MID), canvas.dtype)
        canvas[turn, edge : POSITIONS + edge] = roll_cols(values, col_ref, -4 * (turn - 1)).astype(
            canvas.dtype
        )
    mean, scale = norm_rows(stat_ref[...], stat_ref[2:3, 0:1])
    pair = both_halves((place_ref, own_ref, gain_ref), 0, MID // 2)
    block = 400

    def step(index, carry):
        total = None
        for row in range(3):
            first = pl.multiple_of(index * block + edge * (2 - row), 16)
            for turn in range(3):
                part = dot(canvas[turn, pl.ds(first, block)], w_ref[3 * row + turn], (1, 1))
                total = part if total is None else total + part
        rows = pl.ds(pl.multiple_of(index * block, 16), block)
        normed = (a_ref[rows] - mean) * scale
        up = gelu_slope(pair[0:1] * normed + pair[1:2], crop_ref[rows] * total)
        up_ref[rows] = up
        return (
            carry[0] + jnp.sum(up * normed, 0, keepdims=True),
            carry[1] + jnp.sum(up, 0, keepdims=True),
        )

    zero = jnp.zeros((1, MID), jnp.float32)
    sums = lax.fori_loop(0, POSITIONS // block, step, (zero, zero))
    o_ref[...] = jnp.concatenate([sums[0], sums[1], jnp.zeros((6, MID), jnp.float32)], 0)


def first_back(place, part, other, weights, columns, first_pre, stat, gains, crop):
    return pl.pallas_call(
        first_back_kernel,
        out_shape=[
            jax.ShapeDtypeStruct((POSITIONS, MID), jnp.float32),
            jax.ShapeDtypeStruct((POSITIONS, MID // 2), jnp.bfloat16),
            jax.ShapeDtypeStruct((8, MID), jnp.float32),
        ],
        in_specs=[pl.BlockSpec(memory_space=pltpu.SMEM)] + vmem(9),
        out_specs=vmem(3),
        scratch_shapes=[pltpu.VMEM((3, POSITIONS + 8 * FW, MID), jnp.bfloat16)],
        compiler_params=pltpu.CompilerParams(vmem_limit_bytes=50 << 20),
        cost_estimate=pl.CostEstimate(flops=8 * 10**9, bytes_accessed=20 << 20, transcendentals=0),
        name="first_back",
    )(place, part, other, weights, columns, first_pre, stat, gains[1], gains[2], crop)


ADAM_GROUPS = 8


def adam_kernel(row_share, mid_share, *refs):
    sum_ref, pyramid_ref, trunk_ref, stem_ref, small_ref, norm_ref, task_ref = refs[:7]
    states = [refs[7 + 3 * group : 10 + 3 * group] for group in range(ADAM_GROUPS)]
    base = 7 + 3 * ADAM_GROUPS
    outs = [refs[base + 3 * group : base + 3 + 3 * group] for group in range(ADAM_GROUPS)]
    norm = jnp.sqrt(jnp.sum(sum_ref[0:1], 1, keepdims=True))
    factor = clip_level / jnp.maximum(norm, clip_level)

    def update(group, at, gradient, rate, decay):
        values = [ref[at] for ref in states[group]]
        for ref, value in zip(outs[group], adam_step(*values, gradient, factor, rate, decay)):
            ref[at] = value

    def pyramid_step(tap, carry):
        update(0, tap, pyramid_ref[tap].astype(jnp.float32), (3 * D) ** (-0.5), decay_rate)
        return carry

    lax.fori_loop(0, 29, pyramid_step, 0)
    for which in range(2):
        rows = trunk_ref[which * row_share : (which + 1) * row_share]
        update(1, which, rows, D ** (-0.5), decay_rate)
    for tap in range(9):
        first = 2 * row_share + tap * mid_share
        update(2, tap, trunk_ref[first : first + mid_share], (9 * MID) ** (-0.5), decay_rate)
    every = slice(None)
    update(3, every, stem_ref[...], PATCH ** (-0.5), decay_rate)
    for branch in range(5):
        update(
            4,
            branch,
            small_ref[:, branch * 128 : (branch + 1) * 128],
            (5 * BRANCH) ** (-0.5),
            decay_rate,
        )
    update(5, every, small_ref[:, 640:662], BRANCH ** (-0.5), decay_rate)
    update(6, every, norm_ref[...], 0.3, 0.0)
    update(7, every, task_ref[:, :25], 0.3, 0.0)


def adam_all(row_share, mid_share, gradients, states):
    flat = [part for state in states for part in state]
    return pl.pallas_call(
        functools.partial(adam_kernel, row_share, mid_share),
        out_shape=[jax.ShapeDtypeStruct(part.shape, jnp.float32) for part in flat],
        in_specs=vmem(len(gradients) + len(flat)),
        out_specs=vmem(len(flat)),
        compiler_params=pltpu.CompilerParams(vmem_limit_bytes=50 << 20),
        cost_estimate=pl.CostEstimate(flops=10**8, bytes_accessed=18 << 20, transcendentals=0),
        name="adam",
    )(*gradients, *flat)


def square_kernel(
    place_ref, three_ref, four_ref, one_ref, trunk_ref, pyramid_ref, task_ref, o_ref, norm_ref, task_grad_ref, loss_ref
):
    lower = place_ref[0] == 0
    three = three_ref[...]
    four = four_ref[...]
    mid = MID // 2
    for row in range(2):
        own = jnp.where(lower, four[row : row + 1, :mid], four[row : row + 1, mid:])
        norm_ref[row : row + 1] = jnp.concatenate(
            [own, three[2 * row : 2 * row + 1], three[2 * row + 1 : 2 * row + 2]], 1
        )
    lane = lax.broadcasted_iota(jnp.int32, (1, 128), 1)
    errors = three[4:5, 128:256]

    def lane_sum(values, first, last):
        kept = jnp.where((lane >= first) & (lane < last), values, 0.0)
        return jnp.sum(kept, 1, keepdims=True)

    seg = lane_sum(three[4:5, 256:384], 0, 1)
    off = lane_sum(errors, CLASSES, CLASSES + 2)
    dep = lane_sum(errors, CLASSES + 2, CLASSES + 3)
    is_task = lane < 3
    totals = jnp.where(lane == 0, seg, jnp.where(lane == 1, off, dep))
    means = totals / jnp.where(is_task, one_ref[2:3, :128], 1.0)
    scale = jnp.where(is_task, task_ref[...], 0.0)
    weighted = jnp.exp(-scale) * means
    loss_ref[...] = lane_sum(weighted + scale, 0, 3)
    bias = pltpu.roll(jnp.broadcast_to(three[4:5, :128], (8, 128)), 3, 1)[0:1]
    task_grad = jnp.where(is_task, 1.0 - weighted, jnp.where(lane < 25, bias, 0.0))
    task_grad_ref[...] = task_grad

    def tap_square(tap, total):
        values = pyramid_ref[tap].astype(jnp.float32)
        return total + jnp.sum(values * values, 0, keepdims=True)

    squares = lax.fori_loop(0, 29, tap_square, jnp.zeros((1, 128), jnp.float32))
    first = jnp.where(place_ref[1] == 0, 1.0, 0.0)
    norms = norm_ref[...]
    norm_square = jnp.sum(jnp.sum(norms * norms, 0, keepdims=True), 1, keepdims=True)
    task_square = jnp.sum(task_grad * task_grad, 1, keepdims=True)
    extra = first * (norm_square + jnp.where(lower, 1.0, 0.0) * task_square)
    squares = squares + trunk_ref[0:1] + jnp.where(lane == 0, extra, 0.0)
    o_ref[...] = jnp.concatenate([squares, jnp.zeros((7, 128), jnp.float32)], 0)


def own_squares_of(place, stat_three, stat_four, stat_one, trunk_squares, pyramid, task):
    return pl.pallas_call(
        square_kernel,
        out_shape=[
            jax.ShapeDtypeStruct((8, 128), jnp.float32),
            jax.ShapeDtypeStruct((2, MID // 2 + D // 2), jnp.float32),
            jax.ShapeDtypeStruct((1, 128), jnp.float32),
            jax.ShapeDtypeStruct((1, 1), jnp.float32),
        ],
        in_specs=[pl.BlockSpec(memory_space=pltpu.SMEM)] + vmem(6),
        out_specs=vmem(4),
        name="own_squares",
    )(place, stat_three, stat_four, stat_one, trunk_squares, pyramid, task)


def adam_step(weight, first, second, gradient, factor, rate, decay):
    gradient = gradient * factor
    first_new = 0.5 * first + 0.5 * gradient
    second_new = 0.5 * second + 0.5 * gradient * gradient
    direction = (
        first_new / (1.0 - 0.5**STEP) / (jnp.sqrt(second_new / (1.0 - 0.5**STEP)) + adam_eps)
    )
    return (weight - rate * (direction + decay * weight), first_new, second_new)


def on_device(
    sizes,
    patches,
    labels,
    offset_target,
    offset_valid,
    depth_target,
    lidar_valid,
    crop_mask,
    stem_weight,
    stem_first,
    stem_second,
    bottle_weight,
    bottle_first,
    bottle_second,
    middle_weight,
    middle_first,
    middle_second,
    pyramid_weight,
    pyramid_first,
    pyramid_second,
    project_weight,
    project_first,
    project_second,
    head_weight,
    head_first,
    head_second,
    norm_gains,
    norm_first,
    norm_second,
    task_params,
    task_first,
    task_second,
):
    chan_place = lax.axis_index("chan")
    dp_size = sizes["dp"]
    low = jnp.bfloat16
    crop_field = crop_mask.astype(jnp.float32).reshape(POSITIONS, 1)
    count_masks = jnp.concatenate([crop_mask, offset_valid, lidar_valid], 0)
    half = D // 2
    mid_half = MID // 2

    row_share = bottle_weight.shape[1]
    mid_share = middle_weight.shape[1]
    stem_share = stem_weight.shape[2]
    project_share = project_weight.shape[2]
    head_share = head_weight.shape[0]
    stem_shard = stem_weight.astype(low).reshape(PATCH, stem_share).T
    head_shard = jnp.concatenate(
        [
            project_weight.astype(low).transpose(2, 0, 1).reshape(project_share, 5 * 128),
            jnp.pad(head_weight.astype(low), ((0, 0), (0, 128 - 22))),
        ],
        1,
    )
    bottle_low, middle_low, stem_low, head_low = gather_trunk(
        sizes, bottle_weight.astype(low), middle_weight.astype(low), stem_shard, head_shard
    )
    pyramid_shard = pyramid_weight.astype(low)
    late_shard = pyramid_shard[EARLY_TAPS:]
    pyramid_low = (
        lax.all_gather(pyramid_shard[:EARLY_TAPS], "dp", axis=1, tiled=True),
        lax.all_gather(late_shard, "dp", axis=1, tiled=True),
    )
    own_place = chan_place.reshape(1)
    own_gains = norm_gains.reshape(2, mid_half + half)
    gains = (own_place, own_gains, swap_chan(own_gains))

    def own_bottle(which):
        return lax.dynamic_slice(bottle_low, (which, chan_place * half, 0), (1, half, MID))[0]

    def own_half(values, axis):
        width = values.shape[axis] // 2
        return lax.dynamic_slice_in_dim(values, chan_place * width, width, axis)

    def other_half(values, axis):
        width = values.shape[axis] // 2
        return lax.dynamic_slice_in_dim(values, (1 - chan_place) * width, width, axis)

    columns = jnp.broadcast_to(
        lax.rem(lax.broadcasted_iota(jnp.int32, (POSITIONS, 1), 0), FW).astype(jnp.float32),
        (POSITIONS, 128),
    )
    patch_rows = patches.reshape(POSITIONS, PATCH)
    stream_t, first_pre, stat_one = stem_reduce(
        patch_rows,
        stem_low,
        bottle_low,
        crop_field,
        count_masks,
    )
    stat_one = all_sum(sizes, stat_one, ("dp",), 0)
    hidden_low, hidden_t, second_low = norm_middle(
        first_pre, stat_one, gains, crop_field, middle_low, columns
    )
    expand_pre, stat_two = expand_forward(second_low, bottle_low, crop_field)
    stat_two = all_sum(sizes, stat_two, ("dp",), 1)
    output_low, output_t, pooled = residual_stream(
        patch_rows,
        stem_low,
        expand_pre,
        stat_two,
        stat_one,
        gains,
        crop_field,
    )
    branch_pre, pool_pre, concat_low, project_part = pyramid_forward(
        output_low, pooled, pyramid_low, head_low, columns
    )
    labels, offset_valid, lidar_valid, offset_target, depth_target, stat_one, project_part = (
        lax.optimization_barrier(
            (labels, offset_valid, lidar_valid, offset_target, depth_target, stat_one, project_part)
        )
    )
    offset_field = crop_field[:, 0] * offset_valid.astype(jnp.float32).reshape(POSITIONS)
    lidar_field = crop_field[:, 0] * lidar_valid.astype(jnp.float32).reshape(POSITIONS)
    lane = lax.broadcasted_iota(jnp.int32, (1, 128), 1)
    class_lane = (lane < CLASSES).astype(jnp.float32)
    offset_lane = ((lane >= CLASSES) & (lane < CLASSES + 2)).astype(jnp.float32)
    depth_lane = (lane == CLASSES + 2).astype(jnp.float32)
    onehot = (labels.reshape(POSITIONS, 1) == lane).astype(jnp.float32)
    mask = (
        class_lane * crop_field
        + offset_lane * offset_field[:, None]
        + depth_lane * lidar_field[:, None]
    )
    target = jnp.pad(
        jnp.concatenate([offset_target[0], depth_target], 0).T,
        ((0, 0), (CLASSES, 128 - CLASSES - 3)),
    )
    task_scale = task_params[:3]
    counts = stat_one[2, :3]
    crop_total = counts[0]
    task_weights = jnp.exp(-task_scale) / counts
    lane_rows = jnp.concatenate(
        [
            jnp.pad(task_params[3:], (0, 128 - 22)).reshape(1, 128),
            task_weights[0] * class_lane
            + task_weights[1] * offset_lane
            + task_weights[2] * depth_lane,
            class_lane,
            offset_lane,
            depth_lane,
            jnp.zeros((3, 128), jnp.float32),
        ],
        0,
    )
    feature_low, logit_low, project_grad_low, branch_grads, pool_grad, head_stat = head_step(
        project_part,
        swap_chan(project_part),
        lane_rows,
        onehot,
        target,
        mask,
        head_low,
        branch_pre,
        pool_pre,
    )
    other_parts = []
    later_grads = branch_grads
    for quarter in range(2):
        part = pyramid_field(
            2 - 2 * own_place + quarter,
            half // 2,
            pyramid_low,
            later_grads,
            pool_grad,
            crop_field,
            columns,
        )
        other_parts.append(swap_chan(part))
        later_grads, part = lax.optimization_barrier((later_grads, part))
    own_part, pyramid_grad = own_gradients(
        own_place,
        pyramid_low,
        output_t,
        later_grads,
        pool_grad,
        crop_field,
        columns,
        pooled.reshape(D, 1),
    )
    small_grads = jnp.concatenate(
        [
            dot(project_grad_low, concat_low, (0, 0)).astype(low),
            dot(feature_low, logit_low, (0, 0)).astype(low),
        ],
        1,
    )
    small_rows = project_share * 3
    small_grads = small_grads.reshape(dp_size, small_rows, 256)
    first_other, own_part, pyramid_grad, small_grads = lax.optimization_barrier(
        (other_parts[0], own_part, pyramid_grad, small_grads)
    )
    other_parts, own_part, pyramid_grad = lax.optimization_barrier(
        ([first_other, other_parts[1]], own_part, pyramid_grad)
    )
    pyramid_red = lax.psum_scatter(pyramid_grad, "dp", scatter_dimension=1, tiled=True)

    stat_three = residual_sums(
        own_place, own_part, other_parts, expand_pre, stat_two, stat_one, crop_field, head_stat
    )
    stat_three = all_sum(sizes, stat_three, ("dp",), 2)
    expand_grad_low, second_part = residual_back(
        own_place,
        own_part,
        other_parts,
        expand_pre,
        stat_two,
        stat_one,
        stat_three,
        own_gains,
        crop_field,
        bottle_low,
    )
    second_other = swap_chan(second_part)
    expand_rows = dot(expand_grad_low, second_low, (0, 0)).astype(low)
    second_other, expand_rows, stat_three, own_part = lax.optimization_barrier(
        (second_other, expand_rows, stat_three, own_part)
    )
    expand_sent = swap_chan(other_half(expand_rows, 1))
    upstream_one, second_own, stat_four = first_back(
        own_place,
        second_part,
        second_other,
        middle_low,
        columns,
        first_pre,
        stat_one,
        gains,
        crop_field,
    )
    stat_four = all_sum(sizes, stat_four, ("dp",), 3)
    stat_one, stat_three, stat_four, own_part, expand_sent = lax.optimization_barrier(
        (stat_one, stat_three, stat_four, own_part, expand_sent)
    )
    reduce_grad, stem_grad = late_gradients(
        own_place,
        upstream_one,
        first_pre,
        stat_one,
        stat_four,
        gains,
        crop_field,
        patch_rows.T,
        bottle_low,
        own_part,
        other_parts,
        stream_t,
    )
    middle_grad = middle_weights(hidden_t, second_own, columns)
    expand_own = own_half(expand_rows, 1)
    expand_grad = jnp.where(
        chan_place == 0,
        jnp.concatenate([expand_own, expand_sent], 0),
        jnp.concatenate([expand_sent, expand_own], 0),
    )

    trunk_grads = jnp.concatenate(
        [
            reduce_grad.reshape(dp_size, row_share, 256),
            expand_grad.reshape(dp_size, row_share, 256),
            middle_grad.reshape(9, dp_size, mid_share, 256)
            .transpose(1, 0, 2, 3)
            .reshape(dp_size, 9 * mid_share, 256),
            stem_grad.reshape(dp_size, stem_share * PATCH // 256, 256),
            small_grads,
        ],
        1,
    )
    trunk_red, trunk_squares = scatter_trunk(sizes, trunk_grads)
    start = 2 * row_share + 9 * mid_share
    stem_rows = stem_share * PATCH // 256
    stem_red = trunk_red[start : start + stem_rows].reshape(stem_share, PATCH)
    small_red = trunk_red[start + stem_rows :].reshape(project_share, 768)
    own_squares, norm_grad, task_grad, total_loss = own_squares_of(
        jnp.stack([chan_place, lax.axis_index("dp")]),
        stat_three,
        stat_four,
        stat_one,
        trunk_squares,
        pyramid_red,
        jnp.pad(task_params[:3], (0, 125)).reshape(1, 128),
    )
    total_loss = total_loss.reshape(())
    all_squares = all_sum(sizes, own_squares, ("dp", "chan"), 4)
    grad_norm = jnp.sqrt(jnp.sum(all_squares[0]))

    def turn_stem(part):
        return part.reshape(PATCH, stem_share).T

    def turn_project(part):
        return part.transpose(0, 2, 1)

    def flat_norm(part):
        return part.reshape(2, mid_half + half)

    updated = adam_all(
        row_share,
        mid_share,
        [
            all_squares,
            pyramid_red,
            trunk_red,
            stem_red,
            small_red,
            norm_grad,
            task_grad,
        ],
        [
            (pyramid_weight, pyramid_first, pyramid_second),
            (bottle_weight, bottle_first, bottle_second),
            (middle_weight, middle_first, middle_second),
            tuple(turn_stem(part) for part in (stem_weight, stem_first, stem_second)),
            tuple(turn_project(part) for part in (project_weight, project_first, project_second)),
            (head_weight, head_first, head_second),
            tuple(flat_norm(part) for part in (norm_gains, norm_first, norm_second)),
            tuple(part.reshape(1, 25) for part in (task_params, task_first, task_second)),
        ],
    )
    groups = [updated[3 * group : 3 * group + 3] for group in range(ADAM_GROUPS)]
    new_pyramid, new_bottle, new_middle, new_stem, new_project, new_head, new_norm, new_task = groups
    new_stem = [part.T.reshape(stem_weight.shape) for part in new_stem]
    new_project = [part.transpose(0, 2, 1) for part in new_project]
    new_norm = [part.reshape(norm_gains.shape) for part in new_norm]
    new_task = [part.reshape(25) for part in new_task]
    return (
        total_loss,
        grad_norm,
        new_stem[0],
        new_stem[1],
        new_stem[2],
        new_bottle[0],
        new_bottle[1],
        new_bottle[2],
        new_middle[0],
        new_middle[1],
        new_middle[2],
        new_pyramid[0],
        new_pyramid[1],
        new_pyramid[2],
        new_project[0],
        new_project[1],
        new_project[2],
        new_head[0],
        new_head[1],
        new_head[2],
        new_norm[0],
        new_norm[1],
        new_norm[2],
        new_task[0],
        new_task[1],
        new_task[2],
    )


def solution(mesh):
    return jax.shard_map(
        functools.partial(on_device, dict(mesh.shape)),
        mesh=mesh,
        in_specs=(
            P("dp", None, None),
            P("dp", None),
            P("dp", None, None),
            P("dp", None),
            P("dp", None),
            P("dp", None),
            P("dp", None),
            P(None, "chan", "dp"),
            P(None, "chan", "dp"),
            P(None, "chan", "dp"),
            P(None, "dp", "chan"),
            P(None, "dp", "chan"),
            P(None, "dp", "chan"),
            P(None, "dp", "chan"),
            P(None, "dp", "chan"),
            P(None, "dp", "chan"),
            P(None, "dp", "chan"),
            P(None, "dp", "chan"),
            P(None, "dp", "chan"),
            P(None, "chan", "dp"),
            P(None, "chan", "dp"),
            P(None, "chan", "dp"),
            P("dp", None),
            P("dp", None),
            P("dp", None),
            P(None, "chan", None),
            P(None, "chan", None),
            P(None, "chan", None),
            P(),
            P(),
            P(),
        ),
        out_specs=(
            P(),
            P(),
            P(None, "chan", "dp"),
            P(None, "chan", "dp"),
            P(None, "chan", "dp"),
            P(None, "dp", "chan"),
            P(None, "dp", "chan"),
            P(None, "dp", "chan"),
            P(None, "dp", "chan"),
            P(None, "dp", "chan"),
            P(None, "dp", "chan"),
            P(None, "dp", "chan"),
            P(None, "dp", "chan"),
            P(None, "dp", "chan"),
            P(None, "chan", "dp"),
            P(None, "chan", "dp"),
            P(None, "chan", "dp"),
            P("dp", None),
            P("dp", None),
            P("dp", None),
            P(None, "chan", None),
            P(None, "chan", None),
            P(None, "chan", None),
            P(),
            P(),
            P(),
        ),
        check_vma=False,
    )
```

```python
import functools

import jax
import jax.numpy as jnp
from jax import lax
from jax.experimental import pallas as pl
from jax.experimental.pallas import tpu as pltpu
from jax.sharding import PartitionSpec as P

D = 2048
MID = 512
BRANCH = 256
CLASSES = 19
PATCH = 192
FH = 40
FW = 40
STEP = 10
POSITIONS = 1600


pyramid_rates = (0, 12, 24, 36)
norm_eps = 1e-05
clip_level = 0.01
adam_eps = 1e-08
decay_rate = 0.01


MESH_ID = pl.DeviceIdType.MESH


NEAR = 4


def sum_kernel(near, far, chans, x_ref, o_ref, inner, part, outer, sems_in, sems_out):
    dp = lax.axis_index("dp")
    chan = lax.axis_index("chan")
    layer, spot = lax.div(dp, near), lax.rem(dp, near)
    barrier = pltpu.get_barrier_semaphore()

    def inner_device(step):
        index = lax.rem((spot * chans + (chan if chans > 1 else 0)) + step, near * chans)
        spot_of = lax.div(index, chans)
        other = lax.rem(index, chans) if chans > 1 else chan
        return index, (layer * near + spot_of, other)

    def outer_device(step):
        index = lax.rem(layer + step, far)
        return index, (index * near + spot, chan)

    rounds = (
        (near * chans, inner_device, x_ref, inner, sems_in),
        (far, outer_device, part, outer, sems_out),
    )
    for count, device_of, source, slots, sems in rounds:

        def greet(step, carry, device_of=device_of):
            pl.semaphore_signal(
                barrier, inc=1, device_id=device_of(step)[1], device_id_type=MESH_ID
            )
            return carry

        lax.fori_loop(1, count, greet, 0)
    pl.semaphore_wait(barrier, near * chans + far - 2)
    for count, device_of, source, slots, sems in rounds:
        me = device_of(0)[0]

        def copy_of(step, slot, device_of=device_of, source=source, slots=slots, sems=sems):
            return pltpu.make_async_remote_copy(
                src_ref=source,
                dst_ref=slots.at[slot],
                send_sem=sems.at[0, step],
                recv_sem=sems.at[1, slot],
                device_id=device_of(step)[1],
                device_id_type=MESH_ID,
            )

        def start(step, carry):
            copy_of(step, me).start()
            return carry

        def arrive(step, carry):
            copy_of(step, device_of(step)[0]).wait_recv()
            return carry

        def leave(step, carry):
            copy_of(step, me).wait_send()
            return carry

        lax.fori_loop(1, count, start, 0)
        slots[me] = source[...]
        lax.fori_loop(1, count, arrive, 0)
        total = slots[0]
        for index in range(1, count):
            total = total + slots[index]
        if source is x_ref:
            part[...] = total
        else:
            o_ref[...] = total
        lax.fori_loop(1, count, leave, 0)


def all_sum(sizes, values, axes, collective):
    near, far = NEAR, sizes["dp"] // NEAR
    chans = sizes["chan"] if "chan" in axes else 1
    shape = values.shape
    return pl.pallas_call(
        functools.partial(sum_kernel, near, far, chans),
        out_shape=jax.ShapeDtypeStruct(shape, jnp.float32),
        in_specs=[pl.BlockSpec(memory_space=pltpu.VMEM)],
        out_specs=pl.BlockSpec(memory_space=pltpu.VMEM),
        scratch_shapes=[
            pltpu.VMEM((near * chans,) + shape, jnp.float32),
            pltpu.VMEM(shape, jnp.float32),
            pltpu.VMEM((far,) + shape, jnp.float32),
            pltpu.SemaphoreType.DMA((2, near * chans)),
            pltpu.SemaphoreType.DMA((2, far)),
        ],
        compiler_params=pltpu.CompilerParams(
            collective_id=collective, has_side_effects=True, vmem_limit_bytes=16 << 20
        ),
        name="small_sum",
    )(values)


def swap_chan(values):
    return lax.ppermute(values, "chan", [(0, 1), (1, 0)])


def valid(step, length):
    return max(0, step), length + min(0, step)


def taps_of(rate):
    return [((tap // 3 - 1) * rate, (tap % 3 - 1) * rate) for tap in range(9)]


def shift_field(field, row_step, col_step):
    rows, cols = field.shape[:2]
    r0, r1 = valid(row_step, rows)
    c0, c1 = valid(col_step, cols)
    return jnp.pad(
        field[r0:r1, c0:c1],
        (
            (r0 - row_step, rows - (r1 - row_step)),
            (c0 - col_step, cols - (c1 - col_step)),
            (0, 0),
        ),
    )


def gelu_grad(values, upstream):
    return jax.vjp(jax.nn.gelu, values)[1](upstream)[0]


def dot(left, right, contract=(1, 0)):
    return lax.dot_general(
        left,
        right,
        (((contract[0],), (contract[1],)), ((), ())),
        preferred_element_type=jnp.float32,
    )


def place_of():
    dp = lax.axis_index("dp")
    return lax.div(dp, 4), lax.rem(lax.div(dp, 2), 2), lax.rem(dp, 2), lax.axis_index("chan")


def device_at(z, y, core, x):
    return ((z * 2 + y) * 2 + core, x)


def flip(value, turn):
    return lax.rem(value + turn, 2)


def z_flip(z, turn):
    return flip(lax.div(z, 2), turn // 2) * 2 + flip(lax.rem(z, 2), turn % 2)


def greet_neighbours(layers):
    z, y, core, x = place_of()
    barrier = pltpu.get_barrier_semaphore()
    for target in (
        device_at(z, y, 1 - core, x),
        device_at(z, 1 - y, core, x),
        device_at(z, y, core, 1 - x),
    ):
        pl.semaphore_signal(barrier, inc=1, device_id=target, device_id_type=MESH_ID)

    @pl.when(z > 0)
    def _():
        pl.semaphore_signal(
            barrier, inc=1, device_id=device_at(z - 1, y, core, x), device_id_type=MESH_ID
        )

    @pl.when(z < layers - 1)
    def _():
        pl.semaphore_signal(
            barrier, inc=1, device_id=device_at(z + 1, y, core, x), device_id_type=MESH_ID
        )

    peers = 3 + jnp.where(z > 0, 1, 0) + jnp.where(z < layers - 1, 1, 0)
    pl.semaphore_wait(barrier, peers)


def gather_kernel(
    layers,
    bottle,
    middle,
    small,
    head,
    bottle_all,
    middle_all,
    small_all,
    head_all,
    send_sems,
    recv_sems,
    local_sems,
):
    z, y, core, x = place_of()
    rows = bottle.shape[1]
    mid_rows = middle.shape[1]
    small_rows = small.shape[0]
    head_rows = head.shape[0]
    own_refs = (bottle, middle, small, head)

    def region(kind, block):
        zz, yy, kk, xx = block
        index = (zz * 2 + yy) * 2 + kk
        cols = pl.ds(pl.multiple_of(xx * 256, 256), 256)
        if kind == 0:
            return bottle_all.at[:, pl.ds(pl.multiple_of(index * rows, 16), rows), cols]
        if kind == 1:
            return middle_all.at[:, pl.ds(pl.multiple_of(index * mid_rows, 16), mid_rows), cols]
        if kind == 3:
            return head_all.at[pl.ds(pl.multiple_of(index * head_rows, 16), head_rows)]
        first = xx * (small_all.shape[0] // 2) + index * small_rows
        return small_all.at[pl.ds(pl.multiple_of(first, 16), small_rows)]

    def semaphore(kind, block):
        zz, yy, kk, xx = block
        return recv_sems.at[kind, ((zz * 2 + yy) * 2 + kk) * 2 + xx]

    own = (z, y, core, x)
    pending = []

    def send(kind, block, target, when=None):
        copy = pltpu.make_async_remote_copy(
            src_ref=own_refs[kind] if block is own else region(kind, block),
            dst_ref=region(kind, block),
            send_sem=send_sems.at[len(pending)],
            recv_sem=semaphore(kind, block),
            device_id=target,
            device_id_type=MESH_ID,
        )
        if when is None:
            copy.start()
        else:
            pl.when(when)(copy.start)
        pending.append((when, copy))

    def arrive(kind, block):
        pltpu.make_async_remote_copy(
            src_ref=region(kind, block),
            dst_ref=region(kind, block),
            send_sem=send_sems.at[0],
            recv_sem=semaphore(kind, block),
            device_id=device_at(z, y, 1 - core, x),
            device_id_type=MESH_ID,
        ).wait_recv()

    locals_ = [
        pltpu.make_async_copy(own_refs[kind], region(kind, own), local_sems.at[kind])
        for kind in range(4)
    ]
    for copy in locals_:
        copy.start()
    greet_neighbours(layers)
    sibling = device_at(z, y, 1 - core, x)
    other_x = device_at(z, y, core, 1 - x)
    other_y = device_at(z, 1 - y, core, x)

    def along_z(kind, block):
        if block[0] is z:
            send(kind, block, device_at(z + 1, y, core, x), z < layers - 1)
            send(kind, block, device_at(z - 1, y, core, x), z > 0)
        else:
            below = block[0] < z
            ahead = z + jnp.where(below, 1, -1)
            send(
                kind,
                block,
                device_at(ahead, y, core, x),
                jnp.logical_and(ahead >= 0, ahead < layers),
            )

    for kind in (0, 1):
        along_z(kind, own)
    send(2, own, other_x)
    send(2, own, other_y)
    send(1, own, other_x)
    send(0, own, other_y)
    along_z(2, own)
    along_z(3, own)
    send(3, own, other_y)
    send(0, own, other_x)
    send(1, own, other_y)
    for kind in range(4):
        send(kind, own, sibling)

    block = (z, y, core, 1 - x)
    arrive(2, block)
    send(2, block, other_y)
    along_z(2, block)
    send(2, block, sibling)
    for xx in (x, 1 - x):
        block = (z, 1 - y, core, xx)
        arrive(2, block)
        along_z(2, block)
        send(2, block, sibling)

    for turn in range(layers):
        zz = z if turn == 0 else z_flip(z, turn)
        if turn:
            for kind, near, far in ((0, other_y, other_x), (1, other_x, other_y)):
                block = (zz, y, core, x)
                arrive(kind, block)
                along_z(kind, block)
                send(kind, block, near)
                send(kind, block, far)
                send(kind, block, sibling)
            block = (zz, y, core, x)
            arrive(3, block)
            along_z(3, block)
            send(3, block, other_y)
            send(3, block, sibling)
        block = (zz, 1 - y, core, x)
        arrive(0, block)
        send(0, block, other_x)
        send(0, block, sibling)
        block = (zz, y, core, 1 - x)
        arrive(1, block)
        send(1, block, other_y)
        send(1, block, sibling)
        if turn:
            for yy, xx in ((y, x), (y, 1 - x), (1 - y, x), (1 - y, 1 - x)):
                block = (zz, yy, core, xx)
                arrive(2, block)
                along_z(2, block)
                send(2, block, sibling)
    for turn in range(layers):
        zz = z if turn == 0 else z_flip(z, turn)
        for yy in (y, 1 - y):
            block = (zz, yy, core, 1 - x)
            arrive(0, block)
            send(0, block, sibling)
        for xx in (x, 1 - x):
            block = (zz, 1 - y, core, xx)
            arrive(1, block)
            send(1, block, sibling)
        block = (zz, 1 - y, core, x)
        arrive(3, block)
        send(3, block, sibling)
    for kind in range(4):
        for turn in range(layers):
            zz = z if turn == 0 else z_flip(z, turn)
            for yy in (y, 1 - y):
                for xx in (x, 1 - x) if kind < 3 else (x,):
                    arrive(kind, (zz, yy, 1 - core, xx))
    for copy in locals_:
        copy.wait()
    for when, copy in pending:
        if when is None:
            copy.wait_send()
        else:
            pl.when(when)(copy.wait_send)


def gather_trunk(sizes, bottle, middle, small, head):
    count = sizes["dp"]
    if count != 16 or middle.shape[1] % 16:
        packed = [
            lax.all_gather(
                lax.all_gather(part, "dp", axis=1, tiled=True), "chan", axis=2, tiled=True
            )
            for part in (bottle, middle)
        ]
        return packed + [
            lax.all_gather(small, ("chan", "dp")).reshape(D, small.shape[1]),
            lax.all_gather(head, "dp", axis=0, tiled=True),
        ]
    return pl.pallas_call(
        functools.partial(gather_kernel, count // 4),
        out_shape=[
            jax.ShapeDtypeStruct((2, D, MID), jnp.bfloat16),
            jax.ShapeDtypeStruct((9, MID, MID), jnp.bfloat16),
            jax.ShapeDtypeStruct((D, small.shape[1]), jnp.bfloat16),
            jax.ShapeDtypeStruct((BRANCH, head.shape[1]), jnp.bfloat16),
        ],
        in_specs=[pl.BlockSpec(memory_space=pl.ANY)] * 4,
        out_specs=[pl.BlockSpec(memory_space=pl.ANY)] * 4,
        scratch_shapes=[
            pltpu.SemaphoreType.DMA((176,)),
            pltpu.SemaphoreType.DMA((4, 2 * count)),
            pltpu.SemaphoreType.DMA((4,)),
        ],
        compiler_params=pltpu.CompilerParams(collective_id=5, has_side_effects=True),
        name="gather_trunk",
    )(bottle, middle, small, head)


PAD = 128
PYRAMID_ROWS = (-36, -24, -12, 0, 12, 24, 36)


def taps_by_row():
    fields = [(0, 0)] + [(rate, col * rate) for rate in (12, 24, 36) for col in (-1, 0, 1)]
    groups = []
    for row_step in PYRAMID_ROWS:
        group = []
        for place, (rate, col_step) in enumerate(fields):
            if rate == 0:
                if row_step == 0:
                    group.append((0, place))
            elif row_step == 0 or abs(row_step) == rate:
                turn = (1 if row_step > 0 else -1 if row_step < 0 else 0) + 1
                tap = 1 + 9 * (rate // 12 - 1) + 3 * turn + (col_step // rate + 1)
                group.append((tap, place))
        groups.append(group)
    return fields, groups


FIELDS, ROW_GROUPS = taps_by_row()
TAP_ORDER = [tap for group in ROW_GROUPS for tap, place in group]
PLACE_ORDER = [place for group in ROW_GROUPS for tap, place in group]


EARLY_TAPS = 10


def tap_of(early, late, tap):
    return early.at[tap] if tap < EARLY_TAPS else late.at[tap - EARLY_TAPS]


def roll_cols(values, columns, step):
    if step == 0:
        return values
    moved = pltpu.roll(values, (-step) % values.shape[0], 0)
    target = columns[:, :1] + float(step)
    return jnp.where((target >= 0.0) & (target < float(FW)), moved, 0.0)


def vmem(count):
    return [pl.BlockSpec(memory_space=pltpu.VMEM)] * count


def middle_kernel(back, x_ref, w_ref, col_ref, o_ref, canvas):
    edge = 4 * FW
    mid = x_ref.shape[1]
    values = x_ref[...].astype(jnp.float32)
    sign = -1 if back else 1
    for turn in range(3):
        canvas[turn, :edge] = jnp.zeros((edge, mid), canvas.dtype)
        canvas[turn, POSITIONS + edge :] = jnp.zeros((edge, mid), canvas.dtype)
        canvas[turn, edge : POSITIONS + edge] = roll_cols(
            values, col_ref, sign * 4 * (turn - 1)
        ).astype(canvas.dtype)
    block = 400

    def step(index, carry):
        total = None
        for row in range(3):
            first = pl.multiple_of(index * block + edge * (1 + sign * (row - 1)), 16)
            for turn in range(3):
                part = dot(
                    canvas[turn, pl.ds(first, block)],
                    w_ref[3 * row + turn],
                    (1, 1) if back else (1, 0),
                )
                total = part if total is None else total + part
        o_ref[pl.ds(pl.multiple_of(index * block, 16), block)] = total.astype(o_ref.dtype)
        return carry

    lax.fori_loop(0, POSITIONS // block, step, 0)


def middle_conv(field, weights, columns, back, dtype):
    return pl.pallas_call(
        functools.partial(middle_kernel, back),
        out_shape=jax.ShapeDtypeStruct((POSITIONS, MID), dtype),
        in_specs=vmem(3),
        out_specs=vmem(1)[0],
        scratch_shapes=[pltpu.VMEM((3, POSITIONS + 8 * FW, MID), jnp.bfloat16)],
        compiler_params=pltpu.CompilerParams(vmem_limit_bytes=40 << 20),
        cost_estimate=pl.CostEstimate(
            flops=2 * POSITIONS * 9 * MID * MID, bytes_accessed=16 << 20, transcendentals=0
        ),
        name="middle_back" if back else "middle_fwd",
    )(field, weights, columns)


def middle_weight_kernel(xt_ref, g_ref, col_ref, o_ref, fields):
    width = g_ref.shape[1]
    values = g_ref[...].astype(jnp.float32)
    for turn in range(3):
        fields[turn, :PAD] = jnp.zeros((PAD, width), fields.dtype)
        fields[turn, PAD + POSITIONS :] = jnp.zeros((PAD, width), fields.dtype)
        fields[turn, PAD : PAD + POSITIONS] = roll_cols(values, col_ref, -4 * (turn - 1)).astype(
            fields.dtype
        )
    for row in range(3):
        row_step = 4 * (row - 1)
        r0, r1 = valid(row_step, FH)
        first = r0 * FW // 128 * 128
        last = min(POSITIONS, -(-r1 * FW // 128) * 128)
        base = PAD + first - row_step * FW
        for turn in range(3):
            o_ref[3 * row + turn] = dot(
                xt_ref[:, first:last], fields[turn, base : base + last - first]
            ).astype(o_ref.dtype)


def middle_weights(field_t, grads, columns):
    depth, width = field_t.shape[0], grads.shape[1]
    return pl.pallas_call(
        middle_weight_kernel,
        out_shape=jax.ShapeDtypeStruct((9, depth, width), jnp.bfloat16),
        in_specs=vmem(3),
        out_specs=vmem(1)[0],
        scratch_shapes=[pltpu.VMEM((3, POSITIONS + 2 * PAD, width), jnp.bfloat16)],
        compiler_params=pltpu.CompilerParams(vmem_limit_bytes=40 << 20),
        cost_estimate=pl.CostEstimate(
            flops=2 * POSITIONS * 9 * depth * width, bytes_accessed=6 << 20, transcendentals=0
        ),
        name="middle_weights",
    )(field_t, grads, columns)


def fill_fields(g_ref, col_ref, fields):
    width = g_ref.shape[2]
    for place, (rate, col_step) in enumerate(FIELDS):
        fields[place, :PAD] = jnp.zeros((PAD, width), fields.dtype)
        fields[place, PAD + POSITIONS :] = jnp.zeros((PAD, width), fields.dtype)
        values = g_ref[rate // 12]
        fields[place, PAD : PAD + POSITIONS] = roll_cols(
            values.astype(jnp.float32), col_ref, -col_step
        ).astype(fields.dtype)


def start_field_copies(place_ref, a_hbm, b_hbm, depth, weights, pool_weights, sems):
    width = pool_weights.shape[1]
    rows = pl.ds(pl.multiple_of(place_ref[0] * depth, 16), depth)
    copies = [
        pltpu.make_async_copy(
            tap_of(a_hbm, b_hbm, tap).at[rows],
            weights.at[:, pl.ds(slot * width, width)],
            sems.at[slot],
        )
        for slot, tap in enumerate(TAP_ORDER)
    ]
    copies.append(
        pltpu.make_async_copy(tap_of(a_hbm, b_hbm, 28).at[rows], pool_weights, sems.at[28])
    )
    for copy in copies:
        copy.start()
    return copies


def field_products(pool_ref, crop_ref, o_ref, weights, pool_weights, fields, stack):
    width = pool_weights.shape[1]
    pooled = dot(
        jnp.broadcast_to(pool_ref[...], (16, width)).astype(jnp.bfloat16), pool_weights[...], (1, 1)
    )[0:1] / jnp.sum(crop_ref[...], keepdims=True)
    step_of = [step for step, group in zip(PYRAMID_ROWS, ROW_GROUPS) for entry in group]
    for r0, r1 in ((0, 4), (4, 12), (12, 16), (16, 24), (24, 28), (28, 36), (36, 40)):
        slots = [
            slot for slot, step in enumerate(step_of) if r0 - step >= 0 and r1 - step <= FH
        ]
        count = (r1 - r0) * FW
        for at, slot in enumerate(slots):
            base = PAD + (r0 - step_of[slot]) * FW
            stack[:count, at * width : (at + 1) * width] = fields[
                PLACE_ORDER[slot], base : base + count
            ]
        part = dot(
            stack[:count, : len(slots) * width],
            weights[:, slots[0] * width : (slots[-1] + 1) * width],
            (1, 1),
        )
        o_ref[r0 * FW : r1 * FW] = (part + crop_ref[r0 * FW : r1 * FW] * pooled).astype(
            o_ref.dtype
        )


def field_kernel(
    place_ref, a_hbm, b_hbm, g_ref, pool_ref, crop_ref, col_ref, o_ref, weights, pool_weights, fields, stack, sems
):
    copies = start_field_copies(
        place_ref, a_hbm, b_hbm, o_ref.shape[1], weights, pool_weights, sems
    )
    fill_fields(g_ref, col_ref, fields)
    for copy in copies:
        copy.wait()
    field_products(pool_ref, crop_ref, o_ref, weights, pool_weights, fields, stack)


def own_kernel(
    place_ref,
    a_hbm,
    b_hbm,
    xt_hbm,
    g_ref,
    pool_ref,
    crop_ref,
    col_ref,
    pooled_ref,
    o_ref,
    w_out,
    weights,
    pool_weights,
    fields,
    stack,
    xt_ref,
    stage,
    sems,
    xt_sem,
    out_sems,
):
    copies = start_field_copies(
        place_ref, a_hbm, b_hbm, o_ref.shape[1], weights, pool_weights, sems
    )
    xt_copy = pltpu.make_async_copy(xt_hbm, xt_ref, xt_sem)
    xt_copy.start()
    fill_fields(g_ref, col_ref, fields)
    for copy in copies:
        copy.wait()
    field_products(pool_ref, crop_ref, o_ref, weights, pool_weights, fields, stack)
    xt_copy.wait()
    width = g_ref.shape[2]
    depth = xt_ref.shape[0]
    block = 1024
    waiting = [[], []]
    turn = 0
    for row_step, group in zip(PYRAMID_ROWS, ROW_GROUPS):
        r0, r1 = valid(row_step, FH)
        first = r0 * FW // 128 * 128
        last = min(POSITIONS, -(-r1 * FW // 128) * 128)
        base = PAD + first - row_step * FW
        sets = [group[at : at + 2] for at in range(0, 10, 2)] if row_step == 0 else [group]
        for chosen in sets:
            slot = turn % 2
            turn += 1
            for copy in waiting[slot]:
                copy.wait()
            right = jnp.concatenate(
                [fields[place, base : base + last - first] for tap, place in chosen], 1
            )

            def step(index, carry):
                rows = pl.ds(pl.multiple_of(index * block, 16), block)
                part = dot(xt_ref[rows, first:last], right)
                for offset in range(len(chosen)):
                    stage[slot, offset, rows] = part[
                        :, offset * width : (offset + 1) * width
                    ].astype(stage.dtype)
                return carry

            lax.fori_loop(0, depth // block, step, 0)
            waiting[slot] = [
                pltpu.make_async_copy(
                    stage.at[slot, offset], w_out.at[tap], out_sems.at[slot, offset]
                )
                for offset, (tap, place) in enumerate(chosen)
            ]
            for copy in waiting[slot]:
                copy.start()
    slot = turn % 2
    for copy in waiting[slot]:
        copy.wait()
    stage[slot, 0] = (pooled_ref[...] * pool_ref[...]).astype(stage.dtype)
    last_copy = pltpu.make_async_copy(stage.at[slot, 0], w_out.at[28], out_sems.at[slot, 0])
    last_copy.start()
    for copy in waiting[1 - slot]:
        copy.wait()
    last_copy.wait()


def own_gradients(place, weights, field_t, grads, pool_grad, crop, columns, pooled):
    depth, width = weights[0].shape[1:]
    hbm = pl.BlockSpec(memory_space=pltpu.HBM)
    half = depth // 2
    return pl.pallas_call(
        own_kernel,
        out_shape=[
            jax.ShapeDtypeStruct((POSITIONS, half), jnp.bfloat16),
            jax.ShapeDtypeStruct((29, depth, width), jnp.bfloat16),
        ],
        in_specs=[pl.BlockSpec(memory_space=pltpu.SMEM), hbm, hbm, hbm] + vmem(5),
        out_specs=[pl.BlockSpec(memory_space=pltpu.VMEM), hbm],
        scratch_shapes=[
            pltpu.VMEM((half, 28 * width), jnp.bfloat16),
            pltpu.VMEM((half, width), jnp.bfloat16),
            pltpu.VMEM((10, POSITIONS + 2 * PAD, width), jnp.bfloat16),
            pltpu.VMEM((8 * FW, 19 * width), jnp.bfloat16),
            pltpu.VMEM((depth, POSITIONS), jnp.bfloat16),
            pltpu.VMEM((2, 3, depth, width), jnp.bfloat16),
            pltpu.SemaphoreType.DMA((29,)),
            pltpu.SemaphoreType.DMA,
            pltpu.SemaphoreType.DMA((2, 3)),
        ],
        compiler_params=pltpu.CompilerParams(vmem_limit_bytes=60 << 20),
        cost_estimate=pl.CostEstimate(flops=1000, bytes_accessed=1024, transcendentals=0),
        name="own_gradients",
    )(place, weights[0], weights[1], field_t, grads, pool_grad, crop, columns, pooled)


def pyramid_field(place, depth, weights, grads, pool_grad, crop, columns):
    width = weights[0].shape[2]
    return pl.pallas_call(
        field_kernel,
        out_shape=jax.ShapeDtypeStruct((POSITIONS, depth), jnp.bfloat16),
        in_specs=[
            pl.BlockSpec(memory_space=pltpu.SMEM),
            pl.BlockSpec(memory_space=pltpu.HBM),
            pl.BlockSpec(memory_space=pltpu.HBM),
            pl.BlockSpec(memory_space=pltpu.VMEM),
            pl.BlockSpec(memory_space=pltpu.VMEM),
            pl.BlockSpec(memory_space=pltpu.VMEM),
            pl.BlockSpec(memory_space=pltpu.VMEM),
        ],
        out_specs=vmem(1)[0],
        scratch_shapes=[
            pltpu.VMEM((depth, 28 * width), jnp.bfloat16),
            pltpu.VMEM((depth, width), jnp.bfloat16),
            pltpu.VMEM((10, POSITIONS + 2 * PAD, width), jnp.bfloat16),
            pltpu.VMEM((8 * FW, 19 * width), jnp.bfloat16),
            pltpu.SemaphoreType.DMA((29,)),
        ],
        compiler_params=pltpu.CompilerParams(vmem_limit_bytes=60 << 20),
        cost_estimate=pl.CostEstimate(
            flops=1000, bytes_accessed=1024, transcendentals=0
        ),
        name="pyramid_field",
    )(place, weights[0], weights[1], grads, pool_grad, crop, columns)


BLOCK = 320


def block_rows(index):
    return pl.ds(pl.multiple_of(index * BLOCK, 16), BLOCK)


def gelu_slope(values, upstream):
    return jax.vjp(jax.nn.gelu, values)[1](upstream)[0]


def stem_kernel(p_ref, stem_ref, reduce_ref, crop_ref, mask_ref, xt_ref, a_ref, stat_ref, x_ref):
    def step(index, carry):
        rows = block_rows(index)
        low = (crop_ref[rows] * dot(p_ref[rows], stem_ref[...], (1, 1))).astype(x_ref.dtype)
        x_ref[rows] = low
        value = dot(low, reduce_ref[0])
        a_ref[rows] = value
        return (
            carry[0] + jnp.sum(value, 0, keepdims=True),
            carry[1] + jnp.sum(value * value, 0, keepdims=True),
        )

    zero = jnp.zeros((1, MID), jnp.float32)
    total, square = lax.fori_loop(0, POSITIONS // BLOCK, step, (zero, zero))
    for at in range(0, D, 256):
        xt_ref[at : at + 256] = x_ref[:, at : at + 256].T
    masks = mask_ref[...].astype(jnp.float32)
    lane = lax.broadcasted_iota(jnp.int32, (1, MID), 1)
    counts = jnp.zeros((1, MID), jnp.float32)
    for place in range(3):
        kept = masks[0:1] if place == 0 else masks[0:1] * masks[place : place + 1]
        counts = jnp.where(lane == place, jnp.sum(kept, 1, keepdims=True), counts)
    stat_ref[...] = jnp.concatenate([total, square, counts, jnp.zeros((5, MID), jnp.float32)], 0)


def stem_reduce(patches, stem, bottle, crop, masks):
    return pl.pallas_call(
        stem_kernel,
        grid=(1,),
        out_shape=[
            jax.ShapeDtypeStruct((D, POSITIONS), jnp.bfloat16),
            jax.ShapeDtypeStruct((POSITIONS, MID), jnp.float32),
            jax.ShapeDtypeStruct((8, MID), jnp.float32),
        ],
        in_specs=[
            pl.BlockSpec((POSITIONS, PATCH), lambda i: (0, 0)),
            pl.BlockSpec(stem.shape, lambda i: (0, 0)),
            pl.BlockSpec((1, D, MID), lambda i: (0, 0, 0)),
            pl.BlockSpec((POSITIONS, 1), lambda i: (0, 0)),
            pl.BlockSpec((3, POSITIONS), lambda i: (0, 0)),
        ],
        out_specs=[
            pl.BlockSpec((D, POSITIONS), lambda i: (0, 0)),
            pl.BlockSpec((POSITIONS, MID), lambda i: (0, 0)),
            pl.BlockSpec((8, MID), lambda i: (0, 0)),
        ],
        scratch_shapes=[pltpu.VMEM((POSITIONS, D), jnp.bfloat16)],
        compiler_params=pltpu.CompilerParams(vmem_limit_bytes=50 << 20),
        cost_estimate=pl.CostEstimate(flops=5 * 10**9, bytes_accessed=14 << 20, transcendentals=0),
        name="stem_reduce",
    )(patches, stem, bottle, crop, masks)


def both_halves(gain_refs, first, last):
    place_ref, own_ref, other_ref = gain_refs
    own, other = own_ref[:, first:last], other_ref[:, first:last]
    lower = place_ref[0] == 0
    return jnp.concatenate([jnp.where(lower, own, other), jnp.where(lower, other, own)], 1)


def norm_rows(stat, count):
    mean = stat[0:1] / count
    return mean, lax.rsqrt(stat[1:2] / count - mean * mean + norm_eps)


def norm_middle_kernel(
    a_ref, stat_ref, place_ref, own_ref, other_ref, crop_ref, w_ref, col_ref, h_ref, ht_ref, o_ref, canvas
):
    edge = 4 * FW
    mean, scale = norm_rows(stat_ref[...], stat_ref[2:3, 0:1])
    pair = both_halves((place_ref, own_ref, other_ref), 0, MID // 2)
    gain = pair[0:1] * scale
    shift = pair[1:2] - mean * gain
    low = (crop_ref[...] * jax.nn.gelu(a_ref[...] * gain + shift)).astype(h_ref.dtype)
    h_ref[...] = low
    ht_ref[...] = low.T
    values = low.astype(jnp.float32)
    for turn in range(3):
        canvas[turn, :edge] = jnp.zeros((edge, MID), canvas.dtype)
        canvas[turn, POSITIONS + edge :] = jnp.zeros((edge, MID), canvas.dtype)
        canvas[turn, edge : POSITIONS + edge] = roll_cols(values, col_ref, 4 * (turn - 1)).astype(
            canvas.dtype
        )
    block = 400

    def step(index, carry):
        total = None
        for row in range(3):
            first = pl.multiple_of(index * block + edge * row, 16)
            for turn in range(3):
                part = dot(canvas[turn, pl.ds(first, block)], w_ref[3 * row + turn])
                total = part if total is None else total + part
        o_ref[pl.ds(pl.multiple_of(index * block, 16), block)] = total.astype(o_ref.dtype)
        return carry

    lax.fori_loop(0, POSITIONS // block, step, 0)


def norm_middle(first_pre, stat, gains, crop, weights, columns):
    return pl.pallas_call(
        norm_middle_kernel,
        out_shape=[
            jax.ShapeDtypeStruct((POSITIONS, MID), jnp.bfloat16),
            jax.ShapeDtypeStruct((MID, POSITIONS), jnp.bfloat16),
            jax.ShapeDtypeStruct((POSITIONS, MID), jnp.bfloat16),
        ],
        in_specs=vmem(2) + [pl.BlockSpec(memory_space=pltpu.SMEM)] + vmem(5),
        out_specs=vmem(3),
        scratch_shapes=[pltpu.VMEM((3, POSITIONS + 8 * FW, MID), jnp.bfloat16)],
        compiler_params=pltpu.CompilerParams(vmem_limit_bytes=50 << 20),
        cost_estimate=pl.CostEstimate(flops=8 * 10**9, bytes_accessed=14 << 20, transcendentals=0),
        name="norm_middle",
    )(first_pre, stat, *gains, crop, weights, columns)


def expand_kernel(a_ref, w_ref, crop_ref, y_ref, stat_ref):
    def step(index, carry):
        rows = block_rows(index)
        value = dot(a_ref[rows], w_ref[0], (1, 1))
        y_ref[rows] = value.astype(y_ref.dtype)
        kept = crop_ref[rows] * value
        return (
            carry[0] + jnp.sum(kept, 0, keepdims=True),
            carry[1] + jnp.sum(kept * value, 0, keepdims=True),
        )

    zero = jnp.zeros((1, D), jnp.float32)
    sums = lax.fori_loop(0, POSITIONS // BLOCK, step, (zero, zero))
    for turn, values in enumerate(sums):
        for part in range(4):
            stat_ref[4 * turn + part : 4 * turn + part + 1] = values[
                :, part * MID : (part + 1) * MID
            ]


def expand_forward(second, bottle, crop):
    return pl.pallas_call(
        expand_kernel,
        grid=(1,),
        out_shape=[
            jax.ShapeDtypeStruct((POSITIONS, D), jnp.bfloat16),
            jax.ShapeDtypeStruct((8, MID), jnp.float32),
        ],
        in_specs=[
            pl.BlockSpec((POSITIONS, MID), lambda i: (0, 0)),
            pl.BlockSpec((1, D, MID), lambda i: (1, 0, 0)),
            pl.BlockSpec((POSITIONS, 1), lambda i: (0, 0)),
        ],
        out_specs=[
            pl.BlockSpec((POSITIONS, D), lambda i: (0, 0)),
            pl.BlockSpec((8, MID), lambda i: (0, 0)),
        ],
        compiler_params=pltpu.CompilerParams(vmem_limit_bytes=50 << 20),
        cost_estimate=pl.CostEstimate(flops=4 * 10**9, bytes_accessed=12 << 20, transcendentals=0),
        name="expand_forward",
    )(second, bottle, crop)


def residual_kernel(
    p_ref, stem_ref, y_ref, stat_ref, count_ref, place_ref, own_ref, other_ref, crop_ref, x_ref, xt_ref, pool_ref
):
    count = count_ref[2:3, 0:1]
    stat = stat_ref[...]
    total = jnp.concatenate([stat[part : part + 1] for part in range(4)], 1)
    square = jnp.concatenate([stat[part : part + 1] for part in range(4, 8)], 1)
    mean = total / count
    pair = both_halves((place_ref, own_ref, other_ref), MID // 2, MID // 2 + D // 2)
    gain = pair[0:1] * lax.rsqrt(square / count - mean * mean + norm_eps)
    shift = pair[1:2] - mean * gain

    def residual(index, carry):
        rows = block_rows(index)
        value = dot(p_ref[rows], stem_ref[...], (1, 1)) + (
            y_ref[rows].astype(jnp.float32) * gain + shift
        )
        low = (crop_ref[rows] * value).astype(x_ref.dtype)
        x_ref[rows] = low
        return carry + jnp.sum(low.astype(jnp.float32), 0, keepdims=True)

    pooled = lax.fori_loop(0, POSITIONS // BLOCK, residual, jnp.zeros((1, D), jnp.float32))
    pooled = (pooled / jnp.sum(crop_ref[...], keepdims=True)).astype(jnp.bfloat16)
    pool_ref[...] = pooled.astype(jnp.float32)
    for at in range(0, D, 256):
        xt_ref[at : at + 256] = x_ref[:, at : at + 256].T


def residual_stream(patches, stem, expanded, stat, counts, gains, crop):
    low = jnp.bfloat16
    return pl.pallas_call(
        residual_kernel,
        out_shape=[
            jax.ShapeDtypeStruct((POSITIONS, D), low),
            jax.ShapeDtypeStruct((D, POSITIONS), low),
            jax.ShapeDtypeStruct((1, D), jnp.float32),
        ],
        in_specs=vmem(5) + [pl.BlockSpec(memory_space=pltpu.SMEM)] + vmem(3),
        out_specs=vmem(3),
        compiler_params=pltpu.CompilerParams(vmem_limit_bytes=50 << 20),
        cost_estimate=pl.CostEstimate(flops=2 * 10**9, bytes_accessed=22 << 20, transcendentals=0),
        name="residual_stream",
    )(patches, stem, expanded, stat, counts, *gains, crop)


def pyramid_kernel(
    x_ref,
    pool_ref,
    a_hbm,
    b_hbm,
    project_ref,
    col_ref,
    o_ref,
    pool_pre_ref,
    cat_ref,
    part_ref,
    weights,
    pool_weights,
    fields,
    sems,
):
    width = o_ref.shape[2]
    copies = []
    order = [3, 2, 4, 1, 5, 0, 6]
    starts = []
    place = 0
    for group in ROW_GROUPS:
        starts.append(place)
        place += len(group)
    for turn in order:
        group_copies = []
        for offset, (tap, _) in enumerate(ROW_GROUPS[turn]):
            slot = starts[turn] + offset
            copy = pltpu.make_async_copy(
                tap_of(a_hbm, b_hbm, tap), weights.at[:, pl.ds(slot * width, width)], sems.at[slot]
            )
            copy.start()
            group_copies.append(copy)
        copies.append(group_copies)
    pool_copy = pltpu.make_async_copy(tap_of(a_hbm, b_hbm, 28), pool_weights, sems.at[28])
    pool_copy.start()

    for turn, group_copies in zip(order, copies):
        for copy in group_copies:
            copy.wait()
        row_step = PYRAMID_ROWS[turn]
        group = ROW_GROUPS[turn]
        r0, r1 = valid(row_step, FH)
        length = (r1 - r0) * FW
        block = {1600: 800, 1120: 560, 640: 640, 160: 160}[length]
        cols = pl.ds(starts[turn] * width, len(group) * width)

        def step(index, carry):
            source = pl.multiple_of(index * block + r0 * FW, 16)
            target = pl.multiple_of(index * block + (r0 - row_step) * FW, 16)
            part = dot(x_ref[pl.ds(source, block)], weights[:, cols])
            for offset, (tap, field) in enumerate(group):
                piece = part[:, offset * width : (offset + 1) * width]
                rows = pl.ds(target, block)
                if row_step == 0:
                    fields[field, rows] = piece
                else:
                    fields[field, rows] += piece
            return carry

        lax.fori_loop(0, length // block, step, 0)
    pool_copy.wait()
    pool_pre = dot(jnp.broadcast_to(pool_ref[...], (16, D)).astype(jnp.bfloat16), pool_weights[...])[0:1]
    pool_pre_ref[...] = pool_pre
    for branch in range(4):
        values = fields[0] if branch == 0 else fields[3 * branch - 1]
        if branch:
            for turn in (0, 2):
                place = 3 * branch - 2 + turn
                values = values + roll_cols(fields[place], col_ref, FIELDS[place][1])
        o_ref[branch] = values
        cat_ref[:, branch * width : (branch + 1) * width] = jax.nn.gelu(values).astype(
            cat_ref.dtype
        )
    cat_ref[:, 4 * width :] = jnp.broadcast_to(
        jax.nn.gelu(pool_pre).astype(cat_ref.dtype), (POSITIONS, width)
    )

    def project(index, carry):
        rows = block_rows(index)
        part_ref[rows] = dot(cat_ref[rows], project_ref[:, : 5 * width], (1, 1)).astype(part_ref.dtype)
        return carry

    lax.fori_loop(0, POSITIONS // BLOCK, project, 0)


def pyramid_forward(field, pooled, weights, project, columns):
    depth, width = weights[0].shape[1:]
    low = jnp.bfloat16
    return pl.pallas_call(
        pyramid_kernel,
        out_shape=[
            jax.ShapeDtypeStruct((4, POSITIONS, width), jnp.float32),
            jax.ShapeDtypeStruct((1, width), jnp.float32),
            jax.ShapeDtypeStruct((POSITIONS, 5 * width), low),
            jax.ShapeDtypeStruct((POSITIONS, BRANCH), low),
        ],
        in_specs=vmem(2) + [pl.BlockSpec(memory_space=pltpu.HBM)] * 2 + vmem(2),
        out_specs=vmem(4),
        scratch_shapes=[
            pltpu.VMEM((depth, 28 * width), low),
            pltpu.VMEM((depth, width), low),
            pltpu.VMEM((10, POSITIONS, width), jnp.float32),
            pltpu.SemaphoreType.DMA((29,)),
        ],
        compiler_params=pltpu.CompilerParams(vmem_limit_bytes=60 << 20),
        cost_estimate=pl.CostEstimate(
            flops=2 * POSITIONS * 19 * depth * width, bytes_accessed=40 << 20, transcendentals=0
        ),
        name="pyramid_fwd",
    )(field, pooled, weights[0], weights[1], project, columns)


def head_kernel(
    own_ref,
    other_ref,
    row_ref,
    label_ref,
    target_ref,
    mask_ref,
    project_ref,
    z_ref,
    pool_pre_ref,
    feature_ref,
    logit_ref,
    mixed_ref,
    grad_ref,
    pool_ref,
    stat_ref,
):
    width = grad_ref.shape[2]
    bias, scale = row_ref[0:1], row_ref[1:2]
    class_lane, depth_lane = row_ref[2:3], row_ref[4:5]

    def step(index, carry):
        rows = block_rows(index)
        mixed = own_ref[rows].astype(jnp.float32) + other_ref[rows].astype(jnp.float32)
        feature = jax.nn.gelu(mixed).astype(feature_ref.dtype)
        feature_ref[rows] = feature
        logits = dot(feature, project_ref[:, 5 * width :]) + bias
        is_class = class_lane > 0.0
        top = jnp.max(jnp.where(is_class, logits, -jnp.inf), 1, keepdims=True)
        powers = jnp.where(is_class, jnp.exp(jnp.where(is_class, logits - top, 0.0)), 0.0)
        total = jnp.sum(powers, 1, keepdims=True)
        onehot = label_ref[rows]
        mask = mask_ref[rows]
        seg = mask[:, 0:1] * (
            top + jnp.log(total) - jnp.sum(logits * onehot, 1, keepdims=True)
        )
        is_depth = depth_lane > 0.0
        inverse = jnp.exp(-jnp.abs(logits))
        soft = jnp.maximum(logits, 0.0) + jnp.log(1.0 + inverse)
        slope = jnp.where(logits >= 0.0, 1.0, inverse) / (1.0 + inverse)
        error = jnp.where(is_depth, soft, logits) - target_ref[rows]
        root = jnp.sqrt(error * error + 1.0)
        other = error / root * jnp.where(is_depth, slope, 1.0)
        grad = scale * mask * jnp.where(is_class, powers / total - onehot, other)
        low = grad.astype(logit_ref.dtype)
        logit_ref[rows] = low
        up = gelu_slope(mixed, dot(low, project_ref[:, 5 * width :], (1, 1))).astype(mixed_ref.dtype)
        mixed_ref[rows] = up
        cat = dot(up, project_ref[:, : 5 * width])
        for branch in range(4):
            grad_ref[branch, rows] = gelu_slope(
                z_ref[branch, rows], cat[:, branch * width : (branch + 1) * width]
            ).astype(grad_ref.dtype)
        return (
            carry[0] + jnp.sum(low.astype(jnp.float32), 0, keepdims=True),
            carry[1] + jnp.sum(mask * (root - 1.0), 0, keepdims=True),
            carry[2] + jnp.sum(seg, 0, keepdims=True),
            carry[3] + jnp.sum(cat[:, 4 * width :], 0, keepdims=True),
        )

    zero = jnp.zeros((1, 128), jnp.float32)
    bias_sum, error_sum, seg_sum, pool_sum = lax.fori_loop(
        0,
        POSITIONS // BLOCK,
        step,
        (zero, zero, jnp.zeros((1, 1), jnp.float32), jnp.zeros((1, width), jnp.float32)),
    )
    pool_ref[...] = gelu_slope(pool_pre_ref[...], pool_sum).astype(jnp.bfloat16).astype(jnp.float32)
    stat_ref[...] = jnp.concatenate(
        [bias_sum, error_sum, jnp.broadcast_to(seg_sum, (1, 128)), jnp.zeros((5, 128))], 0
    )


def head_step(own, other, rows, label, target, mask, project, branches, pool_pre):
    width = branches.shape[2]
    low = jnp.bfloat16
    return pl.pallas_call(
        head_kernel,
        out_shape=[
            jax.ShapeDtypeStruct((POSITIONS, BRANCH), low),
            jax.ShapeDtypeStruct((POSITIONS, 128), low),
            jax.ShapeDtypeStruct((POSITIONS, BRANCH), low),
            jax.ShapeDtypeStruct((4, POSITIONS, width), low),
            jax.ShapeDtypeStruct((1, width), jnp.float32),
            jax.ShapeDtypeStruct((8, 128), jnp.float32),
        ],
        in_specs=vmem(9),
        out_specs=vmem(6),
        compiler_params=pltpu.CompilerParams(vmem_limit_bytes=50 << 20),
        cost_estimate=pl.CostEstimate(flops=2 * 10**9, bytes_accessed=16 << 20, transcendentals=0),
        name="head_step",
    )(own, other, rows, label, target, mask, project, branches, pool_pre)


def own_rows(stat, place_ref, first):
    lower = place_ref[0] == 0
    return jnp.concatenate(
        [
            jnp.where(lower, stat[first + part : first + part + 1], stat[first + 2 + part : first + 3 + part])
            for part in range(2)
        ],
        1,
    )


def own_norm(place_ref, stat_ref, count_ref):
    stat = stat_ref[...]
    count = count_ref[2:3, 0:1]
    mean = own_rows(stat, place_ref, 0) / count
    return mean, lax.rsqrt(own_rows(stat, place_ref, 4) / count - mean * mean + norm_eps), count


def start_rows(place_ref, sources, targets, sems):
    depth = targets[0].shape[1]
    half = pl.ds(pl.multiple_of(place_ref[0] * depth, 128), depth)
    own_hbm, first_hbm, second_hbm, y_hbm = sources
    own_ref, other_ref, y_ref = targets
    blocks = []
    for index in range(POSITIONS // BLOCK):
        rows = pl.ds(index * BLOCK, BLOCK)
        pairs = (
            (own_hbm.at[rows], own_ref.at[rows]),
            (first_hbm.at[rows], other_ref.at[rows, : depth // 2]),
            (second_hbm.at[rows], other_ref.at[rows, depth // 2 :]),
            (y_hbm.at[rows, half], y_ref.at[rows]),
        )
        copies = [
            pltpu.make_async_copy(source, target, sems.at[index, at])
            for at, (source, target) in enumerate(pairs)
        ]
        for copy in copies:
            copy.start()
        blocks.append(copies)
    return blocks


def residual_sums_kernel(
    place_ref,
    own_hbm,
    first_hbm,
    second_hbm,
    y_hbm,
    stat_ref,
    count_ref,
    crop_ref,
    head_ref,
    o_ref,
    own_ref,
    other_ref,
    y_ref,
    sems,
):
    depth = own_ref.shape[1]
    blocks = start_rows(
        place_ref, (own_hbm, first_hbm, second_hbm, y_hbm), (own_ref, other_ref, y_ref), sems
    )
    mean, scale, count = own_norm(place_ref, stat_ref, count_ref)
    sums = [jnp.zeros((1, depth), jnp.float32)] * 2
    for index, copies in enumerate(blocks):
        for copy in copies:
            copy.wait()
        rows = slice(index * BLOCK, (index + 1) * BLOCK)
        up = crop_ref[rows] * (
            own_ref[rows].astype(jnp.float32) + other_ref[rows].astype(jnp.float32)
        )
        normed = (y_ref[rows].astype(jnp.float32) - mean) * scale
        sums[0] = sums[0] + jnp.sum(up * normed, 0, keepdims=True)
        sums[1] = sums[1] + jnp.sum(up, 0, keepdims=True)
    for turn, values in enumerate(sums):
        for part in range(2):
            row = 2 * turn + part
            o_ref[row : row + 1] = values[:, part * MID : (part + 1) * MID]
    o_ref[4:5] = jnp.concatenate(
        [head_ref[0:1], head_ref[1:2], head_ref[2:3], jnp.zeros((1, 128), jnp.float32)], 1
    )
    o_ref[5:8] = jnp.zeros((3, MID), jnp.float32)


def residual_sums(place, own, other, expanded, stat, counts, crop, head_stat):
    hbm = pl.BlockSpec(memory_space=pltpu.HBM)
    return pl.pallas_call(
        residual_sums_kernel,
        out_shape=jax.ShapeDtypeStruct((8, MID), jnp.float32),
        in_specs=[pl.BlockSpec(memory_space=pltpu.SMEM)] + [hbm] * 4 + vmem(4),
        out_specs=vmem(1)[0],
        scratch_shapes=[pltpu.VMEM(own.shape, jnp.bfloat16)] * 3
        + [pltpu.SemaphoreType.DMA((POSITIONS // BLOCK, 4))],
        compiler_params=pltpu.CompilerParams(vmem_limit_bytes=60 << 20),
        cost_estimate=pl.CostEstimate(flops=10**8, bytes_accessed=12 << 20, transcendentals=0),
        name="residual_sums",
    )(place, own, *other, expanded, stat, counts, crop, head_stat)


def residual_back_kernel(
    place_ref,
    own_hbm,
    first_hbm,
    second_hbm,
    y_hbm,
    stat_ref,
    count_ref,
    sum_ref,
    gain_ref,
    crop_ref,
    bottle_hbm,
    o_ref,
    part_ref,
    own_ref,
    other_ref,
    y_ref,
    weights,
    sems,
    weight_sem,
):
    depth = own_ref.shape[1]
    half = pl.ds(pl.multiple_of(place_ref[0] * depth, 16), depth)
    weight_copy = pltpu.make_async_copy(bottle_hbm.at[1, half], weights, weight_sem)
    weight_copy.start()
    blocks = start_rows(
        place_ref, (own_hbm, first_hbm, second_hbm, y_hbm), (own_ref, other_ref, y_ref), sems
    )
    mean, scale, count = own_norm(place_ref, stat_ref, count_ref)
    sums = sum_ref[...]
    gain_grad = jnp.concatenate([sums[0:1], sums[1:2]], 1) / count
    shift_grad = jnp.concatenate([sums[2:3], sums[3:4]], 1) / count
    factor = gain_ref[0:1, MID // 2 :] * scale
    weight_copy.wait()
    for index, copies in enumerate(blocks):
        for copy in copies:
            copy.wait()
        rows = slice(index * BLOCK, (index + 1) * BLOCK)
        crop = crop_ref[rows]
        up = crop * (own_ref[rows].astype(jnp.float32) + other_ref[rows].astype(jnp.float32))
        normed = (y_ref[rows].astype(jnp.float32) - mean) * scale
        low = (crop * factor * (up - (shift_grad + normed * gain_grad))).astype(o_ref.dtype)
        o_ref[rows] = low
        part_ref[rows] = dot(low, weights[...]).astype(part_ref.dtype)


def residual_back(place, own, other, expanded, stat, counts, sums, gains, crop, bottle):
    hbm = pl.BlockSpec(memory_space=pltpu.HBM)
    depth = own.shape[1]
    return pl.pallas_call(
        residual_back_kernel,
        out_shape=[
            jax.ShapeDtypeStruct((POSITIONS, depth), jnp.bfloat16),
            jax.ShapeDtypeStruct((POSITIONS, MID), jnp.bfloat16),
        ],
        in_specs=[pl.BlockSpec(memory_space=pltpu.SMEM)] + [hbm] * 4 + vmem(5) + [hbm],
        out_specs=vmem(2),
        scratch_shapes=[pltpu.VMEM(own.shape, jnp.bfloat16)] * 3
        + [
            pltpu.VMEM((depth, MID), jnp.bfloat16),
            pltpu.SemaphoreType.DMA((POSITIONS // BLOCK, 4)),
            pltpu.SemaphoreType.DMA,
        ],
        compiler_params=pltpu.CompilerParams(vmem_limit_bytes=40 << 20),
        cost_estimate=pl.CostEstimate(flops=2 * 10**9, bytes_accessed=16 << 20, transcendentals=0),
        name="residual_back",
    )(place, own, *other, expanded, stat, counts, sums, gains, crop, bottle)


def late_kernel(
    place_ref,
    up_ref,
    a_ref,
    stat_ref,
    sum_ref,
    gain_ref,
    other_gain_ref,
    crop_ref,
    patch_ref,
    bottle_hbm,
    own_hbm,
    first_hbm,
    second_hbm,
    xt_hbm,
    reduce_ref,
    stem_ref,
    weights,
    own_ref,
    other_ref,
    xt_ref,
    low_ref,
    start_ref,
    sems,
):
    depth = own_ref.shape[1]
    half = pl.ds(pl.multiple_of(place_ref[0] * depth, 16), depth)
    copies = [
        pltpu.make_async_copy(source, target, sems.at[at])
        for at, (source, target) in enumerate(
            (
                (bottle_hbm.at[0, half], weights),
                (own_hbm, own_ref),
                (first_hbm, other_ref.at[:, : depth // 2]),
                (second_hbm, other_ref.at[:, depth // 2 :]),
                (xt_hbm, xt_ref),
            )
        )
    ]
    for copy in copies:
        copy.start()
    count = stat_ref[2:3, 0:1]
    mean, scale = norm_rows(stat_ref[...], count)
    pair = both_halves((place_ref, gain_ref, other_gain_ref), 0, MID // 2)
    factor = pair[0:1] * scale
    gain_grad = sum_ref[0:1] / count
    shift_grad = sum_ref[1:2] / count

    def step(index, carry):
        rows = block_rows(index)
        normed = (a_ref[rows] - mean) * scale
        low_ref[rows] = (
            crop_ref[rows] * factor * (up_ref[rows] - (shift_grad + normed * gain_grad))
        ).astype(low_ref.dtype)
        return carry

    lax.fori_loop(0, POSITIONS // BLOCK, step, 0)
    for copy in copies[:4]:
        copy.wait()

    def start_step(index, carry):
        rows = block_rows(index)
        total = dot(low_ref[rows], weights[...], (1, 1)) + (
            own_ref[rows].astype(jnp.float32) + other_ref[rows].astype(jnp.float32)
        )
        start_ref[rows] = (crop_ref[rows] * total).astype(start_ref.dtype)
        return carry

    lax.fori_loop(0, POSITIONS // BLOCK, start_step, 0)
    for at in range(0, depth, 256):
        part = dot(patch_ref[...], start_ref[:, at : at + 256]).astype(stem_ref.dtype)
        stem_ref[at : at + 256] = part.T
    copies[4].wait()
    low = low_ref[...]
    own_low = jnp.where(place_ref[0] == 0, low[:, : MID // 2], low[:, MID // 2 :])
    block = 512

    def reduce_step(index, carry):
        rows = pl.ds(pl.multiple_of(index * block, 16), block)
        reduce_ref[rows] = dot(xt_ref[rows], own_low).astype(reduce_ref.dtype)
        return carry

    lax.fori_loop(0, D // block, reduce_step, 0)


def late_gradients(place, up, first_pre, stat, sums, gains, crop, patches_t, bottle, own, other, xt):
    hbm = pl.BlockSpec(memory_space=pltpu.HBM)
    depth = own.shape[1]
    low = jnp.bfloat16
    return pl.pallas_call(
        late_kernel,
        out_shape=[
            jax.ShapeDtypeStruct((D, MID // 2), low),
            jax.ShapeDtypeStruct((depth, PATCH), low),
        ],
        in_specs=[pl.BlockSpec(memory_space=pltpu.SMEM)] + vmem(8) + [hbm] * 5,
        out_specs=vmem(2),
        scratch_shapes=[
            pltpu.VMEM((depth, MID), low),
            pltpu.VMEM(own.shape, low),
            pltpu.VMEM(own.shape, low),
            pltpu.VMEM(xt.shape, low),
            pltpu.VMEM((POSITIONS, MID), low),
            pltpu.VMEM(own.shape, low),
            pltpu.SemaphoreType.DMA((5,)),
        ],
        compiler_params=pltpu.CompilerParams(vmem_limit_bytes=40 << 20),
        cost_estimate=pl.CostEstimate(flops=4 * 10**9, bytes_accessed=24 << 20, transcendentals=0),
        name="late_gradients",
    )(place, up, first_pre, stat, sums, gains[1], gains[2], crop, patches_t, bottle, own, *other, xt)


def scatter_kernel(
    layers,
    p_ref,
    o_ref,
    square_ref,
    core_in,
    y_out,
    kept,
    y_in,
    z_out,
    z_in,
    core_send,
    core_recv,
    y_send,
    y_recv,
    z_send,
    z_recv,
):
    z, y, core, x = place_of()
    barrier = pltpu.get_barrier_semaphore()
    sibling = device_at(z, y, 1 - core, x)
    other_y = device_at(z, 1 - y, core, x)
    layer_order = [z_flip(z, turn) for turn in range(1, layers)]
    for target in [sibling, other_y] + [device_at(zz, y, core, x) for zz in layer_order]:
        pl.semaphore_signal(barrier, inc=1, device_id=target, device_id_type=MESH_ID)
    pl.semaphore_wait(barrier, layers + 1)
    order = layer_order + [z]
    pending = []

    def send(source, target_ref, sems, place, device):
        copy = pltpu.make_async_remote_copy(
            src_ref=source,
            dst_ref=target_ref,
            send_sem=sems[0].at[place],
            recv_sem=sems[1].at[place],
            device_id=device,
            device_id_type=MESH_ID,
        )
        copy.start()
        pending.append(copy)

    def arrive(target_ref, sems, place):
        pltpu.make_async_remote_copy(
            src_ref=target_ref,
            dst_ref=target_ref,
            send_sem=sems[0].at[place],
            recv_sem=sems[1].at[place],
            device_id=sibling,
            device_id_type=MESH_ID,
        ).wait_recv()

    core_sems, y_sems, z_sems = (core_send, core_recv), (y_send, y_recv), (z_send, z_recv)
    for zz in order:
        for yy in (1 - y, y):
            pair = zz * 2 + yy
            send(p_ref.at[pair * 2 + 1 - core], core_in.at[pair], core_sems, pair, sibling)
    for zz in order:
        for yy in (1 - y, y):
            pair = zz * 2 + yy
            arrive(core_in.at[pair], core_sems, pair)
            total = p_ref[pair * 2 + core].astype(jnp.float32) + core_in[pair].astype(jnp.float32)
            if yy is y:
                kept[zz] = total
            else:
                y_out[zz] = total.astype(y_out.dtype)
                send(y_out.at[zz], y_in.at[zz], y_sems, zz, other_y)
    for zz in order:
        arrive(y_in.at[zz], y_sems, zz)
        total = kept[zz] + y_in[zz].astype(jnp.float32)
        if zz is z:
            o_ref[...] = total
        else:
            z_out[zz] = total.astype(z_out.dtype)
            copy = pltpu.make_async_remote_copy(
                src_ref=z_out.at[zz],
                dst_ref=z_in.at[z],
                send_sem=z_send.at[zz],
                recv_sem=z_recv.at[z],
                device_id=device_at(zz, y, core, x),
                device_id_type=MESH_ID,
            )
            copy.start()
            pending.append(copy)
    for zz in layer_order:
        arrive(z_in.at[zz], z_sems, zz)
        o_ref[...] += z_in[zz].astype(jnp.float32)
    rows = o_ref.shape[0] - 48
    values = o_ref[:rows]
    small = o_ref[rows:]
    row = lax.broadcasted_iota(jnp.int32, (48, 256), 0)
    lane = lax.broadcasted_iota(jnp.int32, (48, 256), 1)
    is_head = jnp.logical_and(row % 3 == 2, lane >= 128)
    small = jnp.where(jnp.logical_and(is_head, x != 0), 0.0, small)
    squares = jnp.sum(values * values, 0, keepdims=True) + jnp.sum(small * small, 0, keepdims=True)
    square_ref[...] = jnp.concatenate(
        [squares[:, :128] + squares[:, 128:], jnp.zeros((7, 128), jnp.float32)], 0
    )
    for copy in pending:
        copy.wait_send()


def scatter_trunk(sizes, grads):
    count, rows = grads.shape[:2]
    if count != 16:
        summed = lax.psum_scatter(grads, "dp", scatter_dimension=0, tiled=True)[0]
        summed = summed.astype(jnp.float32)
        flat = jnp.square(summed).reshape(-1)
        small = 3 * 256 * (BRANCH // count)
        place = lax.rem(lax.broadcasted_iota(jnp.int32, (small,), 0), 768)
        keep = jnp.logical_or(place < 640, lax.axis_index("chan") == 0)
        total = jnp.sum(flat[:-small]) + jnp.sum(jnp.where(keep, flat[-small:], 0.0))
        return summed, jnp.pad(total.reshape(1, 1), ((0, 7), (0, 127)))
    layers = count // 4
    low = jnp.bfloat16
    return pl.pallas_call(
        functools.partial(scatter_kernel, layers),
        out_shape=[
            jax.ShapeDtypeStruct((rows, 256), jnp.float32),
            jax.ShapeDtypeStruct((8, 128), jnp.float32),
        ],
        in_specs=vmem(1),
        out_specs=vmem(2),
        scratch_shapes=[
            pltpu.VMEM((count // 2, rows, 256), low),
            pltpu.VMEM((layers, rows, 256), low),
            pltpu.VMEM((layers, rows, 256), jnp.float32),
            pltpu.VMEM((layers, rows, 256), low),
            pltpu.VMEM((layers, rows, 256), low),
            pltpu.VMEM((layers, rows, 256), low),
            pltpu.SemaphoreType.DMA((count // 2,)),
            pltpu.SemaphoreType.DMA((count // 2,)),
            pltpu.SemaphoreType.DMA((layers,)),
            pltpu.SemaphoreType.DMA((layers,)),
            pltpu.SemaphoreType.DMA((layers,)),
            pltpu.SemaphoreType.DMA((layers,)),
        ],
        compiler_params=pltpu.CompilerParams(
            collective_id=6, has_side_effects=True, vmem_limit_bytes=48 << 20
        ),
        name="scatter_trunk",
    )(grads)


def first_back_kernel(
    place_ref,
    part_ref,
    other_ref,
    w_ref,
    col_ref,
    a_ref,
    stat_ref,
    own_ref,
    gain_ref,
    crop_ref,
    up_ref,
    g_ref,
    o_ref,
    canvas,
):
    edge = 4 * FW
    values = part_ref[...].astype(jnp.float32) + other_ref[...].astype(jnp.float32)
    low = values.astype(jnp.bfloat16)
    g_ref[...] = jnp.where(place_ref[0] == 0, low[:, : MID // 2], low[:, MID // 2 :])
    values = low.astype(jnp.float32)
    for turn in range(3):
        canvas[turn, :edge] = jnp.zeros((edge, MID), canvas.dtype)
        canvas[turn, POSITIONS + edge :] = jnp.zeros((edge, MID), canvas.dtype)
        canvas[turn, edge : POSITIONS + edge] = roll_cols(values, col_ref, -4 * (turn - 1)).astype(
            canvas.dtype
        )
    mean, scale = norm_rows(stat_ref[...], stat_ref[2:3, 0:1])
    pair = both_halves((place_ref, own_ref, gain_ref), 0, MID // 2)
    block = 400

    def step(index, carry):
        total = None
        for row in range(3):
            first = pl.multiple_of(index * block + edge * (2 - row), 16)
            for turn in range(3):
                part = dot(canvas[turn, pl.ds(first, block)], w_ref[3 * row + turn], (1, 1))
                total = part if total is None else total + part
        rows = pl.ds(pl.multiple_of(index * block, 16), block)
        normed = (a_ref[rows] - mean) * scale
        up = gelu_slope(pair[0:1] * normed + pair[1:2], crop_ref[rows] * total)
        up_ref[rows] = up
        return (
            carry[0] + jnp.sum(up * normed, 0, keepdims=True),
            carry[1] + jnp.sum(up, 0, keepdims=True),
        )

    zero = jnp.zeros((1, MID), jnp.float32)
    sums = lax.fori_loop(0, POSITIONS // block, step, (zero, zero))
    o_ref[...] = jnp.concatenate([sums[0], sums[1], jnp.zeros((6, MID), jnp.float32)], 0)


def first_back(place, part, other, weights, columns, first_pre, stat, gains, crop):
    return pl.pallas_call(
        first_back_kernel,
        out_shape=[
            jax.ShapeDtypeStruct((POSITIONS, MID), jnp.float32),
            jax.ShapeDtypeStruct((POSITIONS, MID // 2), jnp.bfloat16),
            jax.ShapeDtypeStruct((8, MID), jnp.float32),
        ],
        in_specs=[pl.BlockSpec(memory_space=pltpu.SMEM)] + vmem(9),
        out_specs=vmem(3),
        scratch_shapes=[pltpu.VMEM((3, POSITIONS + 8 * FW, MID), jnp.bfloat16)],
        compiler_params=pltpu.CompilerParams(vmem_limit_bytes=50 << 20),
        cost_estimate=pl.CostEstimate(flops=8 * 10**9, bytes_accessed=20 << 20, transcendentals=0),
        name="first_back",
    )(place, part, other, weights, columns, first_pre, stat, gains[1], gains[2], crop)


ADAM_GROUPS = 8


def adam_kernel(row_share, mid_share, *refs):
    sum_ref, pyramid_ref, trunk_ref, stem_ref, small_ref, norm_ref, task_ref = refs[:7]
    states = [refs[7 + 3 * group : 10 + 3 * group] for group in range(ADAM_GROUPS)]
    base = 7 + 3 * ADAM_GROUPS
    outs = [refs[base + 3 * group : base + 3 + 3 * group] for group in range(ADAM_GROUPS)]
    norm = jnp.sqrt(jnp.sum(sum_ref[0:1], 1, keepdims=True))
    factor = clip_level / jnp.maximum(norm, clip_level)

    def update(group, at, gradient, rate, decay):
        values = [ref[at] for ref in states[group]]
        for ref, value in zip(outs[group], adam_step(*values, gradient, factor, rate, decay)):
            ref[at] = value

    def pyramid_step(tap, carry):
        update(0, tap, pyramid_ref[tap].astype(jnp.float32), (3 * D) ** (-0.5), decay_rate)
        return carry

    lax.fori_loop(0, 29, pyramid_step, 0)
    for which in range(2):
        rows = trunk_ref[which * row_share : (which + 1) * row_share]
        update(1, which, rows, D ** (-0.5), decay_rate)
    for tap in range(9):
        first = 2 * row_share + tap * mid_share
        update(2, tap, trunk_ref[first : first + mid_share], (9 * MID) ** (-0.5), decay_rate)
    every = slice(None)
    update(3, every, stem_ref[...], PATCH ** (-0.5), decay_rate)
    for branch in range(5):
        update(
            4,
            branch,
            small_ref[:, branch * 128 : (branch + 1) * 128],
            (5 * BRANCH) ** (-0.5),
            decay_rate,
        )
    update(5, every, small_ref[:, 640:662], BRANCH ** (-0.5), decay_rate)
    update(6, every, norm_ref[...], 0.3, 0.0)
    update(7, every, task_ref[:, :25], 0.3, 0.0)


def adam_all(row_share, mid_share, gradients, states):
    flat = [part for state in states for part in state]
    return pl.pallas_call(
        functools.partial(adam_kernel, row_share, mid_share),
        out_shape=[jax.ShapeDtypeStruct(part.shape, jnp.float32) for part in flat],
        in_specs=vmem(len(gradients) + len(flat)),
        out_specs=vmem(len(flat)),
        compiler_params=pltpu.CompilerParams(vmem_limit_bytes=50 << 20),
        cost_estimate=pl.CostEstimate(flops=10**8, bytes_accessed=18 << 20, transcendentals=0),
        name="adam",
    )(*gradients, *flat)


def square_kernel(
    place_ref, three_ref, four_ref, one_ref, trunk_ref, pyramid_ref, task_ref, o_ref, norm_ref, task_grad_ref, loss_ref
):
    lower = place_ref[0] == 0
    three = three_ref[...]
    four = four_ref[...]
    mid = MID // 2
    for row in range(2):
        own = jnp.where(lower, four[row : row + 1, :mid], four[row : row + 1, mid:])
        norm_ref[row : row + 1] = jnp.concatenate(
            [own, three[2 * row : 2 * row + 1], three[2 * row + 1 : 2 * row + 2]], 1
        )
    lane = lax.broadcasted_iota(jnp.int32, (1, 128), 1)
    errors = three[4:5, 128:256]

    def lane_sum(values, first, last):
        kept = jnp.where((lane >= first) & (lane < last), values, 0.0)
        return jnp.sum(kept, 1, keepdims=True)

    seg = lane_sum(three[4:5, 256:384], 0, 1)
    off = lane_sum(errors, CLASSES, CLASSES + 2)
    dep = lane_sum(errors, CLASSES + 2, CLASSES + 3)
    is_task = lane < 3
    totals = jnp.where(lane == 0, seg, jnp.where(lane == 1, off, dep))
    means = totals / jnp.where(is_task, one_ref[2:3, :128], 1.0)
    scale = jnp.where(is_task, task_ref[...], 0.0)
    weighted = jnp.exp(-scale) * means
    loss_ref[...] = lane_sum(weighted + scale, 0, 3)
    bias = pltpu.roll(jnp.broadcast_to(three[4:5, :128], (8, 128)), 3, 1)[0:1]
    task_grad = jnp.where(is_task, 1.0 - weighted, jnp.where(lane < 25, bias, 0.0))
    task_grad_ref[...] = task_grad

    def tap_square(tap, total):
        values = pyramid_ref[tap].astype(jnp.float32)
        return total + jnp.sum(values * values, 0, keepdims=True)

    squares = lax.fori_loop(0, 29, tap_square, jnp.zeros((1, 128), jnp.float32))
    first = jnp.where(place_ref[1] == 0, 1.0, 0.0)
    norms = norm_ref[...]
    norm_square = jnp.sum(jnp.sum(norms * norms, 0, keepdims=True), 1, keepdims=True)
    task_square = jnp.sum(task_grad * task_grad, 1, keepdims=True)
    extra = first * (norm_square + jnp.where(lower, 1.0, 0.0) * task_square)
    squares = squares + trunk_ref[0:1] + jnp.where(lane == 0, extra, 0.0)
    o_ref[...] = jnp.concatenate([squares, jnp.zeros((7, 128), jnp.float32)], 0)


def own_squares_of(place, stat_three, stat_four, stat_one, trunk_squares, pyramid, task):
    return pl.pallas_call(
        square_kernel,
        out_shape=[
            jax.ShapeDtypeStruct((8, 128), jnp.float32),
            jax.ShapeDtypeStruct((2, MID // 2 + D // 2), jnp.float32),
            jax.ShapeDtypeStruct((1, 128), jnp.float32),
            jax.ShapeDtypeStruct((1, 1), jnp.float32),
        ],
        in_specs=[pl.BlockSpec(memory_space=pltpu.SMEM)] + vmem(6),
        out_specs=vmem(4),
        name="own_squares",
    )(place, stat_three, stat_four, stat_one, trunk_squares, pyramid, task)


def adam_step(weight, first, second, gradient, factor, rate, decay):
    gradient = gradient * factor
    first_new = 0.5 * first + 0.5 * gradient
    second_new = 0.5 * second + 0.5 * gradient * gradient
    direction = (
        first_new / (1.0 - 0.5**STEP) / (jnp.sqrt(second_new / (1.0 - 0.5**STEP)) + adam_eps)
    )
    return (weight - rate * (direction + decay * weight), first_new, second_new)


def on_device(
    sizes,
    patches,
    labels,
    offset_target,
    offset_valid,
    depth_target,
    lidar_valid,
    crop_mask,
    stem_weight,
    stem_first,
    stem_second,
    bottle_weight,
    bottle_first,
    bottle_second,
    middle_weight,
    middle_first,
    middle_second,
    pyramid_weight,
    pyramid_first,
    pyramid_second,
    project_weight,
    project_first,
    project_second,
    head_weight,
    head_first,
    head_second,
    norm_gains,
    norm_first,
    norm_second,
    task_params,
    task_first,
    task_second,
):
    chan_place = lax.axis_index("chan")
    dp_size = sizes["dp"]
    low = jnp.bfloat16
    crop_field = crop_mask.astype(jnp.float32).reshape(POSITIONS, 1)
    count_masks = jnp.concatenate([crop_mask, offset_valid, lidar_valid], 0)
    half = D // 2
    mid_half = MID // 2

    row_share = bottle_weight.shape[1]
    mid_share = middle_weight.shape[1]
    stem_share = stem_weight.shape[2]
    project_share = project_weight.shape[2]
    head_share = head_weight.shape[0]
    stem_shard = stem_weight.astype(low).reshape(PATCH, stem_share).T
    head_shard = jnp.concatenate(
        [
            project_weight.astype(low).transpose(2, 0, 1).reshape(project_share, 5 * 128),
            jnp.pad(head_weight.astype(low), ((0, 0), (0, 128 - 22))),
        ],
        1,
    )
    bottle_low, middle_low, stem_low, head_low = gather_trunk(
        sizes, bottle_weight.astype(low), middle_weight.astype(low), stem_shard, head_shard
    )
    pyramid_shard = pyramid_weight.astype(low)
    late_shard = pyramid_shard[EARLY_TAPS:]
    pyramid_low = (
        lax.all_gather(pyramid_shard[:EARLY_TAPS], "dp", axis=1, tiled=True),
        lax.all_gather(late_shard, "dp", axis=1, tiled=True),
    )
    own_place = chan_place.reshape(1)
    own_gains = norm_gains.reshape(2, mid_half + half)
    gains = (own_place, own_gains, swap_chan(own_gains))

    def own_bottle(which):
        return lax.dynamic_slice(bottle_low, (which, chan_place * half, 0), (1, half, MID))[0]

    def own_half(values, axis):
        width = values.shape[axis] // 2
        return lax.dynamic_slice_in_dim(values, chan_place * width, width, axis)

    def other_half(values, axis):
        width = values.shape[axis] // 2
        return lax.dynamic_slice_in_dim(values, (1 - chan_place) * width, width, axis)

    columns = jnp.broadcast_to(
        lax.rem(lax.broadcasted_iota(jnp.int32, (POSITIONS, 1), 0), FW).astype(jnp.float32),
        (POSITIONS, 128),
    )
    patch_rows = patches.reshape(POSITIONS, PATCH)
    stream_t, first_pre, stat_one = stem_reduce(
        patch_rows,
        stem_low,
        bottle_low,
        crop_field,
        count_masks,
    )
    stat_one = all_sum(sizes, stat_one, ("dp",), 0)
    hidden_low, hidden_t, second_low = norm_middle(
        first_pre, stat_one, gains, crop_field, middle_low, columns
    )
    expand_pre, stat_two = expand_forward(second_low, bottle_low, crop_field)
    stat_two = all_sum(sizes, stat_two, ("dp",), 1)
    output_low, output_t, pooled = residual_stream(
        patch_rows,
        stem_low,
        expand_pre,
        stat_two,
        stat_one,
        gains,
        crop_field,
    )
    branch_pre, pool_pre, concat_low, project_part = pyramid_forward(
        output_low, pooled, pyramid_low, head_low, columns
    )
    labels, offset_valid, lidar_valid, offset_target, depth_target, stat_one, project_part = (
        lax.optimization_barrier(
            (labels, offset_valid, lidar_valid, offset_target, depth_target, stat_one, project_part)
        )
    )
    offset_field = crop_field[:, 0] * offset_valid.astype(jnp.float32).reshape(POSITIONS)
    lidar_field = crop_field[:, 0] * lidar_valid.astype(jnp.float32).reshape(POSITIONS)
    lane = lax.broadcasted_iota(jnp.int32, (1, 128), 1)
    class_lane = (lane < CLASSES).astype(jnp.float32)
    offset_lane = ((lane >= CLASSES) & (lane < CLASSES + 2)).astype(jnp.float32)
    depth_lane = (lane == CLASSES + 2).astype(jnp.float32)
    onehot = (labels.reshape(POSITIONS, 1) == lane).astype(jnp.float32)
    mask = (
        class_lane * crop_field
        + offset_lane * offset_field[:, None]
        + depth_lane * lidar_field[:, None]
    )
    target = jnp.pad(
        jnp.concatenate([offset_target[0], depth_target], 0).T,
        ((0, 0), (CLASSES, 128 - CLASSES - 3)),
    )
    task_scale = task_params[:3]
    counts = stat_one[2, :3]
    crop_total = counts[0]
    task_weights = jnp.exp(-task_scale) / counts
    lane_rows = jnp.concatenate(
        [
            jnp.pad(task_params[3:], (0, 128 - 22)).reshape(1, 128),
            task_weights[0] * class_lane
            + task_weights[1] * offset_lane
            + task_weights[2] * depth_lane,
            class_lane,
            offset_lane,
            depth_lane,
            jnp.zeros((3, 128), jnp.float32),
        ],
        0,
    )
    feature_low, logit_low, project_grad_low, branch_grads, pool_grad, head_stat = head_step(
        project_part,
        swap_chan(project_part),
        lane_rows,
        onehot,
        target,
        mask,
        head_low,
        branch_pre,
        pool_pre,
    )
    other_parts = []
    later_grads = branch_grads
    for quarter in range(2):
        part = pyramid_field(
            2 - 2 * own_place + quarter,
            half // 2,
            pyramid_low,
            later_grads,
            pool_grad,
            crop_field,
            columns,
        )
        other_parts.append(swap_chan(part))
        later_grads, part = lax.optimization_barrier((later_grads, part))
    own_part, pyramid_grad = own_gradients(
        own_place,
        pyramid_low,
        output_t,
        later_grads,
        pool_grad,
        crop_field,
        columns,
        pooled.reshape(D, 1),
    )
    small_grads = jnp.concatenate(
        [
            dot(project_grad_low, concat_low, (0, 0)).astype(low),
            dot(feature_low, logit_low, (0, 0)).astype(low),
        ],
        1,
    )
    small_rows = project_share * 3
    small_grads = small_grads.reshape(dp_size, small_rows, 256)
    first_other, own_part, pyramid_grad, small_grads = lax.optimization_barrier(
        (other_parts[0], own_part, pyramid_grad, small_grads)
    )
    other_parts, own_part, pyramid_grad = lax.optimization_barrier(
        ([first_other, other_parts[1]], own_part, pyramid_grad)
    )
    pyramid_red = lax.psum_scatter(pyramid_grad, "dp", scatter_dimension=1, tiled=True)

    stat_three = residual_sums(
        own_place, own_part, other_parts, expand_pre, stat_two, stat_one, crop_field, head_stat
    )
    stat_three = all_sum(sizes, stat_three, ("dp",), 2)
    expand_grad_low, second_part = residual_back(
        own_place,
        own_part,
        other_parts,
        expand_pre,
        stat_two,
        stat_one,
        stat_three,
        own_gains,
        crop_field,
        bottle_low,
    )
    second_other = swap_chan(second_part)
    expand_rows = dot(expand_grad_low, second_low, (0, 0)).astype(low)
    second_other, expand_rows, stat_three, own_part = lax.optimization_barrier(
        (second_other, expand_rows, stat_three, own_part)
    )
    expand_sent = swap_chan(other_half(expand_rows, 1))
    upstream_one, second_own, stat_four = first_back(
        own_place,
        second_part,
        second_other,
        middle_low,
        columns,
        first_pre,
        stat_one,
        gains,
        crop_field,
    )
    stat_four = all_sum(sizes, stat_four, ("dp",), 3)
    stat_one, stat_three, stat_four, own_part, expand_sent = lax.optimization_barrier(
        (stat_one, stat_three, stat_four, own_part, expand_sent)
    )
    reduce_grad, stem_grad = late_gradients(
        own_place,
        upstream_one,
        first_pre,
        stat_one,
        stat_four,
        gains,
        crop_field,
        patch_rows.T,
        bottle_low,
        own_part,
        other_parts,
        stream_t,
    )
    middle_grad = middle_weights(hidden_t, second_own, columns)
    expand_own = own_half(expand_rows, 1)
    expand_grad = jnp.where(
        chan_place == 0,
        jnp.concatenate([expand_own, expand_sent], 0),
        jnp.concatenate([expand_sent, expand_own], 0),
    )

    trunk_grads = jnp.concatenate(
        [
            reduce_grad.reshape(dp_size, row_share, 256),
            expand_grad.reshape(dp_size, row_share, 256),
            middle_grad.reshape(9, dp_size, mid_share, 256)
            .transpose(1, 0, 2, 3)
            .reshape(dp_size, 9 * mid_share, 256),
            stem_grad.reshape(dp_size, stem_share * PATCH // 256, 256),
            small_grads,
        ],
        1,
    )
    trunk_red, trunk_squares = scatter_trunk(sizes, trunk_grads)
    start = 2 * row_share + 9 * mid_share
    stem_rows = stem_share * PATCH // 256
    stem_red = trunk_red[start : start + stem_rows].reshape(stem_share, PATCH)
    small_red = trunk_red[start + stem_rows :].reshape(project_share, 768)
    own_squares, norm_grad, task_grad, total_loss = own_squares_of(
        jnp.stack([chan_place, lax.axis_index("dp")]),
        stat_three,
        stat_four,
        stat_one,
        trunk_squares,
        pyramid_red,
        jnp.pad(task_params[:3], (0, 125)).reshape(1, 128),
    )
    total_loss = total_loss.reshape(())
    all_squares = all_sum(sizes, own_squares, ("dp", "chan"), 4)
    grad_norm = jnp.sqrt(jnp.sum(all_squares[0]))

    def turn_stem(part):
        return part.reshape(PATCH, stem_share).T

    def turn_project(part):
        return part.transpose(0, 2, 1)

    def flat_norm(part):
        return part.reshape(2, mid_half + half)

    updated = adam_all(
        row_share,
        mid_share,
        [
            all_squares,
            pyramid_red,
            trunk_red,
            stem_red,
            small_red,
            norm_grad,
            task_grad,
        ],
        [
            (pyramid_weight, pyramid_first, pyramid_second),
            (bottle_weight, bottle_first, bottle_second),
            (middle_weight, middle_first, middle_second),
            tuple(turn_stem(part) for part in (stem_weight, stem_first, stem_second)),
            tuple(turn_project(part) for part in (project_weight, project_first, project_second)),
            (head_weight, head_first, head_second),
            tuple(flat_norm(part) for part in (norm_gains, norm_first, norm_second)),
            tuple(part.reshape(1, 25) for part in (task_params, task_first, task_second)),
        ],
    )
    groups = [updated[3 * group : 3 * group + 3] for group in range(ADAM_GROUPS)]
    new_pyramid, new_bottle, new_middle, new_stem, new_project, new_head, new_norm, new_task = groups
    new_stem = [part.T.reshape(stem_weight.shape) for part in new_stem]
    new_project = [part.transpose(0, 2, 1) for part in new_project]
    new_norm = [part.reshape(norm_gains.shape) for part in new_norm]
    new_task = [part.reshape(25) for part in new_task]
    return (
        total_loss,
        grad_norm,
        new_stem[0],
        new_stem[1],
        new_stem[2],
        new_bottle[0],
        new_bottle[1],
        new_bottle[2],
        new_middle[0],
        new_middle[1],
        new_middle[2],
        new_pyramid[0],
        new_pyramid[1],
        new_pyramid[2],
        new_project[0],
        new_project[1],
        new_project[2],
        new_head[0],
        new_head[1],
        new_head[2],
        new_norm[0],
        new_norm[1],
        new_norm[2],
        new_task[0],
        new_task[1],
        new_task[2],
    )


def solution(mesh):
    return jax.shard_map(
        functools.partial(on_device, dict(mesh.shape)),
        mesh=mesh,
        in_specs=(
            P("dp", None, None),
            P("dp", None),
            P("dp", None, None),
            P("dp", None),
            P("dp", None),
            P("dp", None),
            P("dp", None),
            P(None, "chan", "dp"),
            P(None, "chan", "dp"),
            P(None, "chan", "dp"),
            P(None, "dp", "chan"),
            P(None, "dp", "chan"),
            P(None, "dp", "chan"),
            P(None, "dp", "chan"),
            P(None, "dp", "chan"),
            P(None, "dp", "chan"),
            P(None, "dp", "chan"),
            P(None, "dp", "chan"),
            P(None, "dp", "chan"),
            P(None, "chan", "dp"),
            P(None, "chan", "dp"),
            P(None, "chan", "dp"),
            P("dp", None),
            P("dp", None),
            P("dp", None),
            P(None, "chan", None),
            P(None, "chan", None),
            P(None, "chan", None),
            P(),
            P(),
            P(),
        ),
        out_specs=(
            P(),
            P(),
            P(None, "chan", "dp"),
            P(None, "chan", "dp"),
            P(None, "chan", "dp"),
            P(None, "dp", "chan"),
            P(None, "dp", "chan"),
            P(None, "dp", "chan"),
            P(None, "dp", "chan"),
            P(None, "dp", "chan"),
            P(None, "dp", "chan"),
            P(None, "dp", "chan"),
            P(None, "dp", "chan"),
            P(None, "dp", "chan"),
            P(None, "chan", "dp"),
            P(None, "chan", "dp"),
            P(None, "chan", "dp"),
            P("dp", None),
            P("dp", None),
            P("dp", None),
            P(None, "chan", None),
            P(None, "chan", None),
            P(None, "chan", None),
            P(),
            P(),
            P(),
        ),
        check_vma=False,
    )
```

```python
import functools

import jax
import jax.numpy as jnp
from jax import lax
from jax.experimental import pallas as pl
from jax.experimental.pallas import tpu as pltpu
from jax.sharding import PartitionSpec as P

D = 2048
MID = 512
BRANCH = 256
CLASSES = 19
PATCH = 192
FH = 40
FW = 40
STEP = 10
POSITIONS = 1600


pyramid_rates = (0, 12, 24, 36)
norm_eps = 1e-05
clip_level = 0.01
adam_eps = 1e-08
decay_rate = 0.01


MESH_ID = pl.DeviceIdType.MESH


NEAR = 4


def sum_kernel(near, far, chans, x_ref, o_ref, inner, part, outer, sems_in, sems_out):
    dp = lax.axis_index("dp")
    chan = lax.axis_index("chan")
    layer, spot = lax.div(dp, near), lax.rem(dp, near)
    barrier = pltpu.get_barrier_semaphore()

    def inner_device(step):
        index = lax.rem((spot * chans + (chan if chans > 1 else 0)) + step, near * chans)
        spot_of = lax.div(index, chans)
        other = lax.rem(index, chans) if chans > 1 else chan
        return index, (layer * near + spot_of, other)

    def outer_device(step):
        index = lax.rem(layer + step, far)
        return index, (index * near + spot, chan)

    rounds = (
        (near * chans, inner_device, x_ref, inner, sems_in),
        (far, outer_device, part, outer, sems_out),
    )
    for count, device_of, source, slots, sems in rounds:

        def greet(step, carry, device_of=device_of):
            pl.semaphore_signal(
                barrier, inc=1, device_id=device_of(step)[1], device_id_type=MESH_ID
            )
            return carry

        lax.fori_loop(1, count, greet, 0)
    pl.semaphore_wait(barrier, near * chans + far - 2)
    for count, device_of, source, slots, sems in rounds:
        me = device_of(0)[0]

        def copy_of(step, slot, device_of=device_of, source=source, slots=slots, sems=sems):
            return pltpu.make_async_remote_copy(
                src_ref=source,
                dst_ref=slots.at[slot],
                send_sem=sems.at[0, step],
                recv_sem=sems.at[1, slot],
                device_id=device_of(step)[1],
                device_id_type=MESH_ID,
            )

        def start(step, carry):
            copy_of(step, me).start()
            return carry

        def arrive(step, carry):
            copy_of(step, device_of(step)[0]).wait_recv()
            return carry

        def leave(step, carry):
            copy_of(step, me).wait_send()
            return carry

        lax.fori_loop(1, count, start, 0)
        slots[me] = source[...]
        lax.fori_loop(1, count, arrive, 0)
        total = slots[0]
        for index in range(1, count):
            total = total + slots[index]
        if source is x_ref:
            part[...] = total
        else:
            o_ref[...] = total
        lax.fori_loop(1, count, leave, 0)


def all_sum(sizes, values, axes, collective):
    near, far = NEAR, sizes["dp"] // NEAR
    chans = sizes["chan"] if "chan" in axes else 1
    shape = values.shape
    return pl.pallas_call(
        functools.partial(sum_kernel, near, far, chans),
        out_shape=jax.ShapeDtypeStruct(shape, jnp.float32),
        in_specs=[pl.BlockSpec(memory_space=pltpu.VMEM)],
        out_specs=pl.BlockSpec(memory_space=pltpu.VMEM),
        scratch_shapes=[
            pltpu.VMEM((near * chans,) + shape, jnp.float32),
            pltpu.VMEM(shape, jnp.float32),
            pltpu.VMEM((far,) + shape, jnp.float32),
            pltpu.SemaphoreType.DMA((2, near * chans)),
            pltpu.SemaphoreType.DMA((2, far)),
        ],
        compiler_params=pltpu.CompilerParams(
            collective_id=collective, has_side_effects=True, vmem_limit_bytes=16 << 20
        ),
        name="small_sum",
    )(values)


def swap_chan(values):
    return lax.ppermute(values, "chan", [(0, 1), (1, 0)])


def valid(step, length):
    return max(0, step), length + min(0, step)


def taps_of(rate):
    return [((tap // 3 - 1) * rate, (tap % 3 - 1) * rate) for tap in range(9)]


def shift_field(field, row_step, col_step):
    rows, cols = field.shape[:2]
    r0, r1 = valid(row_step, rows)
    c0, c1 = valid(col_step, cols)
    return jnp.pad(
        field[r0:r1, c0:c1],
        (
            (r0 - row_step, rows - (r1 - row_step)),
            (c0 - col_step, cols - (c1 - col_step)),
            (0, 0),
        ),
    )


def gelu_grad(values, upstream):
    return jax.vjp(jax.nn.gelu, values)[1](upstream)[0]


def dot(left, right, contract=(1, 0)):
    return lax.dot_general(
        left,
        right,
        (((contract[0],), (contract[1],)), ((), ())),
        preferred_element_type=jnp.float32,
    )


def place_of():
    dp = lax.axis_index("dp")
    return lax.div(dp, 4), lax.rem(lax.div(dp, 2), 2), lax.rem(dp, 2), lax.axis_index("chan")


def device_at(z, y, core, x):
    return ((z * 2 + y) * 2 + core, x)


def flip(value, turn):
    return lax.rem(value + turn, 2)


def z_flip(z, turn):
    return flip(lax.div(z, 2), turn // 2) * 2 + flip(lax.rem(z, 2), turn % 2)


def greet_neighbours(layers):
    z, y, core, x = place_of()
    barrier = pltpu.get_barrier_semaphore()
    for target in (
        device_at(z, y, 1 - core, x),
        device_at(z, 1 - y, core, x),
        device_at(z, y, core, 1 - x),
    ):
        pl.semaphore_signal(barrier, inc=1, device_id=target, device_id_type=MESH_ID)

    @pl.when(z > 0)
    def _():
        pl.semaphore_signal(
            barrier, inc=1, device_id=device_at(z - 1, y, core, x), device_id_type=MESH_ID
        )

    @pl.when(z < layers - 1)
    def _():
        pl.semaphore_signal(
            barrier, inc=1, device_id=device_at(z + 1, y, core, x), device_id_type=MESH_ID
        )

    peers = 3 + jnp.where(z > 0, 1, 0) + jnp.where(z < layers - 1, 1, 0)
    pl.semaphore_wait(barrier, peers)


def gather_kernel(
    layers,
    bottle,
    middle,
    small,
    head,
    bottle_all,
    middle_all,
    small_all,
    head_all,
    send_sems,
    recv_sems,
    local_sems,
):
    z, y, core, x = place_of()
    rows = bottle.shape[1]
    mid_rows = middle.shape[1]
    small_rows = small.shape[0]
    head_rows = head.shape[0]
    own_refs = (bottle, middle, small, head)

    def region(kind, block):
        zz, yy, kk, xx = block
        index = (zz * 2 + yy) * 2 + kk
        cols = pl.ds(pl.multiple_of(xx * 256, 256), 256)
        if kind == 0:
            return bottle_all.at[:, pl.ds(pl.multiple_of(index * rows, 16), rows), cols]
        if kind == 1:
            return middle_all.at[:, pl.ds(pl.multiple_of(index * mid_rows, 16), mid_rows), cols]
        if kind == 3:
            return head_all.at[pl.ds(pl.multiple_of(index * head_rows, 16), head_rows)]
        first = xx * (small_all.shape[0] // 2) + index * small_rows
        return small_all.at[pl.ds(pl.multiple_of(first, 16), small_rows)]

    def semaphore(kind, block):
        zz, yy, kk, xx = block
        return recv_sems.at[kind, ((zz * 2 + yy) * 2 + kk) * 2 + xx]

    own = (z, y, core, x)
    pending = []

    def send(kind, block, target, when=None):
        copy = pltpu.make_async_remote_copy(
            src_ref=own_refs[kind] if block is own else region(kind, block),
            dst_ref=region(kind, block),
            send_sem=send_sems.at[len(pending)],
            recv_sem=semaphore(kind, block),
            device_id=target,
            device_id_type=MESH_ID,
        )
        if when is None:
            copy.start()
        else:
            pl.when(when)(copy.start)
        pending.append((when, copy))

    def arrive(kind, block):
        pltpu.make_async_remote_copy(
            src_ref=region(kind, block),
            dst_ref=region(kind, block),
            send_sem=send_sems.at[0],
            recv_sem=semaphore(kind, block),
            device_id=device_at(z, y, 1 - core, x),
            device_id_type=MESH_ID,
        ).wait_recv()

    locals_ = [
        pltpu.make_async_copy(own_refs[kind], region(kind, own), local_sems.at[kind])
        for kind in range(4)
    ]
    for copy in locals_:
        copy.start()
    greet_neighbours(layers)
    sibling = device_at(z, y, 1 - core, x)
    other_x = device_at(z, y, core, 1 - x)
    other_y = device_at(z, 1 - y, core, x)

    def along_z(kind, block):
        if block[0] is z:
            send(kind, block, device_at(z + 1, y, core, x), z < layers - 1)
            send(kind, block, device_at(z - 1, y, core, x), z > 0)
        else:
            below = block[0] < z
            ahead = z + jnp.where(below, 1, -1)
            send(
                kind,
                block,
                device_at(ahead, y, core, x),
                jnp.logical_and(ahead >= 0, ahead < layers),
            )

    for kind in (0, 1):
        along_z(kind, own)
    send(2, own, other_x)
    send(2, own, other_y)
    send(1, own, other_x)
    send(0, own, other_y)
    along_z(2, own)
    along_z(3, own)
    send(3, own, other_y)
    send(0, own, other_x)
    send(1, own, other_y)
    for kind in range(4):
        send(kind, own, sibling)

    block = (z, y, core, 1 - x)
    arrive(2, block)
    send(2, block, other_y)
    along_z(2, block)
    send(2, block, sibling)
    for xx in (x, 1 - x):
        block = (z, 1 - y, core, xx)
        arrive(2, block)
        along_z(2, block)
        send(2, block, sibling)

    for turn in range(layers):
        zz = z if turn == 0 else z_flip(z, turn)
        if turn:
            for kind, near, far in ((0, other_y, other_x), (1, other_x, other_y)):
                block = (zz, y, core, x)
                arrive(kind, block)
                along_z(kind, block)
                send(kind, block, near)
                send(kind, block, far)
                send(kind, block, sibling)
            block = (zz, y, core, x)
            arrive(3, block)
            along_z(3, block)
            send(3, block, other_y)
            send(3, block, sibling)
        block = (zz, 1 - y, core, x)
        arrive(0, block)
        send(0, block, other_x)
        send(0, block, sibling)
        block = (zz, y, core, 1 - x)
        arrive(1, block)
        send(1, block, other_y)
        send(1, block, sibling)
        if turn:
            for yy, xx in ((y, x), (y, 1 - x), (1 - y, x), (1 - y, 1 - x)):
                block = (zz, yy, core, xx)
                arrive(2, block)
                along_z(2, block)
                send(2, block, sibling)
    for turn in range(layers):
        zz = z if turn == 0 else z_flip(z, turn)
        for yy in (y, 1 - y):
            block = (zz, yy, core, 1 - x)
            arrive(0, block)
            send(0, block, sibling)
        for xx in (x, 1 - x):
            block = (zz, 1 - y, core, xx)
            arrive(1, block)
            send(1, block, sibling)
        block = (zz, 1 - y, core, x)
        arrive(3, block)
        send(3, block, sibling)
    for kind in range(4):
        for turn in range(layers):
            zz = z if turn == 0 else z_flip(z, turn)
            for yy in (y, 1 - y):
                for xx in (x, 1 - x) if kind < 3 else (x,):
                    arrive(kind, (zz, yy, 1 - core, xx))
    for copy in locals_:
        copy.wait()
    for when, copy in pending:
        if when is None:
            copy.wait_send()
        else:
            pl.when(when)(copy.wait_send)


def gather_trunk(sizes, bottle, middle, small, head):
    count = sizes["dp"]
    if count != 16 or middle.shape[1] % 16:
        packed = [
            lax.all_gather(
                lax.all_gather(part, "dp", axis=1, tiled=True), "chan", axis=2, tiled=True
            )
            for part in (bottle, middle)
        ]
        return packed + [
            lax.all_gather(small, ("chan", "dp")).reshape(D, small.shape[1]),
            lax.all_gather(head, "dp", axis=0, tiled=True),
        ]
    return pl.pallas_call(
        functools.partial(gather_kernel, count // 4),
        out_shape=[
            jax.ShapeDtypeStruct((2, D, MID), jnp.bfloat16),
            jax.ShapeDtypeStruct((9, MID, MID), jnp.bfloat16),
            jax.ShapeDtypeStruct((D, small.shape[1]), jnp.bfloat16),
            jax.ShapeDtypeStruct((BRANCH, head.shape[1]), jnp.bfloat16),
        ],
        in_specs=[pl.BlockSpec(memory_space=pl.ANY)] * 4,
        out_specs=[pl.BlockSpec(memory_space=pl.ANY)] * 4,
        scratch_shapes=[
            pltpu.SemaphoreType.DMA((176,)),
            pltpu.SemaphoreType.DMA((4, 2 * count)),
            pltpu.SemaphoreType.DMA((4,)),
        ],
        compiler_params=pltpu.CompilerParams(collective_id=5, has_side_effects=True),
        name="gather_trunk",
    )(bottle, middle, small, head)


PAD = 128
PYRAMID_ROWS = (-36, -24, -12, 0, 12, 24, 36)


def taps_by_row():
    fields = [(0, 0)] + [(rate, col * rate) for rate in (12, 24, 36) for col in (-1, 0, 1)]
    groups = []
    for row_step in PYRAMID_ROWS:
        group = []
        for place, (rate, col_step) in enumerate(fields):
            if rate == 0:
                if row_step == 0:
                    group.append((0, place))
            elif row_step == 0 or abs(row_step) == rate:
                turn = (1 if row_step > 0 else -1 if row_step < 0 else 0) + 1
                tap = 1 + 9 * (rate // 12 - 1) + 3 * turn + (col_step // rate + 1)
                group.append((tap, place))
        groups.append(group)
    return fields, groups


FIELDS, ROW_GROUPS = taps_by_row()
TAP_ORDER = [tap for group in ROW_GROUPS for tap, place in group]
PLACE_ORDER = [place for group in ROW_GROUPS for tap, place in group]


EARLY_TAPS = 10


def tap_of(early, late, tap):
    return early.at[tap] if tap < EARLY_TAPS else late.at[tap - EARLY_TAPS]


def roll_cols(values, columns, step):
    if step == 0:
        return values
    moved = pltpu.roll(values, (-step) % values.shape[0], 0)
    target = columns[:, :1] + float(step)
    return jnp.where((target >= 0.0) & (target < float(FW)), moved, 0.0)


def vmem(count):
    return [pl.BlockSpec(memory_space=pltpu.VMEM)] * count


def middle_kernel(back, x_ref, w_ref, col_ref, o_ref, canvas):
    edge = 4 * FW
    mid = x_ref.shape[1]
    values = x_ref[...].astype(jnp.float32)
    sign = -1 if back else 1
    for turn in range(3):
        canvas[turn, :edge] = jnp.zeros((edge, mid), canvas.dtype)
        canvas[turn, POSITIONS + edge :] = jnp.zeros((edge, mid), canvas.dtype)
        canvas[turn, edge : POSITIONS + edge] = roll_cols(
            values, col_ref, sign * 4 * (turn - 1)
        ).astype(canvas.dtype)
    block = 400

    def step(index, carry):
        total = None
        for row in range(3):
            first = pl.multiple_of(index * block + edge * (1 + sign * (row - 1)), 16)
            for turn in range(3):
                part = dot(
                    canvas[turn, pl.ds(first, block)],
                    w_ref[3 * row + turn],
                    (1, 1) if back else (1, 0),
                )
                total = part if total is None else total + part
        o_ref[pl.ds(pl.multiple_of(index * block, 16), block)] = total.astype(o_ref.dtype)
        return carry

    lax.fori_loop(0, POSITIONS // block, step, 0)


def middle_conv(field, weights, columns, back, dtype):
    return pl.pallas_call(
        functools.partial(middle_kernel, back),
        out_shape=jax.ShapeDtypeStruct((POSITIONS, MID), dtype),
        in_specs=vmem(3),
        out_specs=vmem(1)[0],
        scratch_shapes=[pltpu.VMEM((3, POSITIONS + 8 * FW, MID), jnp.bfloat16)],
        compiler_params=pltpu.CompilerParams(vmem_limit_bytes=40 << 20),
        cost_estimate=pl.CostEstimate(
            flops=2 * POSITIONS * 9 * MID * MID, bytes_accessed=16 << 20, transcendentals=0
        ),
        name="middle_back" if back else "middle_fwd",
    )(field, weights, columns)


def middle_weight_kernel(xt_ref, g_ref, col_ref, o_ref, fields):
    width = g_ref.shape[1]
    values = g_ref[...].astype(jnp.float32)
    for turn in range(3):
        fields[turn, :PAD] = jnp.zeros((PAD, width), fields.dtype)
        fields[turn, PAD + POSITIONS :] = jnp.zeros((PAD, width), fields.dtype)
        fields[turn, PAD : PAD + POSITIONS] = roll_cols(values, col_ref, -4 * (turn - 1)).astype(
            fields.dtype
        )
    for row in range(3):
        row_step = 4 * (row - 1)
        r0, r1 = valid(row_step, FH)
        first = r0 * FW // 128 * 128
        last = min(POSITIONS, -(-r1 * FW // 128) * 128)
        base = PAD + first - row_step * FW
        for turn in range(3):
            o_ref[3 * row + turn] = dot(
                xt_ref[:, first:last], fields[turn, base : base + last - first]
            ).astype(o_ref.dtype)


def middle_weights(field_t, grads, columns):
    depth, width = field_t.shape[0], grads.shape[1]
    return pl.pallas_call(
        middle_weight_kernel,
        out_shape=jax.ShapeDtypeStruct((9, depth, width), jnp.bfloat16),
        in_specs=vmem(3),
        out_specs=vmem(1)[0],
        scratch_shapes=[pltpu.VMEM((3, POSITIONS + 2 * PAD, width), jnp.bfloat16)],
        compiler_params=pltpu.CompilerParams(vmem_limit_bytes=40 << 20),
        cost_estimate=pl.CostEstimate(
            flops=2 * POSITIONS * 9 * depth * width, bytes_accessed=6 << 20, transcendentals=0
        ),
        name="middle_weights",
    )(field_t, grads, columns)


def fill_fields(g_ref, col_ref, fields):
    width = g_ref.shape[2]
    for place, (rate, col_step) in enumerate(FIELDS):
        fields[place, :PAD] = jnp.zeros((PAD, width), fields.dtype)
        fields[place, PAD + POSITIONS :] = jnp.zeros((PAD, width), fields.dtype)
        values = g_ref[rate // 12]
        fields[place, PAD : PAD + POSITIONS] = roll_cols(
            values.astype(jnp.float32), col_ref, -col_step
        ).astype(fields.dtype)


def start_field_copies(place_ref, a_hbm, b_hbm, depth, weights, pool_weights, sems):
    width = pool_weights.shape[1]
    rows = pl.ds(pl.multiple_of(place_ref[0] * depth, 16), depth)
    copies = [
        pltpu.make_async_copy(
            tap_of(a_hbm, b_hbm, tap).at[rows],
            weights.at[:, pl.ds(slot * width, width)],
            sems.at[slot],
        )
        for slot, tap in enumerate(TAP_ORDER)
    ]
    copies.append(
        pltpu.make_async_copy(tap_of(a_hbm, b_hbm, 28).at[rows], pool_weights, sems.at[28])
    )
    for copy in copies:
        copy.start()
    return copies


def field_products(pool_ref, crop_ref, o_ref, weights, pool_weights, fields, stack):
    width = pool_weights.shape[1]
    pooled = dot(
        jnp.broadcast_to(pool_ref[...], (16, width)).astype(jnp.bfloat16), pool_weights[...], (1, 1)
    )[0:1] / jnp.sum(crop_ref[...], keepdims=True)
    step_of = [step for step, group in zip(PYRAMID_ROWS, ROW_GROUPS) for entry in group]
    for r0, r1 in ((0, 4), (4, 12), (12, 16), (16, 24), (24, 28), (28, 36), (36, 40)):
        slots = [
            slot for slot, step in enumerate(step_of) if r0 - step >= 0 and r1 - step <= FH
        ]
        count = (r1 - r0) * FW
        for at, slot in enumerate(slots):
            base = PAD + (r0 - step_of[slot]) * FW
            stack[:count, at * width : (at + 1) * width] = fields[
                PLACE_ORDER[slot], base : base + count
            ]
        part = dot(
            stack[:count, : len(slots) * width],
            weights[:, slots[0] * width : (slots[-1] + 1) * width],
            (1, 1),
        )
        o_ref[r0 * FW : r1 * FW] = (part + crop_ref[r0 * FW : r1 * FW] * pooled).astype(
            o_ref.dtype
        )


def field_kernel(
    place_ref, a_hbm, b_hbm, g_ref, pool_ref, crop_ref, col_ref, o_ref, weights, pool_weights, fields, stack, sems
):
    copies = start_field_copies(
        place_ref, a_hbm, b_hbm, o_ref.shape[1], weights, pool_weights, sems
    )
    fill_fields(g_ref, col_ref, fields)
    for copy in copies:
        copy.wait()
    field_products(pool_ref, crop_ref, o_ref, weights, pool_weights, fields, stack)


def own_kernel(
    place_ref,
    a_hbm,
    b_hbm,
    xt_hbm,
    g_ref,
    pool_ref,
    crop_ref,
    col_ref,
    pooled_ref,
    o_ref,
    w_out,
    weights,
    pool_weights,
    fields,
    stack,
    xt_ref,
    stage,
    sems,
    xt_sem,
    out_sems,
):
    copies = start_field_copies(
        place_ref, a_hbm, b_hbm, o_ref.shape[1], weights, pool_weights, sems
    )
    xt_copy = pltpu.make_async_copy(xt_hbm, xt_ref, xt_sem)
    xt_copy.start()
    fill_fields(g_ref, col_ref, fields)
    for copy in copies:
        copy.wait()
    field_products(pool_ref, crop_ref, o_ref, weights, pool_weights, fields, stack)
    xt_copy.wait()
    width = g_ref.shape[2]
    depth = xt_ref.shape[0]
    block = 1024
    waiting = [[], []]
    turn = 0
    for row_step, group in zip(PYRAMID_ROWS, ROW_GROUPS):
        r0, r1 = valid(row_step, FH)
        first = r0 * FW // 128 * 128
        last = min(POSITIONS, -(-r1 * FW // 128) * 128)
        base = PAD + first - row_step * FW
        sets = [group[at : at + 2] for at in range(0, 10, 2)] if row_step == 0 else [group]
        for chosen in sets:
            slot = turn % 2
            turn += 1
            for copy in waiting[slot]:
                copy.wait()
            right = jnp.concatenate(
                [fields[place, base : base + last - first] for tap, place in chosen], 1
            )

            def step(index, carry):
                rows = pl.ds(pl.multiple_of(index * block, 16), block)
                part = dot(xt_ref[rows, first:last], right)
                for offset in range(len(chosen)):
                    stage[slot, offset, rows] = part[
                        :, offset * width : (offset + 1) * width
                    ].astype(stage.dtype)
                return carry

            lax.fori_loop(0, depth // block, step, 0)
            waiting[slot] = [
                pltpu.make_async_copy(
                    stage.at[slot, offset], w_out.at[tap], out_sems.at[slot, offset]
                )
                for offset, (tap, place) in enumerate(chosen)
            ]
            for copy in waiting[slot]:
                copy.start()
    slot = turn % 2
    for copy in waiting[slot]:
        copy.wait()
    stage[slot, 0] = (pooled_ref[...] * pool_ref[...]).astype(stage.dtype)
    last_copy = pltpu.make_async_copy(stage.at[slot, 0], w_out.at[28], out_sems.at[slot, 0])
    last_copy.start()
    for copy in waiting[1 - slot]:
        copy.wait()
    last_copy.wait()


def own_gradients(place, weights, field_t, grads, pool_grad, crop, columns, pooled):
    depth, width = weights[0].shape[1:]
    hbm = pl.BlockSpec(memory_space=pltpu.HBM)
    half = depth // 2
    return pl.pallas_call(
        own_kernel,
        out_shape=[
            jax.ShapeDtypeStruct((POSITIONS, half), jnp.bfloat16),
            jax.ShapeDtypeStruct((29, depth, width), jnp.bfloat16),
        ],
        in_specs=[pl.BlockSpec(memory_space=pltpu.SMEM), hbm, hbm, hbm] + vmem(5),
        out_specs=[pl.BlockSpec(memory_space=pltpu.VMEM), hbm],
        scratch_shapes=[
            pltpu.VMEM((half, 28 * width), jnp.bfloat16),
            pltpu.VMEM((half, width), jnp.bfloat16),
            pltpu.VMEM((10, POSITIONS + 2 * PAD, width), jnp.bfloat16),
            pltpu.VMEM((8 * FW, 19 * width), jnp.bfloat16),
            pltpu.VMEM((depth, POSITIONS), jnp.bfloat16),
            pltpu.VMEM((2, 3, depth, width), jnp.bfloat16),
            pltpu.SemaphoreType.DMA((29,)),
            pltpu.SemaphoreType.DMA,
            pltpu.SemaphoreType.DMA((2, 3)),
        ],
        compiler_params=pltpu.CompilerParams(vmem_limit_bytes=60 << 20),
        cost_estimate=pl.CostEstimate(flops=1000, bytes_accessed=1024, transcendentals=0),
        name="own_gradients",
    )(place, weights[0], weights[1], field_t, grads, pool_grad, crop, columns, pooled)


def pyramid_field(place, depth, weights, grads, pool_grad, crop, columns):
    width = weights[0].shape[2]
    return pl.pallas_call(
        field_kernel,
        out_shape=jax.ShapeDtypeStruct((POSITIONS, depth), jnp.bfloat16),
        in_specs=[
            pl.BlockSpec(memory_space=pltpu.SMEM),
            pl.BlockSpec(memory_space=pltpu.HBM),
            pl.BlockSpec(memory_space=pltpu.HBM),
            pl.BlockSpec(memory_space=pltpu.VMEM),
            pl.BlockSpec(memory_space=pltpu.VMEM),
            pl.BlockSpec(memory_space=pltpu.VMEM),
            pl.BlockSpec(memory_space=pltpu.VMEM),
        ],
        out_specs=vmem(1)[0],
        scratch_shapes=[
            pltpu.VMEM((depth, 28 * width), jnp.bfloat16),
            pltpu.VMEM((depth, width), jnp.bfloat16),
            pltpu.VMEM((10, POSITIONS + 2 * PAD, width), jnp.bfloat16),
            pltpu.VMEM((8 * FW, 19 * width), jnp.bfloat16),
            pltpu.SemaphoreType.DMA((29,)),
        ],
        compiler_params=pltpu.CompilerParams(vmem_limit_bytes=60 << 20),
        cost_estimate=pl.CostEstimate(
            flops=1000, bytes_accessed=1024, transcendentals=0
        ),
        name="pyramid_field",
    )(place, weights[0], weights[1], grads, pool_grad, crop, columns)


BLOCK = 320


def block_rows(index):
    return pl.ds(pl.multiple_of(index * BLOCK, 16), BLOCK)


def gelu_slope(values, upstream):
    return jax.vjp(jax.nn.gelu, values)[1](upstream)[0]


def stem_kernel(p_ref, stem_ref, reduce_ref, crop_ref, mask_ref, xt_ref, a_ref, stat_ref, x_ref):
    def step(index, carry):
        rows = block_rows(index)
        low = (crop_ref[rows] * dot(p_ref[rows], stem_ref[...], (1, 1))).astype(x_ref.dtype)
        x_ref[rows] = low
        value = dot(low, reduce_ref[0])
        a_ref[rows] = value
        return (
            carry[0] + jnp.sum(value, 0, keepdims=True),
            carry[1] + jnp.sum(value * value, 0, keepdims=True),
        )

    zero = jnp.zeros((1, MID), jnp.float32)
    total, square = lax.fori_loop(0, POSITIONS // BLOCK, step, (zero, zero))
    for at in range(0, D, 256):
        xt_ref[at : at + 256] = x_ref[:, at : at + 256].T
    masks = mask_ref[...].astype(jnp.float32)
    lane = lax.broadcasted_iota(jnp.int32, (1, MID), 1)
    counts = jnp.zeros((1, MID), jnp.float32)
    for place in range(3):
        kept = masks[0:1] if place == 0 else masks[0:1] * masks[place : place + 1]
        counts = jnp.where(lane == place, jnp.sum(kept, 1, keepdims=True), counts)
    stat_ref[...] = jnp.concatenate([total, square, counts, jnp.zeros((5, MID), jnp.float32)], 0)


def stem_reduce(patches, stem, bottle, crop, masks):
    return pl.pallas_call(
        stem_kernel,
        grid=(1,),
        out_shape=[
            jax.ShapeDtypeStruct((D, POSITIONS), jnp.bfloat16),
            jax.ShapeDtypeStruct((POSITIONS, MID), jnp.float32),
            jax.ShapeDtypeStruct((8, MID), jnp.float32),
        ],
        in_specs=[
            pl.BlockSpec((POSITIONS, PATCH), lambda i: (0, 0)),
            pl.BlockSpec(stem.shape, lambda i: (0, 0)),
            pl.BlockSpec((1, D, MID), lambda i: (0, 0, 0)),
            pl.BlockSpec((POSITIONS, 1), lambda i: (0, 0)),
            pl.BlockSpec((3, POSITIONS), lambda i: (0, 0)),
        ],
        out_specs=[
            pl.BlockSpec((D, POSITIONS), lambda i: (0, 0)),
            pl.BlockSpec((POSITIONS, MID), lambda i: (0, 0)),
            pl.BlockSpec((8, MID), lambda i: (0, 0)),
        ],
        scratch_shapes=[pltpu.VMEM((POSITIONS, D), jnp.bfloat16)],
        compiler_params=pltpu.CompilerParams(vmem_limit_bytes=50 << 20),
        cost_estimate=pl.CostEstimate(flops=5 * 10**9, bytes_accessed=14 << 20, transcendentals=0),
        name="stem_reduce",
    )(patches, stem, bottle, crop, masks)


def both_halves(gain_refs, first, last):
    place_ref, own_ref, other_ref = gain_refs
    own, other = own_ref[:, first:last], other_ref[:, first:last]
    lower = place_ref[0] == 0
    return jnp.concatenate([jnp.where(lower, own, other), jnp.where(lower, other, own)], 1)


def norm_rows(stat, count):
    mean = stat[0:1] / count
    return mean, lax.rsqrt(stat[1:2] / count - mean * mean + norm_eps)


def norm_middle_kernel(
    a_ref, stat_ref, place_ref, own_ref, other_ref, crop_ref, w_ref, col_ref, h_ref, ht_ref, o_ref, canvas
):
    edge = 4 * FW
    mean, scale = norm_rows(stat_ref[...], stat_ref[2:3, 0:1])
    pair = both_halves((place_ref, own_ref, other_ref), 0, MID // 2)
    gain = pair[0:1] * scale
    shift = pair[1:2] - mean * gain
    low = (crop_ref[...] * jax.nn.gelu(a_ref[...] * gain + shift)).astype(h_ref.dtype)
    h_ref[...] = low
    ht_ref[...] = low.T
    values = low.astype(jnp.float32)
    for turn in range(3):
        canvas[turn, :edge] = jnp.zeros((edge, MID), canvas.dtype)
        canvas[turn, POSITIONS + edge :] = jnp.zeros((edge, MID), canvas.dtype)
        canvas[turn, edge : POSITIONS + edge] = roll_cols(values, col_ref, 4 * (turn - 1)).astype(
            canvas.dtype
        )
    block = 400

    def step(index, carry):
        total = None
        for row in range(3):
            first = pl.multiple_of(index * block + edge * row, 16)
            for turn in range(3):
                part = dot(canvas[turn, pl.ds(first, block)], w_ref[3 * row + turn])
                total = part if total is None else total + part
        o_ref[pl.ds(pl.multiple_of(index * block, 16), block)] = total.astype(o_ref.dtype)
        return carry

    lax.fori_loop(0, POSITIONS // block, step, 0)


def norm_middle(first_pre, stat, gains, crop, weights, columns):
    return pl.pallas_call(
        norm_middle_kernel,
        out_shape=[
            jax.ShapeDtypeStruct((POSITIONS, MID), jnp.bfloat16),
            jax.ShapeDtypeStruct((MID, POSITIONS), jnp.bfloat16),
            jax.ShapeDtypeStruct((POSITIONS, MID), jnp.bfloat16),
        ],
        in_specs=vmem(2) + [pl.BlockSpec(memory_space=pltpu.SMEM)] + vmem(5),
        out_specs=vmem(3),
        scratch_shapes=[pltpu.VMEM((3, POSITIONS + 8 * FW, MID), jnp.bfloat16)],
        compiler_params=pltpu.CompilerParams(vmem_limit_bytes=50 << 20),
        cost_estimate=pl.CostEstimate(flops=8 * 10**9, bytes_accessed=14 << 20, transcendentals=0),
        name="norm_middle",
    )(first_pre, stat, *gains, crop, weights, columns)


def expand_kernel(a_ref, w_ref, crop_ref, y_ref, stat_ref):
    def step(index, carry):
        rows = block_rows(index)
        value = dot(a_ref[rows], w_ref[0], (1, 1))
        y_ref[rows] = value.astype(y_ref.dtype)
        kept = crop_ref[rows] * value
        return (
            carry[0] + jnp.sum(kept, 0, keepdims=True),
            carry[1] + jnp.sum(kept * value, 0, keepdims=True),
        )

    zero = jnp.zeros((1, D), jnp.float32)
    sums = lax.fori_loop(0, POSITIONS // BLOCK, step, (zero, zero))
    for turn, values in enumerate(sums):
        for part in range(4):
            stat_ref[4 * turn + part : 4 * turn + part + 1] = values[
                :, part * MID : (part + 1) * MID
            ]


def expand_forward(second, bottle, crop):
    return pl.pallas_call(
        expand_kernel,
        grid=(1,),
        out_shape=[
            jax.ShapeDtypeStruct((POSITIONS, D), jnp.bfloat16),
            jax.ShapeDtypeStruct((8, MID), jnp.float32),
        ],
        in_specs=[
            pl.BlockSpec((POSITIONS, MID), lambda i: (0, 0)),
            pl.BlockSpec((1, D, MID), lambda i: (1, 0, 0)),
            pl.BlockSpec((POSITIONS, 1), lambda i: (0, 0)),
        ],
        out_specs=[
            pl.BlockSpec((POSITIONS, D), lambda i: (0, 0)),
            pl.BlockSpec((8, MID), lambda i: (0, 0)),
        ],
        compiler_params=pltpu.CompilerParams(vmem_limit_bytes=50 << 20),
        cost_estimate=pl.CostEstimate(flops=4 * 10**9, bytes_accessed=12 << 20, transcendentals=0),
        name="expand_forward",
    )(second, bottle, crop)


def residual_kernel(
    p_ref, stem_ref, y_ref, stat_ref, count_ref, place_ref, own_ref, other_ref, crop_ref, x_ref, xt_ref, pool_ref
):
    count = count_ref[2:3, 0:1]
    stat = stat_ref[...]
    total = jnp.concatenate([stat[part : part + 1] for part in range(4)], 1)
    square = jnp.concatenate([stat[part : part + 1] for part in range(4, 8)], 1)
    mean = total / count
    pair = both_halves((place_ref, own_ref, other_ref), MID // 2, MID // 2 + D // 2)
    gain = pair[0:1] * lax.rsqrt(square / count - mean * mean + norm_eps)
    shift = pair[1:2] - mean * gain

    def residual(index, carry):
        rows = block_rows(index)
        value = dot(p_ref[rows], stem_ref[...], (1, 1)) + (
            y_ref[rows].astype(jnp.float32) * gain + shift
        )
        low = (crop_ref[rows] * value).astype(x_ref.dtype)
        x_ref[rows] = low
        return carry + jnp.sum(low.astype(jnp.float32), 0, keepdims=True)

    pooled = lax.fori_loop(0, POSITIONS // BLOCK, residual, jnp.zeros((1, D), jnp.float32))
    pooled = (pooled / jnp.sum(crop_ref[...], keepdims=True)).astype(jnp.bfloat16)
    pool_ref[...] = pooled.astype(jnp.float32)
    for at in range(0, D, 256):
        xt_ref[at : at + 256] = x_ref[:, at : at + 256].T


def residual_stream(patches, stem, expanded, stat, counts, gains, crop):
    low = jnp.bfloat16
    return pl.pallas_call(
        residual_kernel,
        out_shape=[
            jax.ShapeDtypeStruct((POSITIONS, D), low),
            jax.ShapeDtypeStruct((D, POSITIONS), low),
            jax.ShapeDtypeStruct((1, D), jnp.float32),
        ],
        in_specs=vmem(5) + [pl.BlockSpec(memory_space=pltpu.SMEM)] + vmem(3),
        out_specs=vmem(3),
        compiler_params=pltpu.CompilerParams(vmem_limit_bytes=50 << 20),
        cost_estimate=pl.CostEstimate(flops=2 * 10**9, bytes_accessed=22 << 20, transcendentals=0),
        name="residual_stream",
    )(patches, stem, expanded, stat, counts, *gains, crop)


def pyramid_kernel(
    x_ref,
    pool_ref,
    a_hbm,
    b_hbm,
    project_ref,
    col_ref,
    o_ref,
    pool_pre_ref,
    cat_ref,
    part_ref,
    weights,
    pool_weights,
    fields,
    sems,
):
    width = o_ref.shape[2]
    copies = []
    order = [3, 2, 4, 1, 5, 0, 6]
    starts = []
    place = 0
    for group in ROW_GROUPS:
        starts.append(place)
        place += len(group)
    for turn in order:
        group_copies = []
        for offset, (tap, _) in enumerate(ROW_GROUPS[turn]):
            slot = starts[turn] + offset
            copy = pltpu.make_async_copy(
                tap_of(a_hbm, b_hbm, tap), weights.at[:, pl.ds(slot * width, width)], sems.at[slot]
            )
            copy.start()
            group_copies.append(copy)
        copies.append(group_copies)
    pool_copy = pltpu.make_async_copy(tap_of(a_hbm, b_hbm, 28), pool_weights, sems.at[28])
    pool_copy.start()

    for turn, group_copies in zip(order, copies):
        for copy in group_copies:
            copy.wait()
        row_step = PYRAMID_ROWS[turn]
        group = ROW_GROUPS[turn]
        r0, r1 = valid(row_step, FH)
        length = (r1 - r0) * FW
        block = {1600: 800, 1120: 560, 640: 640, 160: 160}[length]
        cols = pl.ds(starts[turn] * width, len(group) * width)

        def step(index, carry):
            source = pl.multiple_of(index * block + r0 * FW, 16)
            target = pl.multiple_of(index * block + (r0 - row_step) * FW, 16)
            part = dot(x_ref[pl.ds(source, block)], weights[:, cols])
            for offset, (tap, field) in enumerate(group):
                piece = part[:, offset * width : (offset + 1) * width]
                rows = pl.ds(target, block)
                if row_step == 0:
                    fields[field, rows] = piece
                else:
                    fields[field, rows] += piece
            return carry

        lax.fori_loop(0, length // block, step, 0)
    pool_copy.wait()
    pool_pre = dot(jnp.broadcast_to(pool_ref[...], (16, D)).astype(jnp.bfloat16), pool_weights[...])[0:1]
    pool_pre_ref[...] = pool_pre
    for branch in range(4):
        values = fields[0] if branch == 0 else fields[3 * branch - 1]
        if branch:
            for turn in (0, 2):
                place = 3 * branch - 2 + turn
                values = values + roll_cols(fields[place], col_ref, FIELDS[place][1])
        o_ref[branch] = values
        cat_ref[:, branch * width : (branch + 1) * width] = jax.nn.gelu(values).astype(
            cat_ref.dtype
        )
    cat_ref[:, 4 * width :] = jnp.broadcast_to(
        jax.nn.gelu(pool_pre).astype(cat_ref.dtype), (POSITIONS, width)
    )

    def project(index, carry):
        rows = block_rows(index)
        part_ref[rows] = dot(cat_ref[rows], project_ref[:, : 5 * width], (1, 1)).astype(part_ref.dtype)
        return carry

    lax.fori_loop(0, POSITIONS // BLOCK, project, 0)


def pyramid_forward(field, pooled, weights, project, columns):
    depth, width = weights[0].shape[1:]
    low = jnp.bfloat16
    return pl.pallas_call(
        pyramid_kernel,
        out_shape=[
            jax.ShapeDtypeStruct((4, POSITIONS, width), jnp.float32),
            jax.ShapeDtypeStruct((1, width), jnp.float32),
            jax.ShapeDtypeStruct((POSITIONS, 5 * width), low),
            jax.ShapeDtypeStruct((POSITIONS, BRANCH), low),
        ],
        in_specs=vmem(2) + [pl.BlockSpec(memory_space=pltpu.HBM)] * 2 + vmem(2),
        out_specs=vmem(4),
        scratch_shapes=[
            pltpu.VMEM((depth, 28 * width), low),
            pltpu.VMEM((depth, width), low),
            pltpu.VMEM((10, POSITIONS, width), jnp.float32),
            pltpu.SemaphoreType.DMA((29,)),
        ],
        compiler_params=pltpu.CompilerParams(vmem_limit_bytes=60 << 20),
        cost_estimate=pl.CostEstimate(
            flops=2 * POSITIONS * 19 * depth * width, bytes_accessed=40 << 20, transcendentals=0
        ),
        name="pyramid_fwd",
    )(field, pooled, weights[0], weights[1], project, columns)


def head_kernel(
    own_ref,
    other_ref,
    row_ref,
    label_ref,
    target_ref,
    mask_ref,
    project_ref,
    z_ref,
    pool_pre_ref,
    feature_ref,
    logit_ref,
    mixed_ref,
    grad_ref,
    pool_ref,
    stat_ref,
):
    width = grad_ref.shape[2]
    bias, scale = row_ref[0:1], row_ref[1:2]
    class_lane, depth_lane = row_ref[2:3], row_ref[4:5]

    def step(index, carry):
        rows = block_rows(index)
        mixed = own_ref[rows].astype(jnp.float32) + other_ref[rows].astype(jnp.float32)
        feature = jax.nn.gelu(mixed).astype(feature_ref.dtype)
        feature_ref[rows] = feature
        logits = dot(feature, project_ref[:, 5 * width :]) + bias
        is_class = class_lane > 0.0
        top = jnp.max(jnp.where(is_class, logits, -jnp.inf), 1, keepdims=True)
        powers = jnp.where(is_class, jnp.exp(jnp.where(is_class, logits - top, 0.0)), 0.0)
        total = jnp.sum(powers, 1, keepdims=True)
        onehot = label_ref[rows]
        mask = mask_ref[rows]
        seg = mask[:, 0:1] * (
            top + jnp.log(total) - jnp.sum(logits * onehot, 1, keepdims=True)
        )
        is_depth = depth_lane > 0.0
        inverse = jnp.exp(-jnp.abs(logits))
        soft = jnp.maximum(logits, 0.0) + jnp.log(1.0 + inverse)
        slope = jnp.where(logits >= 0.0, 1.0, inverse) / (1.0 + inverse)
        error = jnp.where(is_depth, soft, logits) - target_ref[rows]
        root = jnp.sqrt(error * error + 1.0)
        other = error / root * jnp.where(is_depth, slope, 1.0)
        grad = scale * mask * jnp.where(is_class, powers / total - onehot, other)
        low = grad.astype(logit_ref.dtype)
        logit_ref[rows] = low
        up = gelu_slope(mixed, dot(low, project_ref[:, 5 * width :], (1, 1))).astype(mixed_ref.dtype)
        mixed_ref[rows] = up
        cat = dot(up, project_ref[:, : 5 * width])
        for branch in range(4):
            grad_ref[branch, rows] = gelu_slope(
                z_ref[branch, rows], cat[:, branch * width : (branch + 1) * width]
            ).astype(grad_ref.dtype)
        return (
            carry[0] + jnp.sum(low.astype(jnp.float32), 0, keepdims=True),
            carry[1] + jnp.sum(mask * (root - 1.0), 0, keepdims=True),
            carry[2] + jnp.sum(seg, 0, keepdims=True),
            carry[3] + jnp.sum(cat[:, 4 * width :], 0, keepdims=True),
        )

    zero = jnp.zeros((1, 128), jnp.float32)
    bias_sum, error_sum, seg_sum, pool_sum = lax.fori_loop(
        0,
        POSITIONS // BLOCK,
        step,
        (zero, zero, jnp.zeros((1, 1), jnp.float32), jnp.zeros((1, width), jnp.float32)),
    )
    pool_ref[...] = gelu_slope(pool_pre_ref[...], pool_sum).astype(jnp.bfloat16).astype(jnp.float32)
    stat_ref[...] = jnp.concatenate(
        [bias_sum, error_sum, jnp.broadcast_to(seg_sum, (1, 128)), jnp.zeros((5, 128))], 0
    )


def head_step(own, other, rows, label, target, mask, project, branches, pool_pre):
    width = branches.shape[2]
    low = jnp.bfloat16
    return pl.pallas_call(
        head_kernel,
        out_shape=[
            jax.ShapeDtypeStruct((POSITIONS, BRANCH), low),
            jax.ShapeDtypeStruct((POSITIONS, 128), low),
            jax.ShapeDtypeStruct((POSITIONS, BRANCH), low),
            jax.ShapeDtypeStruct((4, POSITIONS, width), low),
            jax.ShapeDtypeStruct((1, width), jnp.float32),
            jax.ShapeDtypeStruct((8, 128), jnp.float32),
        ],
        in_specs=vmem(9),
        out_specs=vmem(6),
        compiler_params=pltpu.CompilerParams(vmem_limit_bytes=50 << 20),
        cost_estimate=pl.CostEstimate(flops=2 * 10**9, bytes_accessed=16 << 20, transcendentals=0),
        name="head_step",
    )(own, other, rows, label, target, mask, project, branches, pool_pre)


def own_rows(stat, place_ref, first):
    lower = place_ref[0] == 0
    return jnp.concatenate(
        [
            jnp.where(lower, stat[first + part : first + part + 1], stat[first + 2 + part : first + 3 + part])
            for part in range(2)
        ],
        1,
    )


def own_norm(place_ref, stat_ref, count_ref):
    stat = stat_ref[...]
    count = count_ref[2:3, 0:1]
    mean = own_rows(stat, place_ref, 0) / count
    return mean, lax.rsqrt(own_rows(stat, place_ref, 4) / count - mean * mean + norm_eps), count


def start_rows(place_ref, sources, targets, sems):
    depth = targets[0].shape[1]
    half = pl.ds(pl.multiple_of(place_ref[0] * depth, 128), depth)
    own_hbm, first_hbm, second_hbm, y_hbm = sources
    own_ref, other_ref, y_ref = targets
    blocks = []
    for index in range(POSITIONS // BLOCK):
        rows = pl.ds(index * BLOCK, BLOCK)
        pairs = (
            (own_hbm.at[rows], own_ref.at[rows]),
            (first_hbm.at[rows], other_ref.at[rows, : depth // 2]),
            (second_hbm.at[rows], other_ref.at[rows, depth // 2 :]),
            (y_hbm.at[rows, half], y_ref.at[rows]),
        )
        copies = [
            pltpu.make_async_copy(source, target, sems.at[index, at])
            for at, (source, target) in enumerate(pairs)
        ]
        for copy in copies:
            copy.start()
        blocks.append(copies)
    return blocks


def residual_kernel_back(
    near,
    far,
    own_hbm,
    first_hbm,
    second_hbm,
    y_hbm,
    stat_ref,
    count_ref,
    gain_ref,
    crop_ref,
    head_ref,
    bottle_hbm,
    o_ref,
    part_ref,
    sum_ref,
    own_ref,
    other_ref,
    y_ref,
    weights,
    local_ref,
    inner,
    layer_ref,
    outer,
    sems,
    weight_sem,
    sems_in,
    sems_out,
):
    place = [lax.axis_index("chan")]
    depth = own_ref.shape[1]
    half = pl.ds(pl.multiple_of(place[0] * depth, 128), depth)
    weight_copy = pltpu.make_async_copy(bottle_hbm.at[1, half], weights, weight_sem)
    blocks = start_rows(
        place, (own_hbm, first_hbm, second_hbm, y_hbm), (own_ref, other_ref, y_ref), sems
    )
    weight_copy.start()
    mean, scale, count = own_norm(place, stat_ref, count_ref)

    def upstream(rows):
        up = crop_ref[rows] * (
            own_ref[rows].astype(jnp.float32) + other_ref[rows].astype(jnp.float32)
        )
        return up, (y_ref[rows].astype(jnp.float32) - mean) * scale

    sums = [jnp.zeros((1, depth), jnp.float32)] * 2
    for index, copies in enumerate(blocks):
        for copy in copies:
            copy.wait()
        up, normed = upstream(slice(index * BLOCK, (index + 1) * BLOCK))
        sums[0] = sums[0] + jnp.sum(up * normed, 0, keepdims=True)
        sums[1] = sums[1] + jnp.sum(up, 0, keepdims=True)
    weight_copy.wait()
    for turn, values in enumerate(sums):
        for part in range(2):
            row = 2 * turn + part
            local_ref[row : row + 1] = values[:, part * MID : (part + 1) * MID]
    local_ref[4:5] = jnp.concatenate(
        [head_ref[0:1], head_ref[1:2], head_ref[2:3], jnp.zeros((1, 128), jnp.float32)], 1
    )
    local_ref[5:8] = jnp.zeros((3, MID), jnp.float32)
    sum_kernel(near, far, 1, local_ref, sum_ref, inner, layer_ref, outer, sems_in, sems_out)
    total = sum_ref[...]
    gain_grad = jnp.concatenate([total[0:1], total[1:2]], 1) / count
    shift_grad = jnp.concatenate([total[2:3], total[3:4]], 1) / count
    factor = gain_ref[0:1, MID // 2 :] * scale

    def step(index, carry):
        rows = block_rows(index)
        up, normed = upstream(rows)
        low = (crop_ref[rows] * factor * (up - (shift_grad + normed * gain_grad))).astype(
            o_ref.dtype
        )
        o_ref[rows] = low
        part_ref[rows] = dot(low, weights[...]).astype(part_ref.dtype)
        return carry

    lax.fori_loop(0, POSITIONS // BLOCK, step, 0)


def residual_back(sizes, own, other, expanded, stat, counts, gains, crop, head_stat, bottle):
    hbm = pl.BlockSpec(memory_space=pltpu.HBM)
    depth = own.shape[1]
    near, far = NEAR, sizes["dp"] // NEAR
    shape = (8, MID)
    return pl.pallas_call(
        functools.partial(residual_kernel_back, near, far),
        out_shape=[
            jax.ShapeDtypeStruct((POSITIONS, depth), jnp.bfloat16),
            jax.ShapeDtypeStruct((POSITIONS, MID), jnp.bfloat16),
            jax.ShapeDtypeStruct(shape, jnp.float32),
        ],
        in_specs=[hbm] * 4 + vmem(5) + [hbm],
        out_specs=vmem(3),
        scratch_shapes=[pltpu.VMEM(own.shape, jnp.bfloat16)] * 3
        + [
            pltpu.VMEM((depth, MID), jnp.bfloat16),
            pltpu.VMEM(shape, jnp.float32),
            pltpu.VMEM((near,) + shape, jnp.float32),
            pltpu.VMEM(shape, jnp.float32),
            pltpu.VMEM((far,) + shape, jnp.float32),
            pltpu.SemaphoreType.DMA((POSITIONS // BLOCK, 4)),
            pltpu.SemaphoreType.DMA,
            pltpu.SemaphoreType.DMA((2, near)),
            pltpu.SemaphoreType.DMA((2, far)),
        ],
        compiler_params=pltpu.CompilerParams(
            collective_id=2, has_side_effects=True, vmem_limit_bytes=60 << 20
        ),
        cost_estimate=pl.CostEstimate(flops=2 * 10**9, bytes_accessed=16 << 20, transcendentals=0),
        name="residual_back",
    )(own, *other, expanded, stat, counts, gains, crop, head_stat, bottle)


def late_kernel(
    place_ref,
    up_ref,
    a_ref,
    stat_ref,
    sum_ref,
    gain_ref,
    other_gain_ref,
    crop_ref,
    patch_ref,
    bottle_hbm,
    own_hbm,
    first_hbm,
    second_hbm,
    xt_hbm,
    reduce_ref,
    stem_ref,
    weights,
    own_ref,
    other_ref,
    xt_ref,
    low_ref,
    start_ref,
    sems,
):
    depth = own_ref.shape[1]
    half = pl.ds(pl.multiple_of(place_ref[0] * depth, 16), depth)
    copies = [
        pltpu.make_async_copy(source, target, sems.at[at])
        for at, (source, target) in enumerate(
            (
                (bottle_hbm.at[0, half], weights),
                (own_hbm, own_ref),
                (first_hbm, other_ref.at[:, : depth // 2]),
                (second_hbm, other_ref.at[:, depth // 2 :]),
                (xt_hbm, xt_ref),
            )
        )
    ]
    for copy in copies:
        copy.start()
    count = stat_ref[2:3, 0:1]
    mean, scale = norm_rows(stat_ref[...], count)
    pair = both_halves((place_ref, gain_ref, other_gain_ref), 0, MID // 2)
    factor = pair[0:1] * scale
    gain_grad = sum_ref[0:1] / count
    shift_grad = sum_ref[1:2] / count

    def step(index, carry):
        rows = block_rows(index)
        normed = (a_ref[rows] - mean) * scale
        low_ref[rows] = (
            crop_ref[rows] * factor * (up_ref[rows] - (shift_grad + normed * gain_grad))
        ).astype(low_ref.dtype)
        return carry

    lax.fori_loop(0, POSITIONS // BLOCK, step, 0)
    for copy in copies[:4]:
        copy.wait()

    def start_step(index, carry):
        rows = block_rows(index)
        total = dot(low_ref[rows], weights[...], (1, 1)) + (
            own_ref[rows].astype(jnp.float32) + other_ref[rows].astype(jnp.float32)
        )
        start_ref[rows] = (crop_ref[rows] * total).astype(start_ref.dtype)
        return carry

    lax.fori_loop(0, POSITIONS // BLOCK, start_step, 0)
    for at in range(0, depth, 256):
        part = dot(patch_ref[...], start_ref[:, at : at + 256]).astype(stem_ref.dtype)
        stem_ref[at : at + 256] = part.T
    copies[4].wait()
    low = low_ref[...]
    own_low = jnp.where(place_ref[0] == 0, low[:, : MID // 2], low[:, MID // 2 :])
    block = 512

    def reduce_step(index, carry):
        rows = pl.ds(pl.multiple_of(index * block, 16), block)
        reduce_ref[rows] = dot(xt_ref[rows], own_low).astype(reduce_ref.dtype)
        return carry

    lax.fori_loop(0, D // block, reduce_step, 0)


def late_gradients(place, up, first_pre, stat, sums, gains, crop, patches_t, bottle, own, other, xt):
    hbm = pl.BlockSpec(memory_space=pltpu.HBM)
    depth = own.shape[1]
    low = jnp.bfloat16
    return pl.pallas_call(
        late_kernel,
        out_shape=[
            jax.ShapeDtypeStruct((D, MID // 2), low),
            jax.ShapeDtypeStruct((depth, PATCH), low),
        ],
        in_specs=[pl.BlockSpec(memory_space=pltpu.SMEM)] + vmem(8) + [hbm] * 5,
        out_specs=vmem(2),
        scratch_shapes=[
            pltpu.VMEM((depth, MID), low),
            pltpu.VMEM(own.shape, low),
            pltpu.VMEM(own.shape, low),
            pltpu.VMEM(xt.shape, low),
            pltpu.VMEM((POSITIONS, MID), low),
            pltpu.VMEM(own.shape, low),
            pltpu.SemaphoreType.DMA((5,)),
        ],
        compiler_params=pltpu.CompilerParams(vmem_limit_bytes=40 << 20),
        cost_estimate=pl.CostEstimate(flops=4 * 10**9, bytes_accessed=24 << 20, transcendentals=0),
        name="late_gradients",
    )(place, up, first_pre, stat, sums, gains[1], gains[2], crop, patches_t, bottle, own, *other, xt)


def scatter_kernel(
    layers,
    p_ref,
    o_ref,
    square_ref,
    core_in,
    y_out,
    kept,
    y_in,
    z_out,
    z_in,
    core_send,
    core_recv,
    y_send,
    y_recv,
    z_send,
    z_recv,
):
    z, y, core, x = place_of()
    barrier = pltpu.get_barrier_semaphore()
    sibling = device_at(z, y, 1 - core, x)
    other_y = device_at(z, 1 - y, core, x)
    layer_order = [z_flip(z, turn) for turn in range(1, layers)]
    for target in [sibling, other_y] + [device_at(zz, y, core, x) for zz in layer_order]:
        pl.semaphore_signal(barrier, inc=1, device_id=target, device_id_type=MESH_ID)
    pl.semaphore_wait(barrier, layers + 1)
    order = layer_order + [z]
    pending = []

    def send(source, target_ref, sems, place, device):
        copy = pltpu.make_async_remote_copy(
            src_ref=source,
            dst_ref=target_ref,
            send_sem=sems[0].at[place],
            recv_sem=sems[1].at[place],
            device_id=device,
            device_id_type=MESH_ID,
        )
        copy.start()
        pending.append(copy)

    def arrive(target_ref, sems, place):
        pltpu.make_async_remote_copy(
            src_ref=target_ref,
            dst_ref=target_ref,
            send_sem=sems[0].at[place],
            recv_sem=sems[1].at[place],
            device_id=sibling,
            device_id_type=MESH_ID,
        ).wait_recv()

    core_sems, y_sems, z_sems = (core_send, core_recv), (y_send, y_recv), (z_send, z_recv)
    for zz in order:
        for yy in (1 - y, y):
            pair = zz * 2 + yy
            send(p_ref.at[pair * 2 + 1 - core], core_in.at[pair], core_sems, pair, sibling)
    for zz in order:
        for yy in (1 - y, y):
            pair = zz * 2 + yy
            arrive(core_in.at[pair], core_sems, pair)
            total = p_ref[pair * 2 + core].astype(jnp.float32) + core_in[pair].astype(jnp.float32)
            if yy is y:
                kept[zz] = total
            else:
                y_out[zz] = total.astype(y_out.dtype)
                send(y_out.at[zz], y_in.at[zz], y_sems, zz, other_y)
    for zz in order:
        arrive(y_in.at[zz], y_sems, zz)
        total = kept[zz] + y_in[zz].astype(jnp.float32)
        if zz is z:
            o_ref[...] = total
        else:
            z_out[zz] = total.astype(z_out.dtype)
            copy = pltpu.make_async_remote_copy(
                src_ref=z_out.at[zz],
                dst_ref=z_in.at[z],
                send_sem=z_send.at[zz],
                recv_sem=z_recv.at[z],
                device_id=device_at(zz, y, core, x),
                device_id_type=MESH_ID,
            )
            copy.start()
            pending.append(copy)
    for zz in layer_order:
        arrive(z_in.at[zz], z_sems, zz)
        o_ref[...] += z_in[zz].astype(jnp.float32)
    rows = o_ref.shape[0] - 48
    values = o_ref[:rows]
    small = o_ref[rows:]
    row = lax.broadcasted_iota(jnp.int32, (48, 256), 0)
    lane = lax.broadcasted_iota(jnp.int32, (48, 256), 1)
    is_head = jnp.logical_and(row % 3 == 2, lane >= 128)
    small = jnp.where(jnp.logical_and(is_head, x != 0), 0.0, small)
    squares = jnp.sum(values * values, 0, keepdims=True) + jnp.sum(small * small, 0, keepdims=True)
    square_ref[...] = jnp.concatenate(
        [squares[:, :128] + squares[:, 128:], jnp.zeros((7, 128), jnp.float32)], 0
    )
    for copy in pending:
        copy.wait_send()


def scatter_trunk(sizes, grads):
    count, rows = grads.shape[:2]
    if count != 16:
        summed = lax.psum_scatter(grads, "dp", scatter_dimension=0, tiled=True)[0]
        summed = summed.astype(jnp.float32)
        flat = jnp.square(summed).reshape(-1)
        small = 3 * 256 * (BRANCH // count)
        place = lax.rem(lax.broadcasted_iota(jnp.int32, (small,), 0), 768)
        keep = jnp.logical_or(place < 640, lax.axis_index("chan") == 0)
        total = jnp.sum(flat[:-small]) + jnp.sum(jnp.where(keep, flat[-small:], 0.0))
        return summed, jnp.pad(total.reshape(1, 1), ((0, 7), (0, 127)))
    layers = count // 4
    low = jnp.bfloat16
    return pl.pallas_call(
        functools.partial(scatter_kernel, layers),
        out_shape=[
            jax.ShapeDtypeStruct((rows, 256), jnp.float32),
            jax.ShapeDtypeStruct((8, 128), jnp.float32),
        ],
        in_specs=vmem(1),
        out_specs=vmem(2),
        scratch_shapes=[
            pltpu.VMEM((count // 2, rows, 256), low),
            pltpu.VMEM((layers, rows, 256), low),
            pltpu.VMEM((layers, rows, 256), jnp.float32),
            pltpu.VMEM((layers, rows, 256), low),
            pltpu.VMEM((layers, rows, 256), low),
            pltpu.VMEM((layers, rows, 256), low),
            pltpu.SemaphoreType.DMA((count // 2,)),
            pltpu.SemaphoreType.DMA((count // 2,)),
            pltpu.SemaphoreType.DMA((layers,)),
            pltpu.SemaphoreType.DMA((layers,)),
            pltpu.SemaphoreType.DMA((layers,)),
            pltpu.SemaphoreType.DMA((layers,)),
        ],
        compiler_params=pltpu.CompilerParams(
            collective_id=6, has_side_effects=True, vmem_limit_bytes=48 << 20
        ),
        name="scatter_trunk",
    )(grads)


def first_back_kernel(
    place_ref,
    part_ref,
    other_ref,
    w_ref,
    col_ref,
    a_ref,
    stat_ref,
    own_ref,
    gain_ref,
    crop_ref,
    up_ref,
    g_ref,
    o_ref,
    canvas,
):
    edge = 4 * FW
    values = part_ref[...].astype(jnp.float32) + other_ref[...].astype(jnp.float32)
    low = values.astype(jnp.bfloat16)
    g_ref[...] = jnp.where(place_ref[0] == 0, low[:, : MID // 2], low[:, MID // 2 :])
    values = low.astype(jnp.float32)
    for turn in range(3):
        canvas[turn, :edge] = jnp.zeros((edge, MID), canvas.dtype)
        canvas[turn, POSITIONS + edge :] = jnp.zeros((edge, MID), canvas.dtype)
        canvas[turn, edge : POSITIONS + edge] = roll_cols(values, col_ref, -4 * (turn - 1)).astype(
            canvas.dtype
        )
    mean, scale = norm_rows(stat_ref[...], stat_ref[2:3, 0:1])
    pair = both_halves((place_ref, own_ref, gain_ref), 0, MID // 2)
    block = 400

    def step(index, carry):
        total = None
        for row in range(3):
            first = pl.multiple_of(index * block + edge * (2 - row), 16)
            for turn in range(3):
                part = dot(canvas[turn, pl.ds(first, block)], w_ref[3 * row + turn], (1, 1))
                total = part if total is None else total + part
        rows = pl.ds(pl.multiple_of(index * block, 16), block)
        normed = (a_ref[rows] - mean) * scale
        up = gelu_slope(pair[0:1] * normed + pair[1:2], crop_ref[rows] * total)
        up_ref[rows] = up
        return (
            carry[0] + jnp.sum(up * normed, 0, keepdims=True),
            carry[1] + jnp.sum(up, 0, keepdims=True),
        )

    zero = jnp.zeros((1, MID), jnp.float32)
    sums = lax.fori_loop(0, POSITIONS // block, step, (zero, zero))
    o_ref[...] = jnp.concatenate([sums[0], sums[1], jnp.zeros((6, MID), jnp.float32)], 0)


def first_back(place, part, other, weights, columns, first_pre, stat, gains, crop):
    return pl.pallas_call(
        first_back_kernel,
        out_shape=[
            jax.ShapeDtypeStruct((POSITIONS, MID), jnp.float32),
            jax.ShapeDtypeStruct((POSITIONS, MID // 2), jnp.bfloat16),
            jax.ShapeDtypeStruct((8, MID), jnp.float32),
        ],
        in_specs=[pl.BlockSpec(memory_space=pltpu.SMEM)] + vmem(9),
        out_specs=vmem(3),
        scratch_shapes=[pltpu.VMEM((3, POSITIONS + 8 * FW, MID), jnp.bfloat16)],
        compiler_params=pltpu.CompilerParams(vmem_limit_bytes=50 << 20),
        cost_estimate=pl.CostEstimate(flops=8 * 10**9, bytes_accessed=20 << 20, transcendentals=0),
        name="first_back",
    )(place, part, other, weights, columns, first_pre, stat, gains[1], gains[2], crop)


ADAM_GROUPS = 8


def adam_kernel(row_share, mid_share, *refs):
    sum_ref, pyramid_ref, trunk_ref, stem_ref, small_ref, norm_ref, task_ref = refs[:7]
    states = [refs[7 + 3 * group : 10 + 3 * group] for group in range(ADAM_GROUPS)]
    base = 7 + 3 * ADAM_GROUPS
    outs = [refs[base + 3 * group : base + 3 + 3 * group] for group in range(ADAM_GROUPS)]
    norm = jnp.sqrt(jnp.sum(sum_ref[0:1], 1, keepdims=True))
    factor = clip_level / jnp.maximum(norm, clip_level)

    def update(group, at, gradient, rate, decay):
        values = [ref[at] for ref in states[group]]
        for ref, value in zip(outs[group], adam_step(*values, gradient, factor, rate, decay)):
            ref[at] = value

    def pyramid_step(tap, carry):
        update(0, tap, pyramid_ref[tap].astype(jnp.float32), (3 * D) ** (-0.5), decay_rate)
        return carry

    lax.fori_loop(0, 29, pyramid_step, 0)
    for which in range(2):
        rows = trunk_ref[which * row_share : (which + 1) * row_share]
        update(1, which, rows, D ** (-0.5), decay_rate)
    for tap in range(9):
        first = 2 * row_share + tap * mid_share
        update(2, tap, trunk_ref[first : first + mid_share], (9 * MID) ** (-0.5), decay_rate)
    every = slice(None)
    update(3, every, stem_ref[...], PATCH ** (-0.5), decay_rate)
    for branch in range(5):
        update(
            4,
            branch,
            small_ref[:, branch * 128 : (branch + 1) * 128],
            (5 * BRANCH) ** (-0.5),
            decay_rate,
        )
    update(5, every, small_ref[:, 640:662], BRANCH ** (-0.5), decay_rate)
    update(6, every, norm_ref[...], 0.3, 0.0)
    update(7, every, task_ref[:, :25], 0.3, 0.0)


def adam_all(row_share, mid_share, gradients, states):
    flat = [part for state in states for part in state]
    return pl.pallas_call(
        functools.partial(adam_kernel, row_share, mid_share),
        out_shape=[jax.ShapeDtypeStruct(part.shape, jnp.float32) for part in flat],
        in_specs=vmem(len(gradients) + len(flat)),
        out_specs=vmem(len(flat)),
        compiler_params=pltpu.CompilerParams(vmem_limit_bytes=50 << 20),
        cost_estimate=pl.CostEstimate(flops=10**8, bytes_accessed=18 << 20, transcendentals=0),
        name="adam",
    )(*gradients, *flat)


def square_kernel(
    place_ref, three_ref, four_ref, one_ref, trunk_ref, pyramid_ref, task_ref, o_ref, norm_ref, task_grad_ref, loss_ref
):
    lower = place_ref[0] == 0
    three = three_ref[...]
    four = four_ref[...]
    mid = MID // 2
    for row in range(2):
        own = jnp.where(lower, four[row : row + 1, :mid], four[row : row + 1, mid:])
        norm_ref[row : row + 1] = jnp.concatenate(
            [own, three[2 * row : 2 * row + 1], three[2 * row + 1 : 2 * row + 2]], 1
        )
    lane = lax.broadcasted_iota(jnp.int32, (1, 128), 1)
    errors = three[4:5, 128:256]

    def lane_sum(values, first, last):
        kept = jnp.where((lane >= first) & (lane < last), values, 0.0)
        return jnp.sum(kept, 1, keepdims=True)

    seg = lane_sum(three[4:5, 256:384], 0, 1)
    off = lane_sum(errors, CLASSES, CLASSES + 2)
    dep = lane_sum(errors, CLASSES + 2, CLASSES + 3)
    is_task = lane < 3
    totals = jnp.where(lane == 0, seg, jnp.where(lane == 1, off, dep))
    means = totals / jnp.where(is_task, one_ref[2:3, :128], 1.0)
    scale = jnp.where(is_task, task_ref[...], 0.0)
    weighted = jnp.exp(-scale) * means
    loss_ref[...] = lane_sum(weighted + scale, 0, 3)
    bias = pltpu.roll(jnp.broadcast_to(three[4:5, :128], (8, 128)), 3, 1)[0:1]
    task_grad = jnp.where(is_task, 1.0 - weighted, jnp.where(lane < 25, bias, 0.0))
    task_grad_ref[...] = task_grad

    def tap_square(tap, total):
        values = pyramid_ref[tap].astype(jnp.float32)
        return total + jnp.sum(values * values, 0, keepdims=True)

    squares = lax.fori_loop(0, 29, tap_square, jnp.zeros((1, 128), jnp.float32))
    first = jnp.where(place_ref[1] == 0, 1.0, 0.0)
    norms = norm_ref[...]
    norm_square = jnp.sum(jnp.sum(norms * norms, 0, keepdims=True), 1, keepdims=True)
    task_square = jnp.sum(task_grad * task_grad, 1, keepdims=True)
    extra = first * (norm_square + jnp.where(lower, 1.0, 0.0) * task_square)
    squares = squares + trunk_ref[0:1] + jnp.where(lane == 0, extra, 0.0)
    o_ref[...] = jnp.concatenate([squares, jnp.zeros((7, 128), jnp.float32)], 0)


def own_squares_of(place, stat_three, stat_four, stat_one, trunk_squares, pyramid, task):
    return pl.pallas_call(
        square_kernel,
        out_shape=[
            jax.ShapeDtypeStruct((8, 128), jnp.float32),
            jax.ShapeDtypeStruct((2, MID // 2 + D // 2), jnp.float32),
            jax.ShapeDtypeStruct((1, 128), jnp.float32),
            jax.ShapeDtypeStruct((1, 1), jnp.float32),
        ],
        in_specs=[pl.BlockSpec(memory_space=pltpu.SMEM)] + vmem(6),
        out_specs=vmem(4),
        name="own_squares",
    )(place, stat_three, stat_four, stat_one, trunk_squares, pyramid, task)


def adam_step(weight, first, second, gradient, factor, rate, decay):
    gradient = gradient * factor
    first_new = 0.5 * first + 0.5 * gradient
    second_new = 0.5 * second + 0.5 * gradient * gradient
    direction = (
        first_new / (1.0 - 0.5**STEP) / (jnp.sqrt(second_new / (1.0 - 0.5**STEP)) + adam_eps)
    )
    return (weight - rate * (direction + decay * weight), first_new, second_new)


def on_device(
    sizes,
    patches,
    labels,
    offset_target,
    offset_valid,
    depth_target,
    lidar_valid,
    crop_mask,
    stem_weight,
    stem_first,
    stem_second,
    bottle_weight,
    bottle_first,
    bottle_second,
    middle_weight,
    middle_first,
    middle_second,
    pyramid_weight,
    pyramid_first,
    pyramid_second,
    project_weight,
    project_first,
    project_second,
    head_weight,
    head_first,
    head_second,
    norm_gains,
    norm_first,
    norm_second,
    task_params,
    task_first,
    task_second,
):
    chan_place = lax.axis_index("chan")
    dp_size = sizes["dp"]
    low = jnp.bfloat16
    crop_field = crop_mask.astype(jnp.float32).reshape(POSITIONS, 1)
    count_masks = jnp.concatenate([crop_mask, offset_valid, lidar_valid], 0)
    half = D // 2
    mid_half = MID // 2

    row_share = bottle_weight.shape[1]
    mid_share = middle_weight.shape[1]
    stem_share = stem_weight.shape[2]
    project_share = project_weight.shape[2]
    head_share = head_weight.shape[0]
    stem_shard = stem_weight.astype(low).reshape(PATCH, stem_share).T
    head_shard = jnp.concatenate(
        [
            project_weight.astype(low).transpose(2, 0, 1).reshape(project_share, 5 * 128),
            jnp.pad(head_weight.astype(low), ((0, 0), (0, 128 - 22))),
        ],
        1,
    )
    bottle_low, middle_low, stem_low, head_low = gather_trunk(
        sizes, bottle_weight.astype(low), middle_weight.astype(low), stem_shard, head_shard
    )
    pyramid_shard = pyramid_weight.astype(low)
    late_shard = pyramid_shard[EARLY_TAPS:]
    pyramid_low = (
        lax.all_gather(pyramid_shard[:EARLY_TAPS], "dp", axis=1, tiled=True),
        lax.all_gather(late_shard, "dp", axis=1, tiled=True),
    )
    own_place = chan_place.reshape(1)
    own_gains = norm_gains.reshape(2, mid_half + half)
    gains = (own_place, own_gains, swap_chan(own_gains))

    def own_bottle(which):
        return lax.dynamic_slice(bottle_low, (which, chan_place * half, 0), (1, half, MID))[0]

    def own_half(values, axis):
        width = values.shape[axis] // 2
        return lax.dynamic_slice_in_dim(values, chan_place * width, width, axis)

    def other_half(values, axis):
        width = values.shape[axis] // 2
        return lax.dynamic_slice_in_dim(values, (1 - chan_place) * width, width, axis)

    columns = jnp.broadcast_to(
        lax.rem(lax.broadcasted_iota(jnp.int32, (POSITIONS, 1), 0), FW).astype(jnp.float32),
        (POSITIONS, 128),
    )
    patch_rows = patches.reshape(POSITIONS, PATCH)
    stream_t, first_pre, stat_one = stem_reduce(
        patch_rows,
        stem_low,
        bottle_low,
        crop_field,
        count_masks,
    )
    stat_one = all_sum(sizes, stat_one, ("dp",), 0)
    hidden_low, hidden_t, second_low = norm_middle(
        first_pre, stat_one, gains, crop_field, middle_low, columns
    )
    expand_pre, stat_two = expand_forward(second_low, bottle_low, crop_field)
    stat_two = all_sum(sizes, stat_two, ("dp",), 1)
    output_low, output_t, pooled = residual_stream(
        patch_rows,
        stem_low,
        expand_pre,
        stat_two,
        stat_one,
        gains,
        crop_field,
    )
    branch_pre, pool_pre, concat_low, project_part = pyramid_forward(
        output_low, pooled, pyramid_low, head_low, columns
    )
    labels, offset_valid, lidar_valid, offset_target, depth_target, stat_one, project_part = (
        lax.optimization_barrier(
            (labels, offset_valid, lidar_valid, offset_target, depth_target, stat_one, project_part)
        )
    )
    offset_field = crop_field[:, 0] * offset_valid.astype(jnp.float32).reshape(POSITIONS)
    lidar_field = crop_field[:, 0] * lidar_valid.astype(jnp.float32).reshape(POSITIONS)
    lane = lax.broadcasted_iota(jnp.int32, (1, 128), 1)
    class_lane = (lane < CLASSES).astype(jnp.float32)
    offset_lane = ((lane >= CLASSES) & (lane < CLASSES + 2)).astype(jnp.float32)
    depth_lane = (lane == CLASSES + 2).astype(jnp.float32)
    onehot = (labels.reshape(POSITIONS, 1) == lane).astype(jnp.float32)
    mask = (
        class_lane * crop_field
        + offset_lane * offset_field[:, None]
        + depth_lane * lidar_field[:, None]
    )
    target = jnp.pad(
        jnp.concatenate([offset_target[0], depth_target], 0).T,
        ((0, 0), (CLASSES, 128 - CLASSES - 3)),
    )
    task_scale = task_params[:3]
    counts = stat_one[2, :3]
    crop_total = counts[0]
    task_weights = jnp.exp(-task_scale) / counts
    lane_rows = jnp.concatenate(
        [
            jnp.pad(task_params[3:], (0, 128 - 22)).reshape(1, 128),
            task_weights[0] * class_lane
            + task_weights[1] * offset_lane
            + task_weights[2] * depth_lane,
            class_lane,
            offset_lane,
            depth_lane,
            jnp.zeros((3, 128), jnp.float32),
        ],
        0,
    )
    feature_low, logit_low, project_grad_low, branch_grads, pool_grad, head_stat = head_step(
        project_part,
        swap_chan(project_part),
        lane_rows,
        onehot,
        target,
        mask,
        head_low,
        branch_pre,
        pool_pre,
    )
    other_parts = []
    later_grads = branch_grads
    for quarter in range(2):
        part = pyramid_field(
            2 - 2 * own_place + quarter,
            half // 2,
            pyramid_low,
            later_grads,
            pool_grad,
            crop_field,
            columns,
        )
        other_parts.append(swap_chan(part))
        later_grads, part = lax.optimization_barrier((later_grads, part))
    own_part, pyramid_grad = own_gradients(
        own_place,
        pyramid_low,
        output_t,
        later_grads,
        pool_grad,
        crop_field,
        columns,
        pooled.reshape(D, 1),
    )
    small_grads = jnp.concatenate(
        [
            dot(project_grad_low, concat_low, (0, 0)).astype(low),
            dot(feature_low, logit_low, (0, 0)).astype(low),
        ],
        1,
    )
    small_rows = project_share * 3
    small_grads = small_grads.reshape(dp_size, small_rows, 256)
    first_other, own_part, pyramid_grad, small_grads = lax.optimization_barrier(
        (other_parts[0], own_part, pyramid_grad, small_grads)
    )
    other_parts, own_part, pyramid_grad = lax.optimization_barrier(
        ([first_other, other_parts[1]], own_part, pyramid_grad)
    )
    pyramid_red = lax.psum_scatter(pyramid_grad, "dp", scatter_dimension=1, tiled=True)

    expand_grad_low, second_part, stat_three = residual_back(
        sizes,
        own_part,
        other_parts,
        expand_pre,
        stat_two,
        stat_one,
        own_gains,
        crop_field,
        head_stat,
        bottle_low,
    )
    second_other = swap_chan(second_part)
    expand_rows = dot(expand_grad_low, second_low, (0, 0)).astype(low)
    second_other, expand_rows, stat_three, own_part = lax.optimization_barrier(
        (second_other, expand_rows, stat_three, own_part)
    )
    expand_sent = swap_chan(other_half(expand_rows, 1))
    upstream_one, second_own, stat_four = first_back(
        own_place,
        second_part,
        second_other,
        middle_low,
        columns,
        first_pre,
        stat_one,
        gains,
        crop_field,
    )
    stat_four = all_sum(sizes, stat_four, ("dp",), 3)
    stat_one, stat_three, stat_four, own_part, expand_sent = lax.optimization_barrier(
        (stat_one, stat_three, stat_four, own_part, expand_sent)
    )
    reduce_grad, stem_grad = late_gradients(
        own_place,
        upstream_one,
        first_pre,
        stat_one,
        stat_four,
        gains,
        crop_field,
        patch_rows.T,
        bottle_low,
        own_part,
        other_parts,
        stream_t,
    )
    middle_grad = middle_weights(hidden_t, second_own, columns)
    expand_own = own_half(expand_rows, 1)
    expand_grad = jnp.where(
        chan_place == 0,
        jnp.concatenate([expand_own, expand_sent], 0),
        jnp.concatenate([expand_sent, expand_own], 0),
    )

    trunk_grads = jnp.concatenate(
        [
            reduce_grad.reshape(dp_size, row_share, 256),
            expand_grad.reshape(dp_size, row_share, 256),
            middle_grad.reshape(9, dp_size, mid_share, 256)
            .transpose(1, 0, 2, 3)
            .reshape(dp_size, 9 * mid_share, 256),
            stem_grad.reshape(dp_size, stem_share * PATCH // 256, 256),
            small_grads,
        ],
        1,
    )
    trunk_red, trunk_squares = scatter_trunk(sizes, trunk_grads)
    start = 2 * row_share + 9 * mid_share
    stem_rows = stem_share * PATCH // 256
    stem_red = trunk_red[start : start + stem_rows].reshape(stem_share, PATCH)
    small_red = trunk_red[start + stem_rows :].reshape(project_share, 768)
    own_squares, norm_grad, task_grad, total_loss = own_squares_of(
        jnp.stack([chan_place, lax.axis_index("dp")]),
        stat_three,
        stat_four,
        stat_one,
        trunk_squares,
        pyramid_red,
        jnp.pad(task_params[:3], (0, 125)).reshape(1, 128),
    )
    total_loss = total_loss.reshape(())
    all_squares = all_sum(sizes, own_squares, ("dp", "chan"), 4)
    grad_norm = jnp.sqrt(jnp.sum(all_squares[0]))

    def turn_stem(part):
        return part.reshape(PATCH, stem_share).T

    def turn_project(part):
        return part.transpose(0, 2, 1)

    def flat_norm(part):
        return part.reshape(2, mid_half + half)

    updated = adam_all(
        row_share,
        mid_share,
        [
            all_squares,
            pyramid_red,
            trunk_red,
            stem_red,
            small_red,
            norm_grad,
            task_grad,
        ],
        [
            (pyramid_weight, pyramid_first, pyramid_second),
            (bottle_weight, bottle_first, bottle_second),
            (middle_weight, middle_first, middle_second),
            tuple(turn_stem(part) for part in (stem_weight, stem_first, stem_second)),
            tuple(turn_project(part) for part in (project_weight, project_first, project_second)),
            (head_weight, head_first, head_second),
            tuple(flat_norm(part) for part in (norm_gains, norm_first, norm_second)),
            tuple(part.reshape(1, 25) for part in (task_params, task_first, task_second)),
        ],
    )
    groups = [updated[3 * group : 3 * group + 3] for group in range(ADAM_GROUPS)]
    new_pyramid, new_bottle, new_middle, new_stem, new_project, new_head, new_norm, new_task = groups
    new_stem = [part.T.reshape(stem_weight.shape) for part in new_stem]
    new_project = [part.transpose(0, 2, 1) for part in new_project]
    new_norm = [part.reshape(norm_gains.shape) for part in new_norm]
    new_task = [part.reshape(25) for part in new_task]
    return (
        total_loss,
        grad_norm,
        new_stem[0],
        new_stem[1],
        new_stem[2],
        new_bottle[0],
        new_bottle[1],
        new_bottle[2],
        new_middle[0],
        new_middle[1],
        new_middle[2],
        new_pyramid[0],
        new_pyramid[1],
        new_pyramid[2],
        new_project[0],
        new_project[1],
        new_project[2],
        new_head[0],
        new_head[1],
        new_head[2],
        new_norm[0],
        new_norm[1],
        new_norm[2],
        new_task[0],
        new_task[1],
        new_task[2],
    )


def solution(mesh):
    return jax.shard_map(
        functools.partial(on_device, dict(mesh.shape)),
        mesh=mesh,
        in_specs=(
            P("dp", None, None),
            P("dp", None),
            P("dp", None, None),
            P("dp", None),
            P("dp", None),
            P("dp", None),
            P("dp", None),
            P(None, "chan", "dp"),
            P(None, "chan", "dp"),
            P(None, "chan", "dp"),
            P(None, "dp", "chan"),
            P(None, "dp", "chan"),
            P(None, "dp", "chan"),
            P(None, "dp", "chan"),
            P(None, "dp", "chan"),
            P(None, "dp", "chan"),
            P(None, "dp", "chan"),
            P(None, "dp", "chan"),
            P(None, "dp", "chan"),
            P(None, "chan", "dp"),
            P(None, "chan", "dp"),
            P(None, "chan", "dp"),
            P("dp", None),
            P("dp", None),
            P("dp", None),
            P(None, "chan", None),
            P(None, "chan", None),
            P(None, "chan", None),
            P(),
            P(),
            P(),
        ),
        out_specs=(
            P(),
            P(),
            P(None, "chan", "dp"),
            P(None, "chan", "dp"),
            P(None, "chan", "dp"),
            P(None, "dp", "chan"),
            P(None, "dp", "chan"),
            P(None, "dp", "chan"),
            P(None, "dp", "chan"),
            P(None, "dp", "chan"),
            P(None, "dp", "chan"),
            P(None, "dp", "chan"),
            P(None, "dp", "chan"),
            P(None, "dp", "chan"),
            P(None, "chan", "dp"),
            P(None, "chan", "dp"),
            P(None, "chan", "dp"),
            P("dp", None),
            P("dp", None),
            P("dp", None),
            P(None, "chan", None),
            P(None, "chan", None),
            P(None, "chan", None),
            P(),
            P(),
            P(),
        ),
        check_vma=False,
    )
```
